32 devices in a mesh: wide: 8 (over z, core), node: 4 (over y, x).
Axes of the slice: x: 2, y: 2, z: 4, core: 2. Of those that a mesh axis runs over, the one named last changes fastest.
Arguments:
- act_in: bfloat16 [2, 16, 128, 2560], P(None, 'wide'), may hold values from -6 to 6
- mixing: bfloat16 [2, 16, 32, 128, 128], P(None, 'wide', 'node'), may hold values from 0 to 0.14941406
- cotangent: bfloat16 [2, 16, 128, 2560], P(None, 'wide'), may hold values from -0.125 to 0.125
- w_value: bfloat16 [2560, 2048], P('wide', 'node'), may hold values from -0.125 to 0.125
- w_out: bfloat16 [2560, 2048], P('wide', 'node'), may hold values from -0.125 to 0.125
Outputs:
- layer_out: bfloat16 [2, 16, 128, 2560], P(None, 'wide', None, 'node')
- grad_value: float32 [2560, 2048], P('wide', 'node')
- grad_out: float32 [2560, 2048], P('wide', 'node')
The draws below stay inside these ranges and needn't reach their ends.
All inputs are finite; a program needn't handle non-finite values.
Results may differ from the reference program's by a relative error of at most 0.0095.
Values may be sent and summed in bfloat16 or wider, within the bound.
No kernel may reach another device: no remote copies, remote signals or barrier semaphores. Data moves between devices by JAX's collectives and lax.ppermute only.
A program may use at most 64 MiB of HBM per device.

```python
import jax
import jax.numpy as jnp
from jax import lax

D = 2560
HEADS = 32
HEAD_DIM = 64
SEQ = 128
MICRO = 2
IMG_DEV = 2
IMAGES = 16
HD_NODE = 512
N_WIDE = 8
N_NODE = 4


def strengthened(array, rng, source, target, blocks, factor):
    owner, partner = [(jnp.arange(array.shape[dim]) // (array.shape[dim] // blocks)).reshape([-1 if axis == dim else 1 for axis in range(array.ndim)]) for dim in (source, target)]
    chosen = jax.random.permutation(rng, blocks)[partner]
    strong = (owner == chosen) | (owner == (partner + blocks // 2) % blocks)
    return jnp.where(strong, factor * array, array)


def block_levels(own_key, extent, pieces, smallest, top_value):
    level = 1.0
    for dim, blocks in pieces:
        heights = jax.random.uniform(jax.random.fold_in(jax.random.fold_in(own_key, 6), dim), (blocks,), jnp.float32, smallest / len(pieces), top_value / len(pieces))
        level = level * jnp.repeat(jnp.exp(heights), extent[dim] // blocks).reshape((-1,) + (1,) * (len(extent) - 1 - dim))
    return level


def normal_values(stream_key, dims, width, limit, pieces=(), dtype=jnp.bfloat16):
    values = width * jax.random.normal(stream_key, dims, jnp.float32)
    if pieces:
        values = values * block_levels(stream_key, dims, pieces, -0.22, 0.18)
    return jnp.clip(values, -limit, limit).astype(dtype)


def bell_draw_with(rng, extent, width, limit, cuts, heavy, kind=jnp.bfloat16):
    array = width * jax.random.normal(rng, extent, jnp.float32)
    if cuts:
        array = array * block_levels(rng, extent, cuts, -0.22, 0.18)
    return jnp.clip(strengthened(array, jax.random.fold_in(rng, 3), *heavy), -limit, limit).astype(kind)


def setup_inputs(seed: int = 0) -> dict:
    keys = jax.random.split(jax.random.key(seed), 6)
    act_in = bell_draw_with(keys[0], (MICRO, IMAGES, SEQ, D), 1.0, 6.0, ((1, 8),), (1, 3, 8, 2.0))
    mixing = jnp.clip(0.14941406 * jax.random.uniform(keys[1], (MICRO, IMAGES, HEADS, SEQ, SEQ), jnp.float32) ** block_levels(keys[1], (MICRO, IMAGES, HEADS, SEQ, SEQ), ((1, 8), (2, 4)), -0.2, 0.2), 0.0, 0.14941406).astype(jnp.bfloat16)
    cotangent = bell_draw_with(keys[2], (MICRO, IMAGES, SEQ, D), (MICRO * IMG_DEV * N_WIDE * SEQ) ** -0.5, 0.125, ((1, 8),), (1, 3, 8, 2.0))
    w_value = normal_values(keys[3], (D, HEADS * HEAD_DIM), D ** -0.5, 0.125, ((0, 8), (1, 4)))
    w_out = normal_values(keys[4], (D, HEADS * HEAD_DIM), (HEADS * HEAD_DIM) ** -0.5, 0.125, ((0, 8), (1, 4)))
    return dict(act_in=act_in, mixing=mixing, cotangent=cotangent, w_value=w_value, w_out=w_out)


def reference(act_in, mixing, cotangent, w_value, w_out):
    width_all = HEADS * HEAD_DIM
    token_count = IMAGES * SEQ
    grad_value = jnp.zeros((D, width_all), jnp.float32)
    grad_out = jnp.zeros((D, width_all), jnp.float32)
    outputs = []
    for micro_index in range(MICRO):
        token_rows = act_in[micro_index].reshape(token_count, D)
        upstream = cotangent[micro_index].reshape(token_count, D)
        weights_mix = mixing[micro_index].astype(jnp.float32)
        value_rows = jnp.dot(token_rows, w_value, preferred_element_type=jnp.float32).astype(jnp.bfloat16)
        value_heads = value_rows.reshape(IMAGES, SEQ, HEADS, HEAD_DIM).astype(jnp.float32)
        mixed_rows = jnp.einsum("ihqk,ikhd->iqhd", weights_mix, value_heads).astype(jnp.bfloat16).reshape(token_count, width_all)
        out_total = jnp.zeros((token_count, D), jnp.float32)
        for group_index in range(N_NODE):
            col_start = group_index * HD_NODE
            partial_value = lax.dot_general(mixed_rows[:, col_start:col_start + HD_NODE], w_out[:, col_start:col_start + HD_NODE], (((1,), (1,)), ((), ())), preferred_element_type=jnp.float32)
            out_total = out_total + lax.optimization_barrier(partial_value.astype(jnp.bfloat16)).astype(jnp.float32)
        outputs.append(out_total.astype(jnp.bfloat16).reshape(IMAGES, SEQ, D))
        d_mixed = jnp.dot(upstream, w_out, preferred_element_type=jnp.float32).astype(jnp.bfloat16)
        d_heads = d_mixed.reshape(IMAGES, SEQ, HEADS, HEAD_DIM).astype(jnp.float32)
        d_value = jnp.einsum("ihqk,iqhd->ikhd", weights_mix, d_heads).astype(jnp.bfloat16).reshape(token_count, width_all)
        grad_value = grad_value + lax.dot_general(token_rows, d_value, (((0,), (0,)), ((), ())), preferred_element_type=jnp.float32)
        grad_out = grad_out + lax.dot_general(upstream, mixed_rows, (((0,), (0,)), ((), ())), preferred_element_type=jnp.float32)
    return jnp.stack(outputs, axis=0), grad_value, grad_out
```

```python
import jax
import jax.numpy as jnp
from jax import lax
from jax.sharding import PartitionSpec as P

HEAD_DIM = 64
F32 = jnp.float32
BF16 = jnp.bfloat16


def make_body(n_wide, n_node):
    pairs = n_wide // 2

    def shift(x, j):
        perm = [
            (2 * s + c, 2 * ((s + j) % pairs) + c) for s in range(pairs) for c in range(2)
        ]
        return lax.ppermute(x, "wide", perm)

    def sibling(x):
        return lax.ppermute(x, "wide", [(i, i ^ 1) for i in range(n_wide)])

    def gather(w, z, c):
        depth = w.shape[0]
        full = jnp.zeros((n_wide * depth, w.shape[1]), w.dtype)
        for j in range(pairs):
            own = w if j == 0 else shift(w, j)
            other = sibling(own)
            row = 2 * lax.rem(z - j + pairs, pairs)
            full = lax.dynamic_update_slice(full, own, ((row + c) * depth, 0))
            full = lax.dynamic_update_slice(full, other, ((row + 1 - c) * depth, 0))
        return full

    def scatter(grad, z, c):
        depth = grad.shape[0] // n_wide
        blocks = grad.reshape(pairs, 2, depth, grad.shape[1])
        mine = lax.dynamic_index_in_dim(blocks, c, 1, keepdims=False)
        theirs = lax.dynamic_index_in_dim(blocks, 1 - c, 1, keepdims=False)
        held = mine + sibling(theirs.astype(BF16)).astype(F32)
        total = lax.dynamic_index_in_dim(held, z, 0, keepdims=False)
        for j in range(1, pairs):
            part = lax.dynamic_index_in_dim(held, lax.rem(z + j, pairs), 0, keepdims=False)
            total = total + shift(part.astype(BF16), j).astype(F32)
        return total

    def node_sum(partial, n):
        tokens, width = partial.shape
        blocks = partial.reshape(tokens, n_node, width // n_node)
        total = lax.dynamic_index_in_dim(blocks, n, 1, keepdims=False).astype(F32)
        for j in range(1, n_node):
            dest = lax.bitwise_xor(n, jnp.int32(j))
            part = lax.dynamic_index_in_dim(blocks, dest, 1, keepdims=False)
            got = lax.ppermute(part, "node", [(i, i ^ j) for i in range(n_node)])
            total = total + got.astype(F32)
        return total.astype(BF16)

    def body(act_in, mixing, cotangent, w_value, w_out):
        wide = lax.axis_index("wide")
        n = lax.axis_index("node")
        z, c = wide // 2, lax.rem(wide, 2)
        cols = w_value.shape[1]
        heads = cols // HEAD_DIM
        micro, images, seq, width = act_in.shape
        groups = micro * images
        tokens = groups * seq
        act = act_in.reshape(tokens, width)
        cot = cotangent.reshape(tokens, width)
        mix = mixing.reshape(groups, heads, seq, seq)

        full_value = gather(w_value, z, c)
        full_out = gather(w_out, z, c)

        value = jnp.dot(act, full_value, preferred_element_type=F32).astype(BF16)
        mixed = (
            jnp.einsum(
                "ihqk,ikhd->iqhd",
                mix,
                value.reshape(groups, seq, heads, HEAD_DIM),
                preferred_element_type=F32,
            )
            .astype(BF16)
            .reshape(tokens, cols)
        )
        term_out = lax.dot_general(
            cot, mixed, (((0,), (0,)), ((), ())), preferred_element_type=F32
        )
        grad_out = scatter(term_out, z, c)

        d_mixed = jnp.dot(cot, full_out, preferred_element_type=F32).astype(BF16)
        d_value = (
            jnp.einsum(
                "ihqk,iqhd->ikhd",
                mix,
                d_mixed.reshape(groups, seq, heads, HEAD_DIM),
                preferred_element_type=F32,
            )
            .astype(BF16)
            .reshape(tokens, cols)
        )
        term_value = lax.dot_general(
            act, d_value, (((0,), (0,)), ((), ())), preferred_element_type=F32
        )
        grad_value = scatter(term_value, z, c)

        partial = lax.dot_general(
            mixed, full_out, (((1,), (1,)), ((), ())), preferred_element_type=F32
        ).astype(BF16)
        layer_out = node_sum(partial, n).reshape(micro, images, seq, width // n_node)
        return layer_out, grad_value, grad_out

    return body


def solution(mesh):
    return jax.shard_map(
        make_body(mesh.shape["wide"], mesh.shape["node"]),
        mesh=mesh,
        in_specs=(
            P(None, "wide", None, None),
            P(None, "wide", "node", None, None),
            P(None, "wide", None, None),
            P("wide", "node"),
            P("wide", "node"),
        ),
        out_specs=(P(None, "wide", None, "node"), P("wide", "node"), P("wide", "node")),
        check_vma=False,
    )
```

```python
import functools

import jax
import jax.numpy as jnp
from jax import lax
from jax.experimental import pallas as pl
from jax.experimental.pallas import tpu as pltpu
from jax.sharding import PartitionSpec as P

HEAD_DIM = 64
F32 = jnp.float32
BF16 = jnp.bfloat16
VMEM_LIMIT = 40 * 1024 * 1024


def dot(a, b, ca=1, cb=0):
    return lax.dot_general(a, b, (((ca,), (cb,)), ((), ())), preferred_element_type=F32)


def begin(pairs, sems):
    copies = [pltpu.make_async_copy(s, d, sems.at[i]) for i, (s, d) in enumerate(pairs)]
    for copy in copies:
        copy.start()
    return copies


def rows_at(index, size):
    return pl.ds(pl.multiple_of(index * size, 16), size)


def gradient_rows(left, right_ref, rows_ref, step):
    width = right_ref.shape[1]
    for start in range(0, width, step):
        part = dot(left, right_ref[:, start : start + step])
        rows_ref[start : start + step, :] = part.T.astype(BF16)


def head_pairs(heads):
    return [(h, min(2, heads - h)) for h in range(0, heads, 2)]


def backward_kernel(n_slots, idx, cot_o, cot_s, mix_o, mix_s, act_o, act_s, *rest):
    slots, rest = rest[:n_slots], rest[n_slots:]
    w_out, rest = rest[0], rest[1:]
    outs, (cot_v, act_v, mix_v, left_v, grad_v, sems) = rest[:-6], rest[-6:]
    tokens, cols = cot_o.shape[0], w_out.shape[1]
    groups, _, seq, _ = mix_o.shape
    heads = mix_v.shape[2]
    depth = slots[0].shape[0]
    here = pl.ds(idx[0], heads)
    copies = begin(
        [(cot_o, cot_v.at[0]), (mix_o.at[:, here], mix_v.at[0])]
        + [(cot_s, cot_v.at[1]), (mix_s.at[:, here], mix_v.at[1])]
        + [(act_o, act_v.at[pl.ds(0, tokens)]), (act_s, act_v.at[pl.ds(tokens, tokens)])],
        sems,
    )
    for j in range(n_slots):
        w_out[rows_at(idx[1 + j], depth), :] = slots[j][...]
    for half in range(2):
        copies[2 * half].wait()
        d_mixed = dot(cot_v[half], w_out[...])
        copies[2 * half + 1].wait()
        for g in range(groups):
            turned = d_mixed[g * seq : (g + 1) * seq, :].T.astype(BF16)
            at = (half * groups + g) * seq
            for h, n in head_pairs(heads):
                part = turned[h * HEAD_DIM : (h + n) * HEAD_DIM, :]
                if n == 2:
                    row = lax.broadcasted_iota(jnp.int32, part.shape, 0)
                    zero = jnp.zeros_like(part)
                    part = jnp.concatenate(
                        [
                            jnp.where(row < HEAD_DIM, part, zero),
                            jnp.where(row < HEAD_DIM, zero, part),
                        ],
                        axis=1,
                    )
                weights = mix_v[half, g, h : h + n].reshape(n * seq, seq)
                left_v[h * HEAD_DIM : (h + n) * HEAD_DIM, at : at + seq] = dot(
                    part, weights
                ).astype(BF16)
    copies[4].wait()
    copies[5].wait()
    gradient_rows(left_v[...], act_v, grad_v, 640)
    for i, out in enumerate(outs):
        out[...] = grad_v[rows_at(idx[1 + n_slots + i], depth), :]


def mixed_kernel(n_slots, idx, act_o, act_s, mix_o, mix_s, *rest):
    slots, (mixed_o, mixed_s, w_v, act_v, mix_v, sems) = rest[:n_slots], rest[n_slots:]
    groups, _, seq, _ = mix_o.shape
    heads = mix_v.shape[2]
    depth = slots[0].shape[0]
    here = pl.ds(idx[0], heads)
    copies = begin(
        [(act_o, act_v.at[0]), (mix_o.at[:, here], mix_v.at[0])]
        + [(act_s, act_v.at[1]), (mix_s.at[:, here], mix_v.at[1])],
        sems,
    )
    for j in range(n_slots):
        w_v[rows_at(idx[1 + j], depth), :] = slots[j][...]
    for half, out in enumerate((mixed_o, mixed_s)):
        copies[2 * half].wait()
        value = dot(act_v[half], w_v[...]).astype(BF16)
        copies[2 * half + 1].wait()
        for g in range(groups):
            for h, n in head_pairs(heads):
                part = value[g * seq : (g + 1) * seq, h * HEAD_DIM : (h + n) * HEAD_DIM]
                weights = mix_v[half, g, h]
                if n == 2:
                    lane = lax.broadcasted_iota(jnp.int32, part.shape, 1)
                    zero = jnp.zeros_like(part)
                    part = jnp.concatenate(
                        [
                            jnp.where(lane < HEAD_DIM, part, zero),
                            jnp.where(lane < HEAD_DIM, zero, part),
                        ],
                        axis=0,
                    )
                    weights = jnp.concatenate([weights, mix_v[half, g, h + 1]], axis=1)
                out[g * seq : (g + 1) * seq, h * HEAD_DIM : (h + n) * HEAD_DIM] = dot(
                    weights, part
                ).astype(BF16)


def grad_out_kernel(idx, cot_o, cot_s, mixed_o, mixed_s, *rest):
    outs, (cot_v, left_v, grad_v, sems) = rest[:-4], rest[-4:]
    tokens, _ = cot_o.shape
    depth = outs[0].shape[0]
    copies = begin(
        [(cot_o, cot_v.at[pl.ds(0, tokens)]), (cot_s, cot_v.at[pl.ds(tokens, tokens)])], sems
    )
    left_v[:, :tokens] = mixed_o[...].astype(F32).T.astype(BF16)
    left_v[:, tokens:] = mixed_s[...].astype(F32).T.astype(BF16)
    copies[0].wait()
    copies[1].wait()
    gradient_rows(left_v[...], cot_v, grad_v, 640)
    for i, out in enumerate(outs):
        out[...] = grad_v[rows_at(idx[i], depth), :]


def terms_kernel(n_node, idx, mixed_o, mixed_r, w_o, w_r, *outs):
    depth = w_o.shape[0] // n_node
    half = mixed_o.shape[0] // 2
    for j in range(n_node):
        rows = rows_at(idx[j], depth)
        term = dot(mixed_o[...], w_o[rows, :], 1, 1) + dot(mixed_r[...], w_r[rows, :], 1, 1)
        term = term.astype(BF16)
        if n_node != 4:
            outs[j][...] = term
            continue
        along_x, along_y, kept = outs
        first, second = term[:half], term[half:]
        if j == 0:
            kept[0], kept[2] = first, second
        elif j == 1:
            along_x[0], kept[3] = first, second
        elif j == 2:
            kept[1], along_y[0] = first, second
        else:
            along_x[1], along_y[1] = first, second


ANY = pl.BlockSpec(memory_space=pl.ANY)
SMEM = pl.BlockSpec(memory_space=pltpu.SMEM)
VMEM = pl.BlockSpec(memory_space=pltpu.VMEM)


def call(kernel, name, in_specs, out_shapes, scratch, flops):
    return pl.pallas_call(
        kernel,
        name=name,
        in_specs=in_specs,
        out_specs=[VMEM] * len(out_shapes),
        out_shape=[jax.ShapeDtypeStruct(s, BF16) for s in out_shapes],
        scratch_shapes=scratch,
        compiler_params=pltpu.CompilerParams(vmem_limit_bytes=VMEM_LIMIT),
        cost_estimate=pl.CostEstimate(flops=flops, bytes_accessed=12 << 20, transcendentals=0),
    )


def after(x, *others):
    return lax.optimization_barrier((x, *others))[0]


def make_body(n_wide, n_node):
    planes = n_wide // 2
    line4 = planes == 4

    def move(x, pairs):
        return lax.ppermute(
            x, "wide", [(2 * s + c, 2 * d + c) for s, d in pairs for c in range(2)]
        )

    def sibling(x):
        return lax.ppermute(x, "wide", [(i, i ^ 1) for i in range(n_wide)])

    def flip(x, j):
        return lax.ppermute(x, "node", [(i, i ^ j) for i in range(n_node)])

    def column_half(w, c):
        cols = w.shape[1] // 2
        mine = lax.dynamic_slice_in_dim(w, c * cols, cols, 1)
        got = sibling(lax.dynamic_slice_in_dim(w, (1 - c) * cols, cols, 1))
        low = jnp.where(c == 0, mine, got)
        high = jnp.where(c == 0, got, mine)
        return jnp.concatenate([low, high], axis=0)

    def gather_first(u):
        if not line4:
            return None
        across = move(u, [(0, 2), (1, 3), (2, 0), (3, 1)])
        ends = move(u, [(1, 0), (2, 3)])
        return across, ends

    def gather_rest(u, firsts, z):
        if not line4:
            return [u] + [
                move(u, [(s, (s - j) % planes) for s in range(planes)])
                for j in range(1, planes)
            ]
        across, ends = firsts
        up = move(jnp.where(z == 2, across, u), [(0, 1), (1, 2), (2, 3)])
        down = move(jnp.where(z == 1, across, u), [(3, 2), (2, 1), (1, 0)])
        after_z = jnp.where(z == 0, ends, jnp.where(z == 3, up, down))
        before_z = jnp.where(z == 0, down, jnp.where(z == 3, ends, up))
        return [u, after_z, across, before_z]

    def send_planes(z):
        if not line4:
            return [lax.rem(z + j, planes) for j in range(planes)]
        up = jnp.where(z == 0, 3, jnp.minimum(z + 1, 3))
        down = jnp.where(z == 3, 0, jnp.maximum(z - 1, 0))
        near = jnp.where(z == 0, 1, jnp.where(z == 3, 2, z))
        return [z, up, down, near, lax.rem(z + 2, 4)]

    def scatter(blocks, z):
        if not line4:
            total = blocks[0].astype(F32)
            for j in range(1, planes):
                got = move(blocks[j], [(s, (s + j) % planes) for s in range(planes)])
                total = total + got.astype(F32)
            return total
        own, up, down, near, far = blocks
        up = move(up, [(0, 1), (1, 2), (2, 3)])
        down = move(down, [(3, 2), (2, 1), (1, 0)])
        near = move(near, [(0, 1), (3, 2)])
        add = jnp.where(z == 1, up, jnp.where(z == 2, down, jnp.zeros_like(up)))
        far = move(
            (far.astype(F32) + add.astype(F32)).astype(BF16),
            [(0, 2), (1, 3), (2, 0), (3, 1)],
        )
        total = own.astype(F32) + jnp.where(z <= 1, down, up).astype(F32)
        return total + near.astype(F32) + far.astype(F32)

    def finish(total, c):
        rows = total.shape[0] // 2
        mine = lax.dynamic_slice_in_dim(total, c * rows, rows, 0)
        got = sibling(lax.dynamic_slice_in_dim(total, (1 - c) * rows, rows, 0))
        low = jnp.where(c == 0, mine, got)
        high = jnp.where(c == 0, got, mine)
        return jnp.concatenate([low, high], axis=1)

    def body(act_in, mixing, cotangent, w_value, w_out):
        wide = lax.axis_index("wide")
        n = lax.axis_index("node")
        z, c = wide // 2, lax.rem(wide, 2)
        micro, images, seq, width = act_in.shape
        groups = micro * images
        tokens = groups * seq
        cols = w_value.shape[1] // 2
        heads = cols // HEAD_DIM
        depth = width // planes
        act = act_in.reshape(tokens, width)
        cot = cotangent.reshape(tokens, width)
        mix = mixing.reshape(groups, 2 * heads, seq, seq)
        flops = 4 * tokens * width * cols

        u_out = column_half(w_out, c)
        u_value = column_half(w_value, c)
        out_first = gather_first(u_out)
        cot_s = sibling(after(cot, u_out))
        mix_s = sibling(after(mix, u_out))
        act_s = sibling(after(act, u_out))
        out_slots = gather_rest(u_out, out_first, z)
        if line4:
            u_value = after(u_value, out_first[0])
        value_first = gather_first(u_value)
        value_slots = gather_rest(u_value, value_first, z)

        slot_planes = [lax.rem(z + j, planes) for j in range(planes)]
        sends = send_planes(z)
        first_head = c * heads
        idx_back = jnp.stack([first_head, *slot_planes, *sends]).astype(jnp.int32)
        idx_mixed = jnp.stack([first_head, *slot_planes]).astype(jnp.int32)
        idx_send = jnp.stack(sends).astype(jnp.int32)
        idx_node = jnp.stack([lax.bitwise_xor(n, jnp.int32(j)) for j in range(n_node)])

        mix_scratch = pltpu.VMEM((2, groups, heads, seq, seq), BF16)
        both = pltpu.VMEM((2 * tokens, width), BF16)
        halves = pltpu.VMEM((2, tokens, width), BF16)
        left = pltpu.VMEM((cols, 2 * tokens), BF16)
        rows = pltpu.VMEM((width, cols), BF16)
        send_shapes = [(depth, cols)] * len(sends)

        w_full, *back_sends = call(
            functools.partial(backward_kernel, planes),
            "backward",
            [SMEM] + [ANY] * 6 + [VMEM] * planes,
            [(width, cols)] + send_shapes,
            [halves, both, mix_scratch, left, rows, pltpu.SemaphoreType.DMA((6,))],
            2 * flops,
        )(idx_back, cot, cot_s, mix, mix_s, act, act_s, *out_slots)
        w_full_s = sibling(w_full)
        grad_value = scatter(back_sends, z)

        mixed_o, mixed_s = call(
            functools.partial(mixed_kernel, planes),
            "mixed",
            [SMEM] + [ANY] * 4 + [VMEM] * planes,
            [(tokens, cols)] * 2,
            [rows, halves, mix_scratch, pltpu.SemaphoreType.DMA((4,))],
            flops,
        )(idx_mixed, act, act_s, mix, mix_s, *value_slots)
        mixed_r = sibling(mixed_s)
        out_sends = call(
            grad_out_kernel,
            "grad_out",
            [SMEM] + [ANY] * 2 + [VMEM] * 2,
            send_shapes,
            [both, left, rows, pltpu.SemaphoreType.DMA((2,))],
            flops,
        )(idx_send, cot, cot_s, mixed_o, mixed_s)
        grad_out = scatter(out_sends, z)

        part = width // n_node
        half = tokens // 2
        if n_node == 4:
            term_shapes = [(2, half, part), (2, half, part), (4, half, part)]
        else:
            term_shapes = [(tokens, part)] * n_node
        terms = call(
            functools.partial(terms_kernel, n_node),
            "terms",
            [SMEM] + [VMEM] * 4,
            term_shapes,
            [],
            flops,
        )(idx_node, mixed_o, mixed_r, w_full, w_full_s)
        if n_node == 4:
            along_x, along_y, kept = terms
            kept = kept.astype(F32)
            got_x = flip(along_x, 1).astype(F32)
            got_y = flip(along_y, 2).astype(F32)
            last_y = flip((kept[1] + got_x[1]).astype(BF16), 2)
            last_x = flip((kept[3] + got_y[1]).astype(BF16), 1)
            layer_out = jnp.concatenate(
                [
                    kept[0] + got_x[0] + last_y.astype(F32),
                    kept[2] + got_y[0] + last_x.astype(F32),
                ],
                axis=0,
            )
        else:
            layer_out = terms[0].astype(F32)
            for j in range(1, n_node):
                layer_out = layer_out + flip(terms[j], j).astype(F32)
        layer_out = layer_out.astype(BF16).reshape(micro, images, seq, part)
        return layer_out, finish(grad_value, c), finish(grad_out, c)

    return body


def solution(mesh):
    return jax.shard_map(
        make_body(mesh.shape["wide"], mesh.shape["node"]),
        mesh=mesh,
        in_specs=(
            P(None, "wide", None, None),
            P(None, "wide", "node", None, None),
            P(None, "wide", None, None),
            P("wide", "node"),
            P("wide", "node"),
        ),
        out_specs=(P(None, "wide", None, "node"), P("wide", "node"), P("wide", "node")),
        check_vma=False,
    )
```

```python
import functools
import math

import jax
import jax.numpy as jnp
from jax import lax
from jax.experimental import pallas as pl
from jax.experimental.pallas import tpu as pltpu
from jax.sharding import PartitionSpec as P

HEAD_DIM = 64
F32 = jnp.float32
BF16 = jnp.bfloat16
VMEM_LIMIT = 40 * 1024 * 1024


def dot(a, b, ca=1, cb=0):
    return lax.dot_general(a, b, (((ca,), (cb,)), ((), ())), preferred_element_type=F32)


def begin(pairs, sems):
    copies = [pltpu.make_async_copy(s, d, sems.at[i]) for i, (s, d) in enumerate(pairs)]
    for copy in copies:
        copy.start()
    return copies


def rows_at(index, size):
    return pl.ds(pl.multiple_of(index * size, math.gcd(size, 16)), size)


def place(idx, slots, w_ref):
    core = idx[0]
    for j, slot in enumerate(slots):
        depth = slot.shape[0] // 2

        @pl.when(idx[2 + 2 * j] == 1)
        def _(slot=slot, depth=depth, plane=idx[1 + 2 * j]):
            mine, other = slot[:depth, :], slot[depth:, :]
            low = jnp.where(core == 0, mine, other)
            high = jnp.where(core == 0, other, mine)
            w_ref[rows_at(plane, 2 * depth), :] = jnp.concatenate([low, high], axis=0)


def hand_out(idx, base, grad_v, outs):
    core = idx[0]
    for i, out in enumerate(outs):
        depth = out.shape[1]
        block = grad_v[rows_at(idx[base + i], 2 * depth), :]
        low, high = block[:depth], block[depth:]
        out[0] = jnp.where(core == 0, low, high)
        out[1] = jnp.where(core == 0, high, low)


def gradient_rows(left, right_ref, rows_ref, step):
    width = right_ref.shape[1]
    for start in range(0, width, step):
        part = dot(left, right_ref[:, start : start + step])
        rows_ref[start : start + step, :] = part.T.astype(BF16)


def head_pairs(heads):
    return [(h, min(2, heads - h)) for h in range(0, heads, 2)]


def backward_kernel(n_slots, idx, cot_o, cot_s, mix_o, mix_s, act_o, act_s, *rest):
    slots, rest = rest[:n_slots], rest[n_slots:]
    w_out, rest = rest[0], rest[1:]
    outs, (cot_v, act_v, mix_v, left_v, grad_v, sems) = rest[:-6], rest[-6:]
    tokens, cols = cot_o.shape[0], w_out.shape[1]
    groups, _, seq, _ = mix_o.shape
    heads = mix_v.shape[2]
    here = pl.ds(idx[0] * heads, heads)
    copies = begin(
        [(cot_o, cot_v.at[0]), (mix_o.at[:, here], mix_v.at[0])]
        + [(cot_s, cot_v.at[1]), (mix_s.at[:, here], mix_v.at[1])]
        + [(act_o, act_v.at[pl.ds(0, tokens)]), (act_s, act_v.at[pl.ds(tokens, tokens)])],
        sems,
    )
    place(idx, slots, w_out)
    for half in range(2):
        copies[2 * half].wait()
        d_mixed = dot(cot_v[half], w_out[...])
        copies[2 * half + 1].wait()
        for g in range(groups):
            turned = d_mixed[g * seq : (g + 1) * seq, :].T.astype(BF16)
            at = (half * groups + g) * seq
            for h, n in head_pairs(heads):
                part = turned[h * HEAD_DIM : (h + n) * HEAD_DIM, :]
                if n == 2:
                    row = lax.broadcasted_iota(jnp.int32, part.shape, 0)
                    zero = jnp.zeros_like(part)
                    part = jnp.concatenate(
                        [
                            jnp.where(row < HEAD_DIM, part, zero),
                            jnp.where(row < HEAD_DIM, zero, part),
                        ],
                        axis=1,
                    )
                weights = mix_v[half, g, h : h + n].reshape(n * seq, seq)
                left_v[h * HEAD_DIM : (h + n) * HEAD_DIM, at : at + seq] = dot(
                    part, weights
                ).astype(BF16)
    copies[4].wait()
    copies[5].wait()
    gradient_rows(left_v[...], act_v, grad_v, 640)
    hand_out(idx, 1 + 2 * n_slots, grad_v, outs)


def mixed_kernel(n_slots, idx, act_o, act_s, mix_o, mix_s, *rest):
    slots, (mixed_o, mixed_s, w_v, act_v, mix_v, sems) = rest[:n_slots], rest[n_slots:]
    groups, _, seq, _ = mix_o.shape
    heads = mix_v.shape[2]
    here = pl.ds(idx[0] * heads, heads)
    copies = begin(
        [(act_o, act_v.at[0]), (mix_o.at[:, here], mix_v.at[0])]
        + [(act_s, act_v.at[1]), (mix_s.at[:, here], mix_v.at[1])],
        sems,
    )
    place(idx, slots, w_v)
    for half, out in enumerate((mixed_o, mixed_s)):
        copies[2 * half].wait()
        value = dot(act_v[half], w_v[...]).astype(BF16)
        copies[2 * half + 1].wait()
        for g in range(groups):
            for h, n in head_pairs(heads):
                part = value[g * seq : (g + 1) * seq, h * HEAD_DIM : (h + n) * HEAD_DIM]
                weights = mix_v[half, g, h]
                if n == 2:
                    lane = lax.broadcasted_iota(jnp.int32, part.shape, 1)
                    zero = jnp.zeros_like(part)
                    part = jnp.concatenate(
                        [
                            jnp.where(lane < HEAD_DIM, part, zero),
                            jnp.where(lane < HEAD_DIM, zero, part),
                        ],
                        axis=0,
                    )
                    weights = jnp.concatenate([weights, mix_v[half, g, h + 1]], axis=1)
                out[g * seq : (g + 1) * seq, h * HEAD_DIM : (h + n) * HEAD_DIM] = dot(
                    weights, part
                ).astype(BF16)


def grad_out_kernel(idx, cot_o, cot_s, mixed_o, mixed_s, *rest):
    outs, (cot_v, left_v, grad_v, sems) = rest[:-4], rest[-4:]
    tokens, _ = cot_o.shape
    copies = begin(
        [(cot_o, cot_v.at[pl.ds(0, tokens)]), (cot_s, cot_v.at[pl.ds(tokens, tokens)])], sems
    )
    left_v[:, :tokens] = mixed_o[...].astype(F32).T.astype(BF16)
    left_v[:, tokens:] = mixed_s[...].astype(F32).T.astype(BF16)
    copies[0].wait()
    copies[1].wait()
    gradient_rows(left_v[...], cot_v, grad_v, 640)
    hand_out(idx, 1, grad_v, outs)


def terms_kernel(n_node, idx, mixed_o, mixed_r, w_o, w_r, *outs):
    depth = w_o.shape[0] // n_node
    half = mixed_o.shape[0] // 2
    for j in range(n_node):
        rows = rows_at(idx[j], depth)
        term = dot(mixed_o[...], w_o[rows, :], 1, 1) + dot(mixed_r[...], w_r[rows, :], 1, 1)
        term = term.astype(BF16)
        if n_node != 4:
            outs[j][...] = term
            continue
        along_x, along_y, kept = outs
        first, second = term[:half], term[half:]
        if j == 0:
            kept[0], kept[2] = first, second
        elif j == 1:
            along_x[0], kept[3] = first, second
        elif j == 2:
            kept[1], along_y[0] = first, second
        else:
            along_x[1], along_y[1] = first, second


ANY = pl.BlockSpec(memory_space=pl.ANY)
SMEM = pl.BlockSpec(memory_space=pltpu.SMEM)
VMEM = pl.BlockSpec(memory_space=pltpu.VMEM)


def call(kernel, name, in_specs, out_shapes, scratch, flops):
    return pl.pallas_call(
        kernel,
        name=name,
        in_specs=in_specs,
        out_specs=[VMEM] * len(out_shapes),
        out_shape=[jax.ShapeDtypeStruct(s, BF16) for s in out_shapes],
        scratch_shapes=scratch,
        compiler_params=pltpu.CompilerParams(vmem_limit_bytes=VMEM_LIMIT),
        cost_estimate=pl.CostEstimate(flops=0, bytes_accessed=1024, transcendentals=0),
    )


def after(x, *others):
    return lax.optimization_barrier((x, *others))[0]


def make_body(n_wide, n_node):
    planes = n_wide // 2
    line4 = planes == 4

    def move(x, pairs):
        return lax.ppermute(
            x, "wide", [(2 * s + c, 2 * d + c) for s, d in pairs for c in range(2)]
        )

    def sibling(x):
        return lax.ppermute(x, "wide", [(i, i ^ 1) for i in range(n_wide)])

    def flip(x, j):
        return lax.ppermute(x, "node", [(i, i ^ j) for i in range(n_node)])

    def swap_halves(weights, c):
        cols = weights[0].shape[1] // 2
        low = jnp.stack([w[:, :cols] for w in weights])
        high = jnp.stack([w[:, cols:] for w in weights])
        got = sibling(jnp.where(c == 0, high, low))
        mine = jnp.where(c == 0, low, high)
        return [jnp.concatenate([mine[i], got[i]], axis=0) for i in range(len(weights))]

    def gather_first(u):
        if not line4:
            return [move(u, [(s, (s - j) % planes) for s in range(planes)]) for j in range(1, planes)]
        return [move(u, [(0, 2), (1, 3), (2, 0), (3, 1)]), move(u, [(1, 0), (2, 3)])]

    def gather_rest(u, firsts):
        if not line4:
            return [u, *firsts]
        across, ends = firsts
        up = move(u, [(0, 1), (1, 2)])
        down = move(u, [(3, 2), (2, 1)])
        on = move(across, [(2, 3), (1, 0)])
        return [u, across, ends, on, up, down]

    def slot_planes(z):
        if not line4:
            return [x for j in range(planes) for x in (lax.rem(z + j, planes), 1)]
        edge = ((z == 0) | (z == 3)).astype(jnp.int32)
        ends = jnp.where(z == 0, 1, 2)
        on = jnp.where(z == 0, 3, 0)
        up, down = jnp.maximum(z - 1, 0), jnp.minimum(z + 1, 3)
        return [z, 1, lax.rem(z + 2, 4), 1, ends, edge, on, edge, up, 1 - edge, down, 1 - edge]

    def send_planes(z):
        if not line4:
            return [lax.rem(z + j, planes) for j in range(planes)]
        up = jnp.where(z == 0, 3, jnp.minimum(z + 1, 3))
        down = jnp.where(z == 3, 0, jnp.maximum(z - 1, 0))
        near = jnp.where(z == 0, 1, jnp.where(z == 3, 2, z))
        return [z, up, down, near, lax.rem(z + 2, 4)]

    def scatter_first(blocks):
        _, up, down, _, _ = blocks
        return move(up, [(0, 1), (1, 2), (2, 3)]), move(down, [(3, 2), (2, 1), (1, 0)])

    def scatter_far(blocks, firsts, z):
        up, down = firsts
        add = jnp.where(z == 1, up, jnp.where(z == 2, down, jnp.zeros_like(up)))
        return (blocks[4].astype(F32) + add.astype(F32)).astype(BF16)

    def scatter_near(blocks, firsts, z):
        up, down = firsts
        near = move(after(blocks[3], up, down), [(0, 1), (3, 2)])
        total = blocks[0].astype(F32) + jnp.where(z <= 1, down, up).astype(F32)
        return total + near.astype(F32)

    def join(mine, other, c):
        low = jnp.where(c == 0, mine, other)
        high = jnp.where(c == 0, other, mine)
        return jnp.concatenate([low, high], axis=1)

    def scatter_rest(blocks, firsts, far, z, c, last):
        if last:
            far_other = lax.ppermute(
                far[1],
                "wide",
                [(2 * s + k, 2 * ((s + 2) % 4) + 1 - k) for s in range(4) for k in range(2)],
            )
            far_mine = move(far[0], [(s, (s + 2) % 4) for s in range(4)])
            total = scatter_near(blocks, firsts, z)
            other = sibling(total[1])
            return join(total[0] + far_mine.astype(F32), other + far_other.astype(F32), c)
        far = move(far, [(s, (s + 2) % 4) for s in range(4)])
        return scatter_near(blocks, firsts, z) + far.astype(F32)

    def scatter_ring(blocks, c):
        total = blocks[0].astype(F32)
        for j in range(1, planes):
            got = move(blocks[j], [(s, (s + j) % planes) for s in range(planes)])
            total = total + got.astype(F32)
        return join(total[0], sibling(total[1]), c)

    def body(act_in, mixing, cotangent, w_value, w_out):
        wide = lax.axis_index("wide")
        n = lax.axis_index("node")
        z, c = wide // 2, lax.rem(wide, 2)
        micro, images, seq, width = act_in.shape
        groups = micro * images
        tokens = groups * seq
        cols = w_value.shape[1] // 2
        heads = cols // HEAD_DIM
        depth = width // planes
        act = act_in.reshape(tokens, width)
        cot = cotangent.reshape(tokens, width)
        mix = mixing.reshape(groups, 2 * heads, seq, seq)
        flops = 4 * tokens * width * cols

        u_out, u_value = swap_halves([w_out, w_value], c)
        out_first = gather_first(u_out)
        cot_s = sibling(after(cot, u_out))
        mix_s = sibling(after(mix, u_out))
        act_s = sibling(after(act, u_out))
        out_first = list(lax.optimization_barrier((*out_first, cot_s, mix_s, act_s)))
        *out_first, cot_s, mix_s, act_s = out_first
        out_slots = gather_rest(after(u_out, out_first[0]), out_first)
        u_value = after(u_value, out_first[0])
        value_first = gather_first(u_value)

        info = slot_planes(z)
        sends = send_planes(z)
        n_slots = len(out_slots)
        idx_back = jnp.stack([c, *info, *sends]).astype(jnp.int32)
        idx_mixed = jnp.stack([c, *info]).astype(jnp.int32)
        idx_send = jnp.stack([c, *sends]).astype(jnp.int32)
        idx_node = jnp.stack([lax.bitwise_xor(n, jnp.int32(j)) for j in range(n_node)])

        mix_scratch = pltpu.VMEM((2, groups, heads, seq, seq), BF16)
        both = pltpu.VMEM((2 * tokens, width), BF16)
        halves = pltpu.VMEM((2, tokens, width), BF16)
        left = pltpu.VMEM((cols, 2 * tokens), BF16)
        rows = pltpu.VMEM((width, cols), BF16)
        send_shapes = [(2, depth // 2, cols)] * len(sends)

        w_full, *back_sends = call(
            functools.partial(backward_kernel, n_slots),
            "backward",
            [SMEM] + [ANY] * 6 + [VMEM] * n_slots,
            [(width, cols)] + send_shapes,
            [halves, both, mix_scratch, left, rows, pltpu.SemaphoreType.DMA((6,))],
            2 * flops,
        )(idx_back, cot, cot_s, mix, mix_s, act, act_s, *out_slots)
        if line4:
            value_first = [after(x, back_sends[0]) for x in value_first]
            value_slots = gather_rest(after(u_value, back_sends[0]), value_first)
            back_firsts = scatter_first(back_sends)
            far = scatter_far(back_sends, back_firsts, z)
            value_slots = list(lax.optimization_barrier((*value_slots, far)))[:-1]
            w_full_s = sibling(after(w_full, value_slots[0]))
        else:
            value_slots = gather_rest(u_value, value_first)
            w_full_s = sibling(w_full)

        mixed_o, mixed_s = call(
            functools.partial(mixed_kernel, n_slots),
            "mixed",
            [SMEM] + [ANY] * 4 + [VMEM] * n_slots,
            [(tokens, cols)] * 2,
            [rows, halves, mix_scratch, pltpu.SemaphoreType.DMA((4,))],
            flops,
        )(idx_mixed, act, act_s, mix, mix_s, *value_slots)
        mixed_r = sibling(mixed_s)
        out_sends = call(
            grad_out_kernel,
            "grad_out",
            [SMEM] + [ANY] * 2 + [VMEM] * 2,
            send_shapes,
            [both, left, rows, pltpu.SemaphoreType.DMA((2,))],
            flops,
        )(idx_send, cot, cot_s, mixed_o, mixed_s)
        part = width // n_node
        half = tokens // 2
        if n_node == 4:
            term_shapes = [(2, half, part), (2, half, part), (4, half, part)]
        else:
            term_shapes = [(tokens, part)] * n_node
        terms = call(
            functools.partial(terms_kernel, n_node),
            "terms",
            [SMEM] + [VMEM] * 4,
            term_shapes,
            [],
            flops,
        )(idx_node, mixed_o, mixed_r, w_full, w_full_s)
        if line4:
            grad_value = scatter_rest(back_sends, back_firsts, far, z, c, False)
            *out_sends, grad_value, mixed_r = lax.optimization_barrier(
                (*out_sends, grad_value, mixed_r)
            )
            out_firsts = scatter_first(out_sends)
            *out_firsts, _ = lax.optimization_barrier((*out_firsts, terms[0]))
            out_far = scatter_far(out_sends, out_firsts, z)
            grad_out = scatter_rest(out_sends, out_firsts, out_far, z, c, True)
            grad_value = join(grad_value[0], sibling(grad_value[1]), c)
        else:
            grad_value = scatter_ring(back_sends, c)
            grad_out = scatter_ring(out_sends, c)

        if n_node == 4:
            along_x, along_y, kept = terms
            kept = kept.astype(F32)
            got_x = flip(along_x, 1).astype(F32)
            got_y = flip(along_y, 2).astype(F32)
            last_y = flip((kept[1] + got_x[1]).astype(BF16), 2)
            last_x = flip((kept[3] + got_y[1]).astype(BF16), 1)
            layer_out = jnp.concatenate(
                [
                    kept[0] + got_x[0] + last_y.astype(F32),
                    kept[2] + got_y[0] + last_x.astype(F32),
                ],
                axis=0,
            )
        else:
            layer_out = terms[0].astype(F32)
            for j in range(1, n_node):
                layer_out = layer_out + flip(terms[j], j).astype(F32)
        layer_out = layer_out.astype(BF16).reshape(micro, images, seq, part)
        return layer_out, grad_value, grad_out

    return body


def solution(mesh):
    return jax.shard_map(
        make_body(mesh.shape["wide"], mesh.shape["node"]),
        mesh=mesh,
        in_specs=(
            P(None, "wide", None, None),
            P(None, "wide", "node", None, None),
            P(None, "wide", None, None),
            P("wide", "node"),
            P("wide", "node"),
        ),
        out_specs=(P(None, "wide", None, "node"), P("wide", "node"), P("wide", "node")),
        check_vma=False,
    )
```

```python
import functools
import math

import jax
import jax.numpy as jnp
from jax import lax
from jax.experimental import pallas as pl
from jax.experimental.pallas import tpu as pltpu
from jax.sharding import PartitionSpec as P

HEAD_DIM = 64
F32 = jnp.float32
BF16 = jnp.bfloat16
VMEM_LIMIT = 56 * 1024 * 1024


def dot(a, b, ca=1, cb=0):
    return lax.dot_general(a, b, (((ca,), (cb,)), ((), ())), preferred_element_type=F32)


def begin(pairs, sems):
    copies = [pltpu.make_async_copy(s, d, sems.at[i]) for i, (s, d) in enumerate(pairs)]
    for copy in copies:
        copy.start()
    return copies


def rows_at(index, size):
    return pl.ds(pl.multiple_of(index * size, math.gcd(size, 16)), size)


def place(idx, slots, w_ref):
    core = idx[0]
    for j, slot in enumerate(slots):
        depth = slot.shape[0] // 2

        @pl.when(idx[2 + 2 * j] == 1)
        def _(slot=slot, depth=depth, plane=idx[1 + 2 * j]):
            mine, other = slot[:depth, :], slot[depth:, :]
            low = jnp.where(core == 0, mine, other)
            high = jnp.where(core == 0, other, mine)
            w_ref[rows_at(plane, 2 * depth), :] = jnp.concatenate([low, high], axis=0)


def hand_out(idx, base, grad_v, outs):
    core = idx[0]
    for i, out in enumerate(outs):
        depth = out.shape[1]
        block = grad_v[rows_at(idx[base + i], 2 * depth), :]
        low, high = block[:depth], block[depth:]
        out[0] = jnp.where(core == 0, low, high)
        out[1] = jnp.where(core == 0, high, low)


def gradient_rows(left, right_ref, rows_ref, step):
    width = right_ref.shape[1]
    for start in range(0, width, step):
        part = dot(left, right_ref[:, start : start + step])
        rows_ref[start : start + step, :] = part.T.astype(BF16)


def head_pairs(heads):
    return [(h, min(2, heads - h)) for h in range(0, heads, 2)]


def backward_kernel(n_slots, idx, cot_o, cot_s, mix_o, mix_s, act_o, act_s, *rest):
    slots, rest = rest[:n_slots], rest[n_slots:]
    w_out, rest = rest[0], rest[1:]
    outs, (cot_v, act_v, mix_v, left_v, grad_v, sems) = rest[:-6], rest[-6:]
    tokens, cols = cot_o.shape[0], w_out.shape[1]
    groups, _, seq, _ = mix_o.shape
    heads = mix_v.shape[2]
    here = pl.ds(idx[0] * heads, heads)
    copies = begin(
        [(cot_o, cot_v.at[0]), (mix_o.at[:, here], mix_v.at[0])]
        + [(cot_s, cot_v.at[1]), (mix_s.at[:, here], mix_v.at[1])]
        + [(act_o, act_v.at[pl.ds(0, tokens)]), (act_s, act_v.at[pl.ds(tokens, tokens)])],
        sems,
    )
    place(idx, slots, w_out)
    for half in range(2):
        copies[2 * half].wait()
        d_mixed = dot(cot_v[half], w_out[...])
        copies[2 * half + 1].wait()
        for g in range(groups):
            turned = d_mixed[g * seq : (g + 1) * seq, :].T.astype(BF16)
            at = (half * groups + g) * seq
            for h, n in head_pairs(heads):
                part = turned[h * HEAD_DIM : (h + n) * HEAD_DIM, :]
                if n == 2:
                    row = lax.broadcasted_iota(jnp.int32, part.shape, 0)
                    zero = jnp.zeros_like(part)
                    part = jnp.concatenate(
                        [
                            jnp.where(row < HEAD_DIM, part, zero),
                            jnp.where(row < HEAD_DIM, zero, part),
                        ],
                        axis=1,
                    )
                weights = mix_v[half, g, h : h + n].reshape(n * seq, seq)
                left_v[h * HEAD_DIM : (h + n) * HEAD_DIM, at : at + seq] = dot(
                    part, weights
                ).astype(BF16)
    copies[4].wait()
    copies[5].wait()
    gradient_rows(left_v[...], act_v, grad_v, 640)
    hand_out(idx, 1 + 2 * n_slots, grad_v, outs)


def mixed_kernel(n_slots, idx, act_o, act_s, mix_o, mix_s, *rest):
    slots, (mixed_o, mixed_s, w_v, act_v, mix_v, sems) = rest[:n_slots], rest[n_slots:]
    groups, _, seq, _ = mix_o.shape
    heads = mix_v.shape[2]
    here = pl.ds(idx[0] * heads, heads)
    copies = begin(
        [(act_o, act_v.at[0]), (mix_o.at[:, here], mix_v.at[0])]
        + [(act_s, act_v.at[1]), (mix_s.at[:, here], mix_v.at[1])],
        sems,
    )
    place(idx, slots, w_v)
    for half, out in enumerate((mixed_o, mixed_s)):
        copies[2 * half].wait()
        value = dot(act_v[half], w_v[...]).astype(BF16)
        copies[2 * half + 1].wait()
        for g in range(groups):
            for h, n in head_pairs(heads):
                part = value[g * seq : (g + 1) * seq, h * HEAD_DIM : (h + n) * HEAD_DIM]
                weights = mix_v[half, g, h]
                if n == 2:
                    lane = lax.broadcasted_iota(jnp.int32, part.shape, 1)
                    zero = jnp.zeros_like(part)
                    part = jnp.concatenate(
                        [
                            jnp.where(lane < HEAD_DIM, part, zero),
                            jnp.where(lane < HEAD_DIM, zero, part),
                        ],
                        axis=0,
                    )
                    weights = jnp.concatenate([weights, mix_v[half, g, h + 1]], axis=1)
                out[g * seq : (g + 1) * seq, h * HEAD_DIM : (h + n) * HEAD_DIM] = dot(
                    weights, part
                ).astype(BF16)


def grad_out_kernel(idx, cot_o, cot_s, mixed_o, mixed_s, *rest):
    outs, (cot_v, left_v, grad_v, sems) = rest[:-4], rest[-4:]
    tokens, _ = cot_o.shape
    copies = begin(
        [(cot_o, cot_v.at[pl.ds(0, tokens)]), (cot_s, cot_v.at[pl.ds(tokens, tokens)])], sems
    )
    left_v[:, :tokens] = mixed_o[...].astype(F32).T.astype(BF16)
    left_v[:, tokens:] = mixed_s[...].astype(F32).T.astype(BF16)
    copies[0].wait()
    copies[1].wait()
    gradient_rows(left_v[...], cot_v, grad_v, 640)
    hand_out(idx, 1, grad_v, outs)


def terms_kernel(n_node, idx, mixed_o, mixed_r, w_o, w_r, *outs):
    depth = w_o.shape[0] // n_node
    half = mixed_o.shape[0] // 2
    for j in range(n_node):
        rows = rows_at(idx[j], depth)
        term = dot(mixed_o[...], w_o[rows, :], 1, 1) + dot(mixed_r[...], w_r[rows, :], 1, 1)
        term = term.astype(BF16)
        if n_node != 4:
            outs[j][...] = term
            continue
        along_x, along_y, kept = outs
        first, second = term[:half], term[half:]
        if j == 0:
            kept[0], kept[2] = first, second
        elif j == 1:
            along_x[0], kept[3] = first, second
        elif j == 2:
            kept[1], along_y[0] = first, second
        else:
            along_x[1], along_y[1] = first, second


ANY = pl.BlockSpec(memory_space=pl.ANY)
SMEM = pl.BlockSpec(memory_space=pltpu.SMEM)
VMEM = pl.BlockSpec(memory_space=pltpu.VMEM)


def call(kernel, name, in_specs, out_shapes, scratch, flops):
    return pl.pallas_call(
        kernel,
        name=name,
        in_specs=in_specs,
        out_specs=[VMEM] * len(out_shapes),
        out_shape=[jax.ShapeDtypeStruct(s, BF16) for s in out_shapes],
        scratch_shapes=scratch,
        compiler_params=pltpu.CompilerParams(vmem_limit_bytes=VMEM_LIMIT),
        cost_estimate=pl.CostEstimate(flops=flops, bytes_accessed=12 << 20, transcendentals=0),
    )


def after(x, *others):
    return lax.optimization_barrier((x, *others))[0]


def make_body(n_wide, n_node):
    planes = n_wide // 2
    line4 = planes == 4

    def move(x, pairs):
        return lax.ppermute(
            x, "wide", [(2 * s + c, 2 * d + c) for s, d in pairs for c in range(2)]
        )

    def sibling(x):
        return lax.ppermute(x, "wide", [(i, i ^ 1) for i in range(n_wide)])

    def flip(x, j):
        return lax.ppermute(x, "node", [(i, i ^ j) for i in range(n_node)])

    def swap_halves(weights, c):
        cols = weights[0].shape[1] // 2
        low = jnp.stack([w[:, :cols] for w in weights])
        high = jnp.stack([w[:, cols:] for w in weights])
        got = sibling(jnp.where(c == 0, high, low))
        mine = jnp.where(c == 0, low, high)
        return [jnp.concatenate([mine[i], got[i]], axis=0) for i in range(len(weights))]

    def gather_first(u):
        if not line4:
            return [move(u, [(s, (s - j) % planes) for s in range(planes)]) for j in range(1, planes)]
        return [move(u, [(0, 2), (1, 3), (2, 0), (3, 1)]), move(u, [(1, 0), (2, 3)])]

    def gather_rest(u, firsts):
        if not line4:
            return [u, *firsts]
        across, ends = firsts
        up = move(u, [(0, 1), (1, 2)])
        down = move(u, [(3, 2), (2, 1)])
        on = move(across, [(2, 3), (1, 0)])
        return [u, across, ends, on, up, down]

    def slot_planes(z):
        if not line4:
            return [x for j in range(planes) for x in (lax.rem(z + j, planes), 1)]
        edge = ((z == 0) | (z == 3)).astype(jnp.int32)
        ends = jnp.where(z == 0, 1, 2)
        on = jnp.where(z == 0, 3, 0)
        up, down = jnp.maximum(z - 1, 0), jnp.minimum(z + 1, 3)
        return [z, 1, lax.rem(z + 2, 4), 1, ends, edge, on, edge, up, 1 - edge, down, 1 - edge]

    def send_planes(z):
        if not line4:
            return [lax.rem(z + j, planes) for j in range(planes)]
        up = jnp.where(z == 0, 3, jnp.minimum(z + 1, 3))
        down = jnp.where(z == 3, 0, jnp.maximum(z - 1, 0))
        near = jnp.where(z == 0, 1, jnp.where(z == 3, 2, z))
        return [z, up, down, near, lax.rem(z + 2, 4)]

    def scatter_first(blocks):
        _, up, down, _, _ = blocks
        return move(up, [(0, 1), (1, 2), (2, 3)]), move(down, [(3, 2), (2, 1), (1, 0)])

    def scatter_far(blocks, firsts, z):
        up, down = firsts
        add = jnp.where(z == 1, up, jnp.where(z == 2, down, jnp.zeros_like(up)))
        return (blocks[4].astype(F32) + add.astype(F32)).astype(BF16)

    def scatter_near(blocks, firsts, z):
        up, down = firsts
        near = move(after(blocks[3], up, down), [(0, 1), (3, 2)])
        total = blocks[0].astype(F32) + jnp.where(z <= 1, down, up).astype(F32)
        return total + near.astype(F32)

    def join(mine, other, c):
        low = jnp.where(c == 0, mine, other)
        high = jnp.where(c == 0, other, mine)
        return jnp.concatenate([low, high], axis=1)

    def scatter_rest(blocks, firsts, far, z, c, last):
        if last:
            far_other = lax.ppermute(
                far[1],
                "wide",
                [(2 * s + k, 2 * ((s + 2) % 4) + 1 - k) for s in range(4) for k in range(2)],
            )
            far_mine = move(far[0], [(s, (s + 2) % 4) for s in range(4)])
            total = scatter_near(blocks, firsts, z)
            other = sibling(total[1])
            return join(total[0] + far_mine.astype(F32), other + far_other.astype(F32), c)
        far = move(far, [(s, (s + 2) % 4) for s in range(4)])
        return scatter_near(blocks, firsts, z) + far.astype(F32)

    def scatter_ring(blocks, c):
        total = blocks[0].astype(F32)
        for j in range(1, planes):
            got = move(blocks[j], [(s, (s + j) % planes) for s in range(planes)])
            total = total + got.astype(F32)
        return join(total[0], sibling(total[1]), c)

    def body(act_in, mixing, cotangent, w_value, w_out):
        wide = lax.axis_index("wide")
        n = lax.axis_index("node")
        z, c = wide // 2, lax.rem(wide, 2)
        micro, images, seq, width = act_in.shape
        groups = micro * images
        tokens = groups * seq
        cols = w_value.shape[1] // 2
        heads = cols // HEAD_DIM
        depth = width // planes
        act = act_in.reshape(tokens, width)
        cot = cotangent.reshape(tokens, width)
        mix = mixing.reshape(groups, 2 * heads, seq, seq)
        flops = 4 * tokens * width * cols

        u_out, u_value = swap_halves([w_out, w_value], c)
        out_first = gather_first(u_out)
        cot_s = sibling(after(cot, u_out))
        mix_s = sibling(after(mix, u_out))
        act_s = sibling(after(act, u_out))
        out_first = list(lax.optimization_barrier((*out_first, cot_s, mix_s, act_s)))
        *out_first, cot_s, mix_s, act_s = out_first
        out_slots = gather_rest(after(u_out, out_first[0]), out_first)
        u_value = after(u_value, out_first[0])
        value_first = gather_first(u_value)

        info = slot_planes(z)
        sends = send_planes(z)
        n_slots = len(out_slots)
        idx_back = jnp.stack([c, *info, *sends]).astype(jnp.int32)
        idx_mixed = jnp.stack([c, *info]).astype(jnp.int32)
        idx_send = jnp.stack([c, *sends]).astype(jnp.int32)
        idx_node = jnp.stack([lax.bitwise_xor(n, jnp.int32(j)) for j in range(n_node)])

        mix_scratch = pltpu.VMEM((2, groups, heads, seq, seq), BF16)
        both = pltpu.VMEM((2 * tokens, width), BF16)
        halves = pltpu.VMEM((2, tokens, width), BF16)
        left = pltpu.VMEM((cols, 2 * tokens), BF16)
        rows = pltpu.VMEM((width, cols), BF16)
        send_shapes = [(2, depth // 2, cols)] * len(sends)

        w_full, *back_sends = call(
            functools.partial(backward_kernel, n_slots),
            "backward",
            [SMEM] + [ANY] * 6 + [VMEM] * n_slots,
            [(width, cols)] + send_shapes,
            [halves, both, mix_scratch, left, rows, pltpu.SemaphoreType.DMA((6,))],
            2 * flops,
        )(idx_back, cot, cot_s, mix, mix_s, act, act_s, *out_slots)
        if line4:
            value_first = [after(x, back_sends[0]) for x in value_first]
            value_slots = gather_rest(after(u_value, back_sends[0]), value_first)
            back_firsts = scatter_first(back_sends)
            far = scatter_far(back_sends, back_firsts, z)
            value_slots = list(lax.optimization_barrier((*value_slots, far)))[:-1]
            w_full_s = sibling(after(w_full, value_slots[0]))
        else:
            value_slots = gather_rest(u_value, value_first)
            w_full_s = sibling(w_full)

        mixed_o, mixed_s = call(
            functools.partial(mixed_kernel, n_slots),
            "mixed",
            [SMEM] + [ANY] * 4 + [VMEM] * n_slots,
            [(tokens, cols)] * 2,
            [rows, halves, mix_scratch, pltpu.SemaphoreType.DMA((4,))],
            flops,
        )(idx_mixed, act, act_s, mix, mix_s, *value_slots)
        mixed_r = sibling(mixed_s)
        out_sends = call(
            grad_out_kernel,
            "grad_out",
            [SMEM] + [ANY] * 2 + [VMEM] * 2,
            send_shapes,
            [both, left, rows, pltpu.SemaphoreType.DMA((2,))],
            flops,
        )(idx_send, cot, cot_s, mixed_o, mixed_s)
        part = width // n_node
        half = tokens // 2
        if n_node == 4:
            term_shapes = [(2, half, part), (2, half, part), (4, half, part)]
        else:
            term_shapes = [(tokens, part)] * n_node
        terms = call(
            functools.partial(terms_kernel, n_node),
            "terms",
            [SMEM] + [VMEM] * 4,
            term_shapes,
            [],
            flops,
        )(idx_node, mixed_o, mixed_r, w_full, w_full_s)
        if line4:
            grad_value = scatter_rest(back_sends, back_firsts, far, z, c, False)
            *out_sends, grad_value, mixed_r = lax.optimization_barrier(
                (*out_sends, grad_value, mixed_r)
            )
            out_firsts = scatter_first(out_sends)
            *out_firsts, _ = lax.optimization_barrier((*out_firsts, terms[0]))
            out_far = scatter_far(out_sends, out_firsts, z)
            grad_out = scatter_rest(out_sends, out_firsts, out_far, z, c, True)
            grad_value = join(grad_value[0], sibling(grad_value[1]), c)
        else:
            grad_value = scatter_ring(back_sends, c)
            grad_out = scatter_ring(out_sends, c)

        if n_node == 4:
            along_x, along_y, kept = terms
            kept = kept.astype(F32)
            got_x = flip(along_x, 1).astype(F32)
            got_y = flip(along_y, 2).astype(F32)
            last_y = flip((kept[1] + got_x[1]).astype(BF16), 2)
            last_x = flip((kept[3] + got_y[1]).astype(BF16), 1)
            layer_out = jnp.concatenate(
                [
                    kept[0] + got_x[0] + last_y.astype(F32),
                    kept[2] + got_y[0] + last_x.astype(F32),
                ],
                axis=0,
            )
        else:
            layer_out = terms[0].astype(F32)
            for j in range(1, n_node):
                layer_out = layer_out + flip(terms[j], j).astype(F32)
        layer_out = layer_out.astype(BF16).reshape(micro, images, seq, part)
        return layer_out, grad_value, grad_out

    return body


def solution(mesh):
    return jax.shard_map(
        make_body(mesh.shape["wide"], mesh.shape["node"]),
        mesh=mesh,
        in_specs=(
            P(None, "wide", None, None),
            P(None, "wide", "node", None, None),
            P(None, "wide", None, None),
            P("wide", "node"),
            P("wide", "node"),
        ),
        out_specs=(P(None, "wide", None, "node"), P("wide", "node"), P("wide", "node")),
        check_vma=False,
    )
```

```python
import functools
import math

import jax
import jax.numpy as jnp
from jax import lax
from jax.experimental import pallas as pl
from jax.experimental.pallas import tpu as pltpu
from jax.sharding import PartitionSpec as P

HEAD_DIM = 64
F32 = jnp.float32
BF16 = jnp.bfloat16
VMEM_LIMIT = 24 * 1024 * 1024


def dot(a, b, ca=1, cb=0):
    return lax.dot_general(a, b, (((ca,), (cb,)), ((), ())), preferred_element_type=F32)


def begin(pairs, sems):
    copies = [pltpu.make_async_copy(s, d, sems.at[i]) for i, (s, d) in enumerate(pairs)]
    for copy in copies:
        copy.start()
    return copies


def rows_at(index, size):
    return pl.ds(pl.multiple_of(index * size, math.gcd(size, 16)), size)


def place(idx, slots, w_ref):
    core = idx[0]
    for j, slot in enumerate(slots):
        depth = slot.shape[0] // 2

        @pl.when(idx[2 + 2 * j] == 1)
        def _(slot=slot, depth=depth, plane=idx[1 + 2 * j]):
            mine, other = slot[:depth, :], slot[depth:, :]
            low = jnp.where(core == 0, mine, other)
            high = jnp.where(core == 0, other, mine)
            w_ref[rows_at(plane, 2 * depth), :] = jnp.concatenate([low, high], axis=0)


def hand_out(idx, base, grad_v, outs):
    core = idx[0]
    for i, out in enumerate(outs):
        depth = out.shape[1]
        block = grad_v[rows_at(idx[base + i], 2 * depth), :]
        low, high = block[:depth], block[depth:]
        out[0] = jnp.where(core == 0, low, high)
        out[1] = jnp.where(core == 0, high, low)


def gradient_rows(left, right_ref, rows_ref, step):
    width = right_ref.shape[1]
    for start in range(0, width, step):
        part = dot(left, right_ref[:, start : start + step])
        rows_ref[start : start + step, :] = part.T.astype(BF16)


def head_pairs(heads):
    return [(h, min(2, heads - h)) for h in range(0, heads, 2)]


def d_value_kernel(n_slots, idx, cot_o, cot_s, mix_o, mix_s, *rest):
    slots, (w_out, left_v, cot_v, mix_v, sems) = rest[:n_slots], rest[n_slots:]
    groups, _, seq, _ = mix_o.shape
    heads = mix_v.shape[2]
    here = pl.ds(idx[0] * heads, heads)
    copies = begin(
        [(cot_o, cot_v.at[0]), (mix_o.at[:, here], mix_v.at[0])]
        + [(cot_s, cot_v.at[1]), (mix_s.at[:, here], mix_v.at[1])],
        sems,
    )
    place(idx, slots, w_out)
    for half in range(2):
        copies[2 * half].wait()
        d_mixed = dot(cot_v[half], w_out[...])
        copies[2 * half + 1].wait()
        for g in range(groups):
            turned = d_mixed[g * seq : (g + 1) * seq, :].T.astype(BF16)
            at = (half * groups + g) * seq
            for h, n in head_pairs(heads):
                part = turned[h * HEAD_DIM : (h + n) * HEAD_DIM, :]
                if n == 2:
                    row = lax.broadcasted_iota(jnp.int32, part.shape, 0)
                    zero = jnp.zeros_like(part)
                    part = jnp.concatenate(
                        [
                            jnp.where(row < HEAD_DIM, part, zero),
                            jnp.where(row < HEAD_DIM, zero, part),
                        ],
                        axis=1,
                    )
                weights = mix_v[half, g, h : h + n].reshape(n * seq, seq)
                left_v[h * HEAD_DIM : (h + n) * HEAD_DIM, at : at + seq] = dot(
                    part, weights
                ).astype(BF16)


def gradient_kernel(idx, right_o, right_s, left_ref, *rest):
    outs, (right_v, grad_v, sems) = rest[:-3], rest[-3:]
    tokens, _ = right_o.shape
    copies = begin(
        [(right_o, right_v.at[pl.ds(0, tokens)]), (right_s, right_v.at[pl.ds(tokens, tokens)])],
        sems,
    )
    copies[0].wait()
    copies[1].wait()
    gradient_rows(left_ref[...], right_v, grad_v, 640)
    hand_out(idx, 1, grad_v, outs)


def mixed_kernel(n_slots, idx, act_o, act_s, mix_o, mix_s, *rest):
    slots, (mixed_o, mixed_s, w_v, act_v, mix_v, sems) = rest[:n_slots], rest[n_slots:]
    groups, _, seq, _ = mix_o.shape
    heads = mix_v.shape[2]
    here = pl.ds(idx[0] * heads, heads)
    copies = begin(
        [(act_o, act_v.at[0]), (mix_o.at[:, here], mix_v.at[0])]
        + [(act_s, act_v.at[1]), (mix_s.at[:, here], mix_v.at[1])],
        sems,
    )
    place(idx, slots, w_v)
    for half, out in enumerate((mixed_o, mixed_s)):
        copies[2 * half].wait()
        value = dot(act_v[half], w_v[...]).astype(BF16)
        copies[2 * half + 1].wait()
        for g in range(groups):
            for h, n in head_pairs(heads):
                part = value[g * seq : (g + 1) * seq, h * HEAD_DIM : (h + n) * HEAD_DIM]
                weights = mix_v[half, g, h]
                if n == 2:
                    lane = lax.broadcasted_iota(jnp.int32, part.shape, 1)
                    zero = jnp.zeros_like(part)
                    part = jnp.concatenate(
                        [
                            jnp.where(lane < HEAD_DIM, part, zero),
                            jnp.where(lane < HEAD_DIM, zero, part),
                        ],
                        axis=0,
                    )
                    weights = jnp.concatenate([weights, mix_v[half, g, h + 1]], axis=1)
                out[g * seq : (g + 1) * seq, h * HEAD_DIM : (h + n) * HEAD_DIM] = dot(
                    weights, part
                ).astype(BF16)


def grad_out_kernel(idx, cot_o, cot_s, mixed_o, mixed_s, *rest):
    outs, (cot_v, left_v, grad_v, sems) = rest[:-4], rest[-4:]
    tokens, _ = cot_o.shape
    copies = begin(
        [(cot_o, cot_v.at[pl.ds(0, tokens)]), (cot_s, cot_v.at[pl.ds(tokens, tokens)])], sems
    )
    left_v[:, :tokens] = mixed_o[...].astype(F32).T.astype(BF16)
    left_v[:, tokens:] = mixed_s[...].astype(F32).T.astype(BF16)
    copies[0].wait()
    copies[1].wait()
    gradient_rows(left_v[...], cot_v, grad_v, 640)
    hand_out(idx, 1, grad_v, outs)


def terms_kernel(n_node, idx, mixed_o, mixed_r, w_o, w_r, *outs):
    depth = w_o.shape[0] // n_node
    half = mixed_o.shape[0] // 2
    for j in range(n_node):
        rows = rows_at(idx[j], depth)
        term = dot(mixed_o[...], w_o[rows, :], 1, 1) + dot(mixed_r[...], w_r[rows, :], 1, 1)
        term = term.astype(BF16)
        if n_node != 4:
            outs[j][...] = term
            continue
        along_x, along_y, kept = outs
        first, second = term[:half], term[half:]
        if j == 0:
            kept[0], kept[2] = first, second
        elif j == 1:
            along_x[0], kept[3] = first, second
        elif j == 2:
            kept[1], along_y[0] = first, second
        else:
            along_x[1], along_y[1] = first, second


ANY = pl.BlockSpec(memory_space=pltpu.HBM)
SMEM = pl.BlockSpec(memory_space=pltpu.SMEM)
VMEM = pl.BlockSpec(memory_space=pltpu.VMEM)


def call(kernel, name, in_specs, out_shapes, scratch, flops):
    return pl.pallas_call(
        kernel,
        name=name,
        in_specs=in_specs,
        out_specs=[VMEM] * len(out_shapes),
        out_shape=[jax.ShapeDtypeStruct(s, BF16) for s in out_shapes],
        scratch_shapes=scratch,
        compiler_params=pltpu.CompilerParams(vmem_limit_bytes=VMEM_LIMIT),
        cost_estimate=pl.CostEstimate(flops=flops, bytes_accessed=12 << 20, transcendentals=0),
    )


def after(x, *others):
    return lax.optimization_barrier((x, *others))[0]


def make_body(n_wide, n_node):
    planes = n_wide // 2
    line4 = planes == 4

    def move(x, pairs):
        return lax.ppermute(
            x, "wide", [(2 * s + c, 2 * d + c) for s, d in pairs for c in range(2)]
        )

    def sibling(x):
        return lax.ppermute(x, "wide", [(i, i ^ 1) for i in range(n_wide)])

    def flip(x, j):
        return lax.ppermute(x, "node", [(i, i ^ j) for i in range(n_node)])

    def swap_halves(weights, c):
        cols = weights[0].shape[1] // 2
        low = jnp.stack([w[:, :cols] for w in weights])
        high = jnp.stack([w[:, cols:] for w in weights])
        got = sibling(jnp.where(c == 0, high, low))
        mine = jnp.where(c == 0, low, high)
        return [jnp.concatenate([mine[i], got[i]], axis=0) for i in range(len(weights))]

    right = [[(s, s + 1) for s in range(planes - 1)][k:] for k in range(planes)]
    left = [[(s + 1, s) for s in reversed(range(planes - 1))][k:] for k in range(planes)]

    def gather_ring(u):
        return [u] + [
            move(u, [(s, (s - j) % planes) for s in range(planes)]) for j in range(1, planes)
        ]

    def gather_step(u, k):
        return move(u[0], right[k]), move(u[1], left[k])

    def gather_last(second, z):
        return move(jnp.where(z == 2, *second), right[2] + left[2])

    def slot_planes(z):
        if not line4:
            return [x for j in range(planes) for x in (lax.rem(z + j, planes), 1)]
        last = jnp.where(z == 0, 3, 0)
        return [
            *(z, 1, jnp.maximum(z - 1, 0), z >= 1, jnp.minimum(z + 1, 3), z <= 2),
            *(jnp.maximum(z - 2, 0), z >= 2, jnp.minimum(z + 2, 3), z <= 1),
            *(last, (z == 0) | (z == 3)),
        ]

    def send_planes(z):
        if not line4:
            return [lax.rem(z + j, planes) for j in range(planes)]
        across = jnp.where(z == 0, 3, 0)
        return [z, jnp.minimum(z + 1, 3), jnp.maximum(z - 1, 0), lax.rem(z + 2, 4), across]

    def added(block, got):
        return (block.astype(F32) + got.astype(F32)).astype(BF16)

    def scatter_first(blocks):
        return move(blocks[4], [(0, 1), (3, 2)])

    def scatter_second(blocks, first):
        far = added(blocks[3], first)
        return move(far, [(0, 1), (1, 2)]), move(far, [(3, 2), (2, 1)])

    def scatter_sums(blocks, second):
        return added(blocks[1], second[0]), added(blocks[2], second[1])

    def scatter_third(sums):
        return move(sums[0], right[0]), move(sums[1], left[0])

    def scatter_end(blocks, third, c):
        total = blocks[0].astype(F32) + third[0].astype(F32) + third[1].astype(F32)
        return join(total[0], sibling(total[1]), c)

    def join(mine, other, c):
        low = jnp.where(c == 0, mine, other)
        high = jnp.where(c == 0, other, mine)
        return jnp.concatenate([low, high], axis=1)

    def scatter_ring(blocks, c):
        total = blocks[0].astype(F32)
        for j in range(1, planes):
            got = move(blocks[j], [(s, (s + j) % planes) for s in range(planes)])
            total = total + got.astype(F32)
        return join(total[0], sibling(total[1]), c)

    def body(act_in, mixing, cotangent, w_value, w_out):
        wide = lax.axis_index("wide")
        n = lax.axis_index("node")
        z, c = wide // 2, lax.rem(wide, 2)
        micro, images, seq, width = act_in.shape
        groups = micro * images
        tokens = groups * seq
        cols = w_value.shape[1] // 2
        heads = cols // HEAD_DIM
        depth = width // planes
        act = act_in.reshape(tokens, width)
        cot = cotangent.reshape(tokens, width)
        mix = mixing.reshape(groups, 2 * heads, seq, seq)
        flops = 4 * tokens * width * cols

        u_out, u_value = swap_halves([w_out, w_value], c)
        act_s, mix_s, cot_s = (sibling(after(x, u_value)) for x in (act, mix, cot))
        if line4:
            v1 = gather_step((u_value, u_value), 0)
            v2 = gather_step(v1, 1)
            v2, act_s, mix_s, cot_s = lax.optimization_barrier((v2, act_s, mix_s, cot_s))
            v3 = gather_last(v2, z)
            u_out = after(u_out, *v2)
            o1 = gather_step((u_out, u_out), 0)
            value_slots, o1 = lax.optimization_barrier(([u_value, *v1, *v2, v3], o1))
            o2 = gather_step(o1, 1)
        else:
            value_slots = gather_ring(u_value)
            out_slots = gather_ring(u_out)

        info = slot_planes(z)
        sends = send_planes(z)
        n_slots = len(value_slots)
        idx_slots = jnp.stack([jnp.int32(x) for x in (c, *info)])
        idx_send = jnp.stack([jnp.int32(x) for x in (c, *sends)])
        idx_node = jnp.stack([lax.bitwise_xor(n, jnp.int32(j)) for j in range(n_node)])

        mix_scratch = pltpu.VMEM((2, groups, heads, seq, seq), BF16)
        both = pltpu.VMEM((2 * tokens, width), BF16)
        halves = pltpu.VMEM((2, tokens, width), BF16)
        left_tokens = pltpu.VMEM((cols, 2 * tokens), BF16)
        rows = pltpu.VMEM((width, cols), BF16)
        send_shapes = [(2, depth // 2, cols)] * len(sends)

        mixed_o, mixed_s = call(
            functools.partial(mixed_kernel, n_slots),
            "mixed",
            [SMEM] + [ANY] * 4 + [VMEM] * n_slots,
            [(tokens, cols)] * 2,
            [rows, halves, mix_scratch, pltpu.SemaphoreType.DMA((4,))],
            flops,
        )(idx_slots, act, act_s, mix, mix_s, *value_slots)
        mixed_r = sibling(mixed_s)
        if line4:
            (mixed_o, mixed_s, mixed_r), o2 = lax.optimization_barrier(
                ((mixed_o, mixed_s, mixed_r), o2)
            )
            out_slots = [u_out, *o1, *o2, gather_last(o2, z)]
        out_sends = call(
            grad_out_kernel,
            "grad_out",
            [SMEM] + [ANY] * 2 + [VMEM] * 2,
            send_shapes,
            [both, left_tokens, rows, pltpu.SemaphoreType.DMA((2,))],
            flops,
        )(idx_send, cot, cot_s, mixed_o, mixed_s)
        if line4:
            out_slots, out_sends = lax.optimization_barrier((out_slots, out_sends))
        w_full, left = call(
            functools.partial(d_value_kernel, n_slots),
            "d_value",
            [SMEM] + [ANY] * 4 + [VMEM] * n_slots,
            [(width, cols), (cols, 2 * tokens)],
            [halves, mix_scratch, pltpu.SemaphoreType.DMA((4,))],
            flops,
        )(idx_slots, cot, cot_s, mix, mix_s, *out_slots)
        w_full_s = sibling(w_full)
        if line4:
            out_first = scatter_first(out_sends)
            left, out_first = lax.optimization_barrier((left, out_first))
            out_second = scatter_second(out_sends, out_first)
        back_sends = call(
            gradient_kernel,
            "grad_value",
            [SMEM] + [ANY] * 2 + [VMEM],
            send_shapes,
            [both, rows, pltpu.SemaphoreType.DMA((2,))],
            flops,
        )(idx_send, act, act_s, left)
        if line4:
            back_first = scatter_first(back_sends)
            out_sums = scatter_sums(out_sends, out_second)
            w_full_s, out_sums = lax.optimization_barrier((w_full_s, out_sums))
            out_third = scatter_third(out_sums)

        part = width // n_node
        half = tokens // 2
        if n_node == 4:
            term_shapes = [(2, half, part), (2, half, part), (4, half, part)]
        else:
            term_shapes = [(tokens, part)] * n_node
        terms = call(
            functools.partial(terms_kernel, n_node),
            "terms",
            [SMEM] + [VMEM] * 4,
            term_shapes,
            [],
            flops,
        )(idx_node, mixed_o, mixed_r, w_full, w_full_s)

        if line4:
            back_first = after(back_first, terms[0])
            back_second = scatter_second(back_sends, back_first)
            back_third = scatter_third(scatter_sums(back_sends, back_second))
            grad_out = scatter_end(out_sends, out_third, c)
            grad_value = scatter_end(back_sends, back_third, c)
        else:
            grad_value = scatter_ring(back_sends, c)
            grad_out = scatter_ring(out_sends, c)
        if n_node == 4:
            along_x, along_y, kept = terms
            kept = kept.astype(F32)
            got_x = flip(along_x, 1).astype(F32)
            got_y = flip(along_y, 2).astype(F32)
            last_y = flip((kept[1] + got_x[1]).astype(BF16), 2)
            last_x = flip((kept[3] + got_y[1]).astype(BF16), 1)
            layer_out = jnp.concatenate(
                [
                    kept[0] + got_x[0] + last_y.astype(F32),
                    kept[2] + got_y[0] + last_x.astype(F32),
                ],
                axis=0,
            )
        else:
            layer_out = terms[0].astype(F32)
            for j in range(1, n_node):
                layer_out = layer_out + flip(terms[j], j).astype(F32)
        layer_out = layer_out.astype(BF16).reshape(micro, images, seq, part)
        return layer_out, grad_value, grad_out

    return body


def solution(mesh):
    return jax.shard_map(
        make_body(mesh.shape["wide"], mesh.shape["node"]),
        mesh=mesh,
        in_specs=(
            P(None, "wide", None, None),
            P(None, "wide", "node", None, None),
            P(None, "wide", None, None),
            P("wide", "node"),
            P("wide", "node"),
        ),
        out_specs=(P(None, "wide", None, "node"), P("wide", "node"), P("wide", "node")),
        check_vma=False,
    )
```

```python
import functools
import math

import jax
import jax.numpy as jnp
from jax import lax
from jax.experimental import pallas as pl
from jax.experimental.pallas import tpu as pltpu
from jax.sharding import PartitionSpec as P

HEAD_DIM = 64
F32 = jnp.float32
BF16 = jnp.bfloat16
VMEM_LIMIT = 40 * 1024 * 1024


def dot(a, b, ca=1, cb=0):
    return lax.dot_general(a, b, (((ca,), (cb,)), ((), ())), preferred_element_type=F32)


def begin(pairs, sems):
    copies = [pltpu.make_async_copy(s, d, sems.at[i]) for i, (s, d) in enumerate(pairs)]
    for copy in copies:
        copy.start()
    return copies


def rows_at(index, size):
    return pl.ds(pl.multiple_of(index * size, math.gcd(size, 16)), size)


def place(idx, slots, w_ref):
    core = idx[0]
    for j, slot in enumerate(slots):
        depth = slot.shape[1]

        @pl.when(idx[2 + 2 * j] == 1)
        def _(slot=slot, depth=depth, plane=idx[1 + 2 * j]):
            mine, other = slot[0], slot[1]
            low = jnp.where(core == 0, mine, other)
            high = jnp.where(core == 0, other, mine)
            w_ref[rows_at(plane, 2 * depth), :] = jnp.concatenate([low, high], axis=0)


def hand_out(idx, base, grad_v, outs):
    core = idx[0]
    for i, out in enumerate(outs):
        depth = out.shape[1]
        block = grad_v[rows_at(idx[base + i], 2 * depth), :]
        low, high = block[:depth], block[depth:]
        out[0] = jnp.where(core == 0, low, high)
        out[1] = jnp.where(core == 0, high, low)


def gradient_rows(left, right_ref, rows_ref, step):
    width = right_ref.shape[1]
    for start in range(0, width, step):
        part = dot(left, right_ref[:, start : start + step])
        rows_ref[start : start + step, :] = part.T.astype(BF16)


def head_pairs(heads):
    return [(h, min(2, heads - h)) for h in range(0, heads, 2)]


def d_value_kernel(n_slots, n_ties, idx, cot_o, cot_s, mix_o, mix_s, *rest):
    slots, (w_out, left_v, cot_v, mix_v, sems) = rest[:n_slots], rest[n_slots + n_ties :]
    groups, _, seq, _ = mix_o.shape
    heads = mix_v.shape[2]
    here = pl.ds(idx[0] * heads, heads)
    copies = begin(
        [(cot_o, cot_v.at[0]), (mix_o.at[:, here], mix_v.at[0])]
        + [(cot_s, cot_v.at[1]), (mix_s.at[:, here], mix_v.at[1])],
        sems,
    )
    place(idx, slots, w_out)
    for half in range(2):
        copies[2 * half].wait()
        d_mixed = dot(cot_v[half], w_out[...])
        copies[2 * half + 1].wait()
        for g in range(groups):
            turned = d_mixed[g * seq : (g + 1) * seq, :].T.astype(BF16)
            at = (half * groups + g) * seq
            for h, n in head_pairs(heads):
                part = turned[h * HEAD_DIM : (h + n) * HEAD_DIM, :]
                if n == 2:
                    row = lax.broadcasted_iota(jnp.int32, part.shape, 0)
                    zero = jnp.zeros_like(part)
                    part = jnp.concatenate(
                        [
                            jnp.where(row < HEAD_DIM, part, zero),
                            jnp.where(row < HEAD_DIM, zero, part),
                        ],
                        axis=1,
                    )
                weights = mix_v[half, g, h : h + n].reshape(n * seq, seq)
                left_v[h * HEAD_DIM : (h + n) * HEAD_DIM, at : at + seq] = dot(
                    part, weights
                ).astype(BF16)


def gradient_kernel(n_ties, idx, right_o, right_s, left_ref, *rest):
    outs, (right_v, grad_v, sems) = rest[n_ties:-3], rest[-3:]
    tokens, _ = right_o.shape
    copies = begin(
        [(right_o, right_v.at[pl.ds(0, tokens)]), (right_s, right_v.at[pl.ds(tokens, tokens)])],
        sems,
    )
    copies[0].wait()
    copies[1].wait()
    gradient_rows(left_ref[...], right_v, grad_v, 640)
    hand_out(idx, 1, grad_v, outs)


def mixed_kernel(n_slots, n_ties, idx, act_o, act_s, mix_o, mix_s, *rest):
    slots, (mixed_o, mixed_s, w_v, act_v, mix_v, sems) = rest[:n_slots], rest[n_slots + n_ties :]
    groups, _, seq, _ = mix_o.shape
    heads = mix_v.shape[2]
    here = pl.ds(idx[0] * heads, heads)
    copies = begin(
        [(act_o, act_v.at[0]), (mix_o.at[:, here], mix_v.at[0])]
        + [(act_s, act_v.at[1]), (mix_s.at[:, here], mix_v.at[1])],
        sems,
    )
    place(idx, slots, w_v)
    for half, out in enumerate((mixed_o, mixed_s)):
        copies[2 * half].wait()
        value = dot(act_v[half], w_v[...]).astype(BF16)
        copies[2 * half + 1].wait()
        for g in range(groups):
            for h, n in head_pairs(heads):
                part = value[g * seq : (g + 1) * seq, h * HEAD_DIM : (h + n) * HEAD_DIM]
                weights = mix_v[half, g, h]
                if n == 2:
                    lane = lax.broadcasted_iota(jnp.int32, part.shape, 1)
                    zero = jnp.zeros_like(part)
                    part = jnp.concatenate(
                        [
                            jnp.where(lane < HEAD_DIM, part, zero),
                            jnp.where(lane < HEAD_DIM, zero, part),
                        ],
                        axis=0,
                    )
                    weights = jnp.concatenate([weights, mix_v[half, g, h + 1]], axis=1)
                out[g * seq : (g + 1) * seq, h * HEAD_DIM : (h + n) * HEAD_DIM] = dot(
                    weights, part
                ).astype(BF16)


def grad_out_kernel(n_pass, n_ties, idx, cot_o, cot_s, mixed_o, mixed_s, *rest):
    passed, rest = rest[:n_pass], rest[n_pass + n_ties :]
    outs, (cot_v, left_v, grad_v, sems) = rest[:-4], rest[-4:]
    tokens, _ = cot_o.shape
    copies = begin(
        [(cot_o, cot_v.at[pl.ds(0, tokens)]), (cot_s, cot_v.at[pl.ds(tokens, tokens)])], sems
    )
    left_v[:, :tokens] = mixed_o[...].astype(F32).T.astype(BF16)
    left_v[:, tokens:] = mixed_s[...].astype(F32).T.astype(BF16)
    copies[0].wait()
    copies[1].wait()
    gradient_rows(left_v[...], cot_v, grad_v, 640)
    hand_out(idx, 1, grad_v, outs)
    for j, block in enumerate(passed):

        @pl.when(idx[1 + len(outs) + j] == 1)
        def _(block=block):
            outs[-1][...] = block[...]


def terms_kernel(n_node, n_ties, idx, mixed_o, mixed_r, w_o, w_r, *rest):
    outs = rest[n_ties:]
    depth = w_o.shape[0] // n_node
    half = mixed_o.shape[0] // 2
    for j in range(n_node):
        rows = rows_at(idx[j], depth)
        term = dot(mixed_o[...], w_o[rows, :], 1, 1) + dot(mixed_r[...], w_r[rows, :], 1, 1)
        term = term.astype(BF16)
        if n_node != 4:
            outs[j][...] = term
            continue
        along_x, along_y, kept = outs
        first, second = term[:half], term[half:]
        if j == 0:
            kept[0], kept[2] = first, second
        elif j == 1:
            along_x[0], kept[3] = first, second
        elif j == 2:
            kept[1], along_y[0] = first, second
        else:
            along_x[1], along_y[1] = first, second


ANY = pl.BlockSpec(memory_space=pltpu.HBM)
TIE = pl.BlockSpec(memory_space=pl.ANY)
SMEM = pl.BlockSpec(memory_space=pltpu.SMEM)
VMEM = pl.BlockSpec(memory_space=pltpu.VMEM)


def select_kernel(take, first, second, *rest):
    out = rest[-1]
    out[...] = jnp.where(take[0] == 1, first[...], second[...])


def call(kernel, name, in_specs, out_shapes, scratch, flops):
    return pl.pallas_call(
        kernel,
        name=name,
        in_specs=in_specs,
        out_specs=[VMEM] * len(out_shapes),
        out_shape=[jax.ShapeDtypeStruct(s, BF16) for s in out_shapes],
        scratch_shapes=scratch,
        compiler_params=pltpu.CompilerParams(vmem_limit_bytes=VMEM_LIMIT),
        cost_estimate=pl.CostEstimate(flops=flops, bytes_accessed=12 << 20, transcendentals=0),
    )


def make_body(n_wide, n_node):
    planes = n_wide // 2
    line4 = planes == 4

    def move(x, pairs):
        return lax.ppermute(
            x, "wide", [(2 * s + c, 2 * d + c) for s, d in pairs for c in range(2)]
        )

    def apart(ahead, back, pairs):
        mirror = [(planes - 1 - s, planes - 1 - d) for s, d in pairs]
        lines = (pairs, mirror), (mirror, pairs)
        return tuple(
            lax.ppermute(x, "wide", [(2 * s + c, 2 * d + c) for c in range(2) for s, d in line[c]])
            for x, line in zip((ahead, back), lines)
        )

    def sibling(x):
        return lax.ppermute(x, "wide", [(i, i ^ 1) for i in range(n_wide)])

    def flip(x, j):
        return lax.ppermute(x, "node", [(i, i ^ j) for i in range(n_node)])

    def swap_halves(weights, c):
        cols = weights[0].shape[1] // 2
        low = jnp.stack([w[:, :cols] for w in weights])
        high = jnp.stack([w[:, cols:] for w in weights])
        got = sibling(jnp.where(c == 0, high, low))
        mine = jnp.where(c == 0, low, high)
        return got, [jnp.stack([mine[i], got[i]]) for i in range(len(weights))]

    line = [(s, s + 1) for s in range(planes - 1)]

    def gather_ring(u):
        return [u] + [
            move(u, [(s, (s - j) % planes) for s in range(planes)]) for j in range(1, planes)
        ]

    def slot_planes(z, d):
        if not line4:
            return [x for j in range(planes) for x in (lax.rem(z + j, planes), 1)]
        found = [z, 1]
        for plane in (z - d, z + d, z - 2 * d, z + 2 * d):
            found += [jnp.clip(plane, 0, 3), (plane >= 0) & (plane <= 3)]
        return found + [3 - z, (z == 0) | (z == 3)]

    def send_planes(z, d):
        if not line4:
            return [lax.rem(z + j, planes) for j in range(planes)]
        near = [jnp.clip(plane, 0, 3) for plane in (z + d, z - d)]
        return [z, *near, lax.rem(z + 2, 4), 3 - z]

    def added(block, got):
        return (block.astype(F32) + got.astype(F32)).astype(BF16)

    def scatter_far(blocks, first, z):
        inside = (z == 1) | (z == 2)
        return added(blocks[3], jnp.where(inside, first, jnp.zeros_like(first)))

    def scatter_second(far):
        return apart(far, far, line[:2])

    def scatter_sums(blocks, second):
        return added(blocks[1], second[0]), added(blocks[2], second[1])

    def scatter_third(sums):
        return apart(*sums, line)

    def scatter_end(blocks, third, c):
        total = blocks[0].astype(F32) + third[0].astype(F32) + third[1].astype(F32)
        return join(total[0], sibling(total[1]), c)

    def join(mine, other, c):
        low = jnp.where(c == 0, mine, other)
        high = jnp.where(c == 0, other, mine)
        return jnp.concatenate([low, high], axis=1)

    def scatter_ring(blocks, c):
        total = blocks[0].astype(F32)
        for j in range(1, planes):
            got = move(blocks[j], [(s, (s + j) % planes) for s in range(planes)])
            total = total + got.astype(F32)
        return join(total[0], sibling(total[1]), c)

    def body(act_in, mixing, cotangent, w_value, w_out):
        wide = lax.axis_index("wide")
        n = lax.axis_index("node")
        z, c = wide // 2, lax.rem(wide, 2)
        micro, images, seq, width = act_in.shape
        groups = micro * images
        tokens = groups * seq
        cols = w_value.shape[1] // 2
        heads = cols // HEAD_DIM
        depth = width // planes
        act = act_in.reshape(tokens, width)
        cot = cotangent.reshape(tokens, width)
        mix = mixing.reshape(groups, 2 * heads, seq, seq)
        flops = 4 * tokens * width * cols

        got, (u_out, u_value) = swap_halves([w_out, w_value], c)
        act_s, mix_s, cot_s = (
            sibling(lax.optimization_barrier((x, got))[0]) for x in (act, mix, cot)
        )

        d = 1 - 2 * c
        info = slot_planes(z, d)
        sends = send_planes(z, d)
        pack = lambda *values: jnp.stack([jnp.int32(x) for x in values])
        idx_slots = pack(c, *info)
        idx_send = pack(c, *sends)
        idx_node = pack(*[lax.bitwise_xor(n, jnp.int32(j)) for j in range(n_node)])

        mix_scratch = pltpu.VMEM((2, groups, heads, seq, seq), BF16)
        both = pltpu.VMEM((2 * tokens, width), BF16)
        halves = pltpu.VMEM((2, tokens, width), BF16)
        left_tokens = pltpu.VMEM((cols, 2 * tokens), BF16)
        rows = pltpu.VMEM((width, cols), BF16)
        block = (2, depth // 2, cols)
        send_shapes = [block] * len(sends)

        ties, passed = [], []
        if line4:
            along = jnp.where(c == 0, z == 2, z == 1)
            v1 = apart(u_value, u_value, line)
            v2 = apart(*v1, line[1:])
            forward = call(
                select_kernel,
                "forward",
                [SMEM] + [VMEM] * 2 + [TIE] * 3,
                [block],
                [],
                0,
            )(pack(along), *v2, act_s, mix_s, cot_s)[0]
            v3 = move(forward, [(2, 3), (1, 0)])
            value_slots = [u_value, *v1, *v2, v3]
            o1 = apart(u_out, u_out, line)
            o2 = apart(*o1, line[1:])
            ties = [*o1]
            passed = [*o2]
            idx_pass = pack(c, *sends, (1 - along) & (z % 3 != 0), along)
        else:
            value_slots = gather_ring(u_value)
            out_slots = gather_ring(u_out)
            idx_pass = idx_send
        n_slots = len(value_slots)

        mixed_o, mixed_s = call(
            functools.partial(mixed_kernel, n_slots, len(ties)),
            "mixed",
            [SMEM] + [ANY] * 4 + [VMEM] * n_slots + [TIE] * len(ties),
            [(tokens, cols)] * 2,
            [rows, halves, mix_scratch, pltpu.SemaphoreType.DMA((4,))],
            flops,
        )(idx_slots, act, act_s, mix, mix_s, *value_slots, *ties)
        mixed_r = sibling(mixed_s)
        out_sends = call(
            functools.partial(grad_out_kernel, len(passed), 1),
            "grad_out",
            [SMEM] + [ANY] * 2 + [VMEM] * (2 + len(passed)) + [TIE],
            send_shapes,
            [both, left_tokens, rows, pltpu.SemaphoreType.DMA((2,))],
            flops,
        )(idx_pass, cot, cot_s, mixed_o, mixed_s, *reversed(passed), mixed_r)
        if line4:
            swapped = move(out_sends[4], [(0, 1), (1, 0), (2, 3), (3, 2)])
            out_slots = [u_out, *o1, *o2, swapped]
            far = scatter_far(out_sends, swapped, z)
            out_second = scatter_second(far)
            ties = [far]
        else:
            ties = [out_sends[0]]
        w_full, left = call(
            functools.partial(d_value_kernel, n_slots, len(ties)),
            "d_value",
            [SMEM] + [ANY] * 4 + [VMEM] * n_slots + [TIE] * len(ties),
            [(width, cols), (cols, 2 * tokens)],
            [halves, mix_scratch, pltpu.SemaphoreType.DMA((4,))],
            flops,
        )(idx_slots, cot, cot_s, mix, mix_s, *out_slots, *ties)
        w_full_s = sibling(w_full)
        part = width // n_node
        half = tokens // 2
        if n_node == 4:
            term_shapes = [(2, half, part), (2, half, part), (4, half, part)]
        else:
            term_shapes = [(tokens, part)] * n_node
        terms = call(
            functools.partial(terms_kernel, n_node, 0),
            "terms",
            [SMEM] + [VMEM] * 4,
            term_shapes,
            [],
            flops,
        )(idx_node, mixed_o, mixed_r, w_full, w_full_s)

        ties = [terms[0]]
        if line4:
            out_sums = scatter_sums(out_sends, out_second)
            out_third = scatter_third(out_sums)
            ties += out_sums
        back_sends = call(
            functools.partial(gradient_kernel, len(ties)),
            "grad_value",
            [SMEM] + [ANY] * 2 + [VMEM] + [TIE] * len(ties),
            send_shapes,
            [both, rows, pltpu.SemaphoreType.DMA((2,))],
            flops,
        )(idx_send, act, act_s, left, *ties)
        if line4:
            back_first = move(back_sends[4], [(0, 1), (3, 2)])
            back_second = scatter_second(scatter_far(back_sends, back_first, z))
            back_third = scatter_third(scatter_sums(back_sends, back_second))
            grad_out = scatter_end(out_sends, out_third, c)
            grad_value = scatter_end(back_sends, back_third, c)
        else:
            grad_value = scatter_ring(back_sends, c)
            grad_out = scatter_ring(out_sends, c)
        if n_node == 4:
            along_x, along_y, kept = terms
            kept = kept.astype(F32)
            got_x = flip(along_x, 1).astype(F32)
            got_y = flip(along_y, 2).astype(F32)
            last_y = flip((kept[1] + got_x[1]).astype(BF16), 2)
            last_x = flip((kept[3] + got_y[1]).astype(BF16), 1)
            layer_out = jnp.concatenate(
                [
                    kept[0] + got_x[0] + last_y.astype(F32),
                    kept[2] + got_y[0] + last_x.astype(F32),
                ],
                axis=0,
            )
        else:
            layer_out = terms[0].astype(F32)
            for j in range(1, n_node):
                layer_out = layer_out + flip(terms[j], j).astype(F32)
        layer_out = layer_out.astype(BF16).reshape(micro, images, seq, part)
        return layer_out, grad_value, grad_out

    return body


def solution(mesh):
    return jax.shard_map(
        make_body(mesh.shape["wide"], mesh.shape["node"]),
        mesh=mesh,
        in_specs=(
            P(None, "wide", None, None),
            P(None, "wide", "node", None, None),
            P(None, "wide", None, None),
            P("wide", "node"),
            P("wide", "node"),
        ),
        out_specs=(P(None, "wide", None, "node"), P("wide", "node"), P("wide", "node")),
        check_vma=False,
    )
```

```python
import functools
import math

import jax
import jax.numpy as jnp
from jax import lax
from jax.experimental import pallas as pl
from jax.experimental.pallas import tpu as pltpu
from jax.sharding import PartitionSpec as P

HEAD_DIM = 64
F32 = jnp.float32
BF16 = jnp.bfloat16
VMEM_LIMIT = 20 * 1024 * 1024


def dot(a, b, ca=1, cb=0):
    return lax.dot_general(a, b, (((ca,), (cb,)), ((), ())), preferred_element_type=F32)


def begin(pairs, sems):
    copies = [pltpu.make_async_copy(s, d, sems.at[i]) for i, (s, d) in enumerate(pairs)]
    for copy in copies:
        copy.start()
    return copies


def rows_at(index, size):
    return pl.ds(pl.multiple_of(index * size, math.gcd(size, 16)), size)


def place(idx, slots, w_ref):
    core = idx[0]
    for j, slot in enumerate(slots):
        depth = slot.shape[1]

        @pl.when(idx[2 + 2 * j] == 1)
        def _(slot=slot, depth=depth, plane=idx[1 + 2 * j]):
            mine, other = slot[0], slot[1]
            low = jnp.where(core == 0, mine, other)
            high = jnp.where(core == 0, other, mine)
            w_ref[rows_at(plane, 2 * depth), :] = jnp.concatenate([low, high], axis=0)


def hand_out(idx, base, grad_v, outs):
    core = idx[0]
    for i, out in enumerate(outs):
        depth = out.shape[1]
        block = grad_v[rows_at(idx[base + i], 2 * depth), :]
        low, high = block[:depth], block[depth:]
        out[0] = jnp.where(core == 0, low, high)
        out[1] = jnp.where(core == 0, high, low)


def gradient_rows(left, right_ref, rows_ref, step):
    width = right_ref.shape[1]
    for start in range(0, width, step):
        part = dot(left, right_ref[:, start : start + step])
        rows_ref[start : start + step, :] = part.T.astype(BF16)


def head_pairs(heads):
    return [(h, min(2, heads - h)) for h in range(0, heads, 2)]


def d_value_kernel(n_slots, idx, cot_o, cot_s, mix_o, mix_s, *rest):
    slots, (w_out, left_v, cot_v, mix_v, sems) = rest[:n_slots], rest[n_slots:]
    groups, _, seq, _ = mix_o.shape
    heads = mix_v.shape[2]
    here = pl.ds(idx[0] * heads, heads)
    copies = begin(
        [(cot_o, cot_v.at[0]), (mix_o.at[:, here], mix_v.at[0])]
        + [(cot_s, cot_v.at[1]), (mix_s.at[:, here], mix_v.at[1])],
        sems,
    )
    place(idx, slots, w_out)
    for half in range(2):
        copies[2 * half].wait()
        d_mixed = dot(cot_v[half], w_out[...])
        copies[2 * half + 1].wait()
        for g in range(groups):
            turned = d_mixed[g * seq : (g + 1) * seq, :].T.astype(BF16)
            at = (half * groups + g) * seq
            for h, n in head_pairs(heads):
                part = turned[h * HEAD_DIM : (h + n) * HEAD_DIM, :]
                if n == 2:
                    row = lax.broadcasted_iota(jnp.int32, part.shape, 0)
                    zero = jnp.zeros_like(part)
                    part = jnp.concatenate(
                        [
                            jnp.where(row < HEAD_DIM, part, zero),
                            jnp.where(row < HEAD_DIM, zero, part),
                        ],
                        axis=1,
                    )
                weights = mix_v[half, g, h : h + n].reshape(n * seq, seq)
                left_v[h * HEAD_DIM : (h + n) * HEAD_DIM, at : at + seq] = dot(
                    part, weights
                ).astype(BF16)


def gradient_kernel(idx, right_o, right_s, left_ref, *rest):
    outs, (right_v, grad_v, sems) = rest[:-3], rest[-3:]
    tokens, _ = right_o.shape
    copies = begin(
        [(right_o, right_v.at[pl.ds(0, tokens)]), (right_s, right_v.at[pl.ds(tokens, tokens)])],
        sems,
    )
    copies[0].wait()
    copies[1].wait()
    gradient_rows(left_ref[...], right_v, grad_v, 640)
    hand_out(idx, 1, grad_v, outs)


def mixed_kernel(n_slots, idx, act_o, act_s, mix_o, mix_s, *rest):
    slots, (mixed_o, mixed_s, w_v, act_v, mix_v, sems) = rest[:n_slots], rest[n_slots:]
    groups, _, seq, _ = mix_o.shape
    heads = mix_v.shape[2]
    here = pl.ds(idx[0] * heads, heads)
    copies = begin(
        [(act_o, act_v.at[0]), (mix_o.at[:, here], mix_v.at[0])]
        + [(act_s, act_v.at[1]), (mix_s.at[:, here], mix_v.at[1])],
        sems,
    )
    place(idx, slots, w_v)
    for half, out in enumerate((mixed_o, mixed_s)):
        copies[2 * half].wait()
        value = dot(act_v[half], w_v[...]).astype(BF16)
        copies[2 * half + 1].wait()
        for g in range(groups):
            for h, n in head_pairs(heads):
                part = value[g * seq : (g + 1) * seq, h * HEAD_DIM : (h + n) * HEAD_DIM]
                weights = mix_v[half, g, h]
                if n == 2:
                    lane = lax.broadcasted_iota(jnp.int32, part.shape, 1)
                    zero = jnp.zeros_like(part)
                    part = jnp.concatenate(
                        [
                            jnp.where(lane < HEAD_DIM, part, zero),
                            jnp.where(lane < HEAD_DIM, zero, part),
                        ],
                        axis=0,
                    )
                    weights = jnp.concatenate([weights, mix_v[half, g, h + 1]], axis=1)
                out[g * seq : (g + 1) * seq, h * HEAD_DIM : (h + n) * HEAD_DIM] = dot(
                    weights, part
                ).astype(BF16)


def grad_out_kernel(idx, cot_o, cot_s, mixed_o, mixed_s, *rest):
    outs, (cot_v, left_v, grad_v, sems) = rest[:-4], rest[-4:]
    tokens, _ = cot_o.shape
    copies = begin(
        [(cot_o, cot_v.at[pl.ds(0, tokens)]), (cot_s, cot_v.at[pl.ds(tokens, tokens)])], sems
    )
    left_v[:, :tokens] = mixed_o[...].astype(F32).T.astype(BF16)
    left_v[:, tokens:] = mixed_s[...].astype(F32).T.astype(BF16)
    copies[0].wait()
    copies[1].wait()
    gradient_rows(left_v[...], cot_v, grad_v, 640)
    hand_out(idx, 1, grad_v, outs)


def terms_kernel(n_node, idx, mixed_o, mixed_r, w_o, w_r, *outs):
    depth = w_o.shape[0] // n_node
    half = mixed_o.shape[0] // 2
    for j in range(n_node):
        rows = rows_at(idx[j], depth)
        term = dot(mixed_o[...], w_o[rows, :], 1, 1) + dot(mixed_r[...], w_r[rows, :], 1, 1)
        term = term.astype(BF16)
        if n_node != 4:
            outs[j][...] = term
            continue
        along_x, along_y, kept = outs
        first, second = term[:half], term[half:]
        if j == 0:
            kept[0], kept[2] = first, second
        elif j == 1:
            along_x[0], kept[3] = first, second
        elif j == 2:
            kept[1], along_y[0] = first, second
        else:
            along_x[1], along_y[1] = first, second


ANY = pl.BlockSpec(memory_space=pltpu.HBM)
SMEM = pl.BlockSpec(memory_space=pltpu.SMEM)
VMEM = pl.BlockSpec(memory_space=pltpu.VMEM)


def call(kernel, name, in_specs, out_shapes, scratch, flops):
    return pl.pallas_call(
        kernel,
        name=name,
        in_specs=in_specs,
        out_specs=[VMEM] * len(out_shapes),
        out_shape=[jax.ShapeDtypeStruct(s, BF16) for s in out_shapes],
        scratch_shapes=scratch,
        compiler_params=pltpu.CompilerParams(vmem_limit_bytes=VMEM_LIMIT),
        cost_estimate=pl.CostEstimate(flops=flops, bytes_accessed=12 << 20, transcendentals=0),
    )


def make_body(n_wide, n_node):
    planes = n_wide // 2
    line4 = planes == 4

    def move(x, pairs):
        return lax.ppermute(
            x, "wide", [(2 * s + c, 2 * d + c) for s, d in pairs for c in range(2)]
        )

    outer, middle = [(0, 1), (1, 0), (2, 3), (3, 2)], [(1, 2), (2, 1)]
    outward, inward = [(1, 0), (2, 3)], [(0, 1), (3, 2)]

    def sibling(x):
        return lax.ppermute(x, "wide", [(i, i ^ 1) for i in range(n_wide)])

    def flip(x, j):
        return lax.ppermute(x, "node", [(i, i ^ j) for i in range(n_node)])

    def swap_halves(weights, c):
        cols = weights[0].shape[1] // 2
        low = jnp.stack([w[:, :cols] for w in weights])
        high = jnp.stack([w[:, cols:] for w in weights])
        got = sibling(jnp.where(c == 0, high, low))
        mine = jnp.where(c == 0, low, high)
        return got, [jnp.stack([mine[i], got[i]]) for i in range(len(weights))]

    def gather_ring(u):
        return [u] + [
            move(u, [(s, (s - j) % planes) for s in range(planes)]) for j in range(1, planes)
        ]

    def slot_planes(z):
        if not line4:
            return [x for j in range(planes) for x in (lax.rem(z + j, planes), 1)]
        beside = lax.bitwise_xor(z, 1)
        inside = (z == 1) | (z == 2)
        found = [z, 1, beside, 1, 3 - z, inside, 3 - beside, inside]
        return found + [3 - beside, ~inside, 3 - z, ~inside]

    def send_planes(z):
        if not line4:
            return [lax.rem(z + j, planes) for j in range(planes)]
        beside = lax.bitwise_xor(z, 1)
        return [z, beside, 3 - z, 3 - beside]

    def added(block, got):
        return (block.astype(F32) + got.astype(F32)).astype(BF16)

    def hold(x, *others):
        for y in others:
            x = jnp.where(jnp.isnan(y[(0,) * y.ndim]), jnp.zeros_like(x), x)
        return x

    def scatter_first(blocks, first):
        return added(blocks[3], first), move(blocks[3], inward)

    def scatter_sums(blocks, second, crossed):
        return added(blocks[2], second), added(blocks[1], crossed)

    def scatter_last(sums):
        return move(sums[0], middle), move(sums[1], outer)

    def scatter_end(own, got, c):
        total = own.astype(F32)
        for part in got:
            total = total + part.astype(F32)
        return join(total[0], sibling(total[1]), c)

    def join(mine, other, c):
        low = jnp.where(c == 0, mine, other)
        high = jnp.where(c == 0, other, mine)
        return jnp.concatenate([low, high], axis=1)

    def scatter_ring(blocks, c):
        total = blocks[0].astype(F32)
        for j in range(1, planes):
            got = move(blocks[j], [(s, (s + j) % planes) for s in range(planes)])
            total = total + got.astype(F32)
        return join(total[0], sibling(total[1]), c)

    def body(act_in, mixing, cotangent, w_value, w_out):
        wide = lax.axis_index("wide")
        n = lax.axis_index("node")
        z, c = wide // 2, lax.rem(wide, 2)
        micro, images, seq, width = act_in.shape
        groups = micro * images
        tokens = groups * seq
        cols = w_value.shape[1] // 2
        heads = cols // HEAD_DIM
        depth = width // planes
        act = act_in.reshape(tokens, width)
        cot = cotangent.reshape(tokens, width)
        mix = mixing.reshape(groups, 2 * heads, seq, seq)
        flops = 4 * tokens * width * cols

        got, (u_out, u_value) = swap_halves([w_out, w_value], c)
        act_s, mix_s, cot_s = (
            sibling(lax.optimization_barrier((x, got))[0]) for x in (act, mix, cot)
        )

        info = slot_planes(z)
        sends = send_planes(z)
        pack = lambda *values: jnp.stack([jnp.int32(x) for x in values])
        idx_slots = pack(c, *info)
        idx_send = pack(c, *sends)
        idx_node = pack(*[lax.bitwise_xor(n, jnp.int32(j)) for j in range(n_node)])

        mix_scratch = pltpu.VMEM((2, groups, heads, seq, seq), BF16)
        both = pltpu.VMEM((2 * tokens, width), BF16)
        halves = pltpu.VMEM((2, tokens, width), BF16)
        left_tokens = pltpu.VMEM((cols, 2 * tokens), BF16)
        rows = pltpu.VMEM((width, cols), BF16)
        block = (2, depth // 2, cols)
        send_shapes = [block] * len(sends)

        if line4:
            v_outer, v_middle = move(u_value, outer), move(u_value, middle)
            v_cross = move(v_outer, middle)
            v_out = move(v_middle, outward)
            v_last = move(v_cross, outward)
            value_slots = [u_value, v_outer, v_middle, v_cross, v_out, v_last]
            swaps = act_s, mix_s, cot_s
            o_outer = move(hold(u_out, v_out, *swaps), outer)
            o_middle = move(hold(u_out, v_cross, *swaps), middle)
            o_cross = move(o_outer, middle)
            o_out = move(o_middle, outward)
        else:
            value_slots = gather_ring(u_value)
            out_slots = gather_ring(u_out)
        n_slots = len(value_slots)

        mixed_o, mixed_s = call(
            functools.partial(mixed_kernel, n_slots),
            "mixed",
            [SMEM] + [ANY] * 4 + [VMEM] * n_slots,
            [(tokens, cols)] * 2,
            [rows, halves, mix_scratch, pltpu.SemaphoreType.DMA((4,))],
            flops,
        )(idx_slots, act, act_s, mix, mix_s, *value_slots)
        mixed_r = sibling(mixed_s)
        idx_out = hold(idx_send, o_outer, o_middle, mixed_r) if line4 else idx_send
        out_sends = call(
            grad_out_kernel,
            "grad_out",
            [SMEM] + [ANY] * 2 + [VMEM] * 2,
            send_shapes,
            [both, left_tokens, rows, pltpu.SemaphoreType.DMA((2,))],
            flops,
        )(idx_out, cot, cot_s, mixed_o, mixed_s)
        if line4:
            inside = (z == 1) | (z == 2)
            swapped = move(hold(jnp.where(inside, o_cross, out_sends[2]), o_out), outer)
            out_slots = [u_out, o_outer, o_middle, o_cross, o_out, swapped]
            out_crossing, out_second = scatter_first(out_sends, swapped)
            out_crossed = move(out_crossing, middle)
            idx_value = hold(idx_slots, out_crossing)
        else:
            idx_value = idx_slots
        w_full, left = call(
            functools.partial(d_value_kernel, n_slots),
            "d_value",
            [SMEM] + [ANY] * 4 + [VMEM] * n_slots,
            [(width, cols), (cols, 2 * tokens)],
            [halves, mix_scratch, pltpu.SemaphoreType.DMA((4,))],
            flops,
        )(idx_value, cot, cot_s, mix, mix_s, *out_slots)
        w_full_s = sibling(w_full)
        part = width // n_node
        half = tokens // 2
        if n_node == 4:
            term_shapes = [(2, half, part), (2, half, part), (4, half, part)]
        else:
            term_shapes = [(tokens, part)] * n_node
        terms = call(
            functools.partial(terms_kernel, n_node),
            "terms",
            [SMEM] + [VMEM] * 4,
            term_shapes,
            [],
            flops,
        )(idx_node, mixed_o, mixed_r, w_full, w_full_s)

        if line4:
            out_sums = scatter_sums(out_sends, out_second, out_crossed)
            out_got = scatter_last(out_sums)
            idx_back = hold(idx_send, *out_sums, terms[0])
        else:
            idx_back = idx_send
        back_sends = call(
            gradient_kernel,
            "grad_value",
            [SMEM] + [ANY] * 2 + [VMEM],
            send_shapes,
            [both, rows, pltpu.SemaphoreType.DMA((2,))],
            flops,
        )(idx_back, act, act_s, left)

        if n_node == 4:
            along_x, along_y, kept = terms
            kept = kept.astype(F32)
            got_x = flip(along_x, 1).astype(F32)
            got_y = flip(along_y, 2).astype(F32)
            last_y = flip((kept[1] + got_x[1]).astype(BF16), 2)
            last_x = flip((kept[3] + got_y[1]).astype(BF16), 1)
            early = got_x, got_y
            layer_out = jnp.concatenate(
                [
                    kept[0] + got_x[0] + last_y.astype(F32),
                    kept[2] + got_y[0] + last_x.astype(F32),
                ],
                axis=0,
            )
        else:
            early, layer_out = terms, terms[0].astype(F32)
            for j in range(1, n_node):
                layer_out = layer_out + flip(terms[j], j).astype(F32)
        layer_out = layer_out.astype(BF16).reshape(micro, images, seq, part)
        if line4:
            first = move(back_sends[2], inward)
            crossing, second = scatter_first(back_sends, first)
            crossed = move(hold(crossing, *early), middle)
            got = scatter_last(scatter_sums(back_sends, second, crossed))
            grad_value = scatter_end(back_sends[0], got, c)
            grad_out = scatter_end(out_sends[0], out_got, c)
        else:
            grad_value = scatter_ring(back_sends, c)
            grad_out = scatter_ring(out_sends, c)
        return layer_out, grad_value, grad_out

    return body


def solution(mesh):
    return jax.shard_map(
        make_body(mesh.shape["wide"], mesh.shape["node"]),
        mesh=mesh,
        in_specs=(
            P(None, "wide", None, None),
            P(None, "wide", "node", None, None),
            P(None, "wide", None, None),
            P("wide", "node"),
            P("wide", "node"),
        ),
        out_specs=(P(None, "wide", None, "node"), P("wide", "node"), P("wide", "node")),
        check_vma=False,
    )
```

```python
import functools
import math

import jax
import jax.numpy as jnp
from jax import lax
from jax.experimental import pallas as pl
from jax.experimental.pallas import tpu as pltpu
from jax.sharding import PartitionSpec as P

HEAD_DIM = 64
F32 = jnp.float32
BF16 = jnp.bfloat16
VMEM_LIMIT = 40 * 1024 * 1024


def dot(a, b, ca=1, cb=0):
    return lax.dot_general(a, b, (((ca,), (cb,)), ((), ())), preferred_element_type=F32)


def begin(pairs, sems):
    copies = [pltpu.make_async_copy(s, d, sems.at[i]) for i, (s, d) in enumerate(pairs)]
    for copy in copies:
        copy.start()
    return copies


def rows_at(index, size):
    return pl.ds(pl.multiple_of(index * size, math.gcd(size, 16)), size)


def place(idx, slots, w_ref):
    core = idx[0]
    for j, slot in enumerate(slots):
        depth = slot.shape[1]
        mine, other = slot[0], slot[1]
        low = jnp.where(core == 0, mine, other)
        high = jnp.where(core == 0, other, mine)
        w_ref[rows_at(idx[1 + j], 2 * depth), :] = jnp.concatenate([low, high], axis=0)


def hand_out(idx, base, grad_v, outs):
    core = idx[0]
    for i, out in enumerate(outs):
        depth = out.shape[1]
        block = grad_v[rows_at(idx[base + i], 2 * depth), :]
        low, high = block[:depth], block[depth:]
        out[0] = jnp.where(core == 0, low, high)
        out[1] = jnp.where(core == 0, high, low)


def gradient_rows(left, right_ref, rows_ref, step):
    width = right_ref.shape[1]
    for start in range(0, width, step):
        part = dot(left, right_ref[:, start : start + step])
        rows_ref[start : start + step, :] = part.T.astype(BF16)


def head_pairs(heads):
    return [(h, min(2, heads - h)) for h in range(0, heads, 2)]


def backward_kernel(n_slots, idx, unread, token, cot_o, cot_s, mix_o, mix_s, act_o, act_s, *rest):
    del unread, token
    slots, rest = rest[:n_slots], rest[n_slots:]
    w_out, rest = rest[0], rest[1:]
    outs, (cot_v, act_v, mix_v, left_v, grad_v, sems) = rest[:-6], rest[-6:]
    tokens, cols = cot_o.shape[0], w_out.shape[1]
    groups, _, seq, _ = mix_o.shape
    heads = mix_v.shape[2]
    here = pl.ds(idx[0] * heads, heads)
    copies = begin(
        [(cot_o, cot_v.at[0]), (mix_o.at[:, here], mix_v.at[0])]
        + [(cot_s, cot_v.at[1]), (mix_s.at[:, here], mix_v.at[1])]
        + [(act_o, act_v.at[pl.ds(0, tokens)]), (act_s, act_v.at[pl.ds(tokens, tokens)])],
        sems,
    )
    place(idx, slots, w_out)
    for half in range(2):
        copies[2 * half].wait()
        d_mixed = dot(cot_v[half], w_out[...])
        copies[2 * half + 1].wait()
        for g in range(groups):
            turned = d_mixed[g * seq : (g + 1) * seq, :].T.astype(BF16)
            at = (half * groups + g) * seq
            for h, n in head_pairs(heads):
                part = turned[h * HEAD_DIM : (h + n) * HEAD_DIM, :]
                if n == 2:
                    row = lax.broadcasted_iota(jnp.int32, part.shape, 0)
                    zero = jnp.zeros_like(part)
                    part = jnp.concatenate(
                        [
                            jnp.where(row < HEAD_DIM, part, zero),
                            jnp.where(row < HEAD_DIM, zero, part),
                        ],
                        axis=1,
                    )
                weights = mix_v[half, g, h : h + n].reshape(n * seq, seq)
                left_v[h * HEAD_DIM : (h + n) * HEAD_DIM, at : at + seq] = dot(
                    part, weights
                ).astype(BF16)
    copies[4].wait()
    copies[5].wait()
    gradient_rows(left_v[...], act_v, grad_v, 640)
    hand_out(idx, 1, grad_v, outs)


def mixed_kernel(n_slots, idx, act_o, act_s, mix_o, mix_s, *rest):
    slots, (mixed_o, mixed_s, w_v, act_v, mix_v, sems) = rest[:n_slots], rest[n_slots:]
    groups, _, seq, _ = mix_o.shape
    heads = mix_v.shape[2]
    here = pl.ds(idx[0] * heads, heads)
    copies = begin(
        [(act_o, act_v.at[0]), (mix_o.at[:, here], mix_v.at[0])]
        + [(act_s, act_v.at[1]), (mix_s.at[:, here], mix_v.at[1])],
        sems,
    )
    place(idx, slots, w_v)
    for half, out in enumerate((mixed_o, mixed_s)):
        copies[2 * half].wait()
        value = dot(act_v[half], w_v[...]).astype(BF16)
        copies[2 * half + 1].wait()
        for g in range(groups):
            for h, n in head_pairs(heads):
                part = value[g * seq : (g + 1) * seq, h * HEAD_DIM : (h + n) * HEAD_DIM]
                weights = mix_v[half, g, h]
                if n == 2:
                    lane = lax.broadcasted_iota(jnp.int32, part.shape, 1)
                    zero = jnp.zeros_like(part)
                    part = jnp.concatenate(
                        [
                            jnp.where(lane < HEAD_DIM, part, zero),
                            jnp.where(lane < HEAD_DIM, zero, part),
                        ],
                        axis=0,
                    )
                    weights = jnp.concatenate([weights, mix_v[half, g, h + 1]], axis=1)
                out[g * seq : (g + 1) * seq, h * HEAD_DIM : (h + n) * HEAD_DIM] = dot(
                    weights, part
                ).astype(BF16)


def grad_out_kernel(idx, cot_o, cot_s, mixed_o, mixed_s, unread, token, *rest):
    del unread
    outs, (cot_v, left_v, grad_v, sems) = rest[:-4], rest[-4:]
    token[...] = jnp.zeros_like(token)
    tokens, _ = cot_o.shape
    copies = begin(
        [(cot_o, cot_v.at[pl.ds(0, tokens)]), (cot_s, cot_v.at[pl.ds(tokens, tokens)])], sems
    )
    left_v[:, :tokens] = mixed_o[...].astype(F32).T.astype(BF16)
    left_v[:, tokens:] = mixed_s[...].astype(F32).T.astype(BF16)
    copies[0].wait()
    copies[1].wait()
    gradient_rows(left_v[...], cot_v, grad_v, 640)
    hand_out(idx, 1, grad_v, outs)


def sum_kernel(token, block, got, out):
    del token
    out[...] = (block[...].astype(F32) + got[...].astype(F32)).astype(BF16)


def terms_kernel(n_node, idx, mixed_o, mixed_r, w_o, w_r, token, *outs):
    token[...] = jnp.zeros_like(token)
    depth = w_o.shape[0] // n_node
    half = mixed_o.shape[0] // 2
    for j in range(n_node):
        rows = rows_at(idx[j], depth)
        term = dot(mixed_o[...], w_o[rows, :], 1, 1) + dot(mixed_r[...], w_r[rows, :], 1, 1)
        term = term.astype(BF16)
        if n_node != 4:
            outs[j][...] = term
            continue
        along_x, along_y, kept = outs
        first, second = term[:half], term[half:]
        if j == 0:
            kept[0], kept[2] = first, second
        elif j == 1:
            along_x[0], kept[3] = first, second
        elif j == 2:
            kept[1], along_y[0] = first, second
        else:
            along_x[1], along_y[1] = first, second


ANY = pl.BlockSpec(memory_space=pl.ANY)
SMEM = pl.BlockSpec(memory_space=pltpu.SMEM)
VMEM = pl.BlockSpec(memory_space=pltpu.VMEM)


def call(kernel, name, in_specs, out_shapes, scratch, flops):
    return pl.pallas_call(
        kernel,
        name=name,
        in_specs=in_specs,
        out_specs=[VMEM] * len(out_shapes),
        out_shape=[jax.ShapeDtypeStruct(s, BF16) for s in out_shapes],
        scratch_shapes=scratch,
        compiler_params=pltpu.CompilerParams(vmem_limit_bytes=VMEM_LIMIT),
        cost_estimate=pl.CostEstimate(flops=flops, bytes_accessed=12 << 20, transcendentals=0),
    )


def make_body(n_wide, n_node):
    planes = n_wide // 2
    line4 = planes == 4

    def move(x, pairs):
        return lax.ppermute(
            x, "wide", [(2 * s + c, 2 * d + c) for s, d in pairs for c in range(2)]
        )

    def swap(x, j):
        return move(x, [(s, s ^ j) for s in range(planes)])

    def sibling(x):
        return lax.ppermute(x, "wide", [(i, i ^ 1) for i in range(n_wide)])

    def flip(x, j):
        return lax.ppermute(x, "node", [(i, i ^ j) for i in range(n_node)])

    def swap_cores(w_out, w_value, act, mix, cot, c):
        cols = w_out.shape[1] // 2
        low = jnp.stack([w_out[:, :cols], w_value[:, :cols]])
        high = jnp.stack([w_out[:, cols:], w_value[:, cols:]])
        got = sibling(jnp.where(c == 0, high, low))
        got, act, mix, cot = lax.optimization_barrier((got, act, mix, cot))
        mine = jnp.where(c == 0, low, high)
        u_out, u_value = (jnp.stack([mine[i], got[i]]) for i in range(2))
        return u_out, u_value, sibling(act), sibling(mix), sibling(cot)

    def gather_ring(u):
        return [u] + [
            move(u, [(s, (s - j) % planes) for s in range(planes)]) for j in range(1, planes)
        ]

    def planes_of(z):
        if line4:
            return [lax.bitwise_xor(z, jnp.int32(j)) for j in range(4)]
        return [lax.rem(z + j, planes) for j in range(planes)]

    def added(block, got):
        return (block.astype(F32) + got.astype(F32)).astype(BF16)

    def gather(u):
        if not line4:
            return gather_ring(u)
        far = swap(u, 2)
        return [u, swap(u, 1), far, swap(far, 1)]

    def scatter(blocks, passed, c, add=added):
        if not line4:
            return scatter_ring(blocks, c)
        far = swap(add(blocks[2], passed), 2)
        return scatter_end(blocks[0], (swap(blocks[1], 1), far), c)

    def scatter_end(own, got, c):
        total = own.astype(F32)
        for part in got:
            total = total + part.astype(F32)
        return join(total[0], sibling(total[1]), c)

    def join(mine, other, c):
        low = jnp.where(c == 0, mine, other)
        high = jnp.where(c == 0, other, mine)
        return jnp.concatenate([low, high], axis=1)

    def scatter_ring(blocks, c):
        total = blocks[0].astype(F32)
        for j in range(1, planes):
            got = move(blocks[j], [(s, (s + j) % planes) for s in range(planes)])
            total = total + got.astype(F32)
        return join(total[0], sibling(total[1]), c)

    def body(act_in, mixing, cotangent, w_value, w_out):
        wide = lax.axis_index("wide")
        n = lax.axis_index("node")
        z, c = wide // 2, lax.rem(wide, 2)
        micro, images, seq, width = act_in.shape
        groups = micro * images
        tokens = groups * seq
        cols = w_value.shape[1] // 2
        heads = cols // HEAD_DIM
        depth = width // planes
        act = act_in.reshape(tokens, width)
        cot = cotangent.reshape(tokens, width)
        mix = mixing.reshape(groups, 2 * heads, seq, seq)
        flops = 4 * tokens * width * cols

        u_out, u_value, act_s, mix_s, cot_s = swap_cores(w_out, w_value, act, mix, cot, c)
        value_slots, out_slots = gather(u_value), gather(u_out)
        n_slots = len(out_slots)
        pack = lambda *values: jnp.stack([jnp.int32(x) for x in values])
        idx = pack(c, *planes_of(z))
        idx_node = pack(*[lax.bitwise_xor(n, jnp.int32(j)) for j in range(n_node)])

        mix_scratch = pltpu.VMEM((2, groups, heads, seq, seq), BF16)
        both = pltpu.VMEM((2 * tokens, width), BF16)
        halves = pltpu.VMEM((2, tokens, width), BF16)
        left_tokens = pltpu.VMEM((cols, 2 * tokens), BF16)
        rows = pltpu.VMEM((width, cols), BF16)
        block = (2, depth // 2, cols)
        send_shapes = [block] * n_slots

        mixed_o, mixed_s = call(
            functools.partial(mixed_kernel, n_slots),
            "mixed",
            [SMEM] + [ANY] * 4 + [VMEM] * n_slots,
            [(tokens, cols)] * 2,
            [rows, halves, mix_scratch, pltpu.SemaphoreType.DMA((4,))],
            flops,
        )(idx, act, act_s, mix, mix_s, *value_slots)
        mixed_r = sibling(mixed_s)
        token, *out_sends = call(
            grad_out_kernel,
            "grad_out",
            [SMEM] + [ANY] * 2 + [VMEM] * 2 + [ANY],
            [(16, 128)] + send_shapes,
            [both, left_tokens, rows, pltpu.SemaphoreType.DMA((2,))],
            flops,
        )(idx, cot, cot_s, mixed_o, mixed_s, mixed_r)
        out_passed = swap(out_sends[3], 1) if line4 else token
        grad_out = scatter(out_sends, out_passed, c)
        w_full, *back_sends = call(
            functools.partial(backward_kernel, n_slots),
            "backward",
            [SMEM, ANY, VMEM] + [ANY] * 6 + [VMEM] * n_slots,
            [(width, cols)] + send_shapes,
            [halves, both, mix_scratch, left_tokens, rows, pltpu.SemaphoreType.DMA((6,))],
            2 * flops,
        )(idx, out_passed, token, cot, cot_s, mix, mix_s, act, act_s, *out_slots)
        w_full_s = sibling(w_full)
        back_passed = swap(back_sends[3], 1) if line4 else token

        part = width // n_node
        half = tokens // 2
        if n_node == 4:
            term_shapes = [(2, half, part), (2, half, part), (4, half, part)]
        else:
            term_shapes = [(tokens, part)] * n_node
        token, *terms = call(
            functools.partial(terms_kernel, n_node),
            "terms",
            [SMEM] + [VMEM] * 4,
            [(16, 128)] + term_shapes,
            [],
            flops,
        )(idx_node, mixed_o, mixed_r, w_full, w_full_s)

        def add_after_terms(a, b):
            return call(sum_kernel, "sum", [VMEM] * 3, [block], [], 0)(token, a, b)[0]

        grad_value = scatter(back_sends, back_passed, c, add_after_terms)
        if n_node == 4:
            along_x, along_y, kept = terms
            kept = kept.astype(F32)
            got_x = flip(along_x, 1).astype(F32)
            got_y = flip(along_y, 2).astype(F32)
            last_y = flip((kept[1] + got_x[1]).astype(BF16), 2)
            last_x = flip((kept[3] + got_y[1]).astype(BF16), 1)
            layer_out = jnp.concatenate(
                [
                    kept[0] + got_x[0] + last_y.astype(F32),
                    kept[2] + got_y[0] + last_x.astype(F32),
                ],
                axis=0,
            )
        else:
            layer_out = terms[0].astype(F32)
            for j in range(1, n_node):
                layer_out = layer_out + flip(terms[j], j).astype(F32)
        layer_out = layer_out.astype(BF16).reshape(micro, images, seq, part)
        return layer_out, grad_value, grad_out

    return body


def solution(mesh):
    return jax.shard_map(
        make_body(mesh.shape["wide"], mesh.shape["node"]),
        mesh=mesh,
        in_specs=(
            P(None, "wide", None, None),
            P(None, "wide", "node", None, None),
            P(None, "wide", None, None),
            P("wide", "node"),
            P("wide", "node"),
        ),
        out_specs=(P(None, "wide", None, "node"), P("wide", "node"), P("wide", "node")),
        check_vma=False,
    )
```

```python
import functools
import math

import jax
import jax.numpy as jnp
from jax import lax
from jax.experimental import pallas as pl
from jax.experimental.pallas import tpu as pltpu
from jax.sharding import PartitionSpec as P

HEAD_DIM = 64
F32 = jnp.float32
BF16 = jnp.bfloat16
VMEM_LIMIT = 40 * 1024 * 1024


def dot(a, b, ca=1, cb=0):
    return lax.dot_general(a, b, (((ca,), (cb,)), ((), ())), preferred_element_type=F32)


def begin(pairs, sems):
    copies = [pltpu.make_async_copy(s, d, sems.at[i]) for i, (s, d) in enumerate(pairs)]
    for copy in copies:
        copy.start()
    return copies


def rows_at(index, size):
    return pl.ds(pl.multiple_of(index * size, math.gcd(size, 16)), size)


def place(idx, slots, which, w_ref):
    core = idx[0]
    for j, slot in enumerate(slots):
        slot = slot if len(slot.shape) == 3 else slot.at[which]
        depth = slot.shape[1]
        mine, other = slot[0], slot[1]
        low = jnp.where(core == 0, mine, other)
        high = jnp.where(core == 0, other, mine)
        w_ref[rows_at(idx[1 + j], 2 * depth), :] = jnp.concatenate([low, high], axis=0)


def hand_out(idx, base, grad_v, outs):
    core = idx[0]
    for i, out in enumerate(outs):
        depth = out.shape[1]
        block = grad_v[rows_at(idx[base + i], 2 * depth), :]
        low, high = block[:depth], block[depth:]
        out[0] = jnp.where(core == 0, low, high)
        out[1] = jnp.where(core == 0, high, low)


def gradient_rows(left, right_ref, rows_ref, step):
    width = right_ref.shape[1]
    for start in range(0, width, step):
        part = dot(left, right_ref[:, start : start + step])
        rows_ref[start : start + step, :] = part.T.astype(BF16)


def head_pairs(heads):
    return [(h, min(2, heads - h)) for h in range(0, heads, 2)]


def assemble_kernel(idx, token, *rest):
    del token
    place(idx, rest[:-1], 1, rest[-1])


def d_value_kernel(idx, cot_o, cot_s, mix_o, mix_s, w_out, left_v, cot_v, mix_v, sems):
    groups, _, seq, _ = mix_o.shape
    heads = mix_v.shape[2]
    here = pl.ds(idx[0] * heads, heads)
    copies = begin(
        [(cot_o, cot_v.at[0]), (mix_o.at[:, here], mix_v.at[0])]
        + [(cot_s, cot_v.at[1]), (mix_s.at[:, here], mix_v.at[1])],
        sems,
    )
    for half in range(2):
        copies[2 * half].wait()
        d_mixed = dot(cot_v[half], w_out[...])
        copies[2 * half + 1].wait()
        for g in range(groups):
            turned = d_mixed[g * seq : (g + 1) * seq, :].T.astype(BF16)
            at = (half * groups + g) * seq
            for h, n in head_pairs(heads):
                part = turned[h * HEAD_DIM : (h + n) * HEAD_DIM, :]
                if n == 2:
                    row = lax.broadcasted_iota(jnp.int32, part.shape, 0)
                    zero = jnp.zeros_like(part)
                    part = jnp.concatenate(
                        [
                            jnp.where(row < HEAD_DIM, part, zero),
                            jnp.where(row < HEAD_DIM, zero, part),
                        ],
                        axis=1,
                    )
                weights = mix_v[half, g, h : h + n].reshape(n * seq, seq)
                left_v[h * HEAD_DIM : (h + n) * HEAD_DIM, at : at + seq] = dot(
                    part, weights
                ).astype(BF16)


def gradient_kernel(n_near, idx, token, unread, right_o, right_s, left_ref, *rest):
    del token, unread
    others, rest = rest[:n_near], rest[n_near:]
    outs, (right_v, grad_v, sems) = rest[:-3], rest[-3:]
    tokens, _ = right_o.shape
    copies = begin(
        [(right_o, right_v.at[pl.ds(0, tokens)]), (right_s, right_v.at[pl.ds(tokens, tokens)])],
        sems,
    )
    copies[0].wait()
    copies[1].wait()
    gradient_rows(left_ref[...], right_v, grad_v, 640)
    for other in others:
        outs[1][1] = other[...]
    hand_out(idx, 1, grad_v, [outs[0], outs[1].at[0], *outs[2:]] if n_near else outs)


def mixed_kernel(n_slots, idx, act_o, act_s, mix_o, mix_s, *rest):
    slots, (mixed_o, mixed_s, w_v, act_v, mix_v, sems) = rest[:n_slots], rest[n_slots:]
    groups, _, seq, _ = mix_o.shape
    heads = mix_v.shape[2]
    here = pl.ds(idx[0] * heads, heads)
    copies = begin(
        [(act_o, act_v.at[0]), (mix_o.at[:, here], mix_v.at[0])]
        + [(act_s, act_v.at[1]), (mix_s.at[:, here], mix_v.at[1])],
        sems,
    )
    place(idx, slots, 0, w_v)
    for half, out in enumerate((mixed_o, mixed_s)):
        copies[2 * half].wait()
        value = dot(act_v[half], w_v[...]).astype(BF16)
        copies[2 * half + 1].wait()
        for g in range(groups):
            for h, n in head_pairs(heads):
                part = value[g * seq : (g + 1) * seq, h * HEAD_DIM : (h + n) * HEAD_DIM]
                weights = mix_v[half, g, h]
                if n == 2:
                    lane = lax.broadcasted_iota(jnp.int32, part.shape, 1)
                    zero = jnp.zeros_like(part)
                    part = jnp.concatenate(
                        [
                            jnp.where(lane < HEAD_DIM, part, zero),
                            jnp.where(lane < HEAD_DIM, zero, part),
                        ],
                        axis=0,
                    )
                    weights = jnp.concatenate([weights, mix_v[half, g, h + 1]], axis=1)
                out[g * seq : (g + 1) * seq, h * HEAD_DIM : (h + n) * HEAD_DIM] = dot(
                    weights, part
                ).astype(BF16)


def grad_out_kernel(idx, cot_o, cot_s, mixed_o, mixed_s, unread, token, *rest):
    del unread
    outs, (cot_v, left_v, grad_v, sems) = rest[:-4], rest[-4:]
    token[...] = jnp.zeros_like(token)
    tokens, _ = cot_o.shape
    copies = begin(
        [(cot_o, cot_v.at[pl.ds(0, tokens)]), (cot_s, cot_v.at[pl.ds(tokens, tokens)])], sems
    )
    left_v[:, :tokens] = mixed_o[...].astype(F32).T.astype(BF16)
    left_v[:, tokens:] = mixed_s[...].astype(F32).T.astype(BF16)
    copies[0].wait()
    copies[1].wait()
    gradient_rows(left_v[...], cot_v, grad_v, 640)
    hand_out(idx, 1, grad_v, outs)


def sum_kernel(unread, block, got, out):
    del unread
    out[...] = (block[...].astype(F32) + got[...].astype(F32)).astype(BF16)


def terms_kernel(n_node, idx, mixed_o, mixed_r, w_o, w_r, token, *outs):
    token[...] = jnp.zeros_like(token)
    depth = w_o.shape[0] // n_node
    half = mixed_o.shape[0] // 2
    for j in range(n_node):
        rows = rows_at(idx[j], depth)
        term = dot(mixed_o[...], w_o[rows, :], 1, 1) + dot(mixed_r[...], w_r[rows, :], 1, 1)
        term = term.astype(BF16)
        if n_node != 4:
            outs[j][...] = term
            continue
        along_x, along_y, kept = outs
        first, second = term[:half], term[half:]
        if j == 0:
            kept[0], kept[2] = first, second
        elif j == 1:
            along_x[0], kept[3] = first, second
        elif j == 2:
            kept[1], along_y[0] = first, second
        else:
            along_x[1], along_y[1] = first, second


ANY = pl.BlockSpec(memory_space=pl.ANY)
SMEM = pl.BlockSpec(memory_space=pltpu.SMEM)
VMEM = pl.BlockSpec(memory_space=pltpu.VMEM)


def call(kernel, name, in_specs, out_shapes, scratch, flops):
    return pl.pallas_call(
        kernel,
        name=name,
        in_specs=in_specs,
        out_specs=[VMEM] * len(out_shapes),
        out_shape=[jax.ShapeDtypeStruct(s, BF16) for s in out_shapes],
        scratch_shapes=scratch,
        compiler_params=pltpu.CompilerParams(vmem_limit_bytes=VMEM_LIMIT),
        cost_estimate=pl.CostEstimate(flops=flops, bytes_accessed=12 << 20, transcendentals=0),
    )


def make_body(n_wide, n_node):
    planes = n_wide // 2
    line4 = planes == 4

    def move(x, pairs):
        return lax.ppermute(
            x, "wide", [(2 * s + c, 2 * d + c) for s, d in pairs for c in range(2)]
        )

    def swap(x, j):
        return move(x, [(s, s ^ j) for s in range(planes)])

    def sibling(x):
        return lax.ppermute(x, "wide", [(i, i ^ 1) for i in range(n_wide)])

    def flip(x, j):
        return lax.ppermute(x, "node", [(i, i ^ j) for i in range(n_node)])

    def swap_cores(w_out, w_value, act, mix, cot, c):
        cols = w_out.shape[1] // 2
        low = jnp.stack([w_out[:, :cols], w_value[:, :cols]])
        high = jnp.stack([w_out[:, cols:], w_value[:, cols:]])
        got = sibling(jnp.where(c == 0, high, low))
        got, act, mix, cot = lax.optimization_barrier((got, act, mix, cot))
        mine = jnp.where(c == 0, low, high)
        u_out, u_value = (jnp.stack([mine[i], got[i]]) for i in range(2))
        return u_out, u_value, sibling(act), sibling(mix), sibling(cot)

    def gather_ring(u):
        return [u] + [
            move(u, [(s, (s - j) % planes) for s in range(planes)]) for j in range(1, planes)
        ]

    def planes_of(z):
        if line4:
            return [lax.bitwise_xor(z, jnp.int32(j)) for j in range(4)]
        return [lax.rem(z + j, planes) for j in range(planes)]

    def added(block, got):
        return (block.astype(F32) + got.astype(F32)).astype(BF16)

    def gather_two(u_value, u_out):
        if not line4:
            return gather_ring(u_value), gather_ring(u_out)
        beside = swap(jnp.stack([u_value, u_out]), 1)
        far_value, far_out = swap(u_value, 2), swap(u_out, 2)
        return (
            [u_value, beside, far_value, swap(far_value, 1)],
            [u_out, beside, far_out, swap(far_out, 1)],
        )

    def scatter_end(own, got, c):
        total = own.astype(F32)
        for part in got:
            total = total + part.astype(F32)
        return join(total[0], sibling(total[1]), c)

    def join(mine, other, c):
        low = jnp.where(c == 0, mine, other)
        high = jnp.where(c == 0, other, mine)
        return jnp.concatenate([low, high], axis=1)

    def scatter_ring(blocks, c):
        total = blocks[0].astype(F32)
        for j in range(1, planes):
            got = move(blocks[j], [(s, (s + j) % planes) for s in range(planes)])
            total = total + got.astype(F32)
        return join(total[0], sibling(total[1]), c)

    def body(act_in, mixing, cotangent, w_value, w_out):
        wide = lax.axis_index("wide")
        n = lax.axis_index("node")
        z, c = wide // 2, lax.rem(wide, 2)
        micro, images, seq, width = act_in.shape
        groups = micro * images
        tokens = groups * seq
        cols = w_value.shape[1] // 2
        heads = cols // HEAD_DIM
        depth = width // planes
        act = act_in.reshape(tokens, width)
        cot = cotangent.reshape(tokens, width)
        mix = mixing.reshape(groups, 2 * heads, seq, seq)
        flops = 4 * tokens * width * cols

        u_out, u_value, act_s, mix_s, cot_s = swap_cores(w_out, w_value, act, mix, cot, c)
        value_slots, out_slots = gather_two(u_value, u_out)
        n_slots = len(out_slots)
        pack = lambda *values: jnp.stack([jnp.int32(x) for x in values])
        idx = pack(c, *planes_of(z))
        idx_node = pack(*[lax.bitwise_xor(n, jnp.int32(j)) for j in range(n_node)])

        mix_scratch = pltpu.VMEM((2, groups, heads, seq, seq), BF16)
        both = pltpu.VMEM((2 * tokens, width), BF16)
        halves = pltpu.VMEM((2, tokens, width), BF16)
        left_tokens = pltpu.VMEM((cols, 2 * tokens), BF16)
        rows = pltpu.VMEM((width, cols), BF16)
        block = (2, depth // 2, cols)
        send_shapes = [block] * n_slots

        mixed_o, mixed_s = call(
            functools.partial(mixed_kernel, n_slots),
            "mixed",
            [SMEM] + [ANY] * 4 + [VMEM] * n_slots,
            [(tokens, cols)] * 2,
            [rows, halves, mix_scratch, pltpu.SemaphoreType.DMA((4,))],
            flops,
        )(idx, act, act_s, mix, mix_s, *value_slots)
        mixed_r = sibling(mixed_s)
        token, *out_sends = call(
            grad_out_kernel,
            "grad_out",
            [SMEM] + [ANY] * 2 + [VMEM] * 2 + [ANY],
            [(16, 128)] + send_shapes,
            [both, left_tokens, rows, pltpu.SemaphoreType.DMA((2,))],
            flops,
        )(idx, cot, cot_s, mixed_o, mixed_s, mixed_r)
        out_passed = swap(out_sends[3], 1) if line4 else token
        w_full = call(
            assemble_kernel,
            "assemble",
            [SMEM, ANY] + [VMEM] * n_slots,
            [(width, cols)],
            [],
            0,
        )(idx, token, *out_slots)[0]
        w_full_s = sibling(w_full)
        left = call(
            d_value_kernel,
            "d_value",
            [SMEM] + [ANY] * 4 + [VMEM],
            [(cols, 2 * tokens)],
            [halves, mix_scratch, pltpu.SemaphoreType.DMA((4,))],
            flops,
        )(idx, cot, cot_s, mix, mix_s, w_full)[0]
        if line4:
            out_onward = added(out_sends[2], out_passed)
            out_far = swap(out_onward, 2)
            others = [out_sends[1]]
            back_shapes = [block, (2, *block), block, block]
        else:
            out_onward, others, back_shapes = token, [], send_shapes
        part = width // n_node
        half = tokens // 2
        if n_node == 4:
            term_shapes = [(2, half, part), (2, half, part), (4, half, part)]
        else:
            term_shapes = [(tokens, part)] * n_node
        token, *terms = call(
            functools.partial(terms_kernel, n_node),
            "terms",
            [SMEM] + [VMEM] * 4,
            [(16, 128)] + term_shapes,
            [],
            flops,
        )(idx_node, mixed_o, mixed_r, w_full, w_full_s)

        back_sends = call(
            functools.partial(gradient_kernel, len(others)),
            "grad_value",
            [SMEM] + [ANY] * 4 + [VMEM] * (1 + len(others)),
            back_shapes,
            [both, rows, pltpu.SemaphoreType.DMA((2,))],
            flops,
        )(idx, token, out_onward, act, act_s, left, *others)
        if line4:
            near = swap(back_sends[1], 1)
            back_passed = swap(back_sends[3], 1)
            onward = call(sum_kernel, "sum", [ANY] + [VMEM] * 2, [block], [], 0)(
                out_far, back_sends[2], back_passed
            )[0]
            grad_out = scatter_end(out_sends[0], (near[1], out_far), c)
            grad_value = scatter_end(back_sends[0], (near[0], swap(onward, 2)), c)
        else:
            grad_value = scatter_ring(back_sends, c)
            grad_out = scatter_ring(out_sends, c)

        if n_node == 4:
            along_x, along_y, kept = terms
            kept = kept.astype(F32)
            got_x = flip(along_x, 1).astype(F32)
            got_y = flip(along_y, 2).astype(F32)
            last_y = flip((kept[1] + got_x[1]).astype(BF16), 2)
            last_x = flip((kept[3] + got_y[1]).astype(BF16), 1)
            layer_out = jnp.concatenate(
                [
                    kept[0] + got_x[0] + last_y.astype(F32),
                    kept[2] + got_y[0] + last_x.astype(F32),
                ],
                axis=0,
            )
        else:
            layer_out = terms[0].astype(F32)
            for j in range(1, n_node):
                layer_out = layer_out + flip(terms[j], j).astype(F32)
        layer_out = layer_out.astype(BF16).reshape(micro, images, seq, part)
        return layer_out, grad_value, grad_out

    return body


def solution(mesh):
    return jax.shard_map(
        make_body(mesh.shape["wide"], mesh.shape["node"]),
        mesh=mesh,
        in_specs=(
            P(None, "wide", None, None),
            P(None, "wide", "node", None, None),
            P(None, "wide", None, None),
            P("wide", "node"),
            P("wide", "node"),
        ),
        out_specs=(P(None, "wide", None, "node"), P("wide", "node"), P("wide", "node")),
        check_vma=False,
    )
```

```python
import functools
import math

import jax
import jax.numpy as jnp
from jax import lax
from jax.experimental import pallas as pl
from jax.experimental.pallas import tpu as pltpu
from jax.sharding import PartitionSpec as P

HEAD_DIM = 64
F32 = jnp.float32
BF16 = jnp.bfloat16
VMEM_LIMIT = 40 * 1024 * 1024


def dot(a, b, ca=1, cb=0):
    return lax.dot_general(a, b, (((ca,), (cb,)), ((), ())), preferred_element_type=F32)


def begin(pairs, sems):
    copies = [pltpu.make_async_copy(s, d, sems.at[i]) for i, (s, d) in enumerate(pairs)]
    for copy in copies:
        copy.start()
    return copies


def rows_at(index, size):
    return pl.ds(pl.multiple_of(index * size, math.gcd(size, 16)), size)


def place(idx, slots, which, w_ref):
    core = idx[0]
    for j, slot in enumerate(slots):
        slot = slot if len(slot.shape) == 3 else slot.at[which]
        depth = slot.shape[1]
        mine, other = slot[0], slot[1]
        low = jnp.where(core == 0, mine, other)
        high = jnp.where(core == 0, other, mine)
        w_ref[rows_at(idx[1 + j], 2 * depth), :] = jnp.concatenate([low, high], axis=0)


def hand_out(idx, base, grad_v, outs):
    core = idx[0]
    for i, out in enumerate(outs):
        depth = out.shape[1]
        block = grad_v[rows_at(idx[base + i], 2 * depth), :]
        low, high = block[:depth], block[depth:]
        out[0] = jnp.where(core == 0, low, high)
        out[1] = jnp.where(core == 0, high, low)


def gradient_rows(left, right_ref, rows_ref, step):
    width = right_ref.shape[1]
    for start in range(0, width, step):
        part = dot(left, right_ref[:, start : start + step])
        rows_ref[start : start + step, :] = part.T.astype(BF16)


def head_pairs(heads):
    return [(h, min(2, heads - h)) for h in range(0, heads, 2)]


def assemble_kernel(idx, token, *rest):
    del token
    place(idx, rest[:-1], 1, rest[-1])


def d_value_kernel(idx, cot_o, cot_s, mix_o, mix_s, w_out, left_v, cot_v, mix_v, sems):
    groups, _, seq, _ = mix_o.shape
    heads = mix_v.shape[2]
    here = pl.ds(idx[0] * heads, heads)
    copies = begin(
        [(cot_o, cot_v.at[0]), (mix_o.at[:, here], mix_v.at[0])]
        + [(cot_s, cot_v.at[1]), (mix_s.at[:, here], mix_v.at[1])],
        sems,
    )
    for half in range(2):
        copies[2 * half].wait()
        d_mixed = dot(cot_v[half], w_out[...])
        copies[2 * half + 1].wait()
        for g in range(groups):
            turned = d_mixed[g * seq : (g + 1) * seq, :].T.astype(BF16)
            at = (half * groups + g) * seq
            for h, n in head_pairs(heads):
                part = turned[h * HEAD_DIM : (h + n) * HEAD_DIM, :]
                if n == 2:
                    row = lax.broadcasted_iota(jnp.int32, part.shape, 0)
                    zero = jnp.zeros_like(part)
                    part = jnp.concatenate(
                        [
                            jnp.where(row < HEAD_DIM, part, zero),
                            jnp.where(row < HEAD_DIM, zero, part),
                        ],
                        axis=1,
                    )
                weights = mix_v[half, g, h : h + n].reshape(n * seq, seq)
                left_v[h * HEAD_DIM : (h + n) * HEAD_DIM, at : at + seq] = dot(
                    part, weights
                ).astype(BF16)


def gradient_kernel(idx, token, unread, right_o, right_s, left_ref, *rest):
    del token, unread
    outs, (right_v, grad_v, sems) = rest[:-3], rest[-3:]
    tokens, _ = right_o.shape
    copies = begin(
        [(right_o, right_v.at[pl.ds(0, tokens)]), (right_s, right_v.at[pl.ds(tokens, tokens)])],
        sems,
    )
    copies[0].wait()
    copies[1].wait()
    gradient_rows(left_ref[...], right_v, grad_v, 640)
    hand_out(idx, 1, grad_v, outs)


def mixed_kernel(n_slots, idx, act_o, act_s, mix_o, mix_s, *rest):
    slots, (mixed_o, mixed_s, w_v, act_v, mix_v, sems) = rest[:n_slots], rest[n_slots:]
    groups, _, seq, _ = mix_o.shape
    heads = mix_v.shape[2]
    here = pl.ds(idx[0] * heads, heads)
    copies = begin(
        [(act_o, act_v.at[0]), (mix_o.at[:, here], mix_v.at[0])]
        + [(act_s, act_v.at[1]), (mix_s.at[:, here], mix_v.at[1])],
        sems,
    )
    place(idx, slots, 0, w_v)
    for half, out in enumerate((mixed_o, mixed_s)):
        copies[2 * half].wait()
        value = dot(act_v[half], w_v[...]).astype(BF16)
        copies[2 * half + 1].wait()
        for g in range(groups):
            for h, n in head_pairs(heads):
                part = value[g * seq : (g + 1) * seq, h * HEAD_DIM : (h + n) * HEAD_DIM]
                weights = mix_v[half, g, h]
                if n == 2:
                    lane = lax.broadcasted_iota(jnp.int32, part.shape, 1)
                    zero = jnp.zeros_like(part)
                    part = jnp.concatenate(
                        [
                            jnp.where(lane < HEAD_DIM, part, zero),
                            jnp.where(lane < HEAD_DIM, zero, part),
                        ],
                        axis=0,
                    )
                    weights = jnp.concatenate([weights, mix_v[half, g, h + 1]], axis=1)
                out[g * seq : (g + 1) * seq, h * HEAD_DIM : (h + n) * HEAD_DIM] = dot(
                    weights, part
                ).astype(BF16)


def grad_out_kernel(n_unread, idx, cot_o, cot_s, mixed_o, mixed_s, *rest):
    token, *rest = rest[n_unread:]
    outs, (cot_v, left_v, grad_v, sems) = rest[:-4], rest[-4:]
    token[...] = jnp.zeros_like(token)
    tokens, _ = cot_o.shape
    copies = begin(
        [(cot_o, cot_v.at[pl.ds(0, tokens)]), (cot_s, cot_v.at[pl.ds(tokens, tokens)])], sems
    )
    left_v[:, :tokens] = mixed_o[...].astype(F32).T.astype(BF16)
    left_v[:, tokens:] = mixed_s[...].astype(F32).T.astype(BF16)
    copies[0].wait()
    copies[1].wait()
    gradient_rows(left_v[...], cot_v, grad_v, 640)
    hand_out(idx, 1, grad_v, outs)


def release_kernel(unread, block, out):
    del unread
    out[...] = block[...]


def sum_kernel(block, got, beside, own, near, far, onward, beside_out, total):
    onward[...] = (block[...].astype(F32) + got[...].astype(F32)).astype(BF16)
    beside_out[...] = beside[...]
    total[...] = own[...].astype(F32) + near[...].astype(F32) + far[...].astype(F32)


def terms_kernel(n_node, idx, mixed_o, mixed_r, w_o, w_r, token, *outs):
    token[...] = jnp.zeros_like(token)
    depth = w_o.shape[0] // n_node
    half = mixed_o.shape[0] // 2
    for j in range(n_node):
        rows = rows_at(idx[j], depth)
        term = dot(mixed_o[...], w_o[rows, :], 1, 1) + dot(mixed_r[...], w_r[rows, :], 1, 1)
        term = term.astype(BF16)
        if n_node != 4:
            outs[j][...] = term
            continue
        along_x, along_y, kept = outs
        first, second = term[:half], term[half:]
        if j == 0:
            kept[0], kept[2] = first, second
        elif j == 1:
            along_x[0], kept[3] = first, second
        elif j == 2:
            kept[1], along_y[0] = first, second
        else:
            along_x[1], along_y[1] = first, second


ANY = pl.BlockSpec(memory_space=pl.ANY)
SMEM = pl.BlockSpec(memory_space=pltpu.SMEM)
VMEM = pl.BlockSpec(memory_space=pltpu.VMEM)


def call(kernel, name, in_specs, out_shapes, scratch, flops, kinds=None):
    return pl.pallas_call(
        kernel,
        name=name,
        in_specs=in_specs,
        out_specs=[VMEM] * len(out_shapes),
        out_shape=[
            jax.ShapeDtypeStruct(s, k) for s, k in zip(out_shapes, kinds or [BF16] * len(out_shapes))
        ],
        scratch_shapes=scratch,
        compiler_params=pltpu.CompilerParams(vmem_limit_bytes=VMEM_LIMIT),
        cost_estimate=pl.CostEstimate(flops=flops, bytes_accessed=12 << 20, transcendentals=0),
    )


def make_body(n_wide, n_node):
    planes = n_wide // 2
    line4 = planes == 4

    def move(x, pairs):
        return lax.ppermute(
            x, "wide", [(2 * s + c, 2 * d + c) for s, d in pairs for c in range(2)]
        )

    def swap(x, j):
        return move(x, [(s, s ^ j) for s in range(planes)])

    def sibling(x):
        return lax.ppermute(x, "wide", [(i, i ^ 1) for i in range(n_wide)])

    def flip(x, j):
        return lax.ppermute(x, "node", [(i, i ^ j) for i in range(n_node)])

    def swap_cores(w_out, w_value, act, mix, cot, c):
        cols = w_out.shape[1] // 2
        low = jnp.stack([w_out[:, :cols], w_value[:, :cols]])
        high = jnp.stack([w_out[:, cols:], w_value[:, cols:]])
        got = sibling(jnp.where(c == 0, high, low))
        got, act, mix, cot = lax.optimization_barrier((got, act, mix, cot))
        mine = jnp.where(c == 0, low, high)
        u_out, u_value = (jnp.stack([mine[i], got[i]]) for i in range(2))
        return u_out, u_value, sibling(act), sibling(mix), sibling(cot)

    def gather_ring(u):
        return [u] + [
            move(u, [(s, (s - j) % planes) for s in range(planes)]) for j in range(1, planes)
        ]

    def planes_of(z):
        if line4:
            return [lax.bitwise_xor(z, jnp.int32(j)) for j in range(4)]
        return [lax.rem(z + j, planes) for j in range(planes)]

    def added(block, got):
        return (block.astype(F32) + got.astype(F32)).astype(BF16)

    def gather_steps(u):
        far = swap(u, 2)
        return [u, swap(u, 1), far, swap(far, 1)]

    def scatter_end(own, got, c):
        total = own.astype(F32)
        for part in got:
            total = total + part.astype(F32)
        return join(total[0], sibling(total[1]), c)

    def join(mine, other, c):
        low = jnp.where(c == 0, mine, other)
        high = jnp.where(c == 0, other, mine)
        return jnp.concatenate([low, high], axis=1)

    def scatter_ring(blocks, c):
        total = blocks[0].astype(F32)
        for j in range(1, planes):
            got = move(blocks[j], [(s, (s + j) % planes) for s in range(planes)])
            total = total + got.astype(F32)
        return join(total[0], sibling(total[1]), c)

    def body(act_in, mixing, cotangent, w_value, w_out):
        wide = lax.axis_index("wide")
        n = lax.axis_index("node")
        z, c = wide // 2, lax.rem(wide, 2)
        micro, images, seq, width = act_in.shape
        groups = micro * images
        tokens = groups * seq
        cols = w_value.shape[1] // 2
        heads = cols // HEAD_DIM
        depth = width // planes
        act = act_in.reshape(tokens, width)
        cot = cotangent.reshape(tokens, width)
        mix = mixing.reshape(groups, 2 * heads, seq, seq)
        flops = 4 * tokens * width * cols

        u_out, u_value, act_s, mix_s, cot_s = swap_cores(w_out, w_value, act, mix, cot, c)
        block = u_out.shape
        if line4:
            value_slots = gather_steps(u_value)
            u_out = call(release_kernel, "release", [ANY, VMEM], [block], [], 0)(
                value_slots[3], u_out
            )[0]
            out_slots = gather_steps(u_out)
        else:
            value_slots, out_slots = gather_ring(u_value), gather_ring(u_out)
        n_slots = len(out_slots)
        pack = lambda *values: jnp.stack([jnp.int32(x) for x in values])
        idx = pack(c, *planes_of(z))
        idx_node = pack(*[lax.bitwise_xor(n, jnp.int32(j)) for j in range(n_node)])

        mix_scratch = pltpu.VMEM((2, groups, heads, seq, seq), BF16)
        both = pltpu.VMEM((2 * tokens, width), BF16)
        halves = pltpu.VMEM((2, tokens, width), BF16)
        left_tokens = pltpu.VMEM((cols, 2 * tokens), BF16)
        rows = pltpu.VMEM((width, cols), BF16)
        send_shapes = [block] * n_slots

        mixed_o, mixed_s = call(
            functools.partial(mixed_kernel, n_slots),
            "mixed",
            [SMEM] + [ANY] * 4 + [VMEM] * n_slots,
            [(tokens, cols)] * 2,
            [rows, halves, mix_scratch, pltpu.SemaphoreType.DMA((4,))],
            flops,
        )(idx, act, act_s, mix, mix_s, *value_slots)
        mixed_r = sibling(mixed_s)
        unread = [mixed_r, *(out_slots[1:3] if line4 else [])]
        token, *out_sends = call(
            functools.partial(grad_out_kernel, len(unread)),
            "grad_out",
            [SMEM] + [ANY] * 2 + [VMEM] * 2 + [ANY] * len(unread),
            [(16, 128)] + send_shapes,
            [both, left_tokens, rows, pltpu.SemaphoreType.DMA((2,))],
            flops,
        )(idx, cot, cot_s, mixed_o, mixed_s, *unread)
        out_passed = swap(out_sends[3], 1) if line4 else token
        w_full = call(
            assemble_kernel,
            "assemble",
            [SMEM, ANY] + [VMEM] * n_slots,
            [(width, cols)],
            [],
            0,
        )(idx, token, *out_slots)[0]
        w_full_s = sibling(w_full)
        left = call(
            d_value_kernel,
            "d_value",
            [SMEM] + [ANY] * 4 + [VMEM],
            [(cols, 2 * tokens)],
            [halves, mix_scratch, pltpu.SemaphoreType.DMA((4,))],
            flops,
        )(idx, cot, cot_s, mix, mix_s, w_full)[0]
        if line4:
            out_onward = added(out_sends[2], out_passed)
            out_far = swap(out_onward, 2)
            out_near = swap(out_sends[1], 1)
        else:
            out_onward = token
        part = width // n_node
        half = tokens // 2
        if n_node == 4:
            term_shapes = [(2, half, part), (2, half, part), (4, half, part)]
        else:
            term_shapes = [(tokens, part)] * n_node
        token, *terms = call(
            functools.partial(terms_kernel, n_node),
            "terms",
            [SMEM] + [VMEM] * 4,
            [(16, 128)] + term_shapes,
            [],
            flops,
        )(idx_node, mixed_o, mixed_r, w_full, w_full_s)

        back_sends = call(
            gradient_kernel,
            "grad_value",
            [SMEM] + [ANY] * 4 + [VMEM],
            send_shapes,
            [both, rows, pltpu.SemaphoreType.DMA((2,))],
            flops,
        )(idx, token, out_onward, act, act_s, left)
        if line4:
            back_passed = swap(back_sends[3], 1)
            onward, beside, out_total = call(
                sum_kernel, "sum", [VMEM] * 6, [block] * 3, [], 0, [BF16, BF16, F32]
            )(back_sends[2], back_passed, back_sends[1], out_sends[0], out_near, out_far)
            back_far, back_near = swap(onward, 2), swap(beside, 1)
            grad_out = join(out_total[0], sibling(out_total[1]), c)
            grad_value = scatter_end(back_sends[0], (back_near, back_far), c)
        else:
            grad_value = scatter_ring(back_sends, c)
            grad_out = scatter_ring(out_sends, c)

        if n_node == 4:
            along_x, along_y, kept = terms
            kept = kept.astype(F32)
            got_x = flip(along_x, 1).astype(F32)
            got_y = flip(along_y, 2).astype(F32)
            last_y = flip((kept[1] + got_x[1]).astype(BF16), 2)
            last_x = flip((kept[3] + got_y[1]).astype(BF16), 1)
            layer_out = jnp.concatenate(
                [
                    kept[0] + got_x[0] + last_y.astype(F32),
                    kept[2] + got_y[0] + last_x.astype(F32),
                ],
                axis=0,
            )
        else:
            layer_out = terms[0].astype(F32)
            for j in range(1, n_node):
                layer_out = layer_out + flip(terms[j], j).astype(F32)
        layer_out = layer_out.astype(BF16).reshape(micro, images, seq, part)
        return layer_out, grad_value, grad_out

    return body


def solution(mesh):
    return jax.shard_map(
        make_body(mesh.shape["wide"], mesh.shape["node"]),
        mesh=mesh,
        in_specs=(
            P(None, "wide", None, None),
            P(None, "wide", "node", None, None),
            P(None, "wide", None, None),
            P("wide", "node"),
            P("wide", "node"),
        ),
        out_specs=(P(None, "wide", None, "node"), P("wide", "node"), P("wide", "node")),
        check_vma=False,
    )
```

```python
import functools
import math

import jax
import jax.numpy as jnp
from jax import lax
from jax.experimental import pallas as pl
from jax.experimental.pallas import tpu as pltpu
from jax.sharding import PartitionSpec as P

HEAD_DIM = 64
F32 = jnp.float32
BF16 = jnp.bfloat16
VMEM_LIMIT = 40 * 1024 * 1024


def dot(a, b, ca=1, cb=0):
    return lax.dot_general(a, b, (((ca,), (cb,)), ((), ())), preferred_element_type=F32)


def begin_slots(slots, slots_v, sems):
    return begin([(slot, slots_v.at[j]) for j, slot in enumerate(slots)], sems)


def begin(pairs, sems):
    copies = [pltpu.make_async_copy(s, d, sems.at[i]) for i, (s, d) in enumerate(pairs)]
    for copy in copies:
        copy.start()
    return copies


def rows_at(index, size):
    return pl.ds(pl.multiple_of(index * size, math.gcd(size, 16)), size)


def place(idx, slots_v, w_ref):
    core = idx[0]
    for j in range(slots_v.shape[0]):
        depth = slots_v.shape[2]
        mine, other = slots_v[j, 0], slots_v[j, 1]
        low = jnp.where(core == 0, mine, other)
        high = jnp.where(core == 0, other, mine)
        w_ref[rows_at(idx[1 + j], 2 * depth), :] = jnp.concatenate([low, high], axis=0)


def hand_out(idx, base, grad_v, outs):
    core = idx[0]
    for i, out in enumerate(outs):
        depth = out.shape[1]
        block = grad_v[rows_at(idx[base + i], 2 * depth), :]
        low, high = block[:depth], block[depth:]
        out[0] = jnp.where(core == 0, low, high)
        out[1] = jnp.where(core == 0, high, low)


def gradient_rows(left, right_ref, rows_ref, step):
    width = right_ref.shape[1]
    for start in range(0, width, step):
        part = dot(left, right_ref[:, start : start + step])
        rows_ref[start : start + step, :] = part.T.astype(BF16)


def head_pairs(heads):
    return [(h, min(2, heads - h)) for h in range(0, heads, 2)]


def assemble_kernel(idx, token, *rest):
    del token
    slots, (w_out, slots_v, sems) = rest[:-3], rest[-3:]
    for copy in begin_slots(slots, slots_v, sems):
        copy.wait()
    place(idx, slots_v, w_out)


def d_value_kernel(idx, cot_o, cot_s, mix_o, mix_s, w_out, left_v, cot_v, mix_v, sems):
    groups, _, seq, _ = mix_o.shape
    heads = mix_v.shape[2]
    here = pl.ds(idx[0] * heads, heads)
    copies = begin(
        [(cot_o, cot_v.at[0]), (mix_o.at[:, here], mix_v.at[0])]
        + [(cot_s, cot_v.at[1]), (mix_s.at[:, here], mix_v.at[1])],
        sems,
    )
    for half in range(2):
        copies[2 * half].wait()
        d_mixed = dot(cot_v[half], w_out[...])
        copies[2 * half + 1].wait()
        for g in range(groups):
            turned = d_mixed[g * seq : (g + 1) * seq, :].T.astype(BF16)
            at = (half * groups + g) * seq
            for h, n in head_pairs(heads):
                part = turned[h * HEAD_DIM : (h + n) * HEAD_DIM, :]
                if n == 2:
                    row = lax.broadcasted_iota(jnp.int32, part.shape, 0)
                    zero = jnp.zeros_like(part)
                    part = jnp.concatenate(
                        [
                            jnp.where(row < HEAD_DIM, part, zero),
                            jnp.where(row < HEAD_DIM, zero, part),
                        ],
                        axis=1,
                    )
                weights = mix_v[half, g, h : h + n].reshape(n * seq, seq)
                left_v[h * HEAD_DIM : (h + n) * HEAD_DIM, at : at + seq] = dot(
                    part, weights
                ).astype(BF16)


def gradient_kernel(idx, token, unread, right_o, right_s, left_ref, *rest):
    del token, unread
    outs, (right_v, grad_v, sems) = rest[:-3], rest[-3:]
    tokens, _ = right_o.shape
    copies = begin(
        [(right_o, right_v.at[pl.ds(0, tokens)]), (right_s, right_v.at[pl.ds(tokens, tokens)])],
        sems,
    )
    copies[0].wait()
    copies[1].wait()
    gradient_rows(left_ref[...], right_v, grad_v, 640)
    hand_out(idx, 1, grad_v, outs)


def mixed_kernel(n_slots, idx, act_o, act_s, mix_o, mix_s, *rest):
    slots, rest = rest[:n_slots], rest[n_slots:]
    mixed_o, mixed_s, w_v, act_v, mix_v, sems, slots_v, slot_sems = rest
    groups, _, seq, _ = mix_o.shape
    heads = mix_v.shape[2]
    here = pl.ds(idx[0] * heads, heads)
    slot_copies = begin_slots(slots, slots_v, slot_sems)
    copies = begin(
        [(act_o, act_v.at[0]), (mix_o.at[:, here], mix_v.at[0])]
        + [(act_s, act_v.at[1]), (mix_s.at[:, here], mix_v.at[1])],
        sems,
    )
    for copy in slot_copies:
        copy.wait()
    place(idx, slots_v, w_v)
    for half, out in enumerate((mixed_o, mixed_s)):
        copies[2 * half].wait()
        value = dot(act_v[half], w_v[...]).astype(BF16)
        copies[2 * half + 1].wait()
        for g in range(groups):
            for h, n in head_pairs(heads):
                part = value[g * seq : (g + 1) * seq, h * HEAD_DIM : (h + n) * HEAD_DIM]
                weights = mix_v[half, g, h]
                if n == 2:
                    lane = lax.broadcasted_iota(jnp.int32, part.shape, 1)
                    zero = jnp.zeros_like(part)
                    part = jnp.concatenate(
                        [
                            jnp.where(lane < HEAD_DIM, part, zero),
                            jnp.where(lane < HEAD_DIM, zero, part),
                        ],
                        axis=0,
                    )
                    weights = jnp.concatenate([weights, mix_v[half, g, h + 1]], axis=1)
                out[g * seq : (g + 1) * seq, h * HEAD_DIM : (h + n) * HEAD_DIM] = dot(
                    weights, part
                ).astype(BF16)


def grad_out_kernel(n_unread, idx, cot_o, cot_s, mixed_o, mixed_s, *rest):
    token, *rest = rest[n_unread:]
    outs, (cot_v, left_v, grad_v, sems) = rest[:-4], rest[-4:]
    token[...] = jnp.zeros_like(token)
    tokens, _ = cot_o.shape
    copies = begin(
        [(cot_o, cot_v.at[pl.ds(0, tokens)]), (cot_s, cot_v.at[pl.ds(tokens, tokens)])], sems
    )
    left_v[:, :tokens] = mixed_o[...].astype(F32).T.astype(BF16)
    left_v[:, tokens:] = mixed_s[...].astype(F32).T.astype(BF16)
    copies[0].wait()
    copies[1].wait()
    gradient_rows(left_v[...], cot_v, grad_v, 640)
    hand_out(idx, 1, grad_v, outs)


def release_kernel(unread, block, out):
    del unread
    out[...] = block[...]


def sum_kernel(block, got, beside, own, near, far, onward, beside_out, total):
    onward[...] = (block[...].astype(F32) + got[...].astype(F32)).astype(BF16)
    beside_out[...] = beside[...]
    total[...] = own[...].astype(F32) + near[...].astype(F32) + far[...].astype(F32)


def terms_kernel(n_node, idx, mixed_o, mixed_r, w_o, w_r, token, *outs):
    token[...] = jnp.zeros_like(token)
    depth = w_o.shape[0] // n_node
    half = mixed_o.shape[0] // 2
    for j in range(n_node):
        rows = rows_at(idx[j], depth)
        term = dot(mixed_o[...], w_o[rows, :], 1, 1) + dot(mixed_r[...], w_r[rows, :], 1, 1)
        term = term.astype(BF16)
        if n_node != 4:
            outs[j][...] = term
            continue
        along_x, along_y, kept = outs
        first, second = term[:half], term[half:]
        if j == 0:
            kept[0], kept[2] = first, second
        elif j == 1:
            along_x[0], kept[3] = first, second
        elif j == 2:
            kept[1], along_y[0] = first, second
        else:
            along_x[1], along_y[1] = first, second


ANY = pl.BlockSpec(memory_space=pl.ANY)
SMEM = pl.BlockSpec(memory_space=pltpu.SMEM)
VMEM = pl.BlockSpec(memory_space=pltpu.VMEM)


def call(kernel, name, in_specs, out_shapes, scratch, flops, size=1 << 20, kinds=None):
    return pl.pallas_call(
        kernel,
        name=name,
        in_specs=in_specs,
        out_specs=[VMEM] * len(out_shapes),
        out_shape=[
            jax.ShapeDtypeStruct(s, k) for s, k in zip(out_shapes, kinds or [BF16] * len(out_shapes))
        ],
        scratch_shapes=scratch,
        compiler_params=pltpu.CompilerParams(vmem_limit_bytes=VMEM_LIMIT),
        cost_estimate=pl.CostEstimate(flops=flops, bytes_accessed=size, transcendentals=0),
    )


def make_body(n_wide, n_node):
    planes = n_wide // 2
    line4 = planes == 4

    def move(x, pairs):
        return lax.ppermute(
            x, "wide", [(2 * s + c, 2 * d + c) for s, d in pairs for c in range(2)]
        )

    def swap(x, j):
        return move(x, [(s, s ^ j) for s in range(planes)])

    def sibling(x):
        return lax.ppermute(x, "wide", [(i, i ^ 1) for i in range(n_wide)])

    def flip(x, j):
        return lax.ppermute(x, "node", [(i, i ^ j) for i in range(n_node)])

    def swap_cores(w_out, w_value, act, mix, cot, c):
        cols = w_out.shape[1] // 2
        low = jnp.stack([w_out[:, :cols], w_value[:, :cols]])
        high = jnp.stack([w_out[:, cols:], w_value[:, cols:]])
        got = sibling(jnp.where(c == 0, high, low))
        got, act, mix, cot = lax.optimization_barrier((got, act, mix, cot))
        mine = jnp.where(c == 0, low, high)
        u_out, u_value = (jnp.stack([mine[i], got[i]]) for i in range(2))
        return u_out, u_value, sibling(act), sibling(mix), sibling(cot)

    def gather_ring(u):
        return [u] + [
            move(u, [(s, (s - j) % planes) for s in range(planes)]) for j in range(1, planes)
        ]

    def planes_of(z):
        if line4:
            return [lax.bitwise_xor(z, jnp.int32(j)) for j in range(4)]
        return [lax.rem(z + j, planes) for j in range(planes)]

    def added(block, got):
        return (block.astype(F32) + got.astype(F32)).astype(BF16)

    def scatter_end(own, got, c):
        total = own.astype(F32)
        for part in got:
            total = total + part.astype(F32)
        return join(total[0], sibling(total[1]), c)

    def join(mine, other, c):
        low = jnp.where(c == 0, mine, other)
        high = jnp.where(c == 0, other, mine)
        return jnp.concatenate([low, high], axis=1)

    def scatter_ring(blocks, c):
        total = blocks[0].astype(F32)
        for j in range(1, planes):
            got = move(blocks[j], [(s, (s + j) % planes) for s in range(planes)])
            total = total + got.astype(F32)
        return join(total[0], sibling(total[1]), c)

    def body(act_in, mixing, cotangent, w_value, w_out):
        wide = lax.axis_index("wide")
        n = lax.axis_index("node")
        z, c = wide // 2, lax.rem(wide, 2)
        micro, images, seq, width = act_in.shape
        groups = micro * images
        tokens = groups * seq
        cols = w_value.shape[1] // 2
        heads = cols // HEAD_DIM
        depth = width // planes
        act = act_in.reshape(tokens, width)
        cot = cotangent.reshape(tokens, width)
        mix = mixing.reshape(groups, 2 * heads, seq, seq)
        flops = 4 * tokens * width * cols

        u_out, u_value, act_s, mix_s, cot_s = swap_cores(w_out, w_value, act, mix, cot, c)
        block = u_out.shape
        if line4:
            far, near = swap(u_value, 2), swap(u_value, 1)
            far = call(release_kernel, "relay", [ANY, VMEM], [block], [], 0)(near, far)[0]
            value_slots = [u_value, near, far, swap(far, 1)]
            u_out = call(release_kernel, "release", [ANY, VMEM], [block], [], 0)(
                value_slots[3], u_out
            )[0]
            far = swap(u_out, 2)
            out_slots = [u_out, swap(u_out, 1), far, swap(far, 1)]
        else:
            value_slots, out_slots = gather_ring(u_value), gather_ring(u_out)
        n_slots = len(out_slots)
        pack = lambda *values: jnp.stack([jnp.int32(x) for x in values])
        idx = pack(c, *planes_of(z))
        idx_node = pack(*[lax.bitwise_xor(n, jnp.int32(j)) for j in range(n_node)])

        mix_scratch = pltpu.VMEM((2, groups, heads, seq, seq), BF16)
        both = pltpu.VMEM((2 * tokens, width), BF16)
        halves = pltpu.VMEM((2, tokens, width), BF16)
        left_tokens = pltpu.VMEM((cols, 2 * tokens), BF16)
        rows = pltpu.VMEM((width, cols), BF16)
        send_shapes = [block] * n_slots

        slots_scratch = [
            pltpu.VMEM((n_slots, *block), BF16),
            pltpu.SemaphoreType.DMA((n_slots,)),
        ]
        mixed_o, mixed_s = call(
            functools.partial(mixed_kernel, n_slots),
            "mixed",
            [SMEM] + [ANY] * (4 + n_slots),
            [(tokens, cols)] * 2,
            [rows, halves, mix_scratch, pltpu.SemaphoreType.DMA((4,)), *slots_scratch],
            flops,
            2 * (2 * act.size + mix.size + width * cols + 2 * tokens * cols),
        )(idx, act, act_s, mix, mix_s, *value_slots)
        mixed_r = sibling(mixed_s)
        unread = [mixed_r, *(out_slots[1:3] if line4 else [])]
        token, *out_sends = call(
            functools.partial(grad_out_kernel, len(unread)),
            "grad_out",
            [SMEM] + [ANY] * 2 + [VMEM] * 2 + [ANY] * len(unread),
            [(16, 128)] + send_shapes,
            [both, left_tokens, rows, pltpu.SemaphoreType.DMA((2,))],
            flops,
            2 * (2 * cot.size + 2 * tokens * cols + width * cols),
        )(idx, cot, cot_s, mixed_o, mixed_s, *unread)
        out_passed = swap(out_sends[3], 1) if line4 else token
        w_full = call(
            assemble_kernel,
            "assemble",
            [SMEM] + [ANY] * (1 + n_slots),
            [(width, cols)],
            slots_scratch,
            0,
            4 * width * cols,
        )(idx, token, *out_slots)[0]
        w_full_s = sibling(w_full)
        left = call(
            d_value_kernel,
            "d_value",
            [SMEM] + [ANY] * 4 + [VMEM],
            [(cols, 2 * tokens)],
            [halves, mix_scratch, pltpu.SemaphoreType.DMA((4,))],
            flops,
            2 * (2 * cot.size + mix.size + width * cols + 2 * tokens * cols),
        )(idx, cot, cot_s, mix, mix_s, w_full)[0]
        if line4:
            out_onward = added(out_sends[2], out_passed)
            out_far = swap(out_onward, 2)
            out_near = swap(out_sends[1], 1)
        else:
            out_onward = token
        part = width // n_node
        half = tokens // 2
        if n_node == 4:
            term_shapes = [(2, half, part), (2, half, part), (4, half, part)]
        else:
            term_shapes = [(tokens, part)] * n_node
        token, *terms = call(
            functools.partial(terms_kernel, n_node),
            "terms",
            [SMEM] + [VMEM] * 4,
            [(16, 128)] + term_shapes,
            [],
            flops,
            2 * (2 * tokens * cols + 2 * width * cols + tokens * width),
        )(idx_node, mixed_o, mixed_r, w_full, w_full_s)

        back_sends = call(
            gradient_kernel,
            "grad_value",
            [SMEM] + [ANY] * 4 + [VMEM],
            send_shapes,
            [both, rows, pltpu.SemaphoreType.DMA((2,))],
            flops,
            2 * (2 * act.size + 2 * tokens * cols + width * cols),
        )(idx, token, out_onward, act, act_s, left)
        if line4:
            back_passed = swap(back_sends[3], 1)
            onward, beside, out_total = call(
                sum_kernel, "sum", [VMEM] * 6, [block] * 3, [], 0, kinds=[BF16, BF16, F32]
            )(back_sends[2], back_passed, back_sends[1], out_sends[0], out_near, out_far)
            back_far, back_near = swap(onward, 2), swap(beside, 1)
            grad_out = join(out_total[0], sibling(out_total[1]), c)
            grad_value = scatter_end(back_sends[0], (back_near, back_far), c)
        else:
            grad_value = scatter_ring(back_sends, c)
            grad_out = scatter_ring(out_sends, c)

        if n_node == 4:
            along_x, along_y, kept = terms
            kept = kept.astype(F32)
            got_x = flip(along_x, 1).astype(F32)
            got_y = flip(along_y, 2).astype(F32)
            last_y = flip((kept[1] + got_x[1]).astype(BF16), 2)
            last_x = flip((kept[3] + got_y[1]).astype(BF16), 1)
            layer_out = jnp.concatenate(
                [
                    kept[0] + got_x[0] + last_y.astype(F32),
                    kept[2] + got_y[0] + last_x.astype(F32),
                ],
                axis=0,
            )
        else:
            layer_out = terms[0].astype(F32)
            for j in range(1, n_node):
                layer_out = layer_out + flip(terms[j], j).astype(F32)
        layer_out = layer_out.astype(BF16).reshape(micro, images, seq, part)
        return layer_out, grad_value, grad_out

    return body


def solution(mesh):
    return jax.shard_map(
        make_body(mesh.shape["wide"], mesh.shape["node"]),
        mesh=mesh,
        in_specs=(
            P(None, "wide", None, None),
            P(None, "wide", "node", None, None),
            P(None, "wide", None, None),
            P("wide", "node"),
            P("wide", "node"),
        ),
        out_specs=(P(None, "wide", None, "node"), P("wide", "node"), P("wide", "node")),
        check_vma=False,
    )
```

```python
import functools
import math

import jax
import jax.numpy as jnp
from jax import lax
from jax.experimental import pallas as pl
from jax.experimental.pallas import tpu as pltpu
from jax.sharding import PartitionSpec as P

HEAD_DIM = 64
F32 = jnp.float32
BF16 = jnp.bfloat16


def dot(a, b, ca=1, cb=0):
    return lax.dot_general(a, b, (((ca,), (cb,)), ((), ())), preferred_element_type=F32)


def begin_slots(slots, slots_v, sems):
    return begin([(slot, slots_v.at[j]) for j, slot in enumerate(slots)], sems)


def begin(pairs, sems):
    copies = [pltpu.make_async_copy(s, d, sems.at[i]) for i, (s, d) in enumerate(pairs)]
    for copy in copies:
        copy.start()
    return copies


def rows_at(index, size):
    return pl.ds(pl.multiple_of(index * size, math.gcd(size, 16)), size)


def place(idx, slots_v, w_ref):
    core = idx[0]
    for j in range(slots_v.shape[0]):
        depth = slots_v.shape[2]
        mine, other = slots_v[j, 0], slots_v[j, 1]
        low = jnp.where(core == 0, mine, other)
        high = jnp.where(core == 0, other, mine)
        w_ref[rows_at(idx[1 + j], 2 * depth), :] = jnp.concatenate([low, high], axis=0)


def hand_out(idx, base, grad_v, outs):
    core = idx[0]
    for i, out in enumerate(outs):
        depth = out.shape[1]
        block = grad_v[rows_at(idx[base + i], 2 * depth), :]
        low, high = block[:depth], block[depth:]
        out[0] = jnp.where(core == 0, low, high)
        out[1] = jnp.where(core == 0, high, low)


def gradient_rows(left, right_ref, rows_ref, step):
    width = right_ref.shape[1]
    for start in range(0, width, step):
        part = dot(left, right_ref[:, start : start + step])
        rows_ref[start : start + step, :] = part.T.astype(BF16)


def head_pairs(heads):
    return [(h, min(2, heads - h)) for h in range(0, heads, 2)]


def assemble_kernel(idx, token, *rest):
    del token
    slots, (w_out, slots_v, sems) = rest[:-3], rest[-3:]
    for copy in begin_slots(slots, slots_v, sems):
        copy.wait()
    place(idx, slots_v, w_out)


def d_value_kernel(idx, cot_o, cot_s, mix_o, mix_s, w_out, left_v, cot_v, mix_v, sems):
    groups, _, seq, _ = mix_o.shape
    heads = mix_v.shape[2]
    here = pl.ds(idx[0] * heads, heads)
    copies = begin(
        [(cot_o, cot_v.at[0]), (mix_o.at[:, here], mix_v.at[0])]
        + [(cot_s, cot_v.at[1]), (mix_s.at[:, here], mix_v.at[1])],
        sems,
    )
    for half in range(2):
        copies[2 * half].wait()
        d_mixed = dot(cot_v[half], w_out[...])
        copies[2 * half + 1].wait()
        for g in range(groups):
            turned = d_mixed[g * seq : (g + 1) * seq, :].T.astype(BF16)
            at = (half * groups + g) * seq
            for h, n in head_pairs(heads):
                part = turned[h * HEAD_DIM : (h + n) * HEAD_DIM, :]
                if n == 2:
                    row = lax.broadcasted_iota(jnp.int32, part.shape, 0)
                    zero = jnp.zeros_like(part)
                    part = jnp.concatenate(
                        [
                            jnp.where(row < HEAD_DIM, part, zero),
                            jnp.where(row < HEAD_DIM, zero, part),
                        ],
                        axis=1,
                    )
                weights = mix_v[half, g, h : h + n].reshape(n * seq, seq)
                left_v[h * HEAD_DIM : (h + n) * HEAD_DIM, at : at + seq] = dot(
                    part, weights
                ).astype(BF16)


def gradient_kernel(idx, token, unread, right_o, right_s, left_ref, *rest):
    del token, unread
    outs, (right_v, grad_v, sems) = rest[:-3], rest[-3:]
    tokens, _ = right_o.shape
    copies = begin(
        [(right_o, right_v.at[pl.ds(0, tokens)]), (right_s, right_v.at[pl.ds(tokens, tokens)])],
        sems,
    )
    copies[0].wait()
    copies[1].wait()
    gradient_rows(left_ref[...], right_v, grad_v, 640)
    hand_out(idx, 1, grad_v, outs)


def mixed_kernel(n_slots, idx, act_o, act_s, mix_o, mix_s, *rest):
    slots, rest = rest[:n_slots], rest[n_slots:]
    mixed_o, mixed_s, w_v, act_v, mix_v, sems, slots_v, slot_sems = rest
    groups, _, seq, _ = mix_o.shape
    heads = mix_v.shape[2]
    here = pl.ds(idx[0] * heads, heads)
    slot_copies = begin_slots(slots, slots_v, slot_sems)
    copies = begin(
        [(act_o, act_v.at[0]), (mix_o.at[:, here], mix_v.at[0])]
        + [(act_s, act_v.at[1]), (mix_s.at[:, here], mix_v.at[1])],
        sems,
    )
    for copy in slot_copies:
        copy.wait()
    place(idx, slots_v, w_v)
    for half, out in enumerate((mixed_o, mixed_s)):
        copies[2 * half].wait()
        value = dot(act_v[half], w_v[...]).astype(BF16)
        copies[2 * half + 1].wait()
        for g in range(groups):
            for h, n in head_pairs(heads):
                part = value[g * seq : (g + 1) * seq, h * HEAD_DIM : (h + n) * HEAD_DIM]
                weights = mix_v[half, g, h]
                if n == 2:
                    lane = lax.broadcasted_iota(jnp.int32, part.shape, 1)
                    zero = jnp.zeros_like(part)
                    part = jnp.concatenate(
                        [
                            jnp.where(lane < HEAD_DIM, part, zero),
                            jnp.where(lane < HEAD_DIM, zero, part),
                        ],
                        axis=0,
                    )
                    weights = jnp.concatenate([weights, mix_v[half, g, h + 1]], axis=1)
                out[g * seq : (g + 1) * seq, h * HEAD_DIM : (h + n) * HEAD_DIM] = dot(
                    weights, part
                ).astype(BF16)


def grad_out_kernel(n_unread, idx, cot_o, cot_s, mixed_o, mixed_s, *rest):
    token, *rest = rest[n_unread:]
    outs, (cot_v, left_v, grad_v, sems) = rest[:-4], rest[-4:]
    token[...] = jnp.zeros_like(token)
    tokens, _ = cot_o.shape
    copies = begin(
        [(cot_o, cot_v.at[pl.ds(0, tokens)]), (cot_s, cot_v.at[pl.ds(tokens, tokens)])], sems
    )
    left_v[:, :tokens] = mixed_o[...].astype(F32).T.astype(BF16)
    left_v[:, tokens:] = mixed_s[...].astype(F32).T.astype(BF16)
    copies[0].wait()
    copies[1].wait()
    gradient_rows(left_v[...], cot_v, grad_v, 640)
    hand_out(idx, 1, grad_v, outs)


def relay_kernel(unread, first, second, first_out, second_out):
    del unread
    first_out[...] = first[...]
    second_out[...] = second[...]


def sum_kernel(block, got, beside, own, near, far, onward, beside_out, total):
    onward[...] = (block[...].astype(F32) + got[...].astype(F32)).astype(BF16)
    beside_out[...] = beside[...]
    total[...] = own[...].astype(F32) + near[...].astype(F32) + far[...].astype(F32)


def terms_kernel(n_node, idx, mixed_o, mixed_r, w_o, w_r, token, *outs):
    token[...] = jnp.zeros_like(token)
    depth = w_o.shape[0] // n_node
    half = mixed_o.shape[0] // 2
    for j in range(n_node):
        rows = rows_at(idx[j], depth)
        term = dot(mixed_o[...], w_o[rows, :], 1, 1) + dot(mixed_r[...], w_r[rows, :], 1, 1)
        term = term.astype(BF16)
        if n_node != 4:
            outs[j][...] = term
            continue
        along_x, along_y, kept = outs
        first, second = term[:half], term[half:]
        if j == 0:
            kept[0], kept[2] = first, second
        elif j == 1:
            along_x[0], kept[3] = first, second
        elif j == 2:
            kept[1], along_y[0] = first, second
        else:
            along_x[1], along_y[1] = first, second


ANY = pl.BlockSpec(memory_space=pl.ANY)
SMEM = pl.BlockSpec(memory_space=pltpu.SMEM)
VMEM = pl.BlockSpec(memory_space=pltpu.VMEM)


def call(kernel, name, in_specs, out_shapes, scratch, flops, size=1 << 20, kinds=None, vmem=40):
    return pl.pallas_call(
        kernel,
        name=name,
        in_specs=in_specs,
        out_specs=[VMEM] * len(out_shapes),
        out_shape=[
            jax.ShapeDtypeStruct(s, k) for s, k in zip(out_shapes, kinds or [BF16] * len(out_shapes))
        ],
        scratch_shapes=scratch,
        compiler_params=pltpu.CompilerParams(vmem_limit_bytes=vmem << 20),
        cost_estimate=pl.CostEstimate(flops=flops, bytes_accessed=size, transcendentals=0),
    )


def make_body(n_wide, n_node):
    planes = n_wide // 2
    line4 = planes == 4

    def move(x, pairs):
        return lax.ppermute(
            x, "wide", [(2 * s + c, 2 * d + c) for s, d in pairs for c in range(2)]
        )

    def swap(x, j):
        return move(x, [(s, s ^ j) for s in range(planes)])

    def sibling(x):
        return lax.ppermute(x, "wide", [(i, i ^ 1) for i in range(n_wide)])

    def flip(x, j):
        return lax.ppermute(x, "node", [(i, i ^ j) for i in range(n_node)])

    def swap_cores(w_out, w_value, act, mix, cot, c):
        cols = w_out.shape[1] // 2
        low = jnp.stack([w_out[:, :cols], w_value[:, :cols]])
        high = jnp.stack([w_out[:, cols:], w_value[:, cols:]])
        got = sibling(jnp.where(c == 0, high, low))
        got, act, mix, cot = lax.optimization_barrier((got, act, mix, cot))
        mine = jnp.where(c == 0, low, high)
        u_out, u_value = (jnp.stack([mine[i], got[i]]) for i in range(2))
        return u_out, u_value, sibling(act), sibling(mix), sibling(cot)

    def gather_ring(u):
        return [u] + [
            move(u, [(s, (s - j) % planes) for s in range(planes)]) for j in range(1, planes)
        ]

    def planes_of(z):
        if line4:
            return [lax.bitwise_xor(z, jnp.int32(j)) for j in range(4)]
        return [lax.rem(z + j, planes) for j in range(planes)]

    def added(block, got):
        return (block.astype(F32) + got.astype(F32)).astype(BF16)

    def scatter_end(own, got, c):
        total = own.astype(F32)
        for part in got:
            total = total + part.astype(F32)
        return join(total[0], sibling(total[1]), c)

    def join(mine, other, c):
        low = jnp.where(c == 0, mine, other)
        high = jnp.where(c == 0, other, mine)
        return jnp.concatenate([low, high], axis=1)

    def scatter_ring(blocks, c):
        total = blocks[0].astype(F32)
        for j in range(1, planes):
            got = move(blocks[j], [(s, (s + j) % planes) for s in range(planes)])
            total = total + got.astype(F32)
        return join(total[0], sibling(total[1]), c)

    def body(act_in, mixing, cotangent, w_value, w_out):
        wide = lax.axis_index("wide")
        n = lax.axis_index("node")
        z, c = wide // 2, lax.rem(wide, 2)
        micro, images, seq, width = act_in.shape
        groups = micro * images
        tokens = groups * seq
        cols = w_value.shape[1] // 2
        heads = cols // HEAD_DIM
        depth = width // planes
        act = act_in.reshape(tokens, width)
        cot = cotangent.reshape(tokens, width)
        mix = mixing.reshape(groups, 2 * heads, seq, seq)
        flops = 4 * tokens * width * cols

        u_out, u_value, act_s, mix_s, cot_s = swap_cores(w_out, w_value, act, mix, cot, c)
        block = u_out.shape
        if line4:
            far, near = swap(u_value, 2), swap(u_value, 1)
            far, u_out = call(relay_kernel, "relay", [ANY, VMEM, VMEM], [block] * 2, [], 0)(
                near, far, u_out
            )
            value_slots = [u_value, near, far, swap(far, 1)]
            far = swap(u_out, 2)
            out_slots = [u_out, swap(u_out, 1), far, swap(far, 1)]
        else:
            value_slots, out_slots = gather_ring(u_value), gather_ring(u_out)
        n_slots = len(out_slots)
        pack = lambda *values: jnp.stack([jnp.int32(x) for x in values])
        idx = pack(c, *planes_of(z))
        idx_node = pack(*[lax.bitwise_xor(n, jnp.int32(j)) for j in range(n_node)])

        mix_scratch = pltpu.VMEM((2, groups, heads, seq, seq), BF16)
        both = pltpu.VMEM((2 * tokens, width), BF16)
        halves = pltpu.VMEM((2, tokens, width), BF16)
        left_tokens = pltpu.VMEM((cols, 2 * tokens), BF16)
        rows = pltpu.VMEM((width, cols), BF16)
        send_shapes = [block] * n_slots

        slots_scratch = [
            pltpu.VMEM((n_slots, *block), BF16),
            pltpu.SemaphoreType.DMA((n_slots,)),
        ]
        mixed_o, mixed_s = call(
            functools.partial(mixed_kernel, n_slots),
            "mixed",
            [SMEM] + [ANY] * (4 + n_slots),
            [(tokens, cols)] * 2,
            [rows, halves, mix_scratch, pltpu.SemaphoreType.DMA((4,)), *slots_scratch],
            flops,
            2 * (2 * act.size + mix.size + width * cols + 2 * tokens * cols),
            vmem=60,
        )(idx, act, act_s, mix, mix_s, *value_slots)
        mixed_r = sibling(mixed_s)
        unread = [mixed_r, *(out_slots[1:3] if line4 else [])]
        token, *out_sends = call(
            functools.partial(grad_out_kernel, len(unread)),
            "grad_out",
            [SMEM] + [ANY] * 2 + [VMEM] * 2 + [ANY] * len(unread),
            [(16, 128)] + send_shapes,
            [both, left_tokens, rows, pltpu.SemaphoreType.DMA((2,))],
            flops,
            2 * (2 * cot.size + 2 * tokens * cols + width * cols),
        )(idx, cot, cot_s, mixed_o, mixed_s, *unread)
        out_passed = swap(out_sends[3], 1) if line4 else token
        w_full = call(
            assemble_kernel,
            "assemble",
            [SMEM] + [ANY] * (1 + n_slots),
            [(width, cols)],
            slots_scratch,
            0,
            4 * width * cols,
        )(idx, token, *out_slots)[0]
        w_full_s = sibling(w_full)
        left = call(
            d_value_kernel,
            "d_value",
            [SMEM] + [ANY] * 4 + [VMEM],
            [(cols, 2 * tokens)],
            [halves, mix_scratch, pltpu.SemaphoreType.DMA((4,))],
            flops,
            2 * (2 * cot.size + mix.size + width * cols + 2 * tokens * cols),
        )(idx, cot, cot_s, mix, mix_s, w_full)[0]
        if line4:
            out_onward = added(out_sends[2], out_passed)
            out_far = swap(out_onward, 2)
            out_near = swap(out_sends[1], 1)
        else:
            out_onward = token
        part = width // n_node
        half = tokens // 2
        if n_node == 4:
            term_shapes = [(2, half, part), (2, half, part), (4, half, part)]
        else:
            term_shapes = [(tokens, part)] * n_node
        token, *terms = call(
            functools.partial(terms_kernel, n_node),
            "terms",
            [SMEM] + [VMEM] * 4,
            [(16, 128)] + term_shapes,
            [],
            flops,
            2 * (2 * tokens * cols + 2 * width * cols + tokens * width),
        )(idx_node, mixed_o, mixed_r, w_full, w_full_s)

        back_sends = call(
            gradient_kernel,
            "grad_value",
            [SMEM] + [ANY] * 4 + [VMEM],
            send_shapes,
            [both, rows, pltpu.SemaphoreType.DMA((2,))],
            flops,
            2 * (2 * act.size + 2 * tokens * cols + width * cols),
        )(idx, token, out_onward, act, act_s, left)
        if line4:
            back_passed = swap(back_sends[3], 1)
            onward, beside, out_total = call(
                sum_kernel, "sum", [VMEM] * 6, [block] * 3, [], 0, kinds=[BF16, BF16, F32]
            )(back_sends[2], back_passed, back_sends[1], out_sends[0], out_near, out_far)
            back_far, back_near = swap(onward, 2), swap(beside, 1)
            grad_out = join(out_total[0], sibling(out_total[1]), c)
            grad_value = scatter_end(back_sends[0], (back_near, back_far), c)
        else:
            grad_value = scatter_ring(back_sends, c)
            grad_out = scatter_ring(out_sends, c)

        if n_node == 4:
            along_x, along_y, kept = terms
            kept = kept.astype(F32)
            got_x = flip(along_x, 1).astype(F32)
            got_y = flip(along_y, 2).astype(F32)
            last_y = flip((kept[1] + got_x[1]).astype(BF16), 2)
            last_x = flip((kept[3] + got_y[1]).astype(BF16), 1)
            layer_out = jnp.concatenate(
                [
                    kept[0] + got_x[0] + last_y.astype(F32),
                    kept[2] + got_y[0] + last_x.astype(F32),
                ],
                axis=0,
            )
        else:
            layer_out = terms[0].astype(F32)
            for j in range(1, n_node):
                layer_out = layer_out + flip(terms[j], j).astype(F32)
        layer_out = layer_out.astype(BF16).reshape(micro, images, seq, part)
        return layer_out, grad_value, grad_out

    return body


def solution(mesh):
    return jax.shard_map(
        make_body(mesh.shape["wide"], mesh.shape["node"]),
        mesh=mesh,
        in_specs=(
            P(None, "wide", None, None),
            P(None, "wide", "node", None, None),
            P(None, "wide", None, None),
            P("wide", "node"),
            P("wide", "node"),
        ),
        out_specs=(P(None, "wide", None, "node"), P("wide", "node"), P("wide", "node")),
        check_vma=False,
    )
```

```python
import functools
import math

import jax
import jax.numpy as jnp
from jax import lax
from jax.experimental import pallas as pl
from jax.experimental.pallas import tpu as pltpu
from jax.sharding import PartitionSpec as P

HEAD_DIM = 64
F32 = jnp.float32
BF16 = jnp.bfloat16


def dot(a, b, ca=1, cb=0):
    return lax.dot_general(a, b, (((ca,), (cb,)), ((), ())), preferred_element_type=F32)


def begin_slots(slots, slots_v, sems):
    return begin([(slot, slots_v.at[j]) for j, slot in enumerate(slots)], sems)


def begin(pairs, sems):
    copies = [pltpu.make_async_copy(s, d, sems.at[i]) for i, (s, d) in enumerate(pairs)]
    for copy in copies:
        copy.start()
    return copies


def rows_at(index, size):
    return pl.ds(pl.multiple_of(index * size, math.gcd(size, 16)), size)


def place(idx, core, slots_v, w_ref):
    for j in range(slots_v.shape[0]):
        w_ref[rows_at(idx[1 + j], 2 * slots_v.shape[2]), :] = whole(core, slots_v[j])


def hand_out(idx, base, grad_v, outs):
    core = idx[0]
    for i, out in enumerate(outs):
        depth = out.shape[1]
        block = grad_v[rows_at(idx[base + i], 2 * depth), :]
        low, high = block[:depth], block[depth:]
        out[0] = jnp.where(core == 0, low, high)
        out[1] = jnp.where(core == 0, high, low)


def gradient_rows(left, right_ref, rows_ref, step):
    width = right_ref.shape[1]
    for start in range(0, width, step):
        part = dot(left, right_ref[:, start : start + step])
        rows_ref[start : start + step, :] = part.T.astype(BF16)


def head_pairs(heads):
    return [(h, min(2, heads - h)) for h in range(0, heads, 2)]


def whole(core, slot):
    mine, other = slot[0], slot[1]
    low = jnp.where(core == 0, mine, other)
    high = jnp.where(core == 0, other, mine)
    return jnp.concatenate([low, high], axis=0)


def part_kernel(n_slots, idx, x_o, x_s, mix_o, mix_s, *rest):
    slots, rest = rest[:n_slots], rest[n_slots:]
    part, last, weights, w_v, x_v, slots_v, x_sems, sems, slot_sems = rest
    heads, depth = weights.shape[2], last.shape[2]
    here = pl.ds(idx[0] * heads, heads)
    missing = idx[1 + n_slots]
    columns = pl.ds(pl.multiple_of(missing * depth, 128), depth)
    copies = begin_slots(slots, slots_v, slot_sems)
    halves = begin([(x_o, x_v.at[0]), (x_s, x_v.at[1])], x_sems)
    later = begin(
        [(x_o.at[:, columns], last.at[0]), (x_s.at[:, columns], last.at[1])]
        + [(mix_o.at[:, here], weights.at[0]), (mix_s.at[:, here], weights.at[1])],
        sems,
    )
    for copy in copies:
        copy.wait()
    place(idx, idx[0], slots_v, w_v)
    w_v[rows_at(missing, depth), :] = jnp.zeros((depth, w_v.shape[1]), BF16)
    for half in range(2):
        halves[half].wait()
        part[half] = dot(x_v[half], w_v[...])
    for copy in later:
        copy.wait()


def mix_values(value, weights, out):
    groups, heads, seq, _ = weights.shape
    for g in range(groups):
        for h, n in head_pairs(heads):
            part = value[g * seq : (g + 1) * seq, h * HEAD_DIM : (h + n) * HEAD_DIM]
            both = weights[g, h]
            if n == 2:
                lane = lax.broadcasted_iota(jnp.int32, part.shape, 1)
                zero = jnp.zeros_like(part)
                part = jnp.concatenate(
                    [
                        jnp.where(lane < HEAD_DIM, part, zero),
                        jnp.where(lane < HEAD_DIM, zero, part),
                    ],
                    axis=0,
                )
                both = jnp.concatenate([both, weights[g, h + 1]], axis=1)
            out[g * seq : (g + 1) * seq, h * HEAD_DIM : (h + n) * HEAD_DIM] = dot(
                both, part
            ).astype(BF16)


def mix_back(d_mixed, weights, left_v, start):
    groups, heads, seq, _ = weights.shape
    for g in range(groups):
        turned = d_mixed[g * seq : (g + 1) * seq, :].T.astype(BF16)
        at = start + g * seq
        for h, n in head_pairs(heads):
            part = turned[h * HEAD_DIM : (h + n) * HEAD_DIM, :]
            if n == 2:
                row = lax.broadcasted_iota(jnp.int32, part.shape, 0)
                zero = jnp.zeros_like(part)
                part = jnp.concatenate(
                    [
                        jnp.where(row < HEAD_DIM, part, zero),
                        jnp.where(row < HEAD_DIM, zero, part),
                    ],
                    axis=1,
                )
            both = weights[g, h : h + n].reshape(n * seq, seq)
            left_v[h * HEAD_DIM : (h + n) * HEAD_DIM, at : at + seq] = dot(part, both).astype(BF16)


def mixed_rest_kernel(idx, part, last, weights, slot, mixed_o, mixed_s):
    w_last = whole(idx[0], slot)
    for half, out in enumerate((mixed_o, mixed_s)):
        value = (part[half] + dot(last[half], w_last)).astype(BF16)
        mix_values(value, weights.at[half], out)


def d_value_rest_kernel(idx, part, last, weights, slot, left_v, slot_out):
    slot_out[...] = slot[...]
    w_last = whole(idx[0], slot)
    tokens = part.shape[1]
    for half in range(2):
        mix_back(part[half] + dot(last[half], w_last), weights.at[half], left_v, half * tokens)


def assemble_kernel(n_slots, idx, unread, *rest):
    del unread
    slots, (w_out, slots_v, sems) = rest[:n_slots], rest[n_slots:]
    copies = begin_slots(slots, slots_v, sems)
    planes, depth = idx.shape[0] - 1, 2 * slots_v.shape[2]
    for j in range(n_slots, planes):
        w_out[rows_at(idx[1 + j], depth), :] = jnp.zeros((depth, w_out.shape[1]), BF16)
    for copy in copies:
        copy.wait()
    place(idx, idx[0], slots_v, w_out)


def d_value_kernel(idx, cot_o, cot_s, mix_o, mix_s, w_out, left_v, cot_v, mix_v, sems):
    tokens, heads = cot_o.shape[0], mix_v.shape[2]
    here = pl.ds(idx[0] * heads, heads)
    copies = begin(
        [(cot_o, cot_v.at[0]), (mix_o.at[:, here], mix_v.at[0])]
        + [(cot_s, cot_v.at[1]), (mix_s.at[:, here], mix_v.at[1])],
        sems,
    )
    for half in range(2):
        copies[2 * half].wait()
        d_mixed = dot(cot_v[half], w_out[...])
        copies[2 * half + 1].wait()
        mix_back(d_mixed, mix_v.at[half], left_v, half * tokens)


def gradient_kernel(idx, token, unread, right_o, right_s, left_ref, *rest):
    del token, unread
    outs, (right_v, grad_v, sems) = rest[:-3], rest[-3:]
    tokens, _ = right_o.shape
    copies = begin(
        [(right_o, right_v.at[pl.ds(0, tokens)]), (right_s, right_v.at[pl.ds(tokens, tokens)])],
        sems,
    )
    copies[0].wait()
    copies[1].wait()
    gradient_rows(left_ref[...], right_v, grad_v, 640)
    hand_out(idx, 1, grad_v, outs)


def mixed_kernel(n_slots, idx, act_o, act_s, mix_o, mix_s, *rest):
    slots, rest = rest[:n_slots], rest[n_slots:]
    mixed_o, mixed_s, w_v, act_v, mix_v, sems, slots_v, slot_sems = rest
    heads = mix_v.shape[2]
    here = pl.ds(idx[0] * heads, heads)
    slot_copies = begin_slots(slots, slots_v, slot_sems)
    copies = begin(
        [(act_o, act_v.at[0]), (mix_o.at[:, here], mix_v.at[0])]
        + [(act_s, act_v.at[1]), (mix_s.at[:, here], mix_v.at[1])],
        sems,
    )
    for copy in slot_copies:
        copy.wait()
    place(idx, idx[0], slots_v, w_v)
    for half, out in enumerate((mixed_o, mixed_s)):
        copies[2 * half].wait()
        value = dot(act_v[half], w_v[...]).astype(BF16)
        copies[2 * half + 1].wait()
        mix_values(value, mix_v.at[half], out)


def grad_out_kernel(idx, cot_o, cot_s, mixed_o, mixed_s, w_out, unread, *rest):
    del unread
    *outs, cot_v, left_v, grad_v, sems, last_sems = rest
    part = last = None
    if w_out is not None:
        part, last, *outs = outs
    tokens, _ = cot_o.shape
    copies = begin(
        [(cot_o, cot_v.at[pl.ds(0, tokens)]), (cot_s, cot_v.at[pl.ds(tokens, tokens)])], sems
    )
    if w_out is not None:
        depth = last.shape[2]
        columns = pl.ds(pl.multiple_of(idx[idx.shape[0] - 1] * depth, 128), depth)
        later = begin(
            [(cot_o.at[:, columns], last.at[0]), (cot_s.at[:, columns], last.at[1])], last_sems
        )
    left_v[:, :tokens] = mixed_o[...].astype(F32).T.astype(BF16)
    left_v[:, tokens:] = mixed_s[...].astype(F32).T.astype(BF16)
    copies[0].wait()
    copies[1].wait()
    gradient_rows(left_v[...], cot_v, grad_v, 640)
    hand_out(idx, 1, grad_v, outs)
    if w_out is not None:
        for half in range(2):
            part[half] = dot(cot_v[half * tokens : (half + 1) * tokens, :], w_out[...])
        for copy in later:
            copy.wait()


def grad_out_only_kernel(idx, cot_o, cot_s, mixed_o, mixed_s, unread, *rest):
    grad_out_kernel(idx, cot_o, cot_s, mixed_o, mixed_s, None, unread, *rest)


def relay_kernel(unread, first, second, first_out, second_out):
    del unread
    first_out[...] = first[...]
    second_out[...] = second[...]


def sum_kernel(block, got, beside, own, near, far, onward, beside_out, total):
    onward[...] = (block[...].astype(F32) + got[...].astype(F32)).astype(BF16)
    beside_out[...] = beside[...]
    total[...] = own[...].astype(F32) + near[...].astype(F32) + far[...].astype(F32)


def terms_kernel(n_node, idx, mixed_o, mixed_r, w_o, w_r, *outs):
    depth = w_o.shape[0] // n_node
    for j in range(n_node):
        rows = rows_at(idx[j], depth)
        term = dot(mixed_o[...], w_o[rows, :], 1, 1) + dot(mixed_r[...], w_r[rows, :], 1, 1)
        outs[j][...] = term.astype(BF16)


def terms_line_kernel(idx_node, idx, mixed_o, mixed_r, w_o, w_r, slot, slot_r, *outs):
    token, along_x, along_y, kept = outs
    token[...] = jnp.zeros_like(token)
    core, missing = idx[0], idx[4]
    last_o, last_r = whole(core, slot), whole(1 - core, slot_r)
    half = mixed_o.shape[0] // 2
    for j in range(4):
        rows = rows_at(idx_node[j], last_o.shape[0])
        here = idx_node[j] == missing
        term = dot(mixed_o[...], jnp.where(here, last_o, w_o[rows, :]), 1, 1)
        term += dot(mixed_r[...], jnp.where(here, last_r, w_r[rows, :]), 1, 1)
        term = term.astype(BF16)
        first, second = term[:half], term[half:]
        if j == 0:
            kept[0], kept[2] = first, second
        elif j == 1:
            along_x[0], kept[3] = first, second
        elif j == 2:
            kept[1], along_y[0] = first, second
        else:
            along_x[1], along_y[1] = first, second


ANY = pl.BlockSpec(memory_space=pl.ANY)
SMEM = pl.BlockSpec(memory_space=pltpu.SMEM)
VMEM = pl.BlockSpec(memory_space=pltpu.VMEM)


def call(kernel, name, in_specs, out_shapes, scratch, flops, size=1 << 20, kinds=None, vmem=40):
    return pl.pallas_call(
        kernel,
        name=name,
        in_specs=in_specs,
        out_specs=[VMEM] * len(out_shapes),
        out_shape=[
            jax.ShapeDtypeStruct(s, k) for s, k in zip(out_shapes, kinds or [BF16] * len(out_shapes))
        ],
        scratch_shapes=scratch,
        compiler_params=pltpu.CompilerParams(vmem_limit_bytes=vmem << 20),
        cost_estimate=pl.CostEstimate(flops=flops, bytes_accessed=size, transcendentals=0),
    )


def make_body(n_wide, n_node):
    planes = n_wide // 2
    line4 = planes == 4 and n_node == 4

    def move(x, pairs):
        return lax.ppermute(
            x, "wide", [(2 * s + c, 2 * d + c) for s, d in pairs for c in range(2)]
        )

    def swap(x, j):
        return move(x, [(s, s ^ j) for s in range(planes)])

    def sibling(x):
        return lax.ppermute(x, "wide", [(i, i ^ 1) for i in range(n_wide)])

    def flip(x, j):
        return lax.ppermute(x, "node", [(i, i ^ j) for i in range(n_node)])

    def swap_cores(w_out, w_value, act, mix, cot, c):
        cols = w_out.shape[1] // 2
        low = jnp.stack([w_out[:, :cols], w_value[:, :cols]])
        high = jnp.stack([w_out[:, cols:], w_value[:, cols:]])
        got = sibling(jnp.where(c == 0, high, low))
        got, act, mix, cot = lax.optimization_barrier((got, act, mix, cot))
        mine = jnp.where(c == 0, low, high)
        u_out, u_value = (jnp.stack([mine[i], got[i]]) for i in range(2))
        return u_out, u_value, sibling(act), sibling(mix), sibling(cot)

    def gather_ring(u):
        return [u] + [
            move(u, [(s, (s - j) % planes) for s in range(planes)]) for j in range(1, planes)
        ]

    def planes_of(z):
        if line4:
            return [lax.bitwise_xor(z, jnp.int32(j)) for j in range(4)]
        return [lax.rem(z + j, planes) for j in range(planes)]

    def added(block, got):
        return (block.astype(F32) + got.astype(F32)).astype(BF16)

    def scatter_end(own, got, c):
        total = own.astype(F32)
        for part in got:
            total = total + part.astype(F32)
        return join(total[0], sibling(total[1]), c)

    def join(mine, other, c):
        low = jnp.where(c == 0, mine, other)
        high = jnp.where(c == 0, other, mine)
        return jnp.concatenate([low, high], axis=1)

    def scatter_ring(blocks, c):
        total = blocks[0].astype(F32)
        for j in range(1, planes):
            got = move(blocks[j], [(s, (s + j) % planes) for s in range(planes)])
            total = total + got.astype(F32)
        return join(total[0], sibling(total[1]), c)

    def body(act_in, mixing, cotangent, w_value, w_out):
        wide = lax.axis_index("wide")
        n = lax.axis_index("node")
        z, c = wide // 2, lax.rem(wide, 2)
        micro, images, seq, width = act_in.shape
        groups = micro * images
        tokens = groups * seq
        cols = w_value.shape[1] // 2
        heads = cols // HEAD_DIM
        depth = width // planes
        act = act_in.reshape(tokens, width)
        cot = cotangent.reshape(tokens, width)
        mix = mixing.reshape(groups, 2 * heads, seq, seq)
        flops = 4 * tokens * width * cols

        u_out, u_value, act_s, mix_s, cot_s = swap_cores(w_out, w_value, act, mix, cot, c)
        block = u_out.shape
        if line4:
            far, near = swap(u_value, 2), swap(u_value, 1)
            far, u_out = call(relay_kernel, "relay", [ANY, VMEM, VMEM], [block] * 2, [], 0)(
                near, far, u_out
            )
            value_slots = [u_value, near, far, swap(far, 1)]
            far = swap(u_out, 2)
            out_slots = [u_out, swap(u_out, 1), far, swap(far, 1)]
        else:
            value_slots, out_slots = gather_ring(u_value), gather_ring(u_out)
        n_slots = len(out_slots)
        pack = lambda *values: jnp.stack([jnp.int32(x) for x in values])
        idx = pack(c, *planes_of(z))
        idx_node = pack(*[lax.bitwise_xor(n, jnp.int32(j)) for j in range(n_node)])

        mix_scratch = pltpu.VMEM((2, groups, heads, seq, seq), BF16)
        both = pltpu.VMEM((2 * tokens, width), BF16)
        halves = pltpu.VMEM((2, tokens, width), BF16)
        left_tokens = pltpu.VMEM((cols, 2 * tokens), BF16)
        rows = pltpu.VMEM((width, cols), BF16)
        send_shapes = [block] * n_slots

        slots_scratch = [
            pltpu.VMEM((n_slots, *block), BF16),
            pltpu.SemaphoreType.DMA((n_slots,)),
        ]
        part_shapes = [(2, tokens, cols), (2, tokens, depth)]
        if line4:
            ahead = call(
                functools.partial(part_kernel, n_slots - 1),
                "value_ahead",
                [SMEM] + [ANY] * (3 + n_slots),
                [*part_shapes, (2, groups, heads, seq, seq)],
                [
                    *(rows, halves, pltpu.VMEM((n_slots - 1, *block), BF16)),
                    *(pltpu.SemaphoreType.DMA((k,)) for k in (2, 4, n_slots - 1)),
                ],
                flops,
                2 * (3 * act.size + mix.size + width * cols + 4 * tokens * cols),
                kinds=[F32, BF16, BF16],
            )(idx, act, act_s, mix, mix_s, *value_slots[:-1])
            mixed_o, mixed_s = call(
                mixed_rest_kernel,
                "mixed",
                [SMEM] + [VMEM] * 4,
                [(tokens, cols)] * 2,
                [],
                flops // 4,
                2 * (2 * tokens * depth + mix.size + 6 * tokens * cols),
            )(idx, *ahead, value_slots[-1])
        else:
            mixed_o, mixed_s = call(
                functools.partial(mixed_kernel, n_slots),
                "mixed",
                [SMEM] + [ANY] * (4 + n_slots),
                [(tokens, cols)] * 2,
                [rows, halves, mix_scratch, pltpu.SemaphoreType.DMA((4,)), *slots_scratch],
                flops,
                2 * (2 * act.size + mix.size + width * cols + 2 * tokens * cols),
                )(idx, act, act_s, mix, mix_s, *value_slots)
        mixed_r = sibling(mixed_s)
        grad_scratch = [both, left_tokens, rows] + [pltpu.SemaphoreType.DMA((2,))] * 2
        size = 2 * (3 * cot.size + 6 * tokens * cols + 2 * width * cols)
        if line4:
            w_part = call(
                functools.partial(assemble_kernel, n_slots - 1),
                "assemble",
                [SMEM] + [ANY] * n_slots,
                [(width, cols)],
                [pltpu.VMEM((n_slots - 1, *block), BF16), pltpu.SemaphoreType.DMA((n_slots - 1,))],
                0,
                4 * width * cols,
            )(idx, mixed_s, *out_slots[:-1])[0]
            w_part_s = sibling(w_part)
            *rest, w_mix = ahead
            part, last, *out_sends = call(
                grad_out_kernel,
                "grad_out",
                [SMEM] + [ANY] * 2 + [VMEM] * 3 + [ANY],
                part_shapes + send_shapes,
                grad_scratch,
                2 * flops,
                size,
                kinds=[F32] + [BF16] * (1 + n_slots),
            )(idx, cot, cot_s, mixed_o, mixed_s, w_part, mixed_r)
            out_passed = swap(out_sends[3], 1)
            left, last_block = call(
                d_value_rest_kernel,
                "d_value",
                [SMEM] + [VMEM] * 4,
                [(cols, 2 * tokens), block],
                [],
                flops // 4,
                2 * (2 * tokens * depth + mix.size + 6 * tokens * cols),
            )(idx, part, last, w_mix, out_slots[-1])
            last_s = sibling(last_block)
        else:
            out_sends = call(
                grad_out_only_kernel,
                "grad_out",
                [SMEM] + [ANY] * 2 + [VMEM] * 2 + [ANY],
                send_shapes,
                grad_scratch,
                flops,
                size,
            )(idx, cot, cot_s, mixed_o, mixed_s, mixed_r)
            w_full = call(
                functools.partial(assemble_kernel, n_slots),
                "assemble",
                [SMEM] + [ANY] * (1 + n_slots),
                [(width, cols)],
                slots_scratch,
                0,
                4 * width * cols,
            )(idx, mixed_s, *out_slots)[0]
            left = call(
                d_value_kernel,
                "d_value",
                [SMEM] + [ANY] * 4 + [VMEM],
                [(cols, 2 * tokens)],
                [halves, mix_scratch, pltpu.SemaphoreType.DMA((4,))],
                flops,
                2 * (2 * cot.size + mix.size + width * cols + 2 * tokens * cols),
            )(idx, cot, cot_s, mix, mix_s, w_full)[0]
            w_full_s = sibling(w_full)
            token = left
        if line4:
            out_onward = added(out_sends[2], out_passed)
            out_far = swap(out_onward, 2)
            out_near = swap(out_sends[1], 1)
        else:
            out_onward = token
        part = width // n_node
        half = tokens // 2
        size = 2 * (2 * tokens * cols + 2 * width * cols + tokens * width)
        if line4:
            token, *terms = call(
                terms_line_kernel,
                "terms",
                [SMEM] * 2 + [VMEM] * 6,
                [(16, 128), (2, half, part), (2, half, part), (4, half, part)],
                [],
                flops,
                size,
            )(idx_node, idx, mixed_o, mixed_r, w_part, w_part_s, last_block, last_s)
        else:
            terms = call(
                functools.partial(terms_kernel, n_node),
                "terms",
                [SMEM] + [VMEM] * 4,
                [(tokens, part)] * n_node,
                [],
                flops,
                size,
            )(idx_node, mixed_o, mixed_r, w_full, w_full_s)

        back_sends = call(
            gradient_kernel,
            "grad_value",
            [SMEM] + [ANY] * 4 + [VMEM],
            send_shapes,
            [both, rows, pltpu.SemaphoreType.DMA((2,))],
            flops,
            2 * (2 * act.size + 2 * tokens * cols + width * cols),
        )(idx, token, out_onward, act, act_s, left)
        if line4:
            back_passed = swap(back_sends[3], 1)
            onward, beside, out_total = call(
                sum_kernel, "sum", [VMEM] * 6, [block] * 3, [], 0, kinds=[BF16, BF16, F32]
            )(back_sends[2], back_passed, back_sends[1], out_sends[0], out_near, out_far)
            back_far, back_near = swap(onward, 2), swap(beside, 1)
            grad_out = join(out_total[0], sibling(out_total[1]), c)
            grad_value = scatter_end(back_sends[0], (back_near, back_far), c)
        else:
            grad_value = scatter_ring(back_sends, c)
            grad_out = scatter_ring(out_sends, c)

        if line4:
            along_x, along_y, kept = terms
            kept = kept.astype(F32)
            got_x = flip(along_x, 1).astype(F32)
            got_y = flip(along_y, 2).astype(F32)
            last_y = flip((kept[1] + got_x[1]).astype(BF16), 2)
            last_x = flip((kept[3] + got_y[1]).astype(BF16), 1)
            layer_out = jnp.concatenate(
                [
                    kept[0] + got_x[0] + last_y.astype(F32),
                    kept[2] + got_y[0] + last_x.astype(F32),
                ],
                axis=0,
            )
        else:
            layer_out = terms[0].astype(F32)
            for j in range(1, n_node):
                layer_out = layer_out + flip(terms[j], j).astype(F32)
        layer_out = layer_out.astype(BF16).reshape(micro, images, seq, part)
        return layer_out, grad_value, grad_out

    return body


def solution(mesh):
    return jax.shard_map(
        make_body(mesh.shape["wide"], mesh.shape["node"]),
        mesh=mesh,
        in_specs=(
            P(None, "wide", None, None),
            P(None, "wide", "node", None, None),
            P(None, "wide", None, None),
            P("wide", "node"),
            P("wide", "node"),
        ),
        out_specs=(P(None, "wide", None, "node"), P("wide", "node"), P("wide", "node")),
        check_vma=False,
    )
```

```python
import functools
import math

import jax
import jax.numpy as jnp
from jax import lax
from jax.experimental import pallas as pl
from jax.experimental.pallas import tpu as pltpu
from jax.sharding import PartitionSpec as P

HEAD_DIM = 64
F32 = jnp.float32
BF16 = jnp.bfloat16


def dot(a, b, ca=1, cb=0):
    return lax.dot_general(a, b, (((ca,), (cb,)), ((), ())), preferred_element_type=F32)


def begin_slots(slots, slots_v, sems):
    return begin([(slot, slots_v.at[j]) for j, slot in enumerate(slots)], sems)


def begin(pairs, sems):
    copies = [pltpu.make_async_copy(s, d, sems.at[i]) for i, (s, d) in enumerate(pairs)]
    for copy in copies:
        copy.start()
    return copies


def rows_at(index, size):
    return pl.ds(pl.multiple_of(index * size, math.gcd(size, 16)), size)


def place(idx, core, slots_v, w_ref):
    for j in range(slots_v.shape[0]):
        w_ref[rows_at(idx[1 + j], 2 * slots_v.shape[2]), :] = whole(core, slots_v[j])


def hand_out(idx, base, grad_v, outs):
    core = idx[0]
    for i, out in enumerate(outs):
        depth = out.shape[1]
        block = grad_v[rows_at(idx[base + i], 2 * depth), :]
        low, high = block[:depth], block[depth:]
        out[0] = jnp.where(core == 0, low, high)
        out[1] = jnp.where(core == 0, high, low)


def gradient_rows(left, right_ref, rows_ref, step):
    width = right_ref.shape[1]
    for start in range(0, width, step):
        part = dot(left, right_ref[:, start : start + step])
        rows_ref[start : start + step, :] = part.T.astype(BF16)


def head_pairs(heads):
    return [(h, min(2, heads - h)) for h in range(0, heads, 2)]


def whole(core, slot):
    mine, other = slot[0], slot[1]
    low = jnp.where(core == 0, mine, other)
    high = jnp.where(core == 0, other, mine)
    return jnp.concatenate([low, high], axis=0)


def part_kernel(n_slots, idx, x_o, x_s, mix_o, mix_s, *rest):
    slots, rest = rest[:n_slots], rest[n_slots:]
    part, last, weights, w_v, x_v, slots_v, x_sems, sems, slot_sems = rest
    heads, depth = weights.shape[2], last.shape[2]
    here = pl.ds(idx[0] * heads, heads)
    missing = idx[1 + n_slots]
    columns = pl.ds(pl.multiple_of(missing * depth, 128), depth)
    copies = begin_slots(slots, slots_v, slot_sems)
    halves = begin([(x_o, x_v.at[0]), (x_s, x_v.at[1])], x_sems)
    later = begin(
        [(x_o.at[:, columns], last.at[0]), (x_s.at[:, columns], last.at[1])]
        + [(mix_o.at[:, here], weights.at[0]), (mix_s.at[:, here], weights.at[1])],
        sems,
    )
    for copy in copies:
        copy.wait()
    place(idx, idx[0], slots_v, w_v)
    w_v[rows_at(missing, depth), :] = jnp.zeros((depth, w_v.shape[1]), BF16)
    for half in range(2):
        halves[half].wait()
        part[half] = dot(x_v[half], w_v[...])
    for copy in later:
        copy.wait()


def mix_values(value, weights, out):
    groups, heads, seq, _ = weights.shape
    for g in range(groups):
        for h, n in head_pairs(heads):
            part = value[g * seq : (g + 1) * seq, h * HEAD_DIM : (h + n) * HEAD_DIM]
            both = weights[g, h]
            if n == 2:
                lane = lax.broadcasted_iota(jnp.int32, part.shape, 1)
                zero = jnp.zeros_like(part)
                part = jnp.concatenate(
                    [
                        jnp.where(lane < HEAD_DIM, part, zero),
                        jnp.where(lane < HEAD_DIM, zero, part),
                    ],
                    axis=0,
                )
                both = jnp.concatenate([both, weights[g, h + 1]], axis=1)
            out[g * seq : (g + 1) * seq, h * HEAD_DIM : (h + n) * HEAD_DIM] = dot(
                both, part
            ).astype(BF16)


def mix_back(d_mixed, weights, left_v, start):
    groups, heads, seq, _ = weights.shape
    for g in range(groups):
        turned = d_mixed[g * seq : (g + 1) * seq, :].T.astype(BF16)
        at = start + g * seq
        for h, n in head_pairs(heads):
            part = turned[h * HEAD_DIM : (h + n) * HEAD_DIM, :]
            if n == 2:
                row = lax.broadcasted_iota(jnp.int32, part.shape, 0)
                zero = jnp.zeros_like(part)
                part = jnp.concatenate(
                    [
                        jnp.where(row < HEAD_DIM, part, zero),
                        jnp.where(row < HEAD_DIM, zero, part),
                    ],
                    axis=1,
                )
            both = weights[g, h : h + n].reshape(n * seq, seq)
            left_v[h * HEAD_DIM : (h + n) * HEAD_DIM, at : at + seq] = dot(part, both).astype(BF16)


def mixed_rest_kernel(idx, part, last, weights, slot, mixed_o, mixed_s):
    w_last = whole(idx[0], slot)
    for half, out in enumerate((mixed_o, mixed_s)):
        value = (part[half] + dot(last[half], w_last)).astype(BF16)
        mix_values(value, weights.at[half], out)


def d_value_rest_kernel(idx, part, last, weights, slot, left_v, slot_out):
    slot_out[...] = slot[...]
    w_last = whole(idx[0], slot)
    tokens = part.shape[1]
    for half in range(2):
        mix_back(part[half] + dot(last[half], w_last), weights.at[half], left_v, half * tokens)


def assemble_kernel(n_slots, idx, unread, *rest):
    del unread
    slots, (w_out, slots_v, sems) = rest[:n_slots], rest[n_slots:]
    copies = begin_slots(slots, slots_v, sems)
    planes, depth = idx.shape[0] - 1, 2 * slots_v.shape[2]
    for j in range(n_slots, planes):
        w_out[rows_at(idx[1 + j], depth), :] = jnp.zeros((depth, w_out.shape[1]), BF16)
    for copy in copies:
        copy.wait()
    place(idx, idx[0], slots_v, w_out)


def d_value_kernel(idx, cot_o, cot_s, mix_o, mix_s, w_out, left_v, cot_v, mix_v, sems):
    tokens, heads = cot_o.shape[0], mix_v.shape[2]
    here = pl.ds(idx[0] * heads, heads)
    copies = begin(
        [(cot_o, cot_v.at[0]), (mix_o.at[:, here], mix_v.at[0])]
        + [(cot_s, cot_v.at[1]), (mix_s.at[:, here], mix_v.at[1])],
        sems,
    )
    for half in range(2):
        copies[2 * half].wait()
        d_mixed = dot(cot_v[half], w_out[...])
        copies[2 * half + 1].wait()
        mix_back(d_mixed, mix_v.at[half], left_v, half * tokens)


def gradient_kernel(idx, token, unread, right_o, right_s, left_ref, *rest):
    del token, unread
    outs, (right_v, grad_v, sems) = rest[:-3], rest[-3:]
    tokens, _ = right_o.shape
    copies = begin(
        [(right_o, right_v.at[pl.ds(0, tokens)]), (right_s, right_v.at[pl.ds(tokens, tokens)])],
        sems,
    )
    copies[0].wait()
    copies[1].wait()
    gradient_rows(left_ref[...], right_v, grad_v, 640)
    hand_out(idx, 1, grad_v, outs)


def mixed_kernel(n_slots, idx, act_o, act_s, mix_o, mix_s, *rest):
    slots, rest = rest[:n_slots], rest[n_slots:]
    mixed_o, mixed_s, w_v, act_v, mix_v, sems, slots_v, slot_sems = rest
    heads = mix_v.shape[2]
    here = pl.ds(idx[0] * heads, heads)
    slot_copies = begin_slots(slots, slots_v, slot_sems)
    copies = begin(
        [(act_o, act_v.at[0]), (mix_o.at[:, here], mix_v.at[0])]
        + [(act_s, act_v.at[1]), (mix_s.at[:, here], mix_v.at[1])],
        sems,
    )
    for copy in slot_copies:
        copy.wait()
    place(idx, idx[0], slots_v, w_v)
    for half, out in enumerate((mixed_o, mixed_s)):
        copies[2 * half].wait()
        value = dot(act_v[half], w_v[...]).astype(BF16)
        copies[2 * half + 1].wait()
        mix_values(value, mix_v.at[half], out)


def grad_out_kernel(idx, cot_o, cot_s, mixed_o, mixed_s, w_out, unread, *rest):
    del unread
    *outs, cot_v, left_v, grad_v, sems, last_sems = rest
    part = last = None
    if w_out is not None:
        part, last, *outs = outs
    tokens, _ = cot_o.shape
    copies = begin(
        [(cot_o, cot_v.at[pl.ds(0, tokens)]), (cot_s, cot_v.at[pl.ds(tokens, tokens)])], sems
    )
    if w_out is not None:
        depth = last.shape[2]
        columns = pl.ds(pl.multiple_of(idx[idx.shape[0] - 1] * depth, 128), depth)
        later = begin(
            [(cot_o.at[:, columns], last.at[0]), (cot_s.at[:, columns], last.at[1])], last_sems
        )
    left_v[:, :tokens] = mixed_o[...].astype(F32).T.astype(BF16)
    left_v[:, tokens:] = mixed_s[...].astype(F32).T.astype(BF16)
    copies[0].wait()
    copies[1].wait()
    gradient_rows(left_v[...], cot_v, grad_v, 640)
    hand_out(idx, 1, grad_v, outs)
    if w_out is not None:
        for half in range(2):
            part[half] = dot(cot_v[half * tokens : (half + 1) * tokens, :], w_out[...])
        for copy in later:
            copy.wait()


def grad_out_only_kernel(idx, cot_o, cot_s, mixed_o, mixed_s, unread, *rest):
    grad_out_kernel(idx, cot_o, cot_s, mixed_o, mixed_s, None, unread, *rest)


def relay_kernel(unread, first, second, first_out, second_out):
    del unread
    first_out[...] = first[...]
    second_out[...] = second[...]


def sum_kernel(block, got, beside, own, near, far, onward, beside_out, total):
    onward[...] = (block[...].astype(F32) + got[...].astype(F32)).astype(BF16)
    beside_out[...] = beside[...]
    total[...] = own[...].astype(F32) + near[...].astype(F32) + far[...].astype(F32)


def terms_kernel(n_node, idx, mixed_o, mixed_r, w_o, w_r, *outs):
    depth = w_o.shape[0] // n_node
    for j in range(n_node):
        rows = rows_at(idx[j], depth)
        term = dot(mixed_o[...], w_o[rows, :], 1, 1) + dot(mixed_r[...], w_r[rows, :], 1, 1)
        outs[j][...] = term.astype(BF16)


def terms_line_kernel(idx_node, idx, mixed_o, mixed_r, w_o, w_r, slot, slot_r, *outs):
    token, along_x, along_y, kept = outs
    token[...] = jnp.zeros_like(token)
    core, missing = idx[0], idx[4]
    last_o, last_r = whole(core, slot), whole(1 - core, slot_r)
    half = mixed_o.shape[0] // 2
    for j in range(4):
        rows = rows_at(idx_node[j], last_o.shape[0])
        here = idx_node[j] == missing
        term = dot(mixed_o[...], jnp.where(here, last_o, w_o[rows, :]), 1, 1)
        term += dot(mixed_r[...], jnp.where(here, last_r, w_r[rows, :]), 1, 1)
        term = term.astype(BF16)
        first, second = term[:half], term[half:]
        if j == 0:
            kept[0], kept[2] = first, second
        elif j == 1:
            along_x[0], kept[3] = first, second
        elif j == 2:
            kept[1], along_y[0] = first, second
        else:
            along_x[1], along_y[1] = first, second


ANY = pl.BlockSpec(memory_space=pl.ANY)
SMEM = pl.BlockSpec(memory_space=pltpu.SMEM)
VMEM = pl.BlockSpec(memory_space=pltpu.VMEM)


def call(kernel, name, in_specs, out_shapes, scratch, flops, size=1 << 20, kinds=None, vmem=24):
    return pl.pallas_call(
        kernel,
        name=name,
        in_specs=in_specs,
        out_specs=[VMEM] * len(out_shapes),
        out_shape=[
            jax.ShapeDtypeStruct(s, k) for s, k in zip(out_shapes, kinds or [BF16] * len(out_shapes))
        ],
        scratch_shapes=scratch,
        compiler_params=pltpu.CompilerParams(vmem_limit_bytes=vmem << 20),
        cost_estimate=pl.CostEstimate(flops=flops, bytes_accessed=size, transcendentals=0),
    )


def make_body(n_wide, n_node):
    planes = n_wide // 2
    line4 = planes == 4 and n_node == 4

    def move(x, pairs):
        return lax.ppermute(
            x, "wide", [(2 * s + c, 2 * d + c) for s, d in pairs for c in range(2)]
        )

    def swap(x, j):
        return move(x, [(s, s ^ j) for s in range(planes)])

    def sibling(x):
        return lax.ppermute(x, "wide", [(i, i ^ 1) for i in range(n_wide)])

    def flip(x, j):
        return lax.ppermute(x, "node", [(i, i ^ j) for i in range(n_node)])

    def swap_cores(w_out, w_value, act, mix, cot, c):
        cols = w_out.shape[1] // 2
        low = jnp.stack([w_out[:, :cols], w_value[:, :cols]])
        high = jnp.stack([w_out[:, cols:], w_value[:, cols:]])
        got = sibling(jnp.where(c == 0, high, low))
        got, act, mix, cot = lax.optimization_barrier((got, act, mix, cot))
        mine = jnp.where(c == 0, low, high)
        u_out, u_value = (jnp.stack([mine[i], got[i]]) for i in range(2))
        return u_out, u_value, sibling(act), sibling(mix), sibling(cot)

    def gather_ring(u):
        return [u] + [
            move(u, [(s, (s - j) % planes) for s in range(planes)]) for j in range(1, planes)
        ]

    def planes_of(z):
        if line4:
            return [lax.bitwise_xor(z, jnp.int32(j)) for j in range(4)]
        return [lax.rem(z + j, planes) for j in range(planes)]

    def added(block, got):
        return (block.astype(F32) + got.astype(F32)).astype(BF16)

    def scatter_end(own, got, c):
        total = own.astype(F32)
        for part in got:
            total = total + part.astype(F32)
        return join(total[0], sibling(total[1]), c)

    def join(mine, other, c):
        low = jnp.where(c == 0, mine, other)
        high = jnp.where(c == 0, other, mine)
        return jnp.concatenate([low, high], axis=1)

    def scatter_ring(blocks, c):
        total = blocks[0].astype(F32)
        for j in range(1, planes):
            got = move(blocks[j], [(s, (s + j) % planes) for s in range(planes)])
            total = total + got.astype(F32)
        return join(total[0], sibling(total[1]), c)

    def body(act_in, mixing, cotangent, w_value, w_out):
        wide = lax.axis_index("wide")
        n = lax.axis_index("node")
        z, c = wide // 2, lax.rem(wide, 2)
        micro, images, seq, width = act_in.shape
        groups = micro * images
        tokens = groups * seq
        cols = w_value.shape[1] // 2
        heads = cols // HEAD_DIM
        depth = width // planes
        act = act_in.reshape(tokens, width)
        cot = cotangent.reshape(tokens, width)
        mix = mixing.reshape(groups, 2 * heads, seq, seq)
        flops = 4 * tokens * width * cols

        u_out, u_value, act_s, mix_s, cot_s = swap_cores(w_out, w_value, act, mix, cot, c)
        block = u_out.shape
        if line4:
            far, near = swap(u_value, 2), swap(u_value, 1)
            far, u_out = call(relay_kernel, "relay", [ANY, VMEM, VMEM], [block] * 2, [], 0, vmem=8)(
                near, far, u_out
            )
            value_slots = [u_value, near, far, swap(far, 1)]
            far = swap(u_out, 2)
            out_slots = [u_out, swap(u_out, 1), far, swap(far, 1)]
        else:
            value_slots, out_slots = gather_ring(u_value), gather_ring(u_out)
        n_slots = len(out_slots)
        pack = lambda *values: jnp.stack([jnp.int32(x) for x in values])
        idx = pack(c, *planes_of(z))
        idx_node = pack(*[lax.bitwise_xor(n, jnp.int32(j)) for j in range(n_node)])

        mix_scratch = pltpu.VMEM((2, groups, heads, seq, seq), BF16)
        both = pltpu.VMEM((2 * tokens, width), BF16)
        halves = pltpu.VMEM((2, tokens, width), BF16)
        left_tokens = pltpu.VMEM((cols, 2 * tokens), BF16)
        rows = pltpu.VMEM((width, cols), BF16)
        send_shapes = [block] * n_slots

        slots_scratch = [
            pltpu.VMEM((n_slots, *block), BF16),
            pltpu.SemaphoreType.DMA((n_slots,)),
        ]
        part_shapes = [(2, tokens, cols), (2, tokens, depth)]
        if line4:
            ahead = call(
                functools.partial(part_kernel, n_slots - 1),
                "value_ahead",
                [SMEM] + [ANY] * (3 + n_slots),
                [*part_shapes, (2, groups, heads, seq, seq)],
                [
                    *(rows, halves, pltpu.VMEM((n_slots - 1, *block), BF16)),
                    *(pltpu.SemaphoreType.DMA((k,)) for k in (2, 4, n_slots - 1)),
                ],
                flops,
                2 * (3 * act.size + mix.size + width * cols + 4 * tokens * cols),
                kinds=[F32, BF16, BF16],
            )(idx, act, act_s, mix, mix_s, *value_slots[:-1])
            mixed_o, mixed_s = call(
                mixed_rest_kernel,
                "mixed",
                [SMEM] + [VMEM] * 4,
                [(tokens, cols)] * 2,
                [],
                flops // 4,
                2 * (2 * tokens * depth + mix.size + 6 * tokens * cols),
                vmem=16,
            )(idx, *ahead, value_slots[-1])
        else:
            mixed_o, mixed_s = call(
                functools.partial(mixed_kernel, n_slots),
                "mixed",
                [SMEM] + [ANY] * (4 + n_slots),
                [(tokens, cols)] * 2,
                [rows, halves, mix_scratch, pltpu.SemaphoreType.DMA((4,)), *slots_scratch],
                flops,
                2 * (2 * act.size + mix.size + width * cols + 2 * tokens * cols),
                )(idx, act, act_s, mix, mix_s, *value_slots)
        mixed_r = sibling(mixed_s)
        grad_scratch = [both, left_tokens, rows] + [pltpu.SemaphoreType.DMA((2,))] * 2
        size = 2 * (3 * cot.size + 6 * tokens * cols + 2 * width * cols)
        if line4:
            w_part = call(
                functools.partial(assemble_kernel, n_slots - 1),
                "assemble",
                [SMEM] + [ANY] * n_slots,
                [(width, cols)],
                [pltpu.VMEM((n_slots - 1, *block), BF16), pltpu.SemaphoreType.DMA((n_slots - 1,))],
                0,
                4 * width * cols,
            )(idx, mixed_r, *out_slots[:-1])[0]
            w_part_s = sibling(w_part)
            *rest, w_mix = ahead
            part, last, *out_sends = call(
                grad_out_kernel,
                "grad_out",
                [SMEM] + [ANY] * 2 + [VMEM] * 3 + [ANY],
                part_shapes + send_shapes,
                grad_scratch,
                2 * flops,
                size,
                kinds=[F32] + [BF16] * (1 + n_slots),
            )(idx, cot, cot_s, mixed_o, mixed_s, w_part, mixed_r)
            out_passed = swap(out_sends[3], 1)
            left, last_block = call(
                d_value_rest_kernel,
                "d_value",
                [SMEM] + [VMEM] * 4,
                [(cols, 2 * tokens), block],
                [],
                flops // 4,
                2 * (2 * tokens * depth + mix.size + 6 * tokens * cols),
                vmem=16,
            )(idx, part, last, w_mix, out_slots[-1])
            last_s = sibling(last_block)
        else:
            out_sends = call(
                grad_out_only_kernel,
                "grad_out",
                [SMEM] + [ANY] * 2 + [VMEM] * 2 + [ANY],
                send_shapes,
                grad_scratch,
                flops,
                size,
            )(idx, cot, cot_s, mixed_o, mixed_s, mixed_r)
            w_full = call(
                functools.partial(assemble_kernel, n_slots),
                "assemble",
                [SMEM] + [ANY] * (1 + n_slots),
                [(width, cols)],
                slots_scratch,
                0,
                4 * width * cols,
            )(idx, mixed_s, *out_slots)[0]
            left = call(
                d_value_kernel,
                "d_value",
                [SMEM] + [ANY] * 4 + [VMEM],
                [(cols, 2 * tokens)],
                [halves, mix_scratch, pltpu.SemaphoreType.DMA((4,))],
                flops,
                2 * (2 * cot.size + mix.size + width * cols + 2 * tokens * cols),
            )(idx, cot, cot_s, mix, mix_s, w_full)[0]
            w_full_s = sibling(w_full)
            token = left
        if line4:
            out_onward = added(out_sends[2], out_passed)
            out_far = swap(out_onward, 2)
            out_near = swap(out_sends[1], 1)
        else:
            out_onward = token
        part = width // n_node
        half = tokens // 2
        size = 2 * (2 * tokens * cols + 2 * width * cols + tokens * width)
        if line4:
            token, *terms = call(
                terms_line_kernel,
                "terms",
                [SMEM] * 2 + [VMEM] * 6,
                [(16, 128), (2, half, part), (2, half, part), (4, half, part)],
                [],
                flops,
                size,
            )(idx_node, idx, mixed_o, mixed_r, w_part, w_part_s, last_block, last_s)
        else:
            terms = call(
                functools.partial(terms_kernel, n_node),
                "terms",
                [SMEM] + [VMEM] * 4,
                [(tokens, part)] * n_node,
                [],
                flops,
                size,
            )(idx_node, mixed_o, mixed_r, w_full, w_full_s)

        back_sends = call(
            gradient_kernel,
            "grad_value",
            [SMEM] + [ANY] * 4 + [VMEM],
            send_shapes,
            [both, rows, pltpu.SemaphoreType.DMA((2,))],
            flops,
            2 * (2 * act.size + 2 * tokens * cols + width * cols),
        )(idx, token, out_onward, act, act_s, left)
        if line4:
            back_passed = swap(back_sends[3], 1)
            onward, beside, out_total = call(
                sum_kernel, "sum", [VMEM] * 6, [block] * 3, [], 0, kinds=[BF16, BF16, F32], vmem=8
            )(back_sends[2], back_passed, back_sends[1], out_sends[0], out_near, out_far)
            back_far, back_near = swap(onward, 2), swap(beside, 1)
            grad_out = join(out_total[0], sibling(out_total[1]), c)
            grad_value = scatter_end(back_sends[0], (back_near, back_far), c)
        else:
            grad_value = scatter_ring(back_sends, c)
            grad_out = scatter_ring(out_sends, c)

        if line4:
            along_x, along_y, kept = terms
            kept = kept.astype(F32)
            got_x = flip(along_x, 1).astype(F32)
            got_y = flip(along_y, 2).astype(F32)
            last_y = flip((kept[1] + got_x[1]).astype(BF16), 2)
            last_x = flip((kept[3] + got_y[1]).astype(BF16), 1)
            layer_out = jnp.concatenate(
                [
                    kept[0] + got_x[0] + last_y.astype(F32),
                    kept[2] + got_y[0] + last_x.astype(F32),
                ],
                axis=0,
            )
        else:
            layer_out = terms[0].astype(F32)
            for j in range(1, n_node):
                layer_out = layer_out + flip(terms[j], j).astype(F32)
        layer_out = layer_out.astype(BF16).reshape(micro, images, seq, part)
        return layer_out, grad_value, grad_out

    return body


def solution(mesh):
    return jax.shard_map(
        make_body(mesh.shape["wide"], mesh.shape["node"]),
        mesh=mesh,
        in_specs=(
            P(None, "wide", None, None),
            P(None, "wide", "node", None, None),
            P(None, "wide", None, None),
            P("wide", "node"),
            P("wide", "node"),
        ),
        out_specs=(P(None, "wide", None, "node"), P("wide", "node"), P("wide", "node")),
        check_vma=False,
    )
```

```python
import functools
import math

import jax
import jax.numpy as jnp
from jax import lax
from jax.experimental import pallas as pl
from jax.experimental.pallas import tpu as pltpu
from jax.sharding import PartitionSpec as P

HEAD_DIM = 64
F32 = jnp.float32
BF16 = jnp.bfloat16


def dot(a, b, ca=1, cb=0):
    return lax.dot_general(a, b, (((ca,), (cb,)), ((), ())), preferred_element_type=F32)


def begin_slots(slots, slots_v, sems):
    return begin([(slot, slots_v.at[j]) for j, slot in enumerate(slots)], sems)


def begin(pairs, sems):
    copies = [pltpu.make_async_copy(s, d, sems.at[i]) for i, (s, d) in enumerate(pairs)]
    for copy in copies:
        copy.start()
    return copies


def rows_at(index, size):
    return pl.ds(pl.multiple_of(index * size, math.gcd(size, 16)), size)


def place(idx, core, slots_v, w_ref):
    for j in range(slots_v.shape[0]):
        w_ref[rows_at(idx[1 + j], 2 * slots_v.shape[2]), :] = whole(core, slots_v[j])


def hand_out(idx, base, grad_v, outs):
    core = idx[0]
    for i, out in enumerate(outs):
        depth = out.shape[1]
        block = grad_v[rows_at(idx[base + i], 2 * depth), :]
        low, high = block[:depth], block[depth:]
        out[0] = jnp.where(core == 0, low, high)
        out[1] = jnp.where(core == 0, high, low)


def gradient_rows(left, right_ref, rows_ref, step):
    width = right_ref.shape[1]
    for start in range(0, width, step):
        part = dot(left, right_ref[:, start : start + step])
        rows_ref[start : start + step, :] = part.T.astype(BF16)


def head_pairs(heads):
    return [(h, min(2, heads - h)) for h in range(0, heads, 2)]


def whole(core, slot):
    mine, other = slot[0], slot[1]
    low = jnp.where(core == 0, mine, other)
    high = jnp.where(core == 0, other, mine)
    return jnp.concatenate([low, high], axis=0)


def part_kernel(n_slots, idx, x_o, x_s, mix_o, mix_s, *rest):
    slots, rest = rest[:n_slots], rest[n_slots:]
    part, last, weights, w_v, x_v, slots_v, x_sems, sems, slot_sems = rest
    heads, depth = weights.shape[2], last.shape[2]
    here = pl.ds(idx[0] * heads, heads)
    missing = idx[1 + n_slots]
    columns = pl.ds(pl.multiple_of(missing * depth, 128), depth)
    copies = begin_slots(slots, slots_v, slot_sems)
    halves = begin([(x_o, x_v.at[0]), (x_s, x_v.at[1])], x_sems)
    later = begin(
        [(x_o.at[:, columns], last.at[0]), (x_s.at[:, columns], last.at[1])]
        + [(mix_o.at[:, here], weights.at[0]), (mix_s.at[:, here], weights.at[1])],
        sems,
    )
    for copy in copies:
        copy.wait()
    place(idx, idx[0], slots_v, w_v)
    w_v[rows_at(missing, depth), :] = jnp.zeros((depth, w_v.shape[1]), BF16)
    for half in range(2):
        halves[half].wait()
        part[half] = dot(x_v[half], w_v[...])
    for copy in later:
        copy.wait()


def mix_values(value, weights, out):
    groups, heads, seq, _ = weights.shape
    for g in range(groups):
        for h, n in head_pairs(heads):
            part = value[g * seq : (g + 1) * seq, h * HEAD_DIM : (h + n) * HEAD_DIM]
            both = weights[g, h]
            if n == 2:
                lane = lax.broadcasted_iota(jnp.int32, part.shape, 1)
                zero = jnp.zeros_like(part)
                part = jnp.concatenate(
                    [
                        jnp.where(lane < HEAD_DIM, part, zero),
                        jnp.where(lane < HEAD_DIM, zero, part),
                    ],
                    axis=0,
                )
                both = jnp.concatenate([both, weights[g, h + 1]], axis=1)
            out[g * seq : (g + 1) * seq, h * HEAD_DIM : (h + n) * HEAD_DIM] = dot(
                both, part
            ).astype(BF16)


def mix_back(d_mixed, weights, left_v, start):
    groups, heads, seq, _ = weights.shape
    for g in range(groups):
        turned = d_mixed[g * seq : (g + 1) * seq, :].T.astype(BF16)
        at = start + g * seq
        for h, n in head_pairs(heads):
            part = turned[h * HEAD_DIM : (h + n) * HEAD_DIM, :]
            if n == 2:
                row = lax.broadcasted_iota(jnp.int32, part.shape, 0)
                zero = jnp.zeros_like(part)
                part = jnp.concatenate(
                    [
                        jnp.where(row < HEAD_DIM, part, zero),
                        jnp.where(row < HEAD_DIM, zero, part),
                    ],
                    axis=1,
                )
            both = weights[g, h : h + n].reshape(n * seq, seq)
            left_v[h * HEAD_DIM : (h + n) * HEAD_DIM, at : at + seq] = dot(part, both).astype(BF16)


def mixed_rest_kernel(idx, part, last, weights, slot, mixed_o, mixed_s):
    w_last = whole(idx[0], slot)
    for half, out in enumerate((mixed_o, mixed_s)):
        value = (part[half] + dot(last[half], w_last)).astype(BF16)
        mix_values(value, weights.at[half], out)


def d_value_kernel(n_slots, idx, token, cot_o, cot_s, mix_o, mix_s, *rest):
    del token
    slots, rest = rest[:n_slots], rest[n_slots:]
    left_v, w_out, cot_v, mix_v, sems, slots_v, slot_sems = rest
    tokens, heads = cot_o.shape[0], mix_v.shape[2]
    here = pl.ds(idx[0] * heads, heads)
    slot_copies = begin_slots(slots, slots_v, slot_sems)
    copies = begin(
        [(cot_o, cot_v.at[0]), (mix_o.at[:, here], mix_v.at[0])]
        + [(cot_s, cot_v.at[1]), (mix_s.at[:, here], mix_v.at[1])],
        sems,
    )
    for copy in slot_copies:
        copy.wait()
    place(idx, idx[0], slots_v, w_out)
    for half in range(2):
        copies[2 * half].wait()
        d_mixed = dot(cot_v[half], w_out[...])
        copies[2 * half + 1].wait()
        mix_back(d_mixed, mix_v.at[half], left_v, half * tokens)


def gradient_kernel(idx, token, unread, right_o, right_s, left_ref, *rest):
    del token, unread
    outs, (right_v, grad_v, sems) = rest[:-3], rest[-3:]
    tokens, _ = right_o.shape
    copies = begin(
        [(right_o, right_v.at[pl.ds(0, tokens)]), (right_s, right_v.at[pl.ds(tokens, tokens)])],
        sems,
    )
    copies[0].wait()
    copies[1].wait()
    gradient_rows(left_ref[...], right_v, grad_v, 640)
    hand_out(idx, 1, grad_v, outs)


def mixed_kernel(n_slots, idx, act_o, act_s, mix_o, mix_s, *rest):
    slots, rest = rest[:n_slots], rest[n_slots:]
    mixed_o, mixed_s, w_v, act_v, mix_v, sems, slots_v, slot_sems = rest
    heads = mix_v.shape[2]
    here = pl.ds(idx[0] * heads, heads)
    slot_copies = begin_slots(slots, slots_v, slot_sems)
    copies = begin(
        [(act_o, act_v.at[0]), (mix_o.at[:, here], mix_v.at[0])]
        + [(act_s, act_v.at[1]), (mix_s.at[:, here], mix_v.at[1])],
        sems,
    )
    for copy in slot_copies:
        copy.wait()
    place(idx, idx[0], slots_v, w_v)
    for half, out in enumerate((mixed_o, mixed_s)):
        copies[2 * half].wait()
        value = dot(act_v[half], w_v[...]).astype(BF16)
        copies[2 * half + 1].wait()
        mix_values(value, mix_v.at[half], out)


def grad_out_kernel(n_unread, idx, cot_o, cot_s, mixed_o, mixed_s, *rest):
    token, *outs, cot_v, left_v, grad_v, sems = rest[n_unread:]
    token[...] = jnp.zeros_like(token)
    tokens, _ = cot_o.shape
    copies = begin(
        [(cot_o, cot_v.at[pl.ds(0, tokens)]), (cot_s, cot_v.at[pl.ds(tokens, tokens)])], sems
    )
    left_v[:, :tokens] = mixed_o[...].astype(F32).T.astype(BF16)
    left_v[:, tokens:] = mixed_s[...].astype(F32).T.astype(BF16)
    copies[0].wait()
    copies[1].wait()
    gradient_rows(left_v[...], cot_v, grad_v, 640)
    hand_out(idx, 1, grad_v, outs)


def relay_kernel(unread, first, second, first_out, second_out):
    del unread
    first_out[...] = first[...]
    second_out[...] = second[...]


def sum_kernel(block, got, beside, own, near, far, onward, beside_out, total):
    onward[...] = (block[...].astype(F32) + got[...].astype(F32)).astype(BF16)
    beside_out[...] = beside[...]
    total[...] = own[...].astype(F32) + near[...].astype(F32) + far[...].astype(F32)


def terms_kernel(n_node, idx, mixed_o, mixed_r, w_o, w_r, token, *outs):
    token[...] = jnp.zeros_like(token)
    depth = w_o.shape[0] // n_node
    half = mixed_o.shape[0] // 2
    for j in range(n_node):
        rows = rows_at(idx[j], depth)
        term = dot(mixed_o[...], w_o[rows, :], 1, 1) + dot(mixed_r[...], w_r[rows, :], 1, 1)
        term = term.astype(BF16)
        if n_node != 4:
            outs[j][...] = term
            continue
        along_x, along_y, kept = outs
        first, second = term[:half], term[half:]
        if j == 0:
            kept[0], kept[2] = first, second
        elif j == 1:
            along_x[0], kept[3] = first, second
        elif j == 2:
            kept[1], along_y[0] = first, second
        else:
            along_x[1], along_y[1] = first, second


ANY = pl.BlockSpec(memory_space=pl.ANY)
SMEM = pl.BlockSpec(memory_space=pltpu.SMEM)
VMEM = pl.BlockSpec(memory_space=pltpu.VMEM)


def call(kernel, name, in_specs, out_shapes, scratch, flops, size=1 << 20, kinds=None, vmem=24):
    return pl.pallas_call(
        kernel,
        name=name,
        in_specs=in_specs,
        out_specs=[VMEM] * len(out_shapes),
        out_shape=[
            jax.ShapeDtypeStruct(s, k) for s, k in zip(out_shapes, kinds or [BF16] * len(out_shapes))
        ],
        scratch_shapes=scratch,
        compiler_params=pltpu.CompilerParams(vmem_limit_bytes=vmem << 20),
        cost_estimate=pl.CostEstimate(flops=flops, bytes_accessed=size, transcendentals=0),
    )


def make_body(n_wide, n_node):
    planes = n_wide // 2
    line4 = planes == 4 and n_node == 4

    def move(x, pairs):
        return lax.ppermute(
            x, "wide", [(2 * s + c, 2 * d + c) for s, d in pairs for c in range(2)]
        )

    def swap(x, j):
        return move(x, [(s, s ^ j) for s in range(planes)])

    def sibling(x):
        return lax.ppermute(x, "wide", [(i, i ^ 1) for i in range(n_wide)])

    def flip(x, j):
        return lax.ppermute(x, "node", [(i, i ^ j) for i in range(n_node)])

    def swap_cores(w_out, w_value, act, mix, cot, c):
        cols = w_out.shape[1] // 2
        low = jnp.stack([w_out[:, :cols], w_value[:, :cols]])
        high = jnp.stack([w_out[:, cols:], w_value[:, cols:]])
        got = sibling(jnp.where(c == 0, high, low))
        got, act, mix, cot = lax.optimization_barrier((got, act, mix, cot))
        mine = jnp.where(c == 0, low, high)
        u_out, u_value = (jnp.stack([mine[i], got[i]]) for i in range(2))
        return u_out, u_value, sibling(act), sibling(mix), sibling(cot)

    def gather_ring(u):
        return [u] + [
            move(u, [(s, (s - j) % planes) for s in range(planes)]) for j in range(1, planes)
        ]

    def planes_of(z):
        if line4:
            return [lax.bitwise_xor(z, jnp.int32(j)) for j in range(4)]
        return [lax.rem(z + j, planes) for j in range(planes)]

    def added(block, got):
        return (block.astype(F32) + got.astype(F32)).astype(BF16)

    def scatter_end(own, got, c):
        total = own.astype(F32)
        for part in got:
            total = total + part.astype(F32)
        return join(total[0], sibling(total[1]), c)

    def join(mine, other, c):
        low = jnp.where(c == 0, mine, other)
        high = jnp.where(c == 0, other, mine)
        return jnp.concatenate([low, high], axis=1)

    def scatter_ring(blocks, c):
        total = blocks[0].astype(F32)
        for j in range(1, planes):
            got = move(blocks[j], [(s, (s + j) % planes) for s in range(planes)])
            total = total + got.astype(F32)
        return join(total[0], sibling(total[1]), c)

    def body(act_in, mixing, cotangent, w_value, w_out):
        wide = lax.axis_index("wide")
        n = lax.axis_index("node")
        z, c = wide // 2, lax.rem(wide, 2)
        micro, images, seq, width = act_in.shape
        groups = micro * images
        tokens = groups * seq
        cols = w_value.shape[1] // 2
        heads = cols // HEAD_DIM
        depth = width // planes
        act = act_in.reshape(tokens, width)
        cot = cotangent.reshape(tokens, width)
        mix = mixing.reshape(groups, 2 * heads, seq, seq)
        flops = 4 * tokens * width * cols

        u_out, u_value, act_s, mix_s, cot_s = swap_cores(w_out, w_value, act, mix, cot, c)
        block = u_out.shape
        if line4:
            far, near = swap(u_value, 2), swap(u_value, 1)
            far, u_out = call(relay_kernel, "relay", [ANY, VMEM, VMEM], [block] * 2, [], 0, vmem=8)(
                near, far, u_out
            )
            value_slots = [u_value, near, far, swap(far, 1)]
            far = swap(u_out, 2)
            out_slots = [u_out, swap(u_out, 1), far, swap(far, 1)]
        else:
            value_slots, out_slots = gather_ring(u_value), gather_ring(u_out)
        n_slots = len(out_slots)
        pack = lambda *values: jnp.stack([jnp.int32(x) for x in values])
        idx = pack(c, *planes_of(z))
        idx_node = pack(*[lax.bitwise_xor(n, jnp.int32(j)) for j in range(n_node)])

        mix_scratch = pltpu.VMEM((2, groups, heads, seq, seq), BF16)
        both = pltpu.VMEM((2 * tokens, width), BF16)
        halves = pltpu.VMEM((2, tokens, width), BF16)
        left_tokens = pltpu.VMEM((cols, 2 * tokens), BF16)
        rows = pltpu.VMEM((width, cols), BF16)
        send_shapes = [block] * n_slots

        slots_scratch = [
            pltpu.VMEM((n_slots, *block), BF16),
            pltpu.SemaphoreType.DMA((n_slots,)),
        ]
        part_shapes = [(2, tokens, cols), (2, tokens, depth)]
        if line4:
            ahead = call(
                functools.partial(part_kernel, n_slots - 1),
                "value_ahead",
                [SMEM] + [ANY] * (3 + n_slots),
                [*part_shapes, (2, groups, heads, seq, seq)],
                [
                    *(rows, halves, pltpu.VMEM((n_slots - 1, *block), BF16)),
                    *(pltpu.SemaphoreType.DMA((k,)) for k in (2, 4, n_slots - 1)),
                ],
                flops,
                2 * (3 * act.size + mix.size + width * cols + 4 * tokens * cols),
                kinds=[F32, BF16, BF16],
            )(idx, act, act_s, mix, mix_s, *value_slots[:-1])
            mixed_o, mixed_s = call(
                mixed_rest_kernel,
                "mixed",
                [SMEM] + [VMEM] * 4,
                [(tokens, cols)] * 2,
                [],
                flops // 4,
                2 * (2 * tokens * depth + mix.size + 6 * tokens * cols),
                vmem=16,
            )(idx, *ahead, value_slots[-1])
        else:
            mixed_o, mixed_s = call(
                functools.partial(mixed_kernel, n_slots),
                "mixed",
                [SMEM] + [ANY] * (4 + n_slots),
                [(tokens, cols)] * 2,
                [rows, halves, mix_scratch, pltpu.SemaphoreType.DMA((4,)), *slots_scratch],
                flops,
                2 * (2 * act.size + mix.size + width * cols + 2 * tokens * cols),
                )(idx, act, act_s, mix, mix_s, *value_slots)
        mixed_r = sibling(mixed_s)
        unread = [mixed_r, *(out_slots[1:3] if line4 else [])]
        token, *out_sends = call(
            functools.partial(grad_out_kernel, len(unread)),
            "grad_out",
            [SMEM] + [ANY] * 2 + [VMEM] * 2 + [ANY] * len(unread),
            [(16, 128)] + send_shapes,
            [both, left_tokens, rows, pltpu.SemaphoreType.DMA((2,))],
            flops,
            2 * (2 * cot.size + 2 * tokens * cols + width * cols),
        )(idx, cot, cot_s, mixed_o, mixed_s, *unread)
        out_passed = swap(out_sends[3], 1) if line4 else token
        left, w_full = call(
            functools.partial(d_value_kernel, n_slots),
            "d_value",
            [SMEM] + [ANY] * (5 + n_slots),
            [(cols, 2 * tokens), (width, cols)],
            [halves, mix_scratch, pltpu.SemaphoreType.DMA((4,)), *slots_scratch],
            flops,
            2 * (2 * cot.size + mix.size + 2 * width * cols + 2 * tokens * cols),
        )(idx, token, cot, cot_s, mix, mix_s, *out_slots)
        w_full_s = sibling(w_full)
        if line4:
            out_onward = added(out_sends[2], out_passed)
            out_far = swap(out_onward, 2)
            out_near = swap(out_sends[1], 1)
        else:
            out_onward = left
        part = width // n_node
        half = tokens // 2
        if n_node == 4:
            term_shapes = [(2, half, part), (2, half, part), (4, half, part)]
        else:
            term_shapes = [(tokens, part)] * n_node
        token, *terms = call(
            functools.partial(terms_kernel, n_node),
            "terms",
            [SMEM] + [VMEM] * 4,
            [(16, 128)] + term_shapes,
            [],
            flops,
            2 * (2 * tokens * cols + 2 * width * cols + tokens * width),
        )(idx_node, mixed_o, mixed_r, w_full, w_full_s)
        back_sends = call(
            gradient_kernel,
            "grad_value",
            [SMEM] + [ANY] * 4 + [VMEM],
            send_shapes,
            [both, rows, pltpu.SemaphoreType.DMA((2,))],
            flops,
            2 * (2 * act.size + 2 * tokens * cols + width * cols),
        )(idx, token, out_onward, act, act_s, left)
        if line4:
            back_passed = swap(back_sends[3], 1)
            onward, beside, out_total = call(
                sum_kernel, "sum", [VMEM] * 6, [block] * 3, [], 0, kinds=[BF16, BF16, F32], vmem=8
            )(back_sends[2], back_passed, back_sends[1], out_sends[0], out_near, out_far)
            back_far, back_near = swap(onward, 2), swap(beside, 1)
            grad_out = join(out_total[0], sibling(out_total[1]), c)
            grad_value = scatter_end(back_sends[0], (back_near, back_far), c)
        else:
            grad_value = scatter_ring(back_sends, c)
            grad_out = scatter_ring(out_sends, c)

        if n_node == 4:
            along_x, along_y, kept = terms
            kept = kept.astype(F32)
            got_x = flip(along_x, 1).astype(F32)
            got_y = flip(along_y, 2).astype(F32)
            last_y = flip((kept[1] + got_x[1]).astype(BF16), 2)
            last_x = flip((kept[3] + got_y[1]).astype(BF16), 1)
            layer_out = jnp.concatenate(
                [
                    kept[0] + got_x[0] + last_y.astype(F32),
                    kept[2] + got_y[0] + last_x.astype(F32),
                ],
                axis=0,
            )
        else:
            layer_out = terms[0].astype(F32)
            for j in range(1, n_node):
                layer_out = layer_out + flip(terms[j], j).astype(F32)
        layer_out = layer_out.astype(BF16).reshape(micro, images, seq, part)
        return layer_out, grad_value, grad_out

    return body


def solution(mesh):
    return jax.shard_map(
        make_body(mesh.shape["wide"], mesh.shape["node"]),
        mesh=mesh,
        in_specs=(
            P(None, "wide", None, None),
            P(None, "wide", "node", None, None),
            P(None, "wide", None, None),
            P("wide", "node"),
            P("wide", "node"),
        ),
        out_specs=(P(None, "wide", None, "node"), P("wide", "node"), P("wide", "node")),
        check_vma=False,
    )
```

```python
import functools
import math

import jax
import jax.numpy as jnp
from jax import lax
from jax.experimental import pallas as pl
from jax.experimental.pallas import tpu as pltpu
from jax.sharding import PartitionSpec as P

HEAD_DIM = 64
F32 = jnp.float32
BF16 = jnp.bfloat16


def dot(a, b, ca=1, cb=0):
    return lax.dot_general(a, b, (((ca,), (cb,)), ((), ())), preferred_element_type=F32)


def begin_slots(slots, slots_v, sems):
    return begin([(slot, slots_v.at[j]) for j, slot in enumerate(slots)], sems)


def begin(pairs, sems):
    copies = [pltpu.make_async_copy(s, d, sems.at[i]) for i, (s, d) in enumerate(pairs)]
    for copy in copies:
        copy.start()
    return copies


def rows_at(index, size):
    return pl.ds(pl.multiple_of(index * size, math.gcd(size, 16)), size)


def place(idx, core, slots_v, w_ref):
    for j in range(slots_v.shape[0]):
        w_ref[rows_at(idx[1 + j], 2 * slots_v.shape[2]), :] = whole(core, slots_v[j])


def hand_out(idx, base, grad_v, outs):
    core = idx[0]
    for i, out in enumerate(outs):
        depth = out.shape[1]
        block = grad_v[rows_at(idx[base + i], 2 * depth), :]
        low, high = block[:depth], block[depth:]
        out[0] = jnp.where(core == 0, low, high)
        out[1] = jnp.where(core == 0, high, low)


def gradient_rows(left, right_ref, rows_ref, step):
    width = right_ref.shape[1]
    for start in range(0, width, step):
        part = dot(left, right_ref[:, start : start + step])
        rows_ref[start : start + step, :] = part.T.astype(BF16)


def head_pairs(heads):
    return [(h, min(2, heads - h)) for h in range(0, heads, 2)]


def whole(core, slot):
    mine, other = slot[0], slot[1]
    low = jnp.where(core == 0, mine, other)
    high = jnp.where(core == 0, other, mine)
    return jnp.concatenate([low, high], axis=0)


def part_kernel(n_slots, idx, x_o, x_s, mix_o, mix_s, *rest):
    slots, rest = rest[:n_slots], rest[n_slots:]
    part, last, weights, w_v, x_v, slots_v, x_sems, sems, slot_sems = rest
    heads, depth = weights.shape[2], last.shape[2]
    here = pl.ds(idx[0] * heads, heads)
    missing = idx[1 + n_slots]
    columns = pl.ds(pl.multiple_of(missing * depth, 128), depth)
    copies = begin_slots(slots, slots_v, slot_sems)
    halves = begin([(x_o, x_v.at[0]), (x_s, x_v.at[1])], x_sems)
    later = begin(
        [(x_o.at[:, columns], last.at[0]), (x_s.at[:, columns], last.at[1])]
        + [(mix_o.at[:, here], weights.at[0]), (mix_s.at[:, here], weights.at[1])],
        sems,
    )
    for copy in copies:
        copy.wait()
    place(idx, idx[0], slots_v, w_v)
    w_v[rows_at(missing, depth), :] = jnp.zeros((depth, w_v.shape[1]), BF16)
    for half in range(2):
        halves[half].wait()
        part[half] = dot(x_v[half], w_v[...])
    for copy in later:
        copy.wait()


def mix_values(value, weights, out):
    groups, heads, seq, _ = weights.shape
    for g in range(groups):
        for h, n in head_pairs(heads):
            part = value[g * seq : (g + 1) * seq, h * HEAD_DIM : (h + n) * HEAD_DIM]
            both = weights[g, h]
            if n == 2:
                lane = lax.broadcasted_iota(jnp.int32, part.shape, 1)
                zero = jnp.zeros_like(part)
                part = jnp.concatenate(
                    [
                        jnp.where(lane < HEAD_DIM, part, zero),
                        jnp.where(lane < HEAD_DIM, zero, part),
                    ],
                    axis=0,
                )
                both = jnp.concatenate([both, weights[g, h + 1]], axis=1)
            out[g * seq : (g + 1) * seq, h * HEAD_DIM : (h + n) * HEAD_DIM] = dot(
                both, part
            ).astype(BF16)


def mix_back(d_mixed, weights, left_v, start):
    groups, heads, seq, _ = weights.shape
    for g in range(groups):
        turned = d_mixed[g * seq : (g + 1) * seq, :].T.astype(BF16)
        at = start + g * seq
        for h, n in head_pairs(heads):
            part = turned[h * HEAD_DIM : (h + n) * HEAD_DIM, :]
            if n == 2:
                row = lax.broadcasted_iota(jnp.int32, part.shape, 0)
                zero = jnp.zeros_like(part)
                part = jnp.concatenate(
                    [
                        jnp.where(row < HEAD_DIM, part, zero),
                        jnp.where(row < HEAD_DIM, zero, part),
                    ],
                    axis=1,
                )
            both = weights[g, h : h + n].reshape(n * seq, seq)
            left_v[h * HEAD_DIM : (h + n) * HEAD_DIM, at : at + seq] = dot(part, both).astype(BF16)


def mixed_rest_kernel(idx, part, last, weights, slot, mixed_o, mixed_s):
    w_last = whole(idx[0], slot)
    for half, out in enumerate((mixed_o, mixed_s)):
        value = (part[half] + dot(last[half], w_last)).astype(BF16)
        mix_values(value, weights.at[half], out)


def assemble_kernel(n_slots, idx, unread, unread_too, *rest):
    del unread, unread_too
    slots, (w_out, slots_v, sems) = rest[:n_slots], rest[n_slots:]
    for copy in begin_slots(slots, slots_v, sems):
        copy.wait()
    place(idx, idx[0], slots_v, w_out)


def d_value_kernel(n_slots, idx, token, cot_o, cot_s, mix_o, mix_s, *rest):
    del token
    slots, rest = rest[:n_slots], rest[n_slots:]
    left_v, w_out, cot_v, mix_v, sems, slots_v, slot_sems = rest
    tokens, heads = cot_o.shape[0], mix_v.shape[2]
    here = pl.ds(idx[0] * heads, heads)
    slot_copies = begin_slots(slots, slots_v, slot_sems)
    copies = begin(
        [(cot_o, cot_v.at[0]), (mix_o.at[:, here], mix_v.at[0])]
        + [(cot_s, cot_v.at[1]), (mix_s.at[:, here], mix_v.at[1])],
        sems,
    )
    for copy in slot_copies:
        copy.wait()
    place(idx, idx[0], slots_v, w_out)
    for half in range(2):
        copies[2 * half].wait()
        d_mixed = dot(cot_v[half], w_out[...])
        copies[2 * half + 1].wait()
        mix_back(d_mixed, mix_v.at[half], left_v, half * tokens)


def gradient_kernel(idx, token, unread, right_o, right_s, left_ref, *rest):
    del token, unread
    outs, (right_v, grad_v, sems) = rest[:-3], rest[-3:]
    tokens, _ = right_o.shape
    copies = begin(
        [(right_o, right_v.at[pl.ds(0, tokens)]), (right_s, right_v.at[pl.ds(tokens, tokens)])],
        sems,
    )
    copies[0].wait()
    copies[1].wait()
    gradient_rows(left_ref[...], right_v, grad_v, 640)
    hand_out(idx, 1, grad_v, outs)


def mixed_kernel(n_slots, idx, act_o, act_s, mix_o, mix_s, *rest):
    slots, rest = rest[:n_slots], rest[n_slots:]
    mixed_o, mixed_s, w_v, act_v, mix_v, sems, slots_v, slot_sems = rest
    heads = mix_v.shape[2]
    here = pl.ds(idx[0] * heads, heads)
    slot_copies = begin_slots(slots, slots_v, slot_sems)
    copies = begin(
        [(act_o, act_v.at[0]), (mix_o.at[:, here], mix_v.at[0])]
        + [(act_s, act_v.at[1]), (mix_s.at[:, here], mix_v.at[1])],
        sems,
    )
    for copy in slot_copies:
        copy.wait()
    place(idx, idx[0], slots_v, w_v)
    for half, out in enumerate((mixed_o, mixed_s)):
        copies[2 * half].wait()
        value = dot(act_v[half], w_v[...]).astype(BF16)
        copies[2 * half + 1].wait()
        mix_values(value, mix_v.at[half], out)


def grad_out_kernel(n_unread, idx, cot_o, cot_s, mixed_o, mixed_s, *rest):
    token, *outs, cot_v, left_v, grad_v, sems = rest[n_unread:]
    token[...] = jnp.zeros_like(token)
    tokens, _ = cot_o.shape
    copies = begin(
        [(cot_o, cot_v.at[pl.ds(0, tokens)]), (cot_s, cot_v.at[pl.ds(tokens, tokens)])], sems
    )
    left_v[:, :tokens] = mixed_o[...].astype(F32).T.astype(BF16)
    left_v[:, tokens:] = mixed_s[...].astype(F32).T.astype(BF16)
    copies[0].wait()
    copies[1].wait()
    gradient_rows(left_v[...], cot_v, grad_v, 640)
    hand_out(idx, 1, grad_v, outs)


def relay_kernel(unread, first, second, first_out, second_out):
    del unread
    first_out[...] = first[...]
    second_out[...] = second[...]


def sum_kernel(block, got, beside, own, near, far, onward, beside_out, total):
    onward[...] = (block[...].astype(F32) + got[...].astype(F32)).astype(BF16)
    beside_out[...] = beside[...]
    total[...] = own[...].astype(F32) + near[...].astype(F32) + far[...].astype(F32)


def terms_kernel(n_node, idx, mixed_o, mixed_r, w_o, w_r, token, *outs):
    token[...] = jnp.zeros_like(token)
    depth = w_o.shape[0] // n_node
    half = mixed_o.shape[0] // 2
    for j in range(n_node):
        rows = rows_at(idx[j], depth)
        term = dot(mixed_o[...], w_o[rows, :], 1, 1) + dot(mixed_r[...], w_r[rows, :], 1, 1)
        term = term.astype(BF16)
        if n_node != 4:
            outs[j][...] = term
            continue
        along_x, along_y, kept = outs
        first, second = term[:half], term[half:]
        if j == 0:
            kept[0], kept[2] = first, second
        elif j == 1:
            along_x[0], kept[3] = first, second
        elif j == 2:
            kept[1], along_y[0] = first, second
        else:
            along_x[1], along_y[1] = first, second


ANY = pl.BlockSpec(memory_space=pl.ANY)
SMEM = pl.BlockSpec(memory_space=pltpu.SMEM)
VMEM = pl.BlockSpec(memory_space=pltpu.VMEM)


def call(kernel, name, in_specs, out_shapes, scratch, flops, size=1 << 20, kinds=None, vmem=24):
    return pl.pallas_call(
        kernel,
        name=name,
        in_specs=in_specs,
        out_specs=[VMEM] * len(out_shapes),
        out_shape=[
            jax.ShapeDtypeStruct(s, k) for s, k in zip(out_shapes, kinds or [BF16] * len(out_shapes))
        ],
        scratch_shapes=scratch,
        compiler_params=pltpu.CompilerParams(vmem_limit_bytes=vmem << 20),
        cost_estimate=pl.CostEstimate(flops=flops, bytes_accessed=size, transcendentals=0),
    )


def make_body(n_wide, n_node):
    planes = n_wide // 2
    line4 = planes == 4 and n_node == 4

    def move(x, pairs):
        return lax.ppermute(
            x, "wide", [(2 * s + c, 2 * d + c) for s, d in pairs for c in range(2)]
        )

    def swap(x, j):
        return move(x, [(s, s ^ j) for s in range(planes)])

    def sibling(x):
        return lax.ppermute(x, "wide", [(i, i ^ 1) for i in range(n_wide)])

    def flip(x, j):
        return lax.ppermute(x, "node", [(i, i ^ j) for i in range(n_node)])

    def swap_cores(w_out, w_value, act, mix, cot, c):
        cols = w_out.shape[1] // 2
        low = jnp.stack([w_out[:, :cols], w_value[:, :cols]])
        high = jnp.stack([w_out[:, cols:], w_value[:, cols:]])
        got = sibling(jnp.where(c == 0, high, low))
        got, act, mix, cot = lax.optimization_barrier((got, act, mix, cot))
        mine = jnp.where(c == 0, low, high)
        u_out, u_value = (jnp.stack([mine[i], got[i]]) for i in range(2))
        return u_out, u_value, sibling(act), sibling(mix), sibling(cot)

    def gather_ring(u):
        return [u] + [
            move(u, [(s, (s - j) % planes) for s in range(planes)]) for j in range(1, planes)
        ]

    def planes_of(z):
        if line4:
            return [lax.bitwise_xor(z, jnp.int32(j)) for j in range(4)]
        return [lax.rem(z + j, planes) for j in range(planes)]

    def added(block, got):
        return (block.astype(F32) + got.astype(F32)).astype(BF16)

    def scatter_end(own, got, c):
        total = own.astype(F32)
        for part in got:
            total = total + part.astype(F32)
        return join(total[0], sibling(total[1]), c)

    def join(mine, other, c):
        low = jnp.where(c == 0, mine, other)
        high = jnp.where(c == 0, other, mine)
        return jnp.concatenate([low, high], axis=1)

    def scatter_ring(blocks, c):
        total = blocks[0].astype(F32)
        for j in range(1, planes):
            got = move(blocks[j], [(s, (s + j) % planes) for s in range(planes)])
            total = total + got.astype(F32)
        return join(total[0], sibling(total[1]), c)

    def body(act_in, mixing, cotangent, w_value, w_out):
        wide = lax.axis_index("wide")
        n = lax.axis_index("node")
        z, c = wide // 2, lax.rem(wide, 2)
        micro, images, seq, width = act_in.shape
        groups = micro * images
        tokens = groups * seq
        cols = w_value.shape[1] // 2
        heads = cols // HEAD_DIM
        depth = width // planes
        act = act_in.reshape(tokens, width)
        cot = cotangent.reshape(tokens, width)
        mix = mixing.reshape(groups, 2 * heads, seq, seq)
        flops = 4 * tokens * width * cols

        u_out, u_value, act_s, mix_s, cot_s = swap_cores(w_out, w_value, act, mix, cot, c)
        block = u_out.shape
        if line4:
            far, near = swap(u_value, 2), swap(u_value, 1)
            far, u_out = call(relay_kernel, "relay", [ANY, VMEM, VMEM], [block] * 2, [], 0, vmem=8)(
                near, far, u_out
            )
            value_slots = [u_value, near, far, swap(far, 1)]
            far = swap(u_out, 2)
            out_slots = [u_out, swap(u_out, 1), far, swap(far, 1)]
        else:
            value_slots, out_slots = gather_ring(u_value), gather_ring(u_out)
        n_slots = len(out_slots)
        pack = lambda *values: jnp.stack([jnp.int32(x) for x in values])
        idx = pack(c, *planes_of(z))
        idx_node = pack(*[lax.bitwise_xor(n, jnp.int32(j)) for j in range(n_node)])

        mix_scratch = pltpu.VMEM((2, groups, heads, seq, seq), BF16)
        both = pltpu.VMEM((2 * tokens, width), BF16)
        halves = pltpu.VMEM((2, tokens, width), BF16)
        left_tokens = pltpu.VMEM((cols, 2 * tokens), BF16)
        rows = pltpu.VMEM((width, cols), BF16)
        send_shapes = [block] * n_slots

        slots_scratch = [
            pltpu.VMEM((n_slots, *block), BF16),
            pltpu.SemaphoreType.DMA((n_slots,)),
        ]
        part_shapes = [(2, tokens, cols), (2, tokens, depth)]
        if line4:
            ahead = call(
                functools.partial(part_kernel, n_slots - 1),
                "value_ahead",
                [SMEM] + [ANY] * (3 + n_slots),
                [*part_shapes, (2, groups, heads, seq, seq)],
                [
                    *(rows, halves, pltpu.VMEM((n_slots - 1, *block), BF16)),
                    *(pltpu.SemaphoreType.DMA((k,)) for k in (2, 4, n_slots - 1)),
                ],
                flops,
                2 * (3 * act.size + mix.size + width * cols + 4 * tokens * cols),
                kinds=[F32, BF16, BF16],
            )(idx, act, act_s, mix, mix_s, *value_slots[:-1])
            mixed_o, mixed_s = call(
                mixed_rest_kernel,
                "mixed",
                [SMEM] + [VMEM] * 4,
                [(tokens, cols)] * 2,
                [],
                flops // 4,
                2 * (2 * tokens * depth + mix.size + 6 * tokens * cols),
                vmem=16,
            )(idx, *ahead, value_slots[-1])
        else:
            mixed_o, mixed_s = call(
                functools.partial(mixed_kernel, n_slots),
                "mixed",
                [SMEM] + [ANY] * (4 + n_slots),
                [(tokens, cols)] * 2,
                [rows, halves, mix_scratch, pltpu.SemaphoreType.DMA((4,)), *slots_scratch],
                flops,
                2 * (2 * act.size + mix.size + width * cols + 2 * tokens * cols),
                )(idx, act, act_s, mix, mix_s, *value_slots)
        mixed_r = sibling(mixed_s)
        unread = [mixed_r, *(out_slots[1:3] if line4 else [])]
        token, *out_sends = call(
            functools.partial(grad_out_kernel, len(unread)),
            "grad_out",
            [SMEM] + [ANY] * 2 + [VMEM] * 2 + [ANY] * len(unread),
            [(16, 128)] + send_shapes,
            [both, left_tokens, rows, pltpu.SemaphoreType.DMA((2,))],
            flops,
            2 * (2 * cot.size + 2 * tokens * cols + width * cols),
        )(idx, cot, cot_s, mixed_o, mixed_s, *unread)
        out_passed = swap(out_sends[3], 1) if line4 else token
        left = call(
            functools.partial(d_value_kernel, n_slots),
            "d_value",
            [SMEM] + [ANY] * (5 + n_slots),
            [(cols, 2 * tokens)],
            [rows, halves, mix_scratch, pltpu.SemaphoreType.DMA((4,)), *slots_scratch],
            flops,
            2 * (2 * cot.size + mix.size + width * cols + 2 * tokens * cols),
        )(idx, token, cot, cot_s, mix, mix_s, *out_slots)[0]
        if line4:
            out_onward = added(out_sends[2], out_passed)
            out_far = swap(out_onward, 2)
            out_near = swap(out_sends[1], 1)
        else:
            out_onward = left
        w_full = call(
            functools.partial(assemble_kernel, n_slots),
            "assemble",
            [SMEM] + [ANY] * (2 + n_slots),
            [(width, cols)],
            slots_scratch,
            0,
            4 * width * cols,
        )(idx, out_onward, left, *out_slots)[0]
        w_full_s = sibling(w_full)
        part = width // n_node
        half = tokens // 2
        if n_node == 4:
            term_shapes = [(2, half, part), (2, half, part), (4, half, part)]
        else:
            term_shapes = [(tokens, part)] * n_node
        token, *terms = call(
            functools.partial(terms_kernel, n_node),
            "terms",
            [SMEM] + [VMEM] * 4,
            [(16, 128)] + term_shapes,
            [],
            flops,
            2 * (2 * tokens * cols + 2 * width * cols + tokens * width),
        )(idx_node, mixed_o, mixed_r, w_full, w_full_s)
        back_sends = call(
            gradient_kernel,
            "grad_value",
            [SMEM] + [ANY] * 4 + [VMEM],
            send_shapes,
            [both, rows, pltpu.SemaphoreType.DMA((2,))],
            flops,
            2 * (2 * act.size + 2 * tokens * cols + width * cols),
        )(idx, token, out_onward, act, act_s, left)
        if line4:
            back_passed = swap(back_sends[3], 1)
            onward, beside, out_total = call(
                sum_kernel, "sum", [VMEM] * 6, [block] * 3, [], 0, kinds=[BF16, BF16, F32], vmem=8
            )(back_sends[2], back_passed, back_sends[1], out_sends[0], out_near, out_far)
            back_far, back_near = swap(onward, 2), swap(beside, 1)
            grad_out = join(out_total[0], sibling(out_total[1]), c)
            grad_value = scatter_end(back_sends[0], (back_near, back_far), c)
        else:
            grad_value = scatter_ring(back_sends, c)
            grad_out = scatter_ring(out_sends, c)

        if n_node == 4:
            along_x, along_y, kept = terms
            kept = kept.astype(F32)
            got_x = flip(along_x, 1).astype(F32)
            got_y = flip(along_y, 2).astype(F32)
            last_y = flip((kept[1] + got_x[1]).astype(BF16), 2)
            last_x = flip((kept[3] + got_y[1]).astype(BF16), 1)
            layer_out = jnp.concatenate(
                [
                    kept[0] + got_x[0] + last_y.astype(F32),
                    kept[2] + got_y[0] + last_x.astype(F32),
                ],
                axis=0,
            )
        else:
            layer_out = terms[0].astype(F32)
            for j in range(1, n_node):
                layer_out = layer_out + flip(terms[j], j).astype(F32)
        layer_out = layer_out.astype(BF16).reshape(micro, images, seq, part)
        return layer_out, grad_value, grad_out

    return body


def solution(mesh):
    return jax.shard_map(
        make_body(mesh.shape["wide"], mesh.shape["node"]),
        mesh=mesh,
        in_specs=(
            P(None, "wide", None, None),
            P(None, "wide", "node", None, None),
            P(None, "wide", None, None),
            P("wide", "node"),
            P("wide", "node"),
        ),
        out_specs=(P(None, "wide", None, "node"), P("wide", "node"), P("wide", "node")),
        check_vma=False,
    )
```

```python
import functools
import math

import jax
import jax.numpy as jnp
from jax import lax
from jax.experimental import pallas as pl
from jax.experimental.pallas import tpu as pltpu
from jax.sharding import PartitionSpec as P

HEAD_DIM = 64
F32 = jnp.float32
BF16 = jnp.bfloat16


def dot(a, b, ca=1, cb=0):
    return lax.dot_general(a, b, (((ca,), (cb,)), ((), ())), preferred_element_type=F32)


def begin_slots(slots, slots_v, sems):
    return begin([(slot, slots_v.at[j]) for j, slot in enumerate(slots)], sems)


def begin(pairs, sems):
    copies = [pltpu.make_async_copy(s, d, sems.at[i]) for i, (s, d) in enumerate(pairs)]
    for copy in copies:
        copy.start()
    return copies


def rows_at(index, size):
    return pl.ds(pl.multiple_of(index * size, math.gcd(size, 16)), size)


def place(idx, core, slots_v, w_ref):
    for j in range(slots_v.shape[0]):
        w_ref[rows_at(idx[1 + j], 2 * slots_v.shape[2]), :] = whole(core, slots_v[j])


def hand_out(idx, base, grad_v, outs):
    core = idx[0]
    for i, out in enumerate(outs):
        depth = out.shape[1]
        block = grad_v[rows_at(idx[base + i], 2 * depth), :]
        low, high = block[:depth], block[depth:]
        out[0] = jnp.where(core == 0, low, high)
        out[1] = jnp.where(core == 0, high, low)


def gradient_rows(left, right_ref, rows_ref, step):
    width = right_ref.shape[1]
    for start in range(0, width, step):
        part = dot(left, right_ref[:, start : start + step])
        rows_ref[start : start + step, :] = part.T.astype(BF16)


def head_pairs(heads):
    return [(h, min(2, heads - h)) for h in range(0, heads, 2)]


def whole(core, slot):
    mine, other = slot[0], slot[1]
    low = jnp.where(core == 0, mine, other)
    high = jnp.where(core == 0, other, mine)
    return jnp.concatenate([low, high], axis=0)


def part_kernel(n_slots, idx, x_o, x_s, mix_o, mix_s, *rest):
    slots, rest = rest[:n_slots], rest[n_slots:]
    part, last, weights, w_v, x_v, slots_v, x_sems, sems, slot_sems = rest
    heads, depth = weights.shape[2], last.shape[2]
    here = pl.ds(idx[0] * heads, heads)
    missing = idx[1 + n_slots]
    columns = pl.ds(pl.multiple_of(missing * depth, 128), depth)
    copies = begin_slots(slots, slots_v, slot_sems)
    halves = begin([(x_o, x_v.at[0]), (x_s, x_v.at[1])], x_sems)
    later = begin(
        [(x_o.at[:, columns], last.at[0]), (x_s.at[:, columns], last.at[1])]
        + [(mix_o.at[:, here], weights.at[0]), (mix_s.at[:, here], weights.at[1])],
        sems,
    )
    for copy in copies:
        copy.wait()
    place(idx, idx[0], slots_v, w_v)
    w_v[rows_at(missing, depth), :] = jnp.zeros((depth, w_v.shape[1]), BF16)
    for half in range(2):
        halves[half].wait()
        part[half] = dot(x_v[half], w_v[...])
    for copy in later:
        copy.wait()


def mix_values(value, weights, out):
    groups, heads, seq, _ = weights.shape
    for g in range(groups):
        for h, n in head_pairs(heads):
            part = value[g * seq : (g + 1) * seq, h * HEAD_DIM : (h + n) * HEAD_DIM]
            both = weights[g, h]
            if n == 2:
                lane = lax.broadcasted_iota(jnp.int32, part.shape, 1)
                zero = jnp.zeros_like(part)
                part = jnp.concatenate(
                    [
                        jnp.where(lane < HEAD_DIM, part, zero),
                        jnp.where(lane < HEAD_DIM, zero, part),
                    ],
                    axis=0,
                )
                both = jnp.concatenate([both, weights[g, h + 1]], axis=1)
            out[g * seq : (g + 1) * seq, h * HEAD_DIM : (h + n) * HEAD_DIM] = dot(
                both, part
            ).astype(BF16)


def mix_back(d_mixed, weights, left_v, start):
    groups, heads, seq, _ = weights.shape
    for g in range(groups):
        turned = d_mixed[g * seq : (g + 1) * seq, :].T.astype(BF16)
        at = start + g * seq
        for h, n in head_pairs(heads):
            part = turned[h * HEAD_DIM : (h + n) * HEAD_DIM, :]
            if n == 2:
                row = lax.broadcasted_iota(jnp.int32, part.shape, 0)
                zero = jnp.zeros_like(part)
                part = jnp.concatenate(
                    [
                        jnp.where(row < HEAD_DIM, part, zero),
                        jnp.where(row < HEAD_DIM, zero, part),
                    ],
                    axis=1,
                )
            both = weights[g, h : h + n].reshape(n * seq, seq)
            left_v[h * HEAD_DIM : (h + n) * HEAD_DIM, at : at + seq] = dot(part, both).astype(BF16)


def mixed_rest_kernel(idx, part, last, weights, slot, mixed_o, mixed_s):
    w_last = whole(idx[0], slot)
    for half, out in enumerate((mixed_o, mixed_s)):
        value = (part[half] + dot(last[half], w_last)).astype(BF16)
        mix_values(value, weights.at[half], out)


def assemble_kernel(n_slots, idx, unread, unread_too, *rest):
    del unread, unread_too
    slots, (w_out, slots_v, sems) = rest[:n_slots], rest[n_slots:]
    for copy in begin_slots(slots, slots_v, sems):
        copy.wait()
    place(idx, idx[0], slots_v, w_out)


def d_value_kernel(n_slots, idx, token, cot_o, cot_s, mix_o, mix_s, *rest):
    del token
    slots, rest = rest[:n_slots], rest[n_slots:]
    left_v, w_out, cot_v, mix_v, sems, slots_v, slot_sems = rest
    tokens, heads = cot_o.shape[0], mix_v.shape[2]
    here = pl.ds(idx[0] * heads, heads)
    slot_copies = begin_slots(slots, slots_v, slot_sems)
    copies = begin(
        [(cot_o, cot_v.at[0]), (mix_o.at[:, here], mix_v.at[0])]
        + [(cot_s, cot_v.at[1]), (mix_s.at[:, here], mix_v.at[1])],
        sems,
    )
    for copy in slot_copies:
        copy.wait()
    place(idx, idx[0], slots_v, w_out)
    for half in range(2):
        copies[2 * half].wait()
        d_mixed = dot(cot_v[half], w_out[...])
        copies[2 * half + 1].wait()
        mix_back(d_mixed, mix_v.at[half], left_v, half * tokens)


def gradient_kernel(idx, unread, right_o, right_s, left_ref, *rest):
    del unread
    outs, (right_v, grad_v, sems) = rest[:-3], rest[-3:]
    tokens, _ = right_o.shape
    copies = begin(
        [(right_o, right_v.at[pl.ds(0, tokens)]), (right_s, right_v.at[pl.ds(tokens, tokens)])],
        sems,
    )
    copies[0].wait()
    copies[1].wait()
    gradient_rows(left_ref[...], right_v, grad_v, 640)
    hand_out(idx, 1, grad_v, outs)


def mixed_kernel(n_slots, idx, act_o, act_s, mix_o, mix_s, *rest):
    slots, rest = rest[:n_slots], rest[n_slots:]
    mixed_o, mixed_s, w_v, act_v, mix_v, sems, slots_v, slot_sems = rest
    heads = mix_v.shape[2]
    here = pl.ds(idx[0] * heads, heads)
    slot_copies = begin_slots(slots, slots_v, slot_sems)
    copies = begin(
        [(act_o, act_v.at[0]), (mix_o.at[:, here], mix_v.at[0])]
        + [(act_s, act_v.at[1]), (mix_s.at[:, here], mix_v.at[1])],
        sems,
    )
    for copy in slot_copies:
        copy.wait()
    place(idx, idx[0], slots_v, w_v)
    for half, out in enumerate((mixed_o, mixed_s)):
        copies[2 * half].wait()
        value = dot(act_v[half], w_v[...]).astype(BF16)
        copies[2 * half + 1].wait()
        mix_values(value, mix_v.at[half], out)


def grad_out_kernel(n_unread, idx, cot_o, cot_s, mixed_o, mixed_s, *rest):
    token, *outs, cot_v, left_v, grad_v, sems = rest[n_unread:]
    token[...] = jnp.zeros_like(token)
    tokens, _ = cot_o.shape
    copies = begin(
        [(cot_o, cot_v.at[pl.ds(0, tokens)]), (cot_s, cot_v.at[pl.ds(tokens, tokens)])], sems
    )
    left_v[:, :tokens] = mixed_o[...].astype(F32).T.astype(BF16)
    left_v[:, tokens:] = mixed_s[...].astype(F32).T.astype(BF16)
    copies[0].wait()
    copies[1].wait()
    gradient_rows(left_v[...], cot_v, grad_v, 640)
    hand_out(idx, 1, grad_v, outs)


def relay_kernel(unread, first, second, first_out, second_out):
    del unread
    first_out[...] = first[...]
    second_out[...] = second[...]


def sum_kernel(token, block, got, beside, own, near, far, onward, beside_out, total):
    del token
    onward[...] = (block[...].astype(F32) + got[...].astype(F32)).astype(BF16)
    beside_out[...] = beside[...]
    total[...] = own[...].astype(F32) + near[...].astype(F32) + far[...].astype(F32)


def terms_kernel(n_node, idx, mixed_o, mixed_r, w_o, w_r, token, *outs):
    token[...] = jnp.zeros_like(token)
    depth = w_o.shape[0] // n_node
    half = mixed_o.shape[0] // 2
    for j in range(n_node):
        rows = rows_at(idx[j], depth)
        term = dot(mixed_o[...], w_o[rows, :], 1, 1) + dot(mixed_r[...], w_r[rows, :], 1, 1)
        term = term.astype(BF16)
        if n_node != 4:
            outs[j][...] = term
            continue
        along_x, along_y, kept = outs
        first, second = term[:half], term[half:]
        if j == 0:
            kept[0], kept[2] = first, second
        elif j == 1:
            along_x[0], kept[3] = first, second
        elif j == 2:
            kept[1], along_y[0] = first, second
        else:
            along_x[1], along_y[1] = first, second


ANY = pl.BlockSpec(memory_space=pl.ANY)
SMEM = pl.BlockSpec(memory_space=pltpu.SMEM)
VMEM = pl.BlockSpec(memory_space=pltpu.VMEM)


def call(kernel, name, in_specs, out_shapes, scratch, flops, size=1 << 20, kinds=None, vmem=24):
    return pl.pallas_call(
        kernel,
        name=name,
        in_specs=in_specs,
        out_specs=[VMEM] * len(out_shapes),
        out_shape=[
            jax.ShapeDtypeStruct(s, k) for s, k in zip(out_shapes, kinds or [BF16] * len(out_shapes))
        ],
        scratch_shapes=scratch,
        compiler_params=pltpu.CompilerParams(vmem_limit_bytes=vmem << 20),
        cost_estimate=pl.CostEstimate(flops=flops, bytes_accessed=size, transcendentals=0),
    )


def make_body(n_wide, n_node):
    planes = n_wide // 2
    line4 = planes == 4 and n_node == 4

    def move(x, pairs):
        return lax.ppermute(
            x, "wide", [(2 * s + c, 2 * d + c) for s, d in pairs for c in range(2)]
        )

    def swap(x, j):
        return move(x, [(s, s ^ j) for s in range(planes)])

    def sibling(x):
        return lax.ppermute(x, "wide", [(i, i ^ 1) for i in range(n_wide)])

    def flip(x, j):
        return lax.ppermute(x, "node", [(i, i ^ j) for i in range(n_node)])

    def swap_cores(w_out, w_value, act, mix, cot, c):
        cols = w_out.shape[1] // 2
        low = jnp.stack([w_out[:, :cols], w_value[:, :cols]])
        high = jnp.stack([w_out[:, cols:], w_value[:, cols:]])
        got = sibling(jnp.where(c == 0, high, low))
        got, act, mix, cot = lax.optimization_barrier((got, act, mix, cot))
        mine = jnp.where(c == 0, low, high)
        u_out, u_value = (jnp.stack([mine[i], got[i]]) for i in range(2))
        return u_out, u_value, sibling(act), sibling(mix), sibling(cot)

    def gather_ring(u):
        return [u] + [
            move(u, [(s, (s - j) % planes) for s in range(planes)]) for j in range(1, planes)
        ]

    def planes_of(z):
        if line4:
            return [lax.bitwise_xor(z, jnp.int32(j)) for j in range(4)]
        return [lax.rem(z + j, planes) for j in range(planes)]

    def added(block, got):
        return (block.astype(F32) + got.astype(F32)).astype(BF16)

    def scatter_end(own, got, c):
        total = own.astype(F32)
        for part in got:
            total = total + part.astype(F32)
        return join(total[0], sibling(total[1]), c)

    def join(mine, other, c):
        low = jnp.where(c == 0, mine, other)
        high = jnp.where(c == 0, other, mine)
        return jnp.concatenate([low, high], axis=1)

    def scatter_ring(blocks, c):
        total = blocks[0].astype(F32)
        for j in range(1, planes):
            got = move(blocks[j], [(s, (s + j) % planes) for s in range(planes)])
            total = total + got.astype(F32)
        return join(total[0], sibling(total[1]), c)

    def body(act_in, mixing, cotangent, w_value, w_out):
        wide = lax.axis_index("wide")
        n = lax.axis_index("node")
        z, c = wide // 2, lax.rem(wide, 2)
        micro, images, seq, width = act_in.shape
        groups = micro * images
        tokens = groups * seq
        cols = w_value.shape[1] // 2
        heads = cols // HEAD_DIM
        depth = width // planes
        act = act_in.reshape(tokens, width)
        cot = cotangent.reshape(tokens, width)
        mix = mixing.reshape(groups, 2 * heads, seq, seq)
        flops = 4 * tokens * width * cols

        u_out, u_value, act_s, mix_s, cot_s = swap_cores(w_out, w_value, act, mix, cot, c)
        block = u_out.shape
        if line4:
            far, near = swap(u_value, 2), swap(u_value, 1)
            far, u_out = call(relay_kernel, "relay", [ANY, VMEM, VMEM], [block] * 2, [], 0, vmem=8)(
                near, far, u_out
            )
            value_slots = [u_value, near, far, swap(far, 1)]
            far = swap(u_out, 2)
            out_slots = [u_out, swap(u_out, 1), far, swap(far, 1)]
        else:
            value_slots, out_slots = gather_ring(u_value), gather_ring(u_out)
        n_slots = len(out_slots)
        pack = lambda *values: jnp.stack([jnp.int32(x) for x in values])
        idx = pack(c, *planes_of(z))
        idx_node = pack(*[lax.bitwise_xor(n, jnp.int32(j)) for j in range(n_node)])

        mix_scratch = pltpu.VMEM((2, groups, heads, seq, seq), BF16)
        both = pltpu.VMEM((2 * tokens, width), BF16)
        halves = pltpu.VMEM((2, tokens, width), BF16)
        left_tokens = pltpu.VMEM((cols, 2 * tokens), BF16)
        rows = pltpu.VMEM((width, cols), BF16)
        send_shapes = [block] * n_slots

        slots_scratch = [
            pltpu.VMEM((n_slots, *block), BF16),
            pltpu.SemaphoreType.DMA((n_slots,)),
        ]
        part_shapes = [(2, tokens, cols), (2, tokens, depth)]
        if line4:
            ahead = call(
                functools.partial(part_kernel, n_slots - 1),
                "value_ahead",
                [SMEM] + [ANY] * (3 + n_slots),
                [*part_shapes, (2, groups, heads, seq, seq)],
                [
                    *(rows, halves, pltpu.VMEM((n_slots - 1, *block), BF16)),
                    *(pltpu.SemaphoreType.DMA((k,)) for k in (2, 4, n_slots - 1)),
                ],
                flops,
                2 * (3 * act.size + mix.size + width * cols + 4 * tokens * cols),
                kinds=[F32, BF16, BF16],
            )(idx, act, act_s, mix, mix_s, *value_slots[:-1])
            mixed_o, mixed_s = call(
                mixed_rest_kernel,
                "mixed",
                [SMEM] + [VMEM] * 4,
                [(tokens, cols)] * 2,
                [],
                flops // 4,
                2 * (2 * tokens * depth + mix.size + 6 * tokens * cols),
                vmem=16,
            )(idx, *ahead, value_slots[-1])
        else:
            mixed_o, mixed_s = call(
                functools.partial(mixed_kernel, n_slots),
                "mixed",
                [SMEM] + [ANY] * (4 + n_slots),
                [(tokens, cols)] * 2,
                [rows, halves, mix_scratch, pltpu.SemaphoreType.DMA((4,)), *slots_scratch],
                flops,
                2 * (2 * act.size + mix.size + width * cols + 2 * tokens * cols),
                )(idx, act, act_s, mix, mix_s, *value_slots)
        mixed_r = sibling(mixed_s)
        unread = [mixed_r, *(out_slots[1:3] if line4 else [])]
        token, *out_sends = call(
            functools.partial(grad_out_kernel, len(unread)),
            "grad_out",
            [SMEM] + [ANY] * 2 + [VMEM] * 2 + [ANY] * len(unread),
            [(16, 128)] + send_shapes,
            [both, left_tokens, rows, pltpu.SemaphoreType.DMA((2,))],
            flops,
            2 * (2 * cot.size + 2 * tokens * cols + width * cols),
        )(idx, cot, cot_s, mixed_o, mixed_s, *unread)
        out_passed = swap(out_sends[3], 1) if line4 else token
        left = call(
            functools.partial(d_value_kernel, n_slots),
            "d_value",
            [SMEM] + [ANY] * (5 + n_slots),
            [(cols, 2 * tokens)],
            [rows, halves, mix_scratch, pltpu.SemaphoreType.DMA((4,)), *slots_scratch],
            flops,
            2 * (2 * cot.size + mix.size + width * cols + 2 * tokens * cols),
        )(idx, token, cot, cot_s, mix, mix_s, *out_slots)[0]
        if line4:
            out_onward = added(out_sends[2], out_passed)
            out_far = swap(out_onward, 2)
            out_near = swap(out_sends[1], 1)
        else:
            out_onward = left
        w_full = call(
            functools.partial(assemble_kernel, n_slots),
            "assemble",
            [SMEM] + [ANY] * (2 + n_slots),
            [(width, cols)],
            slots_scratch,
            0,
            4 * width * cols,
        )(idx, out_onward, left, *out_slots)[0]
        w_full_s = sibling(w_full)
        part = width // n_node
        half = tokens // 2
        if n_node == 4:
            term_shapes = [(2, half, part), (2, half, part), (4, half, part)]
        else:
            term_shapes = [(tokens, part)] * n_node
        token, *terms = call(
            functools.partial(terms_kernel, n_node),
            "terms",
            [SMEM] + [VMEM] * 4,
            [(16, 128)] + term_shapes,
            [],
            flops,
            2 * (2 * tokens * cols + 2 * width * cols + tokens * width),
        )(idx_node, mixed_o, mixed_r, w_full, w_full_s)
        back_sends = call(
            gradient_kernel,
            "grad_value",
            [SMEM] + [ANY] * 3 + [VMEM],
            send_shapes,
            [both, rows, pltpu.SemaphoreType.DMA((2,))],
            flops,
            2 * (2 * act.size + 2 * tokens * cols + width * cols),
        )(idx, out_onward, act, act_s, left)
        if line4:
            back_passed = swap(back_sends[3], 1)
            onward, beside, out_total = call(
                sum_kernel, "sum", [ANY] + [VMEM] * 6, [block] * 3, [], 0, kinds=[BF16, BF16, F32], vmem=8
            )(token, back_sends[2], back_passed, back_sends[1], out_sends[0], out_near, out_far)
            back_far, back_near = swap(onward, 2), swap(beside, 1)
            grad_out = join(out_total[0], sibling(out_total[1]), c)
            grad_value = scatter_end(back_sends[0], (back_near, back_far), c)
        else:
            grad_value = scatter_ring(back_sends, c)
            grad_out = scatter_ring(out_sends, c)

        if n_node == 4:
            along_x, along_y, kept = terms
            kept = kept.astype(F32)
            got_x = flip(along_x, 1).astype(F32)
            got_y = flip(along_y, 2).astype(F32)
            last_y = flip((kept[1] + got_x[1]).astype(BF16), 2)
            last_x = flip((kept[3] + got_y[1]).astype(BF16), 1)
            layer_out = jnp.concatenate(
                [
                    kept[0] + got_x[0] + last_y.astype(F32),
                    kept[2] + got_y[0] + last_x.astype(F32),
                ],
                axis=0,
            )
        else:
            layer_out = terms[0].astype(F32)
            for j in range(1, n_node):
                layer_out = layer_out + flip(terms[j], j).astype(F32)
        layer_out = layer_out.astype(BF16).reshape(micro, images, seq, part)
        return layer_out, grad_value, grad_out

    return body


def solution(mesh):
    return jax.shard_map(
        make_body(mesh.shape["wide"], mesh.shape["node"]),
        mesh=mesh,
        in_specs=(
            P(None, "wide", None, None),
            P(None, "wide", "node", None, None),
            P(None, "wide", None, None),
            P("wide", "node"),
            P("wide", "node"),
        ),
        out_specs=(P(None, "wide", None, "node"), P("wide", "node"), P("wide", "node")),
        check_vma=False,
    )
```

```python
import functools
import math

import jax
import jax.numpy as jnp
from jax import lax
from jax.experimental import pallas as pl
from jax.experimental.pallas import tpu as pltpu
from jax.sharding import PartitionSpec as P

HEAD_DIM = 64
F32 = jnp.float32
BF16 = jnp.bfloat16


def dot(a, b, ca=1, cb=0):
    return lax.dot_general(a, b, (((ca,), (cb,)), ((), ())), preferred_element_type=F32)


def begin_slots(slots, slots_v, sems):
    return begin([(slot, slots_v.at[j]) for j, slot in enumerate(slots)], sems)


def begin(pairs, sems):
    copies = [pltpu.make_async_copy(s, d, sems.at[i]) for i, (s, d) in enumerate(pairs)]
    for copy in copies:
        copy.start()
    return copies


def rows_at(index, size):
    return pl.ds(pl.multiple_of(index * size, math.gcd(size, 16)), size)


def place(idx, core, slots_v, w_ref):
    for j in range(slots_v.shape[0]):
        w_ref[rows_at(idx[1 + j], 2 * slots_v.shape[2]), :] = whole(core, slots_v[j])


def hand_out(idx, base, grad_v, outs):
    core = idx[0]
    for i, out in enumerate(outs):
        depth = out.shape[1]
        block = grad_v[rows_at(idx[base + i], 2 * depth), :]
        low, high = block[:depth], block[depth:]
        out[0] = jnp.where(core == 0, low, high)
        out[1] = jnp.where(core == 0, high, low)


def chunk_copies(own, other, right_ref, sems):
    tokens, width = own.shape
    step = width // sems.shape[0]
    copies = []
    for j in range(sems.shape[0]):
        columns = pl.ds(j * step, step)
        pairs = [
            (own.at[:, columns], right_ref.at[pl.ds(0, tokens), columns]),
            (other.at[:, columns], right_ref.at[pl.ds(tokens, tokens), columns]),
        ]
        copies.append(begin(pairs, sems.at[j]))
    return copies


def gradient_rows(left, right_ref, copies, rows_ref):
    step = right_ref.shape[1] // len(copies)
    for j, chunk in enumerate(copies):
        for copy in chunk:
            copy.wait()
        part = dot(left, right_ref[:, j * step : (j + 1) * step])
        rows_ref[j * step : (j + 1) * step, :] = part.T.astype(BF16)


def head_pairs(heads):
    return [(h, min(2, heads - h)) for h in range(0, heads, 2)]


def whole(core, slot):
    mine, other = slot[0], slot[1]
    low = jnp.where(core == 0, mine, other)
    high = jnp.where(core == 0, other, mine)
    return jnp.concatenate([low, high], axis=0)


def part_kernel(n_slots, idx, x_o, x_s, mix_o, mix_s, *rest):
    slots, rest = rest[:n_slots], rest[n_slots:]
    part, last, weights, w_v, x_v, slots_v, x_sems, sems, slot_sems = rest
    heads, depth = weights.shape[2], last.shape[2]
    here = pl.ds(idx[0] * heads, heads)
    missing = idx[1 + n_slots]
    columns = pl.ds(pl.multiple_of(missing * depth, 128), depth)
    copies = begin_slots(slots, slots_v, slot_sems)
    halves = begin([(x_o, x_v.at[0]), (x_s, x_v.at[1])], x_sems)
    later = begin(
        [(x_o.at[:, columns], last.at[0]), (x_s.at[:, columns], last.at[1])]
        + [(mix_o.at[:, here], weights.at[0]), (mix_s.at[:, here], weights.at[1])],
        sems,
    )
    for copy in copies:
        copy.wait()
    place(idx, idx[0], slots_v, w_v)
    w_v[rows_at(missing, depth), :] = jnp.zeros((depth, w_v.shape[1]), BF16)
    for half in range(2):
        halves[half].wait()
        part[half] = dot(x_v[half], w_v[...])
    for copy in later:
        copy.wait()


def mix_values(value, weights, out):
    groups, heads, seq, _ = weights.shape
    for g in range(groups):
        for h, n in head_pairs(heads):
            part = value[g * seq : (g + 1) * seq, h * HEAD_DIM : (h + n) * HEAD_DIM]
            both = weights[g, h]
            if n == 2:
                lane = lax.broadcasted_iota(jnp.int32, part.shape, 1)
                zero = jnp.zeros_like(part)
                part = jnp.concatenate(
                    [
                        jnp.where(lane < HEAD_DIM, part, zero),
                        jnp.where(lane < HEAD_DIM, zero, part),
                    ],
                    axis=0,
                )
                both = jnp.concatenate([both, weights[g, h + 1]], axis=1)
            out[g * seq : (g + 1) * seq, h * HEAD_DIM : (h + n) * HEAD_DIM] = dot(
                both, part
            ).astype(BF16)


def mix_back(d_mixed, weights, left_v, start):
    groups, heads, seq, _ = weights.shape
    for g in range(groups):
        turned = d_mixed[g * seq : (g + 1) * seq, :].T.astype(BF16)
        at = start + g * seq
        for h, n in head_pairs(heads):
            part = turned[h * HEAD_DIM : (h + n) * HEAD_DIM, :]
            if n == 2:
                row = lax.broadcasted_iota(jnp.int32, part.shape, 0)
                zero = jnp.zeros_like(part)
                part = jnp.concatenate(
                    [
                        jnp.where(row < HEAD_DIM, part, zero),
                        jnp.where(row < HEAD_DIM, zero, part),
                    ],
                    axis=1,
                )
            both = weights[g, h : h + n].reshape(n * seq, seq)
            left_v[h * HEAD_DIM : (h + n) * HEAD_DIM, at : at + seq] = dot(part, both).astype(BF16)


def mixed_rest_kernel(idx, part, last, weights, slot, mixed_o, mixed_s):
    w_last = whole(idx[0], slot)
    for half, out in enumerate((mixed_o, mixed_s)):
        value = (part[half] + dot(last[half], w_last)).astype(BF16)
        mix_values(value, weights.at[half], out)


def assemble_kernel(n_slots, idx, unread, unread_too, *rest):
    del unread, unread_too
    slots, (w_out, slots_v, sems) = rest[:n_slots], rest[n_slots:]
    for copy in begin_slots(slots, slots_v, sems):
        copy.wait()
    place(idx, idx[0], slots_v, w_out)


def d_value_kernel(n_slots, idx, token, cot_o, cot_s, mix_o, mix_s, *rest):
    del token
    slots, rest = rest[:n_slots], rest[n_slots:]
    left_v, w_out, cot_v, mix_v, sems, slots_v, slot_sems = rest
    tokens, heads = cot_o.shape[0], mix_v.shape[2]
    here = pl.ds(idx[0] * heads, heads)
    slot_copies = begin_slots(slots, slots_v, slot_sems)
    copies = begin(
        [(cot_o, cot_v.at[0]), (mix_o.at[:, here], mix_v.at[0])]
        + [(cot_s, cot_v.at[1]), (mix_s.at[:, here], mix_v.at[1])],
        sems,
    )
    for copy in slot_copies:
        copy.wait()
    place(idx, idx[0], slots_v, w_out)
    for half in range(2):
        copies[2 * half].wait()
        d_mixed = dot(cot_v[half], w_out[...])
        copies[2 * half + 1].wait()
        mix_back(d_mixed, mix_v.at[half], left_v, half * tokens)


def gradient_kernel(idx, token, unread, right_o, right_s, left_ref, *rest):
    del token, unread
    outs, (right_v, grad_v, sems) = rest[:-3], rest[-3:]
    copies = chunk_copies(right_o, right_s, right_v, sems)
    gradient_rows(left_ref[...], right_v, copies, grad_v)
    hand_out(idx, 1, grad_v, outs)


def mixed_kernel(n_slots, idx, act_o, act_s, mix_o, mix_s, *rest):
    slots, rest = rest[:n_slots], rest[n_slots:]
    mixed_o, mixed_s, w_v, act_v, mix_v, sems, slots_v, slot_sems = rest
    heads = mix_v.shape[2]
    here = pl.ds(idx[0] * heads, heads)
    slot_copies = begin_slots(slots, slots_v, slot_sems)
    copies = begin(
        [(act_o, act_v.at[0]), (mix_o.at[:, here], mix_v.at[0])]
        + [(act_s, act_v.at[1]), (mix_s.at[:, here], mix_v.at[1])],
        sems,
    )
    for copy in slot_copies:
        copy.wait()
    place(idx, idx[0], slots_v, w_v)
    for half, out in enumerate((mixed_o, mixed_s)):
        copies[2 * half].wait()
        value = dot(act_v[half], w_v[...]).astype(BF16)
        copies[2 * half + 1].wait()
        mix_values(value, mix_v.at[half], out)


def grad_out_kernel(n_unread, idx, cot_o, cot_s, mixed_o, mixed_s, *rest):
    token, *outs, cot_v, left_v, grad_v, sems = rest[n_unread:]
    token[...] = jnp.zeros_like(token)
    tokens, _ = cot_o.shape
    copies = chunk_copies(cot_o, cot_s, cot_v, sems)
    left_v[:, :tokens] = mixed_o[...].astype(F32).T.astype(BF16)
    left_v[:, tokens:] = mixed_s[...].astype(F32).T.astype(BF16)
    gradient_rows(left_v[...], cot_v, copies, grad_v)
    hand_out(idx, 1, grad_v, outs)


def relay_kernel(unread, first, second, first_out, second_out):
    del unread
    first_out[...] = first[...]
    second_out[...] = second[...]


def sum_kernel(block, got, beside, own, near, far, onward, beside_out, total):
    onward[...] = (block[...].astype(F32) + got[...].astype(F32)).astype(BF16)
    beside_out[...] = beside[...]
    total[...] = own[...].astype(F32) + near[...].astype(F32) + far[...].astype(F32)


def terms_kernel(n_node, idx, mixed_o, mixed_r, w_o, w_r, token, *outs):
    token[...] = jnp.zeros_like(token)
    depth = w_o.shape[0] // n_node
    half = mixed_o.shape[0] // 2
    for j in range(n_node):
        rows = rows_at(idx[j], depth)
        term = dot(mixed_o[...], w_o[rows, :], 1, 1) + dot(mixed_r[...], w_r[rows, :], 1, 1)
        term = term.astype(BF16)
        if n_node != 4:
            outs[j][...] = term
            continue
        along_x, along_y, kept = outs
        first, second = term[:half], term[half:]
        if j == 0:
            kept[0], kept[2] = first, second
        elif j == 1:
            along_x[0], kept[3] = first, second
        elif j == 2:
            kept[1], along_y[0] = first, second
        else:
            along_x[1], along_y[1] = first, second


ANY = pl.BlockSpec(memory_space=pl.ANY)
SMEM = pl.BlockSpec(memory_space=pltpu.SMEM)
VMEM = pl.BlockSpec(memory_space=pltpu.VMEM)


def call(kernel, name, in_specs, out_shapes, scratch, flops, size=1 << 20, kinds=None, vmem=24):
    return pl.pallas_call(
        kernel,
        name=name,
        in_specs=in_specs,
        out_specs=[VMEM] * len(out_shapes),
        out_shape=[
            jax.ShapeDtypeStruct(s, k) for s, k in zip(out_shapes, kinds or [BF16] * len(out_shapes))
        ],
        scratch_shapes=scratch,
        compiler_params=pltpu.CompilerParams(vmem_limit_bytes=vmem << 20),
        cost_estimate=pl.CostEstimate(flops=flops, bytes_accessed=size, transcendentals=0),
    )


def make_body(n_wide, n_node):
    planes = n_wide // 2
    line4 = planes == 4 and n_node == 4

    def move(x, pairs):
        return lax.ppermute(
            x, "wide", [(2 * s + c, 2 * d + c) for s, d in pairs for c in range(2)]
        )

    def swap(x, j):
        return move(x, [(s, s ^ j) for s in range(planes)])

    def sibling(x):
        return lax.ppermute(x, "wide", [(i, i ^ 1) for i in range(n_wide)])

    def flip(x, j):
        return lax.ppermute(x, "node", [(i, i ^ j) for i in range(n_node)])

    def swap_cores(w_out, w_value, act, mix, cot, c):
        cols = w_out.shape[1] // 2
        low = jnp.stack([w_out[:, :cols], w_value[:, :cols]])
        high = jnp.stack([w_out[:, cols:], w_value[:, cols:]])
        got = sibling(jnp.where(c == 0, high, low))
        got, act, mix, cot = lax.optimization_barrier((got, act, mix, cot))
        mine = jnp.where(c == 0, low, high)
        u_out, u_value = (jnp.stack([mine[i], got[i]]) for i in range(2))
        return u_out, u_value, sibling(act), sibling(mix), sibling(cot)

    def gather_ring(u):
        return [u] + [
            move(u, [(s, (s - j) % planes) for s in range(planes)]) for j in range(1, planes)
        ]

    def planes_of(z):
        if line4:
            return [lax.bitwise_xor(z, jnp.int32(j)) for j in range(4)]
        return [lax.rem(z + j, planes) for j in range(planes)]

    def added(block, got):
        return (block.astype(F32) + got.astype(F32)).astype(BF16)

    def scatter_end(own, got, c):
        total = own.astype(F32)
        for part in got:
            total = total + part.astype(F32)
        return join(total[0], sibling(total[1]), c)

    def join(mine, other, c):
        low = jnp.where(c == 0, mine, other)
        high = jnp.where(c == 0, other, mine)
        return jnp.concatenate([low, high], axis=1)

    def scatter_ring(blocks, c):
        total = blocks[0].astype(F32)
        for j in range(1, planes):
            got = move(blocks[j], [(s, (s + j) % planes) for s in range(planes)])
            total = total + got.astype(F32)
        return join(total[0], sibling(total[1]), c)

    def body(act_in, mixing, cotangent, w_value, w_out):
        wide = lax.axis_index("wide")
        n = lax.axis_index("node")
        z, c = wide // 2, lax.rem(wide, 2)
        micro, images, seq, width = act_in.shape
        groups = micro * images
        tokens = groups * seq
        cols = w_value.shape[1] // 2
        heads = cols // HEAD_DIM
        depth = width // planes
        act = act_in.reshape(tokens, width)
        cot = cotangent.reshape(tokens, width)
        mix = mixing.reshape(groups, 2 * heads, seq, seq)
        flops = 4 * tokens * width * cols

        u_out, u_value, act_s, mix_s, cot_s = swap_cores(w_out, w_value, act, mix, cot, c)
        block = u_out.shape
        if line4:
            far, near = swap(u_value, 2), swap(u_value, 1)
            far, u_out = call(relay_kernel, "relay", [ANY, VMEM, VMEM], [block] * 2, [], 0, vmem=8)(
                near, far, u_out
            )
            value_slots = [u_value, near, far, swap(far, 1)]
            far = swap(u_out, 2)
            out_slots = [u_out, swap(u_out, 1), far, swap(far, 1)]
        else:
            value_slots, out_slots = gather_ring(u_value), gather_ring(u_out)
        n_slots = len(out_slots)
        pack = lambda *values: jnp.stack([jnp.int32(x) for x in values])
        idx = pack(c, *planes_of(z))
        idx_node = pack(*[lax.bitwise_xor(n, jnp.int32(j)) for j in range(n_node)])

        mix_scratch = pltpu.VMEM((2, groups, heads, seq, seq), BF16)
        both = pltpu.VMEM((2 * tokens, width), BF16)
        halves = pltpu.VMEM((2, tokens, width), BF16)
        left_tokens = pltpu.VMEM((cols, 2 * tokens), BF16)
        rows = pltpu.VMEM((width, cols), BF16)
        send_shapes = [block] * n_slots

        slots_scratch = [
            pltpu.VMEM((n_slots, *block), BF16),
            pltpu.SemaphoreType.DMA((n_slots,)),
        ]
        part_shapes = [(2, tokens, cols), (2, tokens, depth)]
        if line4:
            ahead = call(
                functools.partial(part_kernel, n_slots - 1),
                "value_ahead",
                [SMEM] + [ANY] * (3 + n_slots),
                [*part_shapes, (2, groups, heads, seq, seq)],
                [
                    *(rows, halves, pltpu.VMEM((n_slots - 1, *block), BF16)),
                    *(pltpu.SemaphoreType.DMA((k,)) for k in (2, 4, n_slots - 1)),
                ],
                flops,
                2 * (3 * act.size + mix.size + width * cols + 4 * tokens * cols),
                kinds=[F32, BF16, BF16],
            )(idx, act, act_s, mix, mix_s, *value_slots[:-1])
            mixed_o, mixed_s = call(
                mixed_rest_kernel,
                "mixed",
                [SMEM] + [VMEM] * 4,
                [(tokens, cols)] * 2,
                [],
                flops // 4,
                2 * (2 * tokens * depth + mix.size + 6 * tokens * cols),
                vmem=16,
            )(idx, *ahead, value_slots[-1])
        else:
            mixed_o, mixed_s = call(
                functools.partial(mixed_kernel, n_slots),
                "mixed",
                [SMEM] + [ANY] * (4 + n_slots),
                [(tokens, cols)] * 2,
                [rows, halves, mix_scratch, pltpu.SemaphoreType.DMA((4,)), *slots_scratch],
                flops,
                2 * (2 * act.size + mix.size + width * cols + 2 * tokens * cols),
                )(idx, act, act_s, mix, mix_s, *value_slots)
        mixed_r = sibling(mixed_s)
        unread = [mixed_r, *(out_slots[1:3] if line4 else [])]
        token, *out_sends = call(
            functools.partial(grad_out_kernel, len(unread)),
            "grad_out",
            [SMEM] + [ANY] * 2 + [VMEM] * 2 + [ANY] * len(unread),
            [(16, 128)] + send_shapes,
            [both, left_tokens, rows, pltpu.SemaphoreType.DMA((4, 2))],
            flops,
            2 * (2 * cot.size + 2 * tokens * cols + width * cols),
        )(idx, cot, cot_s, mixed_o, mixed_s, *unread)
        out_passed = swap(out_sends[3], 1) if line4 else token
        left = call(
            functools.partial(d_value_kernel, n_slots),
            "d_value",
            [SMEM] + [ANY] * (5 + n_slots),
            [(cols, 2 * tokens)],
            [rows, halves, mix_scratch, pltpu.SemaphoreType.DMA((4,)), *slots_scratch],
            flops,
            2 * (2 * cot.size + mix.size + width * cols + 2 * tokens * cols),
        )(idx, token, cot, cot_s, mix, mix_s, *out_slots)[0]
        if line4:
            out_onward = added(out_sends[2], out_passed)
            out_far = swap(out_onward, 2)
            out_near = swap(out_sends[1], 1)
        else:
            out_onward = left
        w_full = call(
            functools.partial(assemble_kernel, n_slots),
            "assemble",
            [SMEM] + [ANY] * (2 + n_slots),
            [(width, cols)],
            slots_scratch,
            0,
            4 * width * cols,
        )(idx, out_onward, left, *out_slots)[0]
        w_full_s = sibling(w_full)
        part = width // n_node
        half = tokens // 2
        if n_node == 4:
            term_shapes = [(2, half, part), (2, half, part), (4, half, part)]
        else:
            term_shapes = [(tokens, part)] * n_node
        token, *terms = call(
            functools.partial(terms_kernel, n_node),
            "terms",
            [SMEM] + [VMEM] * 4,
            [(16, 128)] + term_shapes,
            [],
            flops,
            2 * (2 * tokens * cols + 2 * width * cols + tokens * width),
        )(idx_node, mixed_o, mixed_r, w_full, w_full_s)
        back_sends = call(
            gradient_kernel,
            "grad_value",
            [SMEM] + [ANY] * 4 + [VMEM],
            send_shapes,
            [both, rows, pltpu.SemaphoreType.DMA((4, 2))],
            flops,
            2 * (2 * act.size + 2 * tokens * cols + width * cols),
        )(idx, token, out_onward, act, act_s, left)
        if line4:
            back_passed = swap(back_sends[3], 1)
            onward, beside, out_total = call(
                sum_kernel, "sum", [VMEM] * 6, [block] * 3, [], 0, kinds=[BF16, BF16, F32], vmem=8
            )(back_sends[2], back_passed, back_sends[1], out_sends[0], out_near, out_far)
            back_far, back_near = swap(onward, 2), swap(beside, 1)
            grad_out = join(out_total[0], sibling(out_total[1]), c)
            grad_value = scatter_end(back_sends[0], (back_near, back_far), c)
        else:
            grad_value = scatter_ring(back_sends, c)
            grad_out = scatter_ring(out_sends, c)

        if n_node == 4:
            along_x, along_y, kept = terms
            kept = kept.astype(F32)
            got_x = flip(along_x, 1).astype(F32)
            got_y = flip(along_y, 2).astype(F32)
            last_y = flip((kept[1] + got_x[1]).astype(BF16), 2)
            last_x = flip((kept[3] + got_y[1]).astype(BF16), 1)
            layer_out = jnp.concatenate(
                [
                    kept[0] + got_x[0] + last_y.astype(F32),
                    kept[2] + got_y[0] + last_x.astype(F32),
                ],
                axis=0,
            )
        else:
            layer_out = terms[0].astype(F32)
            for j in range(1, n_node):
                layer_out = layer_out + flip(terms[j], j).astype(F32)
        layer_out = layer_out.astype(BF16).reshape(micro, images, seq, part)
        return layer_out, grad_value, grad_out

    return body


def solution(mesh):
    return jax.shard_map(
        make_body(mesh.shape["wide"], mesh.shape["node"]),
        mesh=mesh,
        in_specs=(
            P(None, "wide", None, None),
            P(None, "wide", "node", None, None),
            P(None, "wide", None, None),
            P("wide", "node"),
            P("wide", "node"),
        ),
        out_specs=(P(None, "wide", None, "node"), P("wide", "node"), P("wide", "node")),
        check_vma=False,
    )
```

```python
import functools
import math

import jax
import jax.numpy as jnp
from jax import lax
from jax.experimental import pallas as pl
from jax.experimental.pallas import tpu as pltpu
from jax.sharding import PartitionSpec as P

HEAD_DIM = 64
F32 = jnp.float32
BF16 = jnp.bfloat16


def dot(a, b, ca=1, cb=0):
    return lax.dot_general(a, b, (((ca,), (cb,)), ((), ())), preferred_element_type=F32)


def begin_slots(slots, slots_v, sems):
    return begin([(slot, slots_v.at[j]) for j, slot in enumerate(slots)], sems)


def begin(pairs, sems):
    copies = [pltpu.make_async_copy(s, d, sems.at[i]) for i, (s, d) in enumerate(pairs)]
    for copy in copies:
        copy.start()
    return copies


def rows_at(index, size):
    return pl.ds(pl.multiple_of(index * size, math.gcd(size, 16)), size)


def place(idx, core, slots_v, w_ref):
    for j in range(slots_v.shape[0]):
        w_ref[rows_at(idx[1 + j], 2 * slots_v.shape[2]), :] = whole(core, slots_v[j])


def hand_out(idx, base, grad_v, outs):
    core = idx[0]
    for i, out in enumerate(outs):
        depth = out.shape[1]
        block = grad_v[rows_at(idx[base + i], 2 * depth), :]
        low, high = block[:depth], block[depth:]
        out[0] = jnp.where(core == 0, low, high)
        out[1] = jnp.where(core == 0, high, low)


def chunk_copies(own, other, right_ref, sems):
    tokens, width = own.shape
    step = width // sems.shape[0]
    copies = []
    for j in range(sems.shape[0]):
        columns = pl.ds(j * step, step)
        pairs = [
            (own.at[:, columns], right_ref.at[pl.ds(0, tokens), columns]),
            (other.at[:, columns], right_ref.at[pl.ds(tokens, tokens), columns]),
        ]
        copies.append(begin(pairs, sems.at[j]))
    return copies


def gradient_rows(left, right_ref, copies, rows_ref):
    step = right_ref.shape[1] // len(copies)
    for j, chunk in enumerate(copies):
        for copy in chunk:
            copy.wait()
        part = dot(left, right_ref[:, j * step : (j + 1) * step])
        rows_ref[j * step : (j + 1) * step, :] = part.astype(BF16).T


def head_pairs(heads):
    return [(h, min(2, heads - h)) for h in range(0, heads, 2)]


def whole(core, slot):
    mine, other = slot[0], slot[1]
    low = jnp.where(core == 0, mine, other)
    high = jnp.where(core == 0, other, mine)
    return jnp.concatenate([low, high], axis=0)


def part_kernel(n_slots, idx, x_o, x_s, mix_o, mix_s, *rest):
    slots, rest = rest[:n_slots], rest[n_slots:]
    part, last, weights, w_v, x_v, slots_v, x_sems, sems, slot_sems = rest
    heads, depth = weights.shape[2], last.shape[2]
    here = pl.ds(idx[0] * heads, heads)
    missing = idx[1 + n_slots]
    columns = pl.ds(pl.multiple_of(missing * depth, 128), depth)
    copies = begin_slots(slots, slots_v, slot_sems)
    halves = begin([(x_o, x_v.at[0]), (x_s, x_v.at[1])], x_sems)
    later = begin(
        [(x_o.at[:, columns], last.at[0]), (x_s.at[:, columns], last.at[1])]
        + [(mix_o.at[:, here], weights.at[0]), (mix_s.at[:, here], weights.at[1])],
        sems,
    )
    for copy in copies:
        copy.wait()
    place(idx, idx[0], slots_v, w_v)
    w_v[rows_at(missing, depth), :] = jnp.zeros((depth, w_v.shape[1]), BF16)
    for half in range(2):
        halves[half].wait()
        part[half] = dot(x_v[half], w_v[...])
    for copy in later:
        copy.wait()


def mix_values(value, weights, out):
    groups, heads, seq, _ = weights.shape
    for g in range(groups):
        for h, n in head_pairs(heads):
            part = value[g * seq : (g + 1) * seq, h * HEAD_DIM : (h + n) * HEAD_DIM]
            both = weights[g, h]
            if n == 2:
                lane = lax.broadcasted_iota(jnp.int32, part.shape, 1)
                zero = jnp.zeros_like(part)
                part = jnp.concatenate(
                    [
                        jnp.where(lane < HEAD_DIM, part, zero),
                        jnp.where(lane < HEAD_DIM, zero, part),
                    ],
                    axis=0,
                )
                both = jnp.concatenate([both, weights[g, h + 1]], axis=1)
            out[g * seq : (g + 1) * seq, h * HEAD_DIM : (h + n) * HEAD_DIM] = dot(
                both, part
            ).astype(BF16)


def mix_back(d_mixed, weights, left_v, start):
    groups, heads, seq, _ = weights.shape
    for g in range(groups):
        turned = d_mixed[g * seq : (g + 1) * seq, :].astype(BF16).T
        at = start + g * seq
        for h, n in head_pairs(heads):
            part = turned[h * HEAD_DIM : (h + n) * HEAD_DIM, :]
            if n == 2:
                row = lax.broadcasted_iota(jnp.int32, part.shape, 0)
                zero = jnp.zeros_like(part)
                part = jnp.concatenate(
                    [
                        jnp.where(row < HEAD_DIM, part, zero),
                        jnp.where(row < HEAD_DIM, zero, part),
                    ],
                    axis=1,
                )
            both = weights[g, h : h + n].reshape(n * seq, seq)
            left_v[h * HEAD_DIM : (h + n) * HEAD_DIM, at : at + seq] = dot(part, both).astype(BF16)


def mixed_rest_kernel(idx, part, last, weights, slot, mixed_o, mixed_s):
    w_last = whole(idx[0], slot)
    for half, out in enumerate((mixed_o, mixed_s)):
        value = (part[half] + dot(last[half], w_last)).astype(BF16)
        mix_values(value, weights.at[half], out)


def d_value_kernel(n_slots, idx, token, cot_o, cot_s, mix_o, mix_s, *rest):
    del token
    slots, rest = rest[:n_slots], rest[n_slots:]
    left_v, w_out, w_v, cot_v, mix_v, sems, slots_v, slot_sems, out_sems = rest
    tokens, heads = cot_o.shape[0], mix_v.shape[2]
    here = pl.ds(idx[0] * heads, heads)
    slot_copies = begin_slots(slots, slots_v, slot_sems)
    copies = begin(
        [(cot_o, cot_v.at[0]), (mix_o.at[:, here], mix_v.at[0])]
        + [(cot_s, cot_v.at[1]), (mix_s.at[:, here], mix_v.at[1])],
        sems,
    )
    for copy in slot_copies:
        copy.wait()
    place(idx, idx[0], slots_v, w_v)
    handed = begin([(w_v, w_out)], out_sems)
    for half in range(2):
        copies[2 * half].wait()
        d_mixed = dot(cot_v[half], w_v[...])
        copies[2 * half + 1].wait()
        mix_back(d_mixed, mix_v.at[half], left_v, half * tokens)
    handed[0].wait()


def gradient_kernel(idx, token, unread, right_o, right_s, left_ref, *rest):
    del token, unread
    outs, (right_v, grad_v, sems) = rest[:-3], rest[-3:]
    copies = chunk_copies(right_o, right_s, right_v, sems)
    gradient_rows(left_ref[...], right_v, copies, grad_v)
    hand_out(idx, 1, grad_v, outs)


def mixed_kernel(n_slots, idx, act_o, act_s, mix_o, mix_s, *rest):
    slots, rest = rest[:n_slots], rest[n_slots:]
    mixed_o, mixed_s, w_v, act_v, mix_v, sems, slots_v, slot_sems = rest
    heads = mix_v.shape[2]
    here = pl.ds(idx[0] * heads, heads)
    slot_copies = begin_slots(slots, slots_v, slot_sems)
    copies = begin(
        [(act_o, act_v.at[0]), (mix_o.at[:, here], mix_v.at[0])]
        + [(act_s, act_v.at[1]), (mix_s.at[:, here], mix_v.at[1])],
        sems,
    )
    for copy in slot_copies:
        copy.wait()
    place(idx, idx[0], slots_v, w_v)
    for half, out in enumerate((mixed_o, mixed_s)):
        copies[2 * half].wait()
        value = dot(act_v[half], w_v[...]).astype(BF16)
        copies[2 * half + 1].wait()
        mix_values(value, mix_v.at[half], out)


def grad_out_kernel(n_unread, idx, cot_o, cot_s, mixed_o, mixed_s, *rest):
    token, *outs, cot_v, left_v, grad_v, sems = rest[n_unread:]
    token[...] = jnp.zeros_like(token)
    tokens, _ = cot_o.shape
    copies = chunk_copies(cot_o, cot_s, cot_v, sems)
    left_v[:, :tokens] = mixed_o[...].T
    left_v[:, tokens:] = mixed_s[...].T
    gradient_rows(left_v[...], cot_v, copies, grad_v)
    hand_out(idx, 1, grad_v, outs)


def relay_kernel(unread, first, second, first_out, second_out):
    del unread
    first_out[...] = first[...]
    second_out[...] = second[...]


def sum_kernel(block, got, beside, own, near, far, onward, beside_out, total):
    onward[...] = (block[...].astype(F32) + got[...].astype(F32)).astype(BF16)
    beside_out[...] = beside[...]
    total[...] = own[...].astype(F32) + near[...].astype(F32) + far[...].astype(F32)


def terms_kernel(n_node, idx, mixed_o, mixed_r, w_o, w_r, token, *outs):
    token[...] = jnp.zeros_like(token)
    depth = w_o.shape[0] // n_node
    half = mixed_o.shape[0] // 2
    for j in range(n_node):
        rows = rows_at(idx[j], depth)
        term = dot(mixed_o[...], w_o[rows, :], 1, 1) + dot(mixed_r[...], w_r[rows, :], 1, 1)
        term = term.astype(BF16)
        if n_node != 4:
            outs[j][...] = term
            continue
        along_x, along_y, kept = outs
        first, second = term[:half], term[half:]
        if j == 0:
            kept[0], kept[2] = first, second
        elif j == 1:
            along_x[0], kept[3] = first, second
        elif j == 2:
            kept[1], along_y[0] = first, second
        else:
            along_x[1], along_y[1] = first, second


ANY = pl.BlockSpec(memory_space=pl.ANY)
SMEM = pl.BlockSpec(memory_space=pltpu.SMEM)
VMEM = pl.BlockSpec(memory_space=pltpu.VMEM)


def call(kernel, name, in_specs, out_shapes, scratch, flops, size=1 << 20, kinds=None, vmem=24, out_specs=None):
    return pl.pallas_call(
        kernel,
        name=name,
        in_specs=in_specs,
        out_specs=out_specs or [VMEM] * len(out_shapes),
        out_shape=[
            jax.ShapeDtypeStruct(s, k) for s, k in zip(out_shapes, kinds or [BF16] * len(out_shapes))
        ],
        scratch_shapes=scratch,
        compiler_params=pltpu.CompilerParams(vmem_limit_bytes=vmem << 20),
        cost_estimate=pl.CostEstimate(flops=flops, bytes_accessed=size, transcendentals=0),
    )


def in_order(x, earlier):
    def kernel(*refs):
        del refs

    return pl.pallas_call(
        kernel,
        name="in_order",
        in_specs=[ANY, ANY],
        out_specs=ANY,
        out_shape=jax.ShapeDtypeStruct(x.shape, x.dtype),
        input_output_aliases={0: 0},
    )(x, earlier)


def make_body(n_wide, n_node):
    planes = n_wide // 2
    line4 = planes == 4 and n_node == 4

    def move(x, pairs):
        return lax.ppermute(
            x, "wide", [(2 * s + c, 2 * d + c) for s, d in pairs for c in range(2)]
        )

    def swap(x, j):
        return move(x, [(s, s ^ j) for s in range(planes)])

    def sibling(x):
        return lax.ppermute(x, "wide", [(i, i ^ 1) for i in range(n_wide)])

    def flip(x, j):
        return lax.ppermute(x, "node", [(i, i ^ j) for i in range(n_node)])

    def swap_cores(w_out, w_value, act, mix, cot, c):
        cols = w_out.shape[1] // 2
        low = jnp.stack([w_out[:, :cols], w_value[:, :cols]])
        high = jnp.stack([w_out[:, cols:], w_value[:, cols:]])
        got = sibling(jnp.where(c == 0, high, low))
        got, act, mix, cot = lax.optimization_barrier((got, act, mix, cot))
        mine = jnp.where(c == 0, low, high)
        u_out, u_value = (jnp.stack([mine[i], got[i]]) for i in range(2))
        return u_out, u_value, sibling(act), sibling(mix), sibling(cot)

    def gather_ring(u):
        return [u] + [
            move(u, [(s, (s - j) % planes) for s in range(planes)]) for j in range(1, planes)
        ]

    def planes_of(z):
        if line4:
            return [lax.bitwise_xor(z, jnp.int32(j)) for j in range(4)]
        return [lax.rem(z + j, planes) for j in range(planes)]

    def added(block, got):
        return (block.astype(F32) + got.astype(F32)).astype(BF16)

    def scatter_end(own, got, c):
        total = own.astype(F32)
        for part in got:
            total = total + part.astype(F32)
        return join(total[0], sibling(total[1]), c)

    def join(mine, other, c):
        low = jnp.where(c == 0, mine, other)
        high = jnp.where(c == 0, other, mine)
        return jnp.concatenate([low, high], axis=1)

    def scatter_ring(blocks, c):
        total = blocks[0].astype(F32)
        for j in range(1, planes):
            got = move(blocks[j], [(s, (s + j) % planes) for s in range(planes)])
            total = total + got.astype(F32)
        return join(total[0], sibling(total[1]), c)

    def body(act_in, mixing, cotangent, w_value, w_out):
        wide = lax.axis_index("wide")
        n = lax.axis_index("node")
        z, c = wide // 2, lax.rem(wide, 2)
        micro, images, seq, width = act_in.shape
        groups = micro * images
        tokens = groups * seq
        cols = w_value.shape[1] // 2
        heads = cols // HEAD_DIM
        depth = width // planes
        act = act_in.reshape(tokens, width)
        cot = cotangent.reshape(tokens, width)
        mix = mixing.reshape(groups, 2 * heads, seq, seq)
        flops = 4 * tokens * width * cols

        u_out, u_value, act_s, mix_s, cot_s = swap_cores(w_out, w_value, act, mix, cot, c)
        block = u_out.shape
        if line4:
            far, near = swap(u_value, 2), swap(u_value, 1)
            far, u_out = call(relay_kernel, "relay", [ANY, VMEM, VMEM], [block] * 2, [], 0, vmem=8)(
                near, far, u_out
            )
            value_slots = [u_value, near, far, swap(far, 1)]
            far = swap(u_out, 2)
            out_slots = [u_out, swap(u_out, 1), far, swap(far, 1)]
        else:
            value_slots, out_slots = gather_ring(u_value), gather_ring(u_out)
        n_slots = len(out_slots)
        pack = lambda *values: jnp.stack([jnp.int32(x) for x in values])
        idx = pack(c, *planes_of(z))
        idx_node = pack(*[lax.bitwise_xor(n, jnp.int32(j)) for j in range(n_node)])

        mix_scratch = pltpu.VMEM((2, groups, heads, seq, seq), BF16)
        both = pltpu.VMEM((2 * tokens, width), BF16)
        halves = pltpu.VMEM((2, tokens, width), BF16)
        left_tokens = pltpu.VMEM((cols, 2 * tokens), BF16)
        rows = pltpu.VMEM((width, cols), BF16)
        send_shapes = [block] * n_slots

        slots_scratch = [
            pltpu.VMEM((n_slots, *block), BF16),
            pltpu.SemaphoreType.DMA((n_slots,)),
        ]
        part_shapes = [(2, tokens, cols), (2, tokens, depth)]
        if line4:
            ahead = call(
                functools.partial(part_kernel, n_slots - 1),
                "value_ahead",
                [SMEM] + [ANY] * (3 + n_slots),
                [*part_shapes, (2, groups, heads, seq, seq)],
                [
                    *(rows, halves, pltpu.VMEM((n_slots - 1, *block), BF16)),
                    *(pltpu.SemaphoreType.DMA((k,)) for k in (2, 4, n_slots - 1)),
                ],
                flops,
                2 * (3 * act.size + mix.size + width * cols + 4 * tokens * cols),
                kinds=[F32, BF16, BF16],
            )(idx, act, act_s, mix, mix_s, *value_slots[:-1])
            mixed_o, mixed_s = call(
                mixed_rest_kernel,
                "mixed",
                [SMEM] + [VMEM] * 4,
                [(tokens, cols)] * 2,
                [],
                flops // 4,
                2 * (2 * tokens * depth + mix.size + 6 * tokens * cols),
                vmem=16,
            )(idx, *ahead, value_slots[-1])
        else:
            mixed_o, mixed_s = call(
                functools.partial(mixed_kernel, n_slots),
                "mixed",
                [SMEM] + [ANY] * (4 + n_slots),
                [(tokens, cols)] * 2,
                [rows, halves, mix_scratch, pltpu.SemaphoreType.DMA((4,)), *slots_scratch],
                flops,
                2 * (2 * act.size + mix.size + width * cols + 2 * tokens * cols),
                )(idx, act, act_s, mix, mix_s, *value_slots)
        mixed_r = sibling(mixed_s)
        unread = [mixed_r, *(out_slots[1:3] if line4 else [])]
        token, *out_sends = call(
            functools.partial(grad_out_kernel, len(unread)),
            "grad_out",
            [SMEM] + [ANY] * 2 + [VMEM] * 2 + [ANY] * len(unread),
            [(16, 128)] + send_shapes,
            [both, left_tokens, rows, pltpu.SemaphoreType.DMA((4, 2))],
            flops,
            2 * (2 * cot.size + 2 * tokens * cols + width * cols),
        )(idx, cot, cot_s, mixed_o, mixed_s, *unread)
        out_passed = swap(out_sends[3], 1) if line4 else token
        left, w_full = call(
            functools.partial(d_value_kernel, n_slots),
            "d_value",
            [SMEM] + [ANY] * (5 + n_slots),
            [(cols, 2 * tokens), (width, cols)],
            [rows, halves, mix_scratch, pltpu.SemaphoreType.DMA((4,)), *slots_scratch]
            + [pltpu.SemaphoreType.DMA((1,))],
            flops,
            2 * (2 * cot.size + mix.size + 2 * width * cols + 2 * tokens * cols),
            out_specs=[VMEM, ANY],
        )(idx, token, cot, cot_s, mix, mix_s, *out_slots)
        if line4:
            out_onward = added(out_sends[2], out_passed)
            out_far = swap(out_onward, 2)
            out_near = swap(out_sends[1], 1)
        else:
            out_onward = left
        w_full = in_order(w_full, out_onward)
        w_full_s = sibling(w_full)
        part = width // n_node
        half = tokens // 2
        if n_node == 4:
            term_shapes = [(2, half, part), (2, half, part), (4, half, part)]
        else:
            term_shapes = [(tokens, part)] * n_node
        token, *terms = call(
            functools.partial(terms_kernel, n_node),
            "terms",
            [SMEM] + [VMEM] * 4,
            [(16, 128)] + term_shapes,
            [],
            flops,
            2 * (2 * tokens * cols + 2 * width * cols + tokens * width),
        )(idx_node, mixed_o, mixed_r, w_full, w_full_s)
        back_sends = call(
            gradient_kernel,
            "grad_value",
            [SMEM] + [ANY] * 4 + [VMEM],
            send_shapes,
            [both, rows, pltpu.SemaphoreType.DMA((4, 2))],
            flops,
            2 * (2 * act.size + 2 * tokens * cols + width * cols),
        )(idx, token, out_onward, act, act_s, left)
        if line4:
            back_passed = swap(back_sends[3], 1)
            onward, beside, out_total = call(
                sum_kernel, "sum", [VMEM] * 6, [block] * 3, [], 0, kinds=[BF16, BF16, F32], vmem=8
            )(back_sends[2], back_passed, back_sends[1], out_sends[0], out_near, out_far)
            back_far, back_near = swap(onward, 2), swap(beside, 1)
            grad_out = join(out_total[0], sibling(out_total[1]), c)
            grad_value = scatter_end(back_sends[0], (back_near, back_far), c)
        else:
            grad_value = scatter_ring(back_sends, c)
            grad_out = scatter_ring(out_sends, c)

        if n_node == 4:
            along_x, along_y, kept = terms
            kept = kept.astype(F32)
            got_x = flip(along_x, 1).astype(F32)
            got_y = flip(along_y, 2).astype(F32)
            last_y = flip((kept[1] + got_x[1]).astype(BF16), 2)
            last_x = flip((kept[3] + got_y[1]).astype(BF16), 1)
            layer_out = jnp.concatenate(
                [
                    kept[0] + got_x[0] + last_y.astype(F32),
                    kept[2] + got_y[0] + last_x.astype(F32),
                ],
                axis=0,
            )
        else:
            layer_out = terms[0].astype(F32)
            for j in range(1, n_node):
                layer_out = layer_out + flip(terms[j], j).astype(F32)
        layer_out = layer_out.astype(BF16).reshape(micro, images, seq, part)
        return layer_out, grad_value, grad_out

    return body


def solution(mesh):
    return jax.shard_map(
        make_body(mesh.shape["wide"], mesh.shape["node"]),
        mesh=mesh,
        in_specs=(
            P(None, "wide", None, None),
            P(None, "wide", "node", None, None),
            P(None, "wide", None, None),
            P("wide", "node"),
            P("wide", "node"),
        ),
        out_specs=(P(None, "wide", None, "node"), P("wide", "node"), P("wide", "node")),
        check_vma=False,
    )
```

```python
import functools
import math

import jax
import jax.numpy as jnp
from jax import lax
from jax.experimental import pallas as pl
from jax.experimental.pallas import tpu as pltpu
from jax.sharding import PartitionSpec as P

HEAD_DIM = 64
F32 = jnp.float32
BF16 = jnp.bfloat16


def dot(a, b, ca=1, cb=0):
    return lax.dot_general(a, b, (((ca,), (cb,)), ((), ())), preferred_element_type=F32)


def begin_slots(slots, slots_v, sems):
    return begin([(slot, slots_v.at[j]) for j, slot in enumerate(slots)], sems)


def begin(pairs, sems):
    copies = [pltpu.make_async_copy(s, d, sems.at[i]) for i, (s, d) in enumerate(pairs)]
    for copy in copies:
        copy.start()
    return copies


def rows_at(index, size):
    return pl.ds(pl.multiple_of(index * size, math.gcd(size, 16)), size)


def place(idx, core, slots_v, w_ref):
    for j in range(slots_v.shape[0]):
        w_ref[rows_at(idx[1 + j], 2 * slots_v.shape[2]), :] = whole(core, slots_v[j])


def hand_out(idx, base, grad_v, outs):
    core = idx[0]
    for i, out in enumerate(outs):
        depth = out.shape[1]
        block = grad_v[rows_at(idx[base + i], 2 * depth), :]
        low, high = block[:depth], block[depth:]
        out[0] = jnp.where(core == 0, low, high)
        out[1] = jnp.where(core == 0, high, low)


def chunk_copies(own, other, right_ref, sems):
    tokens, width = own.shape
    step = width // sems.shape[0]
    copies = []
    for j in range(sems.shape[0]):
        columns = pl.ds(j * step, step)
        pairs = [
            (own.at[:, columns], right_ref.at[pl.ds(0, tokens), columns]),
            (other.at[:, columns], right_ref.at[pl.ds(tokens, tokens), columns]),
        ]
        copies.append(begin(pairs, sems.at[j]))
    return copies


def gradient_rows(left, right_ref, copies, rows_ref):
    step = right_ref.shape[1] // len(copies)
    for j, chunk in enumerate(copies):
        for copy in chunk:
            copy.wait()
        part = dot(left, right_ref[:, j * step : (j + 1) * step])
        rows_ref[j * step : (j + 1) * step, :] = part.astype(BF16).T


def head_pairs(heads):
    return [(h, min(2, heads - h)) for h in range(0, heads, 2)]


def whole(core, slot):
    mine, other = slot[0], slot[1]
    low = jnp.where(core == 0, mine, other)
    high = jnp.where(core == 0, other, mine)
    return jnp.concatenate([low, high], axis=0)


def part_kernel(n_slots, idx, x_o, x_s, mix_o, mix_s, *rest):
    slots, rest = rest[:n_slots], rest[n_slots:]
    part, last, weights, w_v, x_v, slots_v, x_sems, sems, slot_sems = rest
    heads, depth = weights.shape[2], last.shape[2]
    here = pl.ds(idx[0] * heads, heads)
    missing = idx[1 + n_slots]
    columns = pl.ds(pl.multiple_of(missing * depth, 128), depth)
    copies = begin_slots(slots, slots_v, slot_sems)
    halves = begin([(x_o, x_v.at[0]), (x_s, x_v.at[1])], x_sems)
    later = begin(
        [(x_o.at[:, columns], last.at[0]), (x_s.at[:, columns], last.at[1])]
        + [(mix_o.at[:, here], weights.at[0]), (mix_s.at[:, here], weights.at[1])],
        sems,
    )
    for copy in copies:
        copy.wait()
    place(idx, idx[0], slots_v, w_v)
    w_v[rows_at(missing, depth), :] = jnp.zeros((depth, w_v.shape[1]), BF16)
    for half in range(2):
        halves[half].wait()
        part[half] = dot(x_v[half], w_v[...])
    for copy in later:
        copy.wait()


def mix_values(value, weights, out):
    groups, heads, seq, _ = weights.shape
    for g in range(groups):
        for h, n in head_pairs(heads):
            part = value[g * seq : (g + 1) * seq, h * HEAD_DIM : (h + n) * HEAD_DIM]
            both = weights[g, h]
            if n == 2:
                lane = lax.broadcasted_iota(jnp.int32, part.shape, 1)
                zero = jnp.zeros_like(part)
                part = jnp.concatenate(
                    [
                        jnp.where(lane < HEAD_DIM, part, zero),
                        jnp.where(lane < HEAD_DIM, zero, part),
                    ],
                    axis=0,
                )
                both = jnp.concatenate([both, weights[g, h + 1]], axis=1)
            out[g * seq : (g + 1) * seq, h * HEAD_DIM : (h + n) * HEAD_DIM] = dot(
                both, part
            ).astype(BF16)


def mix_back(d_mixed, weights, left_v, start):
    groups, heads, seq, _ = weights.shape
    for g in range(groups):
        turned = d_mixed[g * seq : (g + 1) * seq, :].astype(BF16).T
        at = start + g * seq
        for h, n in head_pairs(heads):
            part = turned[h * HEAD_DIM : (h + n) * HEAD_DIM, :]
            if n == 2:
                row = lax.broadcasted_iota(jnp.int32, part.shape, 0)
                zero = jnp.zeros_like(part)
                part = jnp.concatenate(
                    [
                        jnp.where(row < HEAD_DIM, part, zero),
                        jnp.where(row < HEAD_DIM, zero, part),
                    ],
                    axis=1,
                )
            both = weights[g, h : h + n].reshape(n * seq, seq)
            left_v[h * HEAD_DIM : (h + n) * HEAD_DIM, at : at + seq] = dot(part, both).astype(BF16)


def mixed_rest_kernel(idx, part, last, weights, slot, mixed_o, mixed_s):
    w_last = whole(idx[0], slot)
    for half, out in enumerate((mixed_o, mixed_s)):
        value = (part[half] + dot(last[half], w_last)).astype(BF16)
        mix_values(value, weights.at[half], out)


def d_value_kernel(n_slots, idx, token, cot_o, cot_s, mix_o, mix_s, *rest):
    del token
    slots, rest = rest[:n_slots], rest[n_slots:]
    left_v, w_out, w_v, cot_v, mix_v, sems, slots_v, slot_sems, out_sems = rest
    tokens, heads = cot_o.shape[0], mix_v.shape[2]
    here = pl.ds(idx[0] * heads, heads)
    slot_copies = begin_slots(slots, slots_v, slot_sems)
    copies = begin(
        [(cot_o, cot_v.at[0]), (mix_o.at[:, here], mix_v.at[0])]
        + [(cot_s, cot_v.at[1]), (mix_s.at[:, here], mix_v.at[1])],
        sems,
    )
    for copy in slot_copies:
        copy.wait()
    place(idx, idx[0], slots_v, w_v)
    handed = begin([(w_v, w_out)], out_sems)
    for half in range(2):
        copies[2 * half].wait()
        d_mixed = dot(cot_v[half], w_v[...])
        copies[2 * half + 1].wait()
        mix_back(d_mixed, mix_v.at[half], left_v, half * tokens)
    handed[0].wait()


def gradient_kernel(idx, token, unread, right_o, right_s, left_ref, *rest):
    del token, unread
    outs, (right_v, grad_v, sems) = rest[:-3], rest[-3:]
    copies = chunk_copies(right_o, right_s, right_v, sems)
    gradient_rows(left_ref[...], right_v, copies, grad_v)
    hand_out(idx, 1, grad_v, outs)


def mixed_kernel(n_slots, idx, act_o, act_s, mix_o, mix_s, *rest):
    slots, rest = rest[:n_slots], rest[n_slots:]
    mixed_o, mixed_s, w_v, act_v, mix_v, sems, slots_v, slot_sems = rest
    heads = mix_v.shape[2]
    here = pl.ds(idx[0] * heads, heads)
    slot_copies = begin_slots(slots, slots_v, slot_sems)
    copies = begin(
        [(act_o, act_v.at[0]), (mix_o.at[:, here], mix_v.at[0])]
        + [(act_s, act_v.at[1]), (mix_s.at[:, here], mix_v.at[1])],
        sems,
    )
    for copy in slot_copies:
        copy.wait()
    place(idx, idx[0], slots_v, w_v)
    for half, out in enumerate((mixed_o, mixed_s)):
        copies[2 * half].wait()
        value = dot(act_v[half], w_v[...]).astype(BF16)
        copies[2 * half + 1].wait()
        mix_values(value, mix_v.at[half], out)


def grad_out_kernel(n_unread, idx, cot_o, cot_s, mixed_o, mixed_s, *rest):
    token, *outs, cot_v, left_v, grad_v, sems = rest[n_unread:]
    token[...] = jnp.zeros_like(token)
    tokens, _ = cot_o.shape
    copies = chunk_copies(cot_o, cot_s, cot_v, sems)
    left_v[:, :tokens] = mixed_o[...].T
    left_v[:, tokens:] = mixed_s[...].T
    gradient_rows(left_v[...], cot_v, copies, grad_v)
    hand_out(idx, 1, grad_v, outs)


def relay_kernel(unread, first, second, first_out, second_out):
    del unread
    first_out[...] = first[...]
    second_out[...] = second[...]


def sum_kernel(block, got, beside, own, near, far, onward, beside_out, total):
    onward[...] = (block[...].astype(F32) + got[...].astype(F32)).astype(BF16)
    beside_out[...] = beside[...]
    total[...] = own[...].astype(F32) + near[...].astype(F32) + far[...].astype(F32)


def terms_kernel(n_node, idx, mixed_o, mixed_r, w_o, w_r, token, *rest):
    *outs, mixed_v, w_v, mixed_sems, sems = rest
    copies = begin([(w_o, w_v.at[0]), (w_r, w_v.at[1])], sems)
    copies += begin([(mixed_o, mixed_v.at[0]), (mixed_r, mixed_v.at[1])], mixed_sems)
    token[...] = jnp.zeros_like(token)
    depth = w_o.shape[0] // n_node
    half = mixed_o.shape[0] // 2
    for copy in copies:
        copy.wait()
    for j in range(n_node):
        rows = rows_at(idx[j], depth)
        term = dot(mixed_v[0], w_v[0, rows, :], 1, 1) + dot(mixed_v[1], w_v[1, rows, :], 1, 1)
        term = term.astype(BF16)
        if n_node != 4:
            outs[j][...] = term
            continue
        along_x, along_y, kept = outs
        first, second = term[:half], term[half:]
        if j == 0:
            kept[0], kept[2] = first, second
        elif j == 1:
            along_x[0], kept[3] = first, second
        elif j == 2:
            kept[1], along_y[0] = first, second
        else:
            along_x[1], along_y[1] = first, second


ANY = pl.BlockSpec(memory_space=pl.ANY)
SMEM = pl.BlockSpec(memory_space=pltpu.SMEM)
VMEM = pl.BlockSpec(memory_space=pltpu.VMEM)


def call(kernel, name, in_specs, out_shapes, scratch, flops, size=1 << 20, kinds=None, vmem=24, out_specs=None):
    return pl.pallas_call(
        kernel,
        name=name,
        in_specs=in_specs,
        out_specs=out_specs or [VMEM] * len(out_shapes),
        out_shape=[
            jax.ShapeDtypeStruct(s, k) for s, k in zip(out_shapes, kinds or [BF16] * len(out_shapes))
        ],
        scratch_shapes=scratch,
        compiler_params=pltpu.CompilerParams(vmem_limit_bytes=vmem << 20),
        cost_estimate=pl.CostEstimate(flops=flops, bytes_accessed=size, transcendentals=0),
    )


def in_order(x, earlier):
    def kernel(*refs):
        del refs

    return pl.pallas_call(
        kernel,
        name="in_order",
        in_specs=[ANY, ANY],
        out_specs=ANY,
        out_shape=jax.ShapeDtypeStruct(x.shape, x.dtype),
        input_output_aliases={0: 0},
    )(x, earlier)


def make_body(n_wide, n_node):
    planes = n_wide // 2
    line4 = planes == 4 and n_node == 4

    def move(x, pairs):
        return lax.ppermute(
            x, "wide", [(2 * s + c, 2 * d + c) for s, d in pairs for c in range(2)]
        )

    def swap(x, j):
        return move(x, [(s, s ^ j) for s in range(planes)])

    def sibling(x):
        return lax.ppermute(x, "wide", [(i, i ^ 1) for i in range(n_wide)])

    def flip(x, j):
        return lax.ppermute(x, "node", [(i, i ^ j) for i in range(n_node)])

    def swap_cores(w_out, w_value, act, mix, cot, c):
        cols = w_out.shape[1] // 2
        low = jnp.stack([w_out[:, :cols], w_value[:, :cols]])
        high = jnp.stack([w_out[:, cols:], w_value[:, cols:]])
        got = sibling(jnp.where(c == 0, high, low))
        got, act, mix, cot = lax.optimization_barrier((got, act, mix, cot))
        mine = jnp.where(c == 0, low, high)
        u_out, u_value = (jnp.stack([mine[i], got[i]]) for i in range(2))
        return u_out, u_value, sibling(act), sibling(mix), sibling(cot)

    def gather_ring(u):
        return [u] + [
            move(u, [(s, (s - j) % planes) for s in range(planes)]) for j in range(1, planes)
        ]

    def planes_of(z):
        if line4:
            return [lax.bitwise_xor(z, jnp.int32(j)) for j in range(4)]
        return [lax.rem(z + j, planes) for j in range(planes)]

    def added(block, got):
        return (block.astype(F32) + got.astype(F32)).astype(BF16)

    def scatter_end(own, got, c):
        total = own.astype(F32)
        for part in got:
            total = total + part.astype(F32)
        return join(total[0], sibling(total[1]), c)

    def join(mine, other, c):
        low = jnp.where(c == 0, mine, other)
        high = jnp.where(c == 0, other, mine)
        return jnp.concatenate([low, high], axis=1)

    def scatter_ring(blocks, c):
        total = blocks[0].astype(F32)
        for j in range(1, planes):
            got = move(blocks[j], [(s, (s + j) % planes) for s in range(planes)])
            total = total + got.astype(F32)
        return join(total[0], sibling(total[1]), c)

    def body(act_in, mixing, cotangent, w_value, w_out):
        wide = lax.axis_index("wide")
        n = lax.axis_index("node")
        z, c = wide // 2, lax.rem(wide, 2)
        micro, images, seq, width = act_in.shape
        groups = micro * images
        tokens = groups * seq
        cols = w_value.shape[1] // 2
        heads = cols // HEAD_DIM
        depth = width // planes
        act = act_in.reshape(tokens, width)
        cot = cotangent.reshape(tokens, width)
        mix = mixing.reshape(groups, 2 * heads, seq, seq)
        flops = 4 * tokens * width * cols

        u_out, u_value, act_s, mix_s, cot_s = swap_cores(w_out, w_value, act, mix, cot, c)
        block = u_out.shape
        if line4:
            far, near = swap(u_value, 2), swap(u_value, 1)
            far, u_out = call(relay_kernel, "relay", [ANY, VMEM, VMEM], [block] * 2, [], 0, vmem=8)(
                near, far, u_out
            )
            value_slots = [u_value, near, far, swap(far, 1)]
            far = swap(u_out, 2)
            out_slots = [u_out, swap(u_out, 1), far, swap(far, 1)]
        else:
            value_slots, out_slots = gather_ring(u_value), gather_ring(u_out)
        n_slots = len(out_slots)
        pack = lambda *values: jnp.stack([jnp.int32(x) for x in values])
        idx = pack(c, *planes_of(z))
        idx_node = pack(*[lax.bitwise_xor(n, jnp.int32(j)) for j in range(n_node)])

        mix_scratch = pltpu.VMEM((2, groups, heads, seq, seq), BF16)
        both = pltpu.VMEM((2 * tokens, width), BF16)
        halves = pltpu.VMEM((2, tokens, width), BF16)
        left_tokens = pltpu.VMEM((cols, 2 * tokens), BF16)
        rows = pltpu.VMEM((width, cols), BF16)
        send_shapes = [block] * n_slots

        slots_scratch = [
            pltpu.VMEM((n_slots, *block), BF16),
            pltpu.SemaphoreType.DMA((n_slots,)),
        ]
        part_shapes = [(2, tokens, cols), (2, tokens, depth)]
        if line4:
            ahead = call(
                functools.partial(part_kernel, n_slots - 1),
                "value_ahead",
                [SMEM] + [ANY] * (3 + n_slots),
                [*part_shapes, (2, groups, heads, seq, seq)],
                [
                    *(rows, halves, pltpu.VMEM((n_slots - 1, *block), BF16)),
                    *(pltpu.SemaphoreType.DMA((k,)) for k in (2, 4, n_slots - 1)),
                ],
                flops,
                2 * (3 * act.size + mix.size + width * cols + 4 * tokens * cols),
                kinds=[F32, BF16, BF16],
            )(idx, act, act_s, mix, mix_s, *value_slots[:-1])
            mixed_o, mixed_s = call(
                mixed_rest_kernel,
                "mixed",
                [SMEM] + [VMEM] * 4,
                [(tokens, cols)] * 2,
                [],
                flops // 4,
                2 * (2 * tokens * depth + mix.size + 6 * tokens * cols),
                vmem=16,
            )(idx, *ahead, value_slots[-1])
        else:
            mixed_o, mixed_s = call(
                functools.partial(mixed_kernel, n_slots),
                "mixed",
                [SMEM] + [ANY] * (4 + n_slots),
                [(tokens, cols)] * 2,
                [rows, halves, mix_scratch, pltpu.SemaphoreType.DMA((4,)), *slots_scratch],
                flops,
                2 * (2 * act.size + mix.size + width * cols + 2 * tokens * cols),
                )(idx, act, act_s, mix, mix_s, *value_slots)
        mixed_r = sibling(mixed_s)
        unread = [mixed_r, *(out_slots[1:3] if line4 else [])]
        token, *out_sends = call(
            functools.partial(grad_out_kernel, len(unread)),
            "grad_out",
            [SMEM] + [ANY] * 2 + [VMEM] * 2 + [ANY] * len(unread),
            [(16, 128)] + send_shapes,
            [both, left_tokens, rows, pltpu.SemaphoreType.DMA((4, 2))],
            flops,
            2 * (2 * cot.size + 2 * tokens * cols + width * cols),
        )(idx, cot, cot_s, mixed_o, mixed_s, *unread)
        out_passed = swap(out_sends[3], 1) if line4 else token
        left, w_full = call(
            functools.partial(d_value_kernel, n_slots),
            "d_value",
            [SMEM] + [ANY] * (5 + n_slots),
            [(cols, 2 * tokens), (width, cols)],
            [rows, halves, mix_scratch, pltpu.SemaphoreType.DMA((4,)), *slots_scratch]
            + [pltpu.SemaphoreType.DMA((1,))],
            flops,
            2 * (2 * cot.size + mix.size + 2 * width * cols + 2 * tokens * cols),
            vmem=60,
            out_specs=[VMEM, ANY],
        )(idx, token, cot, cot_s, mix, mix_s, *out_slots)
        if line4:
            out_onward = added(out_sends[2], out_passed)
            out_far = swap(out_onward, 2)
            out_near = swap(out_sends[1], 1)
        else:
            out_onward = left
        w_full = in_order(w_full, out_onward)
        w_full_s = sibling(w_full)
        part = width // n_node
        half = tokens // 2
        if n_node == 4:
            term_shapes = [(2, half, part), (2, half, part), (4, half, part)]
        else:
            term_shapes = [(tokens, part)] * n_node
        token, *terms = call(
            functools.partial(terms_kernel, n_node),
            "terms",
            [SMEM] + [ANY] * 4,
            [(16, 128)] + term_shapes,
            [pltpu.VMEM((2, tokens, cols), BF16), pltpu.VMEM((2, width, cols), BF16)]
            + [pltpu.SemaphoreType.DMA((2,))] * 2,
            flops,
            2 * (2 * tokens * cols + 2 * width * cols + tokens * width),
            vmem=60,
        )(idx_node, mixed_o, mixed_r, w_full, w_full_s)
        back_sends = call(
            gradient_kernel,
            "grad_value",
            [SMEM] + [ANY] * 4 + [VMEM],
            send_shapes,
            [both, rows, pltpu.SemaphoreType.DMA((4, 2))],
            flops,
            2 * (2 * act.size + 2 * tokens * cols + width * cols),
        )(idx, token, out_onward, act, act_s, left)
        if line4:
            back_passed = swap(back_sends[3], 1)
            onward, beside, out_total = call(
                sum_kernel, "sum", [VMEM] * 6, [block] * 3, [], 0, kinds=[BF16, BF16, F32], vmem=8
            )(back_sends[2], back_passed, back_sends[1], out_sends[0], out_near, out_far)
            back_far, back_near = swap(onward, 2), swap(beside, 1)
            grad_out = join(out_total[0], sibling(out_total[1]), c)
            grad_value = scatter_end(back_sends[0], (back_near, back_far), c)
        else:
            grad_value = scatter_ring(back_sends, c)
            grad_out = scatter_ring(out_sends, c)

        if n_node == 4:
            along_x, along_y, kept = terms
            kept = kept.astype(F32)
            got_x = flip(along_x, 1).astype(F32)
            got_y = flip(along_y, 2).astype(F32)
            last_y = flip((kept[1] + got_x[1]).astype(BF16), 2)
            last_x = flip((kept[3] + got_y[1]).astype(BF16), 1)
            layer_out = jnp.concatenate(
                [
                    kept[0] + got_x[0] + last_y.astype(F32),
                    kept[2] + got_y[0] + last_x.astype(F32),
                ],
                axis=0,
            )
        else:
            layer_out = terms[0].astype(F32)
            for j in range(1, n_node):
                layer_out = layer_out + flip(terms[j], j).astype(F32)
        layer_out = layer_out.astype(BF16).reshape(micro, images, seq, part)
        return layer_out, grad_value, grad_out

    return body


def solution(mesh):
    return jax.shard_map(
        make_body(mesh.shape["wide"], mesh.shape["node"]),
        mesh=mesh,
        in_specs=(
            P(None, "wide", None, None),
            P(None, "wide", "node", None, None),
            P(None, "wide", None, None),
            P("wide", "node"),
            P("wide", "node"),
        ),
        out_specs=(P(None, "wide", None, "node"), P("wide", "node"), P("wide", "node")),
        check_vma=False,
    )
```

```python
import functools
import math

import jax
import jax.numpy as jnp
from jax import lax
from jax.experimental import pallas as pl
from jax.experimental.pallas import tpu as pltpu
from jax.sharding import PartitionSpec as P

HEAD_DIM = 64
F32 = jnp.float32
BF16 = jnp.bfloat16


def dot(a, b, ca=1, cb=0):
    return lax.dot_general(a, b, (((ca,), (cb,)), ((), ())), preferred_element_type=F32)


def begin_slots(slots, slots_v, sems):
    return begin([(slot, slots_v.at[j]) for j, slot in enumerate(slots)], sems)


def begin(pairs, sems):
    copies = [pltpu.make_async_copy(s, d, sems.at[i]) for i, (s, d) in enumerate(pairs)]
    for copy in copies:
        copy.start()
    return copies


def rows_at(index, size):
    return pl.ds(pl.multiple_of(index * size, math.gcd(size, 16)), size)


def place(idx, core, slots_v, w_ref):
    for j in range(slots_v.shape[0]):
        w_ref[rows_at(idx[1 + j], 2 * slots_v.shape[2]), :] = whole(core, slots_v[j])


def hand_out(idx, base, grad_v, outs):
    core = idx[0]
    for i, out in enumerate(outs):
        depth = out.shape[1]
        block = grad_v[rows_at(idx[base + i], 2 * depth), :]
        low, high = block[:depth], block[depth:]
        out[0] = jnp.where(core == 0, low, high)
        out[1] = jnp.where(core == 0, high, low)


def chunk_copies(own, other, right_ref, sems):
    tokens, width = own.shape
    step = width // sems.shape[0]
    copies = []
    for j in range(sems.shape[0]):
        columns = pl.ds(j * step, step)
        pairs = [
            (own.at[:, columns], right_ref.at[pl.ds(0, tokens), columns]),
            (other.at[:, columns], right_ref.at[pl.ds(tokens, tokens), columns]),
        ]
        copies.append(begin(pairs, sems.at[j]))
    return copies


def gradient_rows(left, right_ref, copies, rows_ref):
    step = right_ref.shape[1] // len(copies)
    for j, chunk in enumerate(copies):
        for copy in chunk:
            copy.wait()
        part = dot(left, right_ref[:, j * step : (j + 1) * step])
        rows_ref[j * step : (j + 1) * step, :] = part.astype(BF16).T


def head_pairs(heads):
    return [(h, min(2, heads - h)) for h in range(0, heads, 2)]


def whole(core, slot):
    mine, other = slot[0], slot[1]
    low = jnp.where(core == 0, mine, other)
    high = jnp.where(core == 0, other, mine)
    return jnp.concatenate([low, high], axis=0)


def part_kernel(n_slots, idx, x_o, x_s, mix_o, mix_s, *rest):
    slots, rest = rest[:n_slots], rest[n_slots:]
    part, last, weights, w_v, x_v, slots_v, x_sems, sems, slot_sems = rest
    heads, depth = weights.shape[2], last.shape[2]
    here = pl.ds(idx[0] * heads, heads)
    missing = idx[1 + n_slots]
    columns = pl.ds(pl.multiple_of(missing * depth, 128), depth)
    copies = begin_slots(slots, slots_v, slot_sems)
    halves = begin([(x_o, x_v.at[0]), (x_s, x_v.at[1])], x_sems)
    later = begin(
        [(x_o.at[:, columns], last.at[0]), (x_s.at[:, columns], last.at[1])]
        + [(mix_o.at[:, here], weights.at[0]), (mix_s.at[:, here], weights.at[1])],
        sems,
    )
    for copy in copies:
        copy.wait()
    place(idx, idx[0], slots_v, w_v)
    w_v[rows_at(missing, depth), :] = jnp.zeros((depth, w_v.shape[1]), BF16)
    for half in range(2):
        halves[half].wait()
        part[half] = dot(x_v[half], w_v[...])
    for copy in later:
        copy.wait()


def mix_values(value, weights, out):
    groups, heads, seq, _ = weights.shape
    for g in range(groups):
        for h, n in head_pairs(heads):
            part = value[g * seq : (g + 1) * seq, h * HEAD_DIM : (h + n) * HEAD_DIM]
            both = weights[g, h]
            if n == 2:
                lane = lax.broadcasted_iota(jnp.int32, part.shape, 1)
                zero = jnp.zeros_like(part)
                part = jnp.concatenate(
                    [
                        jnp.where(lane < HEAD_DIM, part, zero),
                        jnp.where(lane < HEAD_DIM, zero, part),
                    ],
                    axis=0,
                )
                both = jnp.concatenate([both, weights[g, h + 1]], axis=1)
            out[g * seq : (g + 1) * seq, h * HEAD_DIM : (h + n) * HEAD_DIM] = dot(
                both, part
            ).astype(BF16)


def mix_back(d_mixed, weights, left_v, start):
    groups, heads, seq, _ = weights.shape
    for g in range(groups):
        turned = d_mixed[g * seq : (g + 1) * seq, :].astype(BF16).T
        at = start + g * seq
        for h, n in head_pairs(heads):
            part = turned[h * HEAD_DIM : (h + n) * HEAD_DIM, :]
            if n == 2:
                row = lax.broadcasted_iota(jnp.int32, part.shape, 0)
                zero = jnp.zeros_like(part)
                part = jnp.concatenate(
                    [
                        jnp.where(row < HEAD_DIM, part, zero),
                        jnp.where(row < HEAD_DIM, zero, part),
                    ],
                    axis=1,
                )
            both = weights[g, h : h + n].reshape(n * seq, seq)
            left_v[h * HEAD_DIM : (h + n) * HEAD_DIM, at : at + seq] = dot(part, both).astype(BF16)


def mixed_rest_kernel(idx, part, last, weights, slot, mixed_o, mixed_s):
    w_last = whole(idx[0], slot)
    for half, out in enumerate((mixed_o, mixed_s)):
        value = (part[half] + dot(last[half], w_last)).astype(BF16)
        mix_values(value, weights.at[half], out)


def d_value_kernel(n_slots, idx, token, cot_o, cot_s, mix_o, mix_s, *rest):
    del token
    slots, rest = rest[:n_slots], rest[n_slots:]
    left_v, w_out, w_v, cot_v, mix_v, sems, slots_v, slot_sems, out_sems = rest
    tokens, heads = cot_o.shape[0], mix_v.shape[2]
    here = pl.ds(idx[0] * heads, heads)
    slot_copies = begin_slots(slots, slots_v, slot_sems)
    copies = begin(
        [(cot_o, cot_v.at[0]), (mix_o.at[:, here], mix_v.at[0])]
        + [(cot_s, cot_v.at[1]), (mix_s.at[:, here], mix_v.at[1])],
        sems,
    )
    for copy in slot_copies:
        copy.wait()
    place(idx, idx[0], slots_v, w_v)
    handed = begin([(w_v, w_out)], out_sems)
    for half in range(2):
        copies[2 * half].wait()
        d_mixed = dot(cot_v[half], w_v[...])
        copies[2 * half + 1].wait()
        mix_back(d_mixed, mix_v.at[half], left_v, half * tokens)
    handed[0].wait()


def gradient_kernel(idx, token, unread, right_o, right_s, left_ref, *rest):
    del token, unread
    outs, (right_v, grad_v, sems) = rest[:-3], rest[-3:]
    copies = chunk_copies(right_o, right_s, right_v, sems)
    gradient_rows(left_ref[...], right_v, copies, grad_v)
    hand_out(idx, 1, grad_v, outs)


def mixed_kernel(n_slots, idx, act_o, act_s, mix_o, mix_s, *rest):
    slots, rest = rest[:n_slots], rest[n_slots:]
    mixed_o, mixed_s, w_v, act_v, mix_v, sems, slots_v, slot_sems = rest
    heads = mix_v.shape[2]
    here = pl.ds(idx[0] * heads, heads)
    slot_copies = begin_slots(slots, slots_v, slot_sems)
    copies = begin(
        [(act_o, act_v.at[0]), (mix_o.at[:, here], mix_v.at[0])]
        + [(act_s, act_v.at[1]), (mix_s.at[:, here], mix_v.at[1])],
        sems,
    )
    for copy in slot_copies:
        copy.wait()
    place(idx, idx[0], slots_v, w_v)
    for half, out in enumerate((mixed_o, mixed_s)):
        copies[2 * half].wait()
        value = dot(act_v[half], w_v[...]).astype(BF16)
        copies[2 * half + 1].wait()
        mix_values(value, mix_v.at[half], out)


def grad_out_kernel(n_unread, idx, cot_o, cot_s, mixed_o, mixed_s, *rest):
    token, *outs, cot_v, left_v, grad_v, sems = rest[n_unread:]
    token[...] = jnp.zeros_like(token)
    tokens, _ = cot_o.shape
    copies = chunk_copies(cot_o, cot_s, cot_v, sems)
    left_v[:, :tokens] = mixed_o[...].astype(F32).T.astype(BF16)
    left_v[:, tokens:] = mixed_s[...].astype(F32).T.astype(BF16)
    gradient_rows(left_v[...], cot_v, copies, grad_v)
    hand_out(idx, 1, grad_v, outs)


def relay_kernel(unread, first, second, first_out, second_out):
    del unread
    first_out[...] = first[...]
    second_out[...] = second[...]


def sum_kernel(block, got, beside, own, near, far, onward, beside_out, total):
    onward[...] = (block[...].astype(F32) + got[...].astype(F32)).astype(BF16)
    beside_out[...] = beside[...]
    total[...] = own[...].astype(F32) + near[...].astype(F32) + far[...].astype(F32)


def terms_kernel(n_node, idx, mixed_o, mixed_r, w_o, w_r, token, *rest):
    *outs, mixed_v, w_v, mixed_sems, sems = rest
    copies = begin([(w_o, w_v.at[0]), (w_r, w_v.at[1])], sems)
    copies += begin([(mixed_o, mixed_v.at[0]), (mixed_r, mixed_v.at[1])], mixed_sems)
    token[...] = jnp.zeros_like(token)
    depth = w_o.shape[0] // n_node
    half = mixed_o.shape[0] // 2
    for copy in copies:
        copy.wait()
    for j in range(n_node):
        rows = rows_at(idx[j], depth)
        term = dot(mixed_v[0], w_v[0, rows, :], 1, 1) + dot(mixed_v[1], w_v[1, rows, :], 1, 1)
        term = term.astype(BF16)
        if n_node != 4:
            outs[j][...] = term
            continue
        along_x, along_y, kept = outs
        first, second = term[:half], term[half:]
        if j == 0:
            kept[0], kept[2] = first, second
        elif j == 1:
            along_x[0], kept[3] = first, second
        elif j == 2:
            kept[1], along_y[0] = first, second
        else:
            along_x[1], along_y[1] = first, second


ANY = pl.BlockSpec(memory_space=pl.ANY)
SMEM = pl.BlockSpec(memory_space=pltpu.SMEM)
VMEM = pl.BlockSpec(memory_space=pltpu.VMEM)


def call(kernel, name, in_specs, out_shapes, scratch, flops, size=1 << 20, kinds=None, vmem=24, out_specs=None):
    return pl.pallas_call(
        kernel,
        name=name,
        in_specs=in_specs,
        out_specs=out_specs or [VMEM] * len(out_shapes),
        out_shape=[
            jax.ShapeDtypeStruct(s, k) for s, k in zip(out_shapes, kinds or [BF16] * len(out_shapes))
        ],
        scratch_shapes=scratch,
        compiler_params=pltpu.CompilerParams(vmem_limit_bytes=vmem << 20),
        cost_estimate=pl.CostEstimate(flops=flops, bytes_accessed=size, transcendentals=0),
    )


def in_order(x, earlier):
    def kernel(*refs):
        del refs

    return pl.pallas_call(
        kernel,
        name="in_order",
        in_specs=[ANY, ANY],
        out_specs=ANY,
        out_shape=jax.ShapeDtypeStruct(x.shape, x.dtype),
        input_output_aliases={0: 0},
    )(x, earlier)


def make_body(n_wide, n_node):
    planes = n_wide // 2
    line4 = planes == 4 and n_node == 4

    def move(x, pairs):
        return lax.ppermute(
            x, "wide", [(2 * s + c, 2 * d + c) for s, d in pairs for c in range(2)]
        )

    def swap(x, j):
        return move(x, [(s, s ^ j) for s in range(planes)])

    def sibling(x):
        return lax.ppermute(x, "wide", [(i, i ^ 1) for i in range(n_wide)])

    def flip(x, j):
        return lax.ppermute(x, "node", [(i, i ^ j) for i in range(n_node)])

    def swap_cores(w_out, w_value, act, mix, cot, c):
        cols = w_out.shape[1] // 2
        low = jnp.stack([w_out[:, :cols], w_value[:, :cols]])
        high = jnp.stack([w_out[:, cols:], w_value[:, cols:]])
        got = sibling(jnp.where(c == 0, high, low))
        got, act, mix, cot = lax.optimization_barrier((got, act, mix, cot))
        mine = jnp.where(c == 0, low, high)
        u_out, u_value = (jnp.stack([mine[i], got[i]]) for i in range(2))
        return u_out, u_value, sibling(act), sibling(mix), sibling(cot)

    def gather_ring(u):
        return [u] + [
            move(u, [(s, (s - j) % planes) for s in range(planes)]) for j in range(1, planes)
        ]

    def planes_of(z):
        if line4:
            return [lax.bitwise_xor(z, jnp.int32(j)) for j in range(4)]
        return [lax.rem(z + j, planes) for j in range(planes)]

    def added(block, got):
        return (block.astype(F32) + got.astype(F32)).astype(BF16)

    def scatter_end(own, got, c):
        total = own.astype(F32)
        for part in got:
            total = total + part.astype(F32)
        return join(total[0], sibling(total[1]), c)

    def join(mine, other, c):
        low = jnp.where(c == 0, mine, other)
        high = jnp.where(c == 0, other, mine)
        return jnp.concatenate([low, high], axis=1)

    def scatter_ring(blocks, c):
        total = blocks[0].astype(F32)
        for j in range(1, planes):
            got = move(blocks[j], [(s, (s + j) % planes) for s in range(planes)])
            total = total + got.astype(F32)
        return join(total[0], sibling(total[1]), c)

    def body(act_in, mixing, cotangent, w_value, w_out):
        wide = lax.axis_index("wide")
        n = lax.axis_index("node")
        z, c = wide // 2, lax.rem(wide, 2)
        micro, images, seq, width = act_in.shape
        groups = micro * images
        tokens = groups * seq
        cols = w_value.shape[1] // 2
        heads = cols // HEAD_DIM
        depth = width // planes
        act = act_in.reshape(tokens, width)
        cot = cotangent.reshape(tokens, width)
        mix = mixing.reshape(groups, 2 * heads, seq, seq)
        flops = 4 * tokens * width * cols

        u_out, u_value, act_s, mix_s, cot_s = swap_cores(w_out, w_value, act, mix, cot, c)
        block = u_out.shape
        if line4:
            far, near = swap(u_value, 2), swap(u_value, 1)
            far, u_out = call(relay_kernel, "relay", [ANY, VMEM, VMEM], [block] * 2, [], 0, vmem=8)(
                near, far, u_out
            )
            value_slots = [u_value, near, far, swap(far, 1)]
            far = swap(u_out, 2)
            out_slots = [u_out, swap(u_out, 1), far, swap(far, 1)]
        else:
            value_slots, out_slots = gather_ring(u_value), gather_ring(u_out)
        n_slots = len(out_slots)
        pack = lambda *values: jnp.stack([jnp.int32(x) for x in values])
        idx = pack(c, *planes_of(z))
        idx_node = pack(*[lax.bitwise_xor(n, jnp.int32(j)) for j in range(n_node)])

        mix_scratch = pltpu.VMEM((2, groups, heads, seq, seq), BF16)
        both = pltpu.VMEM((2 * tokens, width), BF16)
        halves = pltpu.VMEM((2, tokens, width), BF16)
        left_tokens = pltpu.VMEM((cols, 2 * tokens), BF16)
        rows = pltpu.VMEM((width, cols), BF16)
        send_shapes = [block] * n_slots

        slots_scratch = [
            pltpu.VMEM((n_slots, *block), BF16),
            pltpu.SemaphoreType.DMA((n_slots,)),
        ]
        part_shapes = [(2, tokens, cols), (2, tokens, depth)]
        if line4:
            ahead = call(
                functools.partial(part_kernel, n_slots - 1),
                "value_ahead",
                [SMEM] + [ANY] * (3 + n_slots),
                [*part_shapes, (2, groups, heads, seq, seq)],
                [
                    *(rows, halves, pltpu.VMEM((n_slots - 1, *block), BF16)),
                    *(pltpu.SemaphoreType.DMA((k,)) for k in (2, 4, n_slots - 1)),
                ],
                flops,
                2 * (3 * act.size + mix.size + width * cols + 4 * tokens * cols),
                kinds=[F32, BF16, BF16],
            )(idx, act, act_s, mix, mix_s, *value_slots[:-1])
            mixed_o, mixed_s = call(
                mixed_rest_kernel,
                "mixed",
                [SMEM] + [VMEM] * 4,
                [(tokens, cols)] * 2,
                [],
                flops // 4,
                2 * (2 * tokens * depth + mix.size + 6 * tokens * cols),
                vmem=16,
            )(idx, *ahead, value_slots[-1])
        else:
            mixed_o, mixed_s = call(
                functools.partial(mixed_kernel, n_slots),
                "mixed",
                [SMEM] + [ANY] * (4 + n_slots),
                [(tokens, cols)] * 2,
                [rows, halves, mix_scratch, pltpu.SemaphoreType.DMA((4,)), *slots_scratch],
                flops,
                2 * (2 * act.size + mix.size + width * cols + 2 * tokens * cols),
                )(idx, act, act_s, mix, mix_s, *value_slots)
        mixed_r = sibling(mixed_s)
        unread = [mixed_r, *(out_slots[1:3] if line4 else [])]
        token, *out_sends = call(
            functools.partial(grad_out_kernel, len(unread)),
            "grad_out",
            [SMEM] + [ANY] * 2 + [VMEM] * 2 + [ANY] * len(unread),
            [(16, 128)] + send_shapes,
            [both, left_tokens, rows, pltpu.SemaphoreType.DMA((4, 2))],
            flops,
            2 * (2 * cot.size + 2 * tokens * cols + width * cols),
        )(idx, cot, cot_s, mixed_o, mixed_s, *unread)
        out_passed = swap(out_sends[3], 1) if line4 else token
        left, w_full = call(
            functools.partial(d_value_kernel, n_slots),
            "d_value",
            [SMEM] + [ANY] * (5 + n_slots),
            [(cols, 2 * tokens), (width, cols)],
            [rows, halves, mix_scratch, pltpu.SemaphoreType.DMA((4,)), *slots_scratch]
            + [pltpu.SemaphoreType.DMA((1,))],
            flops,
            2 * (2 * cot.size + mix.size + 2 * width * cols + 2 * tokens * cols),
            out_specs=[VMEM, ANY],
        )(idx, token, cot, cot_s, mix, mix_s, *out_slots)
        if line4:
            out_onward = added(out_sends[2], out_passed)
            out_far = swap(out_onward, 2)
            out_near = swap(out_sends[1], 1)
        else:
            out_onward = left
        w_full = in_order(w_full, out_onward)
        w_full_s = sibling(w_full)
        part = width // n_node
        half = tokens // 2
        if n_node == 4:
            term_shapes = [(2, half, part), (2, half, part), (4, half, part)]
        else:
            term_shapes = [(tokens, part)] * n_node
        token, *terms = call(
            functools.partial(terms_kernel, n_node),
            "terms",
            [SMEM] + [ANY] * 4,
            [(16, 128)] + term_shapes,
            [pltpu.VMEM((2, tokens, cols), BF16), pltpu.VMEM((2, width, cols), BF16)]
            + [pltpu.SemaphoreType.DMA((2,))] * 2,
            flops,
            2 * (2 * tokens * cols + 2 * width * cols + tokens * width),
            vmem=60,
        )(idx_node, mixed_o, mixed_r, w_full, w_full_s)
        back_sends = call(
            gradient_kernel,
            "grad_value",
            [SMEM] + [ANY] * 4 + [VMEM],
            send_shapes,
            [both, rows, pltpu.SemaphoreType.DMA((4, 2))],
            flops,
            2 * (2 * act.size + 2 * tokens * cols + width * cols),
        )(idx, token, out_onward, act, act_s, left)
        if line4:
            back_passed = swap(back_sends[3], 1)
            onward, beside, out_total = call(
                sum_kernel, "sum", [VMEM] * 6, [block] * 3, [], 0, kinds=[BF16, BF16, F32], vmem=8
            )(back_sends[2], back_passed, back_sends[1], out_sends[0], out_near, out_far)
            back_far, back_near = swap(onward, 2), swap(beside, 1)
            grad_out = join(out_total[0], sibling(out_total[1]), c)
            grad_value = scatter_end(back_sends[0], (back_near, back_far), c)
        else:
            grad_value = scatter_ring(back_sends, c)
            grad_out = scatter_ring(out_sends, c)

        if n_node == 4:
            along_x, along_y, kept = terms
            kept = kept.astype(F32)
            got_x = flip(along_x, 1).astype(F32)
            got_y = flip(along_y, 2).astype(F32)
            last_y = flip((kept[1] + got_x[1]).astype(BF16), 2)
            last_x = flip((kept[3] + got_y[1]).astype(BF16), 1)
            layer_out = jnp.concatenate(
                [
                    kept[0] + got_x[0] + last_y.astype(F32),
                    kept[2] + got_y[0] + last_x.astype(F32),
                ],
                axis=0,
            )
        else:
            layer_out = terms[0].astype(F32)
            for j in range(1, n_node):
                layer_out = layer_out + flip(terms[j], j).astype(F32)
        layer_out = layer_out.astype(BF16).reshape(micro, images, seq, part)
        return layer_out, grad_value, grad_out

    return body


def solution(mesh):
    return jax.shard_map(
        make_body(mesh.shape["wide"], mesh.shape["node"]),
        mesh=mesh,
        in_specs=(
            P(None, "wide", None, None),
            P(None, "wide", "node", None, None),
            P(None, "wide", None, None),
            P("wide", "node"),
            P("wide", "node"),
        ),
        out_specs=(P(None, "wide", None, "node"), P("wide", "node"), P("wide", "node")),
        check_vma=False,
    )
```

```python
import functools
import math

import jax
import jax.numpy as jnp
from jax import lax
from jax.experimental import pallas as pl
from jax.experimental.pallas import tpu as pltpu
from jax.sharding import PartitionSpec as P

HEAD_DIM = 64
F32 = jnp.float32
BF16 = jnp.bfloat16


def dot(a, b, ca=1, cb=0):
    return lax.dot_general(a, b, (((ca,), (cb,)), ((), ())), preferred_element_type=F32)


def begin_slots(slots, slots_v, sems):
    return begin([(slot, slots_v.at[j]) for j, slot in enumerate(slots)], sems)


def begin(pairs, sems):
    copies = [pltpu.make_async_copy(s, d, sems.at[i]) for i, (s, d) in enumerate(pairs)]
    for copy in copies:
        copy.start()
    return copies


def rows_at(index, size):
    return pl.ds(pl.multiple_of(index * size, math.gcd(size, 16)), size)


def place(idx, core, slots_v, w_ref):
    for j in range(slots_v.shape[0]):
        w_ref[rows_at(idx[1 + j], 2 * slots_v.shape[2]), :] = whole(core, slots_v[j])


def hand_out(idx, base, grad_v, outs):
    core = idx[0]
    for i, out in enumerate(outs):
        depth = out.shape[1]
        block = grad_v[rows_at(idx[base + i], 2 * depth), :]
        low, high = block[:depth], block[depth:]
        out[0] = jnp.where(core == 0, low, high)
        out[1] = jnp.where(core == 0, high, low)


def chunk_copies(own, other, right_ref, sems):
    tokens, width = own.shape
    step = width // sems.shape[0]
    copies = []
    for j in range(sems.shape[0]):
        columns = pl.ds(j * step, step)
        pairs = [
            (own.at[:, columns], right_ref.at[pl.ds(0, tokens), columns]),
            (other.at[:, columns], right_ref.at[pl.ds(tokens, tokens), columns]),
        ]
        copies.append(begin(pairs, sems.at[j]))
    return copies


def gradient_rows(left, right_ref, copies, rows_ref):
    step = right_ref.shape[1] // len(copies)
    for j, chunk in enumerate(copies):
        for copy in chunk:
            copy.wait()
        part = dot(left, right_ref[:, j * step : (j + 1) * step])
        rows_ref[j * step : (j + 1) * step, :] = part.astype(BF16).T


def head_pairs(heads):
    return [(h, min(2, heads - h)) for h in range(0, heads, 2)]


def whole(core, slot):
    mine, other = slot[0], slot[1]
    low = jnp.where(core == 0, mine, other)
    high = jnp.where(core == 0, other, mine)
    return jnp.concatenate([low, high], axis=0)


def part_kernel(n_slots, idx, x_o, x_s, mix_o, mix_s, *rest):
    slots, rest = rest[:n_slots], rest[n_slots:]
    part, last, weights, w_v, x_v, slots_v, x_sems, sems, slot_sems = rest
    heads, depth = weights.shape[2], last.shape[2]
    here = pl.ds(idx[0] * heads, heads)
    missing = idx[1 + n_slots]
    columns = pl.ds(pl.multiple_of(missing * depth, 128), depth)
    copies = begin_slots(slots, slots_v, slot_sems)
    halves = begin([(x_o, x_v.at[0]), (x_s, x_v.at[1])], x_sems)
    later = begin(
        [(x_o.at[:, columns], last.at[0]), (x_s.at[:, columns], last.at[1])]
        + [(mix_o.at[:, here], weights.at[0]), (mix_s.at[:, here], weights.at[1])],
        sems,
    )
    for copy in copies:
        copy.wait()
    place(idx, idx[0], slots_v, w_v)
    w_v[rows_at(missing, depth), :] = jnp.zeros((depth, w_v.shape[1]), BF16)
    for half in range(2):
        halves[half].wait()
        part[half] = dot(x_v[half], w_v[...])
    for copy in later:
        copy.wait()


def mix_values(value, weights, out):
    groups, heads, seq, _ = weights.shape
    for g in range(groups):
        for h, n in head_pairs(heads):
            part = value[g * seq : (g + 1) * seq, h * HEAD_DIM : (h + n) * HEAD_DIM]
            both = weights[g, h]
            if n == 2:
                lane = lax.broadcasted_iota(jnp.int32, part.shape, 1)
                zero = jnp.zeros_like(part)
                part = jnp.concatenate(
                    [
                        jnp.where(lane < HEAD_DIM, part, zero),
                        jnp.where(lane < HEAD_DIM, zero, part),
                    ],
                    axis=0,
                )
                both = jnp.concatenate([both, weights[g, h + 1]], axis=1)
            out[g * seq : (g + 1) * seq, h * HEAD_DIM : (h + n) * HEAD_DIM] = dot(
                both, part
            ).astype(BF16)


def mix_back(d_mixed, weights, left_v, start):
    groups, heads, seq, _ = weights.shape
    for g in range(groups):
        turned = d_mixed[g * seq : (g + 1) * seq, :].astype(BF16).T
        at = start + g * seq
        for h, n in head_pairs(heads):
            part = turned[h * HEAD_DIM : (h + n) * HEAD_DIM, :]
            if n == 2:
                row = lax.broadcasted_iota(jnp.int32, part.shape, 0)
                zero = jnp.zeros_like(part)
                part = jnp.concatenate(
                    [
                        jnp.where(row < HEAD_DIM, part, zero),
                        jnp.where(row < HEAD_DIM, zero, part),
                    ],
                    axis=1,
                )
            both = weights[g, h : h + n].reshape(n * seq, seq)
            left_v[h * HEAD_DIM : (h + n) * HEAD_DIM, at : at + seq] = dot(part, both).astype(BF16)


def mixed_rest_kernel(idx, part, last, weights, slot, mixed_o, mixed_s):
    w_last = whole(idx[0], slot)
    for half, out in enumerate((mixed_o, mixed_s)):
        value = (part[half] + dot(last[half], w_last)).astype(BF16)
        mix_values(value, weights.at[half], out)


def d_value_kernel(n_slots, idx, token, cot_o, cot_s, mix_o, mix_s, *rest):
    del token
    slots, rest = rest[:n_slots], rest[n_slots:]
    left_v, w_out, w_v, cot_v, mix_v, sems, slots_v, slot_sems, out_sems = rest
    tokens, heads = cot_o.shape[0], mix_v.shape[2]
    here = pl.ds(idx[0] * heads, heads)
    slot_copies = begin_slots(slots, slots_v, slot_sems)
    copies = begin(
        [(cot_o, cot_v.at[0]), (mix_o.at[:, here], mix_v.at[0])]
        + [(cot_s, cot_v.at[1]), (mix_s.at[:, here], mix_v.at[1])],
        sems,
    )
    for copy in slot_copies:
        copy.wait()
    place(idx, idx[0], slots_v, w_v)
    handed = begin([(w_v, w_out)], out_sems)
    for half in range(2):
        copies[2 * half].wait()
        d_mixed = dot(cot_v[half], w_v[...])
        copies[2 * half + 1].wait()
        mix_back(d_mixed, mix_v.at[half], left_v, half * tokens)
    handed[0].wait()


def gradient_kernel(idx, token, unread, right_o, right_s, left_ref, *rest):
    del token, unread
    outs, (right_v, grad_v, sems) = rest[:-3], rest[-3:]
    copies = chunk_copies(right_o, right_s, right_v, sems)
    gradient_rows(left_ref[...], right_v, copies, grad_v)
    hand_out(idx, 1, grad_v, outs)


def mixed_kernel(n_slots, idx, act_o, act_s, mix_o, mix_s, *rest):
    slots, rest = rest[:n_slots], rest[n_slots:]
    mixed_o, mixed_s, w_v, act_v, mix_v, sems, slots_v, slot_sems = rest
    heads = mix_v.shape[2]
    here = pl.ds(idx[0] * heads, heads)
    slot_copies = begin_slots(slots, slots_v, slot_sems)
    copies = begin(
        [(act_o, act_v.at[0]), (mix_o.at[:, here], mix_v.at[0])]
        + [(act_s, act_v.at[1]), (mix_s.at[:, here], mix_v.at[1])],
        sems,
    )
    for copy in slot_copies:
        copy.wait()
    place(idx, idx[0], slots_v, w_v)
    for half, out in enumerate((mixed_o, mixed_s)):
        copies[2 * half].wait()
        value = dot(act_v[half], w_v[...]).astype(BF16)
        copies[2 * half + 1].wait()
        mix_values(value, mix_v.at[half], out)


def grad_out_kernel(n_unread, idx, cot_o, cot_s, mixed_o, mixed_s, *rest):
    token, *outs, cot_v, left_v, grad_v, sems = rest[n_unread:]
    token[...] = jnp.zeros_like(token)
    tokens, _ = cot_o.shape
    copies = chunk_copies(cot_o, cot_s, cot_v, sems)
    left_v[:, :tokens] = mixed_o[...].astype(F32).T.astype(BF16)
    left_v[:, tokens:] = mixed_s[...].astype(F32).T.astype(BF16)
    gradient_rows(left_v[...], cot_v, copies, grad_v)
    hand_out(idx, 1, grad_v, outs)


def relay_kernel(unread, first, second, first_out, second_out, again_out):
    del unread
    first_out[...] = first[...]
    second_out[...] = second[...]
    again_out[...] = second[...]


def sum_kernel(block, got, beside, own, near, far, onward, beside_out, total):
    onward[...] = (block[...].astype(F32) + got[...].astype(F32)).astype(BF16)
    beside_out[...] = beside[...]
    total[...] = own[...].astype(F32) + near[...].astype(F32) + far[...].astype(F32)


def terms_kernel(n_node, idx, mixed_o, mixed_r, w_o, w_r, token, *outs):
    token[...] = jnp.zeros_like(token)
    depth = w_o.shape[0] // n_node
    half = mixed_o.shape[0] // 2
    for j in range(n_node):
        rows = rows_at(idx[j], depth)
        term = dot(mixed_o[...], w_o[rows, :], 1, 1) + dot(mixed_r[...], w_r[rows, :], 1, 1)
        term = term.astype(BF16)
        if n_node != 4:
            outs[j][...] = term
            continue
        along_x, along_y, kept = outs
        first, second = term[:half], term[half:]
        if j == 0:
            kept[0], kept[2] = first, second
        elif j == 1:
            along_x[0], kept[3] = first, second
        elif j == 2:
            kept[1], along_y[0] = first, second
        else:
            along_x[1], along_y[1] = first, second


ANY = pl.BlockSpec(memory_space=pl.ANY)
SMEM = pl.BlockSpec(memory_space=pltpu.SMEM)
VMEM = pl.BlockSpec(memory_space=pltpu.VMEM)


def call(kernel, name, in_specs, out_shapes, scratch, flops, size=1 << 20, kinds=None, vmem=24, out_specs=None):
    return pl.pallas_call(
        kernel,
        name=name,
        in_specs=in_specs,
        out_specs=out_specs or [VMEM] * len(out_shapes),
        out_shape=[
            jax.ShapeDtypeStruct(s, k) for s, k in zip(out_shapes, kinds or [BF16] * len(out_shapes))
        ],
        scratch_shapes=scratch,
        compiler_params=pltpu.CompilerParams(vmem_limit_bytes=vmem << 20),
        cost_estimate=pl.CostEstimate(flops=flops, bytes_accessed=size, transcendentals=0),
    )


def in_order(x, earlier):
    def kernel(*refs):
        del refs

    return pl.pallas_call(
        kernel,
        name="in_order",
        in_specs=[ANY, ANY],
        out_specs=ANY,
        out_shape=jax.ShapeDtypeStruct(x.shape, x.dtype),
        input_output_aliases={0: 0},
    )(x, earlier)


def make_body(n_wide, n_node):
    planes = n_wide // 2
    line4 = planes == 4 and n_node == 4

    def move(x, pairs):
        return lax.ppermute(
            x, "wide", [(2 * s + c, 2 * d + c) for s, d in pairs for c in range(2)]
        )

    def swap(x, j):
        return move(x, [(s, s ^ j) for s in range(planes)])

    def sibling(x):
        return lax.ppermute(x, "wide", [(i, i ^ 1) for i in range(n_wide)])

    def flip(x, j):
        return lax.ppermute(x, "node", [(i, i ^ j) for i in range(n_node)])

    def swap_cores(w_out, w_value, act, mix, cot, c):
        cols = w_out.shape[1] // 2
        low = jnp.stack([w_out[:, :cols], w_value[:, :cols]])
        high = jnp.stack([w_out[:, cols:], w_value[:, cols:]])
        got = sibling(jnp.where(c == 0, high, low))
        got, act, mix, cot = lax.optimization_barrier((got, act, mix, cot))
        mine = jnp.where(c == 0, low, high)
        u_out, u_value = (jnp.stack([mine[i], got[i]]) for i in range(2))
        return u_out, u_value, sibling(act), sibling(mix), sibling(cot)

    def gather_ring(u):
        return [u] + [
            move(u, [(s, (s - j) % planes) for s in range(planes)]) for j in range(1, planes)
        ]

    def planes_of(z):
        if line4:
            return [lax.bitwise_xor(z, jnp.int32(j)) for j in range(4)]
        return [lax.rem(z + j, planes) for j in range(planes)]

    def added(block, got):
        return (block.astype(F32) + got.astype(F32)).astype(BF16)

    def scatter_end(own, got, c):
        total = own.astype(F32)
        for part in got:
            total = total + part.astype(F32)
        return join(total[0], sibling(total[1]), c)

    def join(mine, other, c):
        low = jnp.where(c == 0, mine, other)
        high = jnp.where(c == 0, other, mine)
        return jnp.concatenate([low, high], axis=1)

    def scatter_ring(blocks, c):
        total = blocks[0].astype(F32)
        for j in range(1, planes):
            got = move(blocks[j], [(s, (s + j) % planes) for s in range(planes)])
            total = total + got.astype(F32)
        return join(total[0], sibling(total[1]), c)

    def body(act_in, mixing, cotangent, w_value, w_out):
        wide = lax.axis_index("wide")
        n = lax.axis_index("node")
        z, c = wide // 2, lax.rem(wide, 2)
        micro, images, seq, width = act_in.shape
        groups = micro * images
        tokens = groups * seq
        cols = w_value.shape[1] // 2
        heads = cols // HEAD_DIM
        depth = width // planes
        act = act_in.reshape(tokens, width)
        cot = cotangent.reshape(tokens, width)
        mix = mixing.reshape(groups, 2 * heads, seq, seq)
        flops = 4 * tokens * width * cols

        u_out, u_value, act_s, mix_s, cot_s = swap_cores(w_out, w_value, act, mix, cot, c)
        block = u_out.shape
        if line4:
            far, near = swap(u_value, 2), swap(u_value, 1)
            far, u_out, again = call(relay_kernel, "relay", [ANY, VMEM, VMEM], [block] * 3, [], 0, vmem=8)(
                near, far, u_out
            )
            value_slots = [u_value, near, far, swap(far, 1)]
            far = swap(u_out, 2)
            out_slots = [u_out, swap(in_order(again, mix_s), 1), far, swap(far, 1)]
        else:
            value_slots, out_slots = gather_ring(u_value), gather_ring(u_out)
        n_slots = len(out_slots)
        pack = lambda *values: jnp.stack([jnp.int32(x) for x in values])
        idx = pack(c, *planes_of(z))
        idx_node = pack(*[lax.bitwise_xor(n, jnp.int32(j)) for j in range(n_node)])

        mix_scratch = pltpu.VMEM((2, groups, heads, seq, seq), BF16)
        both = pltpu.VMEM((2 * tokens, width), BF16)
        halves = pltpu.VMEM((2, tokens, width), BF16)
        left_tokens = pltpu.VMEM((cols, 2 * tokens), BF16)
        rows = pltpu.VMEM((width, cols), BF16)
        send_shapes = [block] * n_slots

        slots_scratch = [
            pltpu.VMEM((n_slots, *block), BF16),
            pltpu.SemaphoreType.DMA((n_slots,)),
        ]
        part_shapes = [(2, tokens, cols), (2, tokens, depth)]
        if line4:
            ahead = call(
                functools.partial(part_kernel, n_slots - 1),
                "value_ahead",
                [SMEM] + [ANY] * (3 + n_slots),
                [*part_shapes, (2, groups, heads, seq, seq)],
                [
                    *(rows, halves, pltpu.VMEM((n_slots - 1, *block), BF16)),
                    *(pltpu.SemaphoreType.DMA((k,)) for k in (2, 4, n_slots - 1)),
                ],
                flops,
                2 * (3 * act.size + mix.size + width * cols + 4 * tokens * cols),
                kinds=[F32, BF16, BF16],
            )(idx, act, act_s, mix, mix_s, *value_slots[:-1])
            mixed_o, mixed_s = call(
                mixed_rest_kernel,
                "mixed",
                [SMEM] + [VMEM] * 4,
                [(tokens, cols)] * 2,
                [],
                flops // 4,
                2 * (2 * tokens * depth + mix.size + 6 * tokens * cols),
                vmem=16,
            )(idx, *ahead, value_slots[-1])
        else:
            mixed_o, mixed_s = call(
                functools.partial(mixed_kernel, n_slots),
                "mixed",
                [SMEM] + [ANY] * (4 + n_slots),
                [(tokens, cols)] * 2,
                [rows, halves, mix_scratch, pltpu.SemaphoreType.DMA((4,)), *slots_scratch],
                flops,
                2 * (2 * act.size + mix.size + width * cols + 2 * tokens * cols),
                )(idx, act, act_s, mix, mix_s, *value_slots)
        mixed_r = sibling(mixed_s)
        unread = [mixed_r, *(out_slots[1:3] if line4 else [])]
        token, *out_sends = call(
            functools.partial(grad_out_kernel, len(unread)),
            "grad_out",
            [SMEM] + [ANY] * 2 + [VMEM] * 2 + [ANY] * len(unread),
            [(16, 128)] + send_shapes,
            [both, left_tokens, rows, pltpu.SemaphoreType.DMA((4, 2))],
            flops,
            2 * (2 * cot.size + 2 * tokens * cols + width * cols),
        )(idx, cot, cot_s, mixed_o, mixed_s, *unread)
        out_passed = swap(out_sends[3], 1) if line4 else token
        left, w_full = call(
            functools.partial(d_value_kernel, n_slots),
            "d_value",
            [SMEM] + [ANY] * (5 + n_slots),
            [(cols, 2 * tokens), (width, cols)],
            [rows, halves, mix_scratch, pltpu.SemaphoreType.DMA((4,)), *slots_scratch]
            + [pltpu.SemaphoreType.DMA((1,))],
            flops,
            2 * (2 * cot.size + mix.size + 2 * width * cols + 2 * tokens * cols),
            out_specs=[VMEM, ANY],
        )(idx, token, cot, cot_s, mix, mix_s, *out_slots)
        if line4:
            out_onward = added(out_sends[2], out_passed)
            out_far = swap(out_onward, 2)
            out_near = swap(out_sends[1], 1)
        else:
            out_onward = left
        w_full = in_order(w_full, out_onward)
        w_full_s = sibling(w_full)
        part = width // n_node
        half = tokens // 2
        if n_node == 4:
            term_shapes = [(2, half, part), (2, half, part), (4, half, part)]
        else:
            term_shapes = [(tokens, part)] * n_node
        token, *terms = call(
            functools.partial(terms_kernel, n_node),
            "terms",
            [SMEM] + [VMEM] * 4,
            [(16, 128)] + term_shapes,
            [],
            flops,
            2 * (2 * tokens * cols + 2 * width * cols + tokens * width),
        )(idx_node, mixed_o, mixed_r, w_full, w_full_s)
        back_sends = call(
            gradient_kernel,
            "grad_value",
            [SMEM] + [ANY] * 4 + [VMEM],
            send_shapes,
            [both, rows, pltpu.SemaphoreType.DMA((4, 2))],
            flops,
            2 * (2 * act.size + 2 * tokens * cols + width * cols),
        )(idx, token, out_onward, act, act_s, left)
        if line4:
            back_passed = swap(back_sends[3], 1)
            onward, beside, out_total = call(
                sum_kernel, "sum", [VMEM] * 6, [block] * 3, [], 0, kinds=[BF16, BF16, F32], vmem=8
            )(back_sends[2], back_passed, back_sends[1], out_sends[0], out_near, out_far)
            back_far, back_near = swap(onward, 2), swap(beside, 1)
            grad_out = join(out_total[0], sibling(out_total[1]), c)
            grad_value = scatter_end(back_sends[0], (back_near, back_far), c)
        else:
            grad_value = scatter_ring(back_sends, c)
            grad_out = scatter_ring(out_sends, c)

        if n_node == 4:
            along_x, along_y, kept = terms
            kept = kept.astype(F32)
            got_x = flip(along_x, 1).astype(F32)
            got_y = flip(along_y, 2).astype(F32)
            last_y = flip((kept[1] + got_x[1]).astype(BF16), 2)
            last_x = flip((kept[3] + got_y[1]).astype(BF16), 1)
            layer_out = jnp.concatenate(
                [
                    kept[0] + got_x[0] + last_y.astype(F32),
                    kept[2] + got_y[0] + last_x.astype(F32),
                ],
                axis=0,
            )
        else:
            layer_out = terms[0].astype(F32)
            for j in range(1, n_node):
                layer_out = layer_out + flip(terms[j], j).astype(F32)
        layer_out = layer_out.astype(BF16).reshape(micro, images, seq, part)
        return layer_out, grad_value, grad_out

    return body


def solution(mesh):
    return jax.shard_map(
        make_body(mesh.shape["wide"], mesh.shape["node"]),
        mesh=mesh,
        in_specs=(
            P(None, "wide", None, None),
            P(None, "wide", "node", None, None),
            P(None, "wide", None, None),
            P("wide", "node"),
            P("wide", "node"),
        ),
        out_specs=(P(None, "wide", None, "node"), P("wide", "node"), P("wide", "node")),
        check_vma=False,
    )
```

```python
import functools
import math

import jax
import jax.numpy as jnp
from jax import lax
from jax.experimental import pallas as pl
from jax.experimental.pallas import tpu as pltpu
from jax.sharding import PartitionSpec as P

HEAD_DIM = 64
F32 = jnp.float32
BF16 = jnp.bfloat16


def dot(a, b, ca=1, cb=0):
    return lax.dot_general(a, b, (((ca,), (cb,)), ((), ())), preferred_element_type=F32)


def begin_slots(slots, slots_v, sems):
    return begin([(slot, slots_v.at[j]) for j, slot in enumerate(slots)], sems)


def begin(pairs, sems):
    copies = [pltpu.make_async_copy(s, d, sems.at[i]) for i, (s, d) in enumerate(pairs)]
    for copy in copies:
        copy.start()
    return copies


def rows_at(index, size):
    return pl.ds(pl.multiple_of(index * size, math.gcd(size, 16)), size)


def place(idx, core, slots_v, w_ref):
    for j in range(slots_v.shape[0]):
        w_ref[rows_at(idx[1 + j], 2 * slots_v.shape[2]), :] = whole(core, slots_v[j])


def hand_out(idx, base, grad_v, outs):
    core = idx[0]
    for i, out in enumerate(outs):
        depth = out.shape[1]
        block = grad_v[rows_at(idx[base + i], 2 * depth), :]
        low, high = block[:depth], block[depth:]
        out[0] = jnp.where(core == 0, low, high)
        out[1] = jnp.where(core == 0, high, low)


def chunk_copies(own, other, right_ref, sems):
    tokens, width = own.shape
    step = width // sems.shape[0]
    copies = []
    for j in range(sems.shape[0]):
        columns = pl.ds(j * step, step)
        pairs = [
            (own.at[:, columns], right_ref.at[pl.ds(0, tokens), columns]),
            (other.at[:, columns], right_ref.at[pl.ds(tokens, tokens), columns]),
        ]
        copies.append(begin(pairs, sems.at[j]))
    return copies


def gradient_rows(left, right_ref, copies, rows_ref):
    step = right_ref.shape[1] // len(copies)
    for j, chunk in enumerate(copies):
        for copy in chunk:
            copy.wait()
        part = dot(left, right_ref[:, j * step : (j + 1) * step])
        rows_ref[j * step : (j + 1) * step, :] = part.astype(BF16).T


def head_pairs(heads):
    return [(h, min(2, heads - h)) for h in range(0, heads, 2)]


def whole(core, slot):
    mine, other = slot[0], slot[1]
    low = jnp.where(core == 0, mine, other)
    high = jnp.where(core == 0, other, mine)
    return jnp.concatenate([low, high], axis=0)


def part_kernel(n_slots, idx, x_o, x_s, mix_o, mix_s, *rest):
    slots, rest = rest[:n_slots], rest[n_slots:]
    part, last, weights, w_v, x_v, slots_v, x_sems, sems, slot_sems = rest
    heads, depth = weights.shape[2], last.shape[2]
    here = pl.ds(idx[0] * heads, heads)
    missing = idx[1 + n_slots]
    columns = pl.ds(pl.multiple_of(missing * depth, 128), depth)
    copies = begin_slots(slots, slots_v, slot_sems)
    halves = begin([(x_o, x_v.at[0]), (x_s, x_v.at[1])], x_sems)
    later = begin(
        [(x_o.at[:, columns], last.at[0]), (x_s.at[:, columns], last.at[1])]
        + [(mix_o.at[:, here], weights.at[0]), (mix_s.at[:, here], weights.at[1])],
        sems,
    )
    for copy in copies:
        copy.wait()
    place(idx, idx[0], slots_v, w_v)
    w_v[rows_at(missing, depth), :] = jnp.zeros((depth, w_v.shape[1]), BF16)
    for half in range(2):
        halves[half].wait()
        part[half] = dot(x_v[half], w_v[...])
    for copy in later:
        copy.wait()


def mix_values(value, weights, out):
    groups, heads, seq, _ = weights.shape
    for g in range(groups):
        for h, n in head_pairs(heads):
            part = value[g * seq : (g + 1) * seq, h * HEAD_DIM : (h + n) * HEAD_DIM]
            both = weights[g, h]
            if n == 2:
                lane = lax.broadcasted_iota(jnp.int32, part.shape, 1)
                zero = jnp.zeros_like(part)
                part = jnp.concatenate(
                    [
                        jnp.where(lane < HEAD_DIM, part, zero),
                        jnp.where(lane < HEAD_DIM, zero, part),
                    ],
                    axis=0,
                )
                both = jnp.concatenate([both, weights[g, h + 1]], axis=1)
            out[g * seq : (g + 1) * seq, h * HEAD_DIM : (h + n) * HEAD_DIM] = dot(
                both, part
            ).astype(BF16)


def mix_back(d_mixed, weights, left_v, start):
    groups, heads, seq, _ = weights.shape
    for g in range(groups):
        turned = d_mixed[g * seq : (g + 1) * seq, :].astype(BF16).T
        at = start + g * seq
        for h, n in head_pairs(heads):
            part = turned[h * HEAD_DIM : (h + n) * HEAD_DIM, :]
            if n == 2:
                row = lax.broadcasted_iota(jnp.int32, part.shape, 0)
                zero = jnp.zeros_like(part)
                part = jnp.concatenate(
                    [
                        jnp.where(row < HEAD_DIM, part, zero),
                        jnp.where(row < HEAD_DIM, zero, part),
                    ],
                    axis=1,
                )
            both = weights[g, h : h + n].reshape(n * seq, seq)
            left_v[h * HEAD_DIM : (h + n) * HEAD_DIM, at : at + seq] = dot(part, both).astype(BF16)


def mixed_rest_kernel(idx, part, last, weights, slot, mixed_o, mixed_s):
    w_last = whole(idx[0], slot)
    for half, out in enumerate((mixed_o, mixed_s)):
        value = (part[half] + dot(last[half], w_last)).astype(BF16)
        mix_values(value, weights.at[half], out)


def d_value_kernel(n_slots, idx, token, cot_o, cot_s, mix_o, mix_s, *rest):
    del token
    slots, rest = rest[:n_slots], rest[n_slots:]
    left_v, w_out, cot_v, mix_v, sems, slots_v, slot_sems = rest
    tokens, heads = cot_o.shape[0], mix_v.shape[2]
    here = pl.ds(idx[0] * heads, heads)
    slot_copies = begin_slots(slots, slots_v, slot_sems)
    copies = begin(
        [(cot_o, cot_v.at[0]), (mix_o.at[:, here], mix_v.at[0])]
        + [(cot_s, cot_v.at[1]), (mix_s.at[:, here], mix_v.at[1])],
        sems,
    )
    for copy in slot_copies:
        copy.wait()
    place(idx, idx[0], slots_v, w_out)
    for half in range(2):
        copies[2 * half].wait()
        d_mixed = dot(cot_v[half], w_out[...])
        copies[2 * half + 1].wait()
        mix_back(d_mixed, mix_v.at[half], left_v, half * tokens)


def gradient_kernel(idx, token, unread, right_o, right_s, left_ref, *rest):
    del token, unread
    outs, (right_v, grad_v, sems) = rest[:-3], rest[-3:]
    copies = chunk_copies(right_o, right_s, right_v, sems)
    gradient_rows(left_ref[...], right_v, copies, grad_v)
    hand_out(idx, 1, grad_v, outs)


def mixed_kernel(n_slots, idx, act_o, act_s, mix_o, mix_s, *rest):
    slots, rest = rest[:n_slots], rest[n_slots:]
    mixed_o, mixed_s, w_v, act_v, mix_v, sems, slots_v, slot_sems = rest
    heads = mix_v.shape[2]
    here = pl.ds(idx[0] * heads, heads)
    slot_copies = begin_slots(slots, slots_v, slot_sems)
    copies = begin(
        [(act_o, act_v.at[0]), (mix_o.at[:, here], mix_v.at[0])]
        + [(act_s, act_v.at[1]), (mix_s.at[:, here], mix_v.at[1])],
        sems,
    )
    for copy in slot_copies:
        copy.wait()
    place(idx, idx[0], slots_v, w_v)
    for half, out in enumerate((mixed_o, mixed_s)):
        copies[2 * half].wait()
        value = dot(act_v[half], w_v[...]).astype(BF16)
        copies[2 * half + 1].wait()
        mix_values(value, mix_v.at[half], out)


def grad_out_kernel(n_unread, idx, cot_o, cot_s, mixed_o, mixed_s, *rest):
    token, *outs, cot_v, left_v, grad_v, sems = rest[n_unread:]
    token[...] = jnp.zeros_like(token)
    tokens, _ = cot_o.shape
    copies = chunk_copies(cot_o, cot_s, cot_v, sems)
    left_v[:, :tokens] = mixed_o[...].astype(F32).T.astype(BF16)
    left_v[:, tokens:] = mixed_s[...].astype(F32).T.astype(BF16)
    gradient_rows(left_v[...], cot_v, copies, grad_v)
    hand_out(idx, 1, grad_v, outs)


def relay_kernel(unread, *refs):
    del unread
    blocks, outs = refs[: len(refs) // 2], refs[len(refs) // 2 :]
    for block, out in zip(blocks, outs):
        out[...] = block[...]


def sum_kernel(block, got, beside, own, near, far, onward, beside_out, total):
    onward[...] = (block[...].astype(F32) + got[...].astype(F32)).astype(BF16)
    beside_out[...] = beside[...]
    total[...] = own[...].astype(F32) + near[...].astype(F32) + far[...].astype(F32)


def terms_kernel(n_node, idx, mixed_o, mixed_r, w_o, w_r, token, *outs):
    token[...] = jnp.zeros_like(token)
    depth = w_o.shape[0] // n_node
    half = mixed_o.shape[0] // 2
    for j in range(n_node):
        rows = rows_at(idx[j], depth)
        term = dot(mixed_o[...], w_o[rows, :], 1, 1) + dot(mixed_r[...], w_r[rows, :], 1, 1)
        term = term.astype(BF16)
        if n_node != 4:
            outs[j][...] = term
            continue
        along_x, along_y, kept = outs
        first, second = term[:half], term[half:]
        if j == 0:
            kept[0], kept[2] = first, second
        elif j == 1:
            along_x[0], kept[3] = first, second
        elif j == 2:
            kept[1], along_y[0] = first, second
        else:
            along_x[1], along_y[1] = first, second


ANY = pl.BlockSpec(memory_space=pl.ANY)
SMEM = pl.BlockSpec(memory_space=pltpu.SMEM)
VMEM = pl.BlockSpec(memory_space=pltpu.VMEM)


def call(kernel, name, in_specs, out_shapes, scratch, flops, size=1 << 20, kinds=None, vmem=24):
    return pl.pallas_call(
        kernel,
        name=name,
        in_specs=in_specs,
        out_specs=[VMEM] * len(out_shapes),
        out_shape=[
            jax.ShapeDtypeStruct(s, k) for s, k in zip(out_shapes, kinds or [BF16] * len(out_shapes))
        ],
        scratch_shapes=scratch,
        compiler_params=pltpu.CompilerParams(vmem_limit_bytes=vmem << 20),
        cost_estimate=pl.CostEstimate(flops=flops, bytes_accessed=size, transcendentals=0),
    )


def in_order(x, earlier):
    def kernel(*refs):
        del refs

    return pl.pallas_call(
        kernel,
        name="in_order",
        in_specs=[ANY, ANY],
        out_specs=ANY,
        out_shape=jax.ShapeDtypeStruct(x.shape, x.dtype),
        input_output_aliases={0: 0},
    )(x, earlier)


def make_body(n_wide, n_node):
    planes = n_wide // 2
    line4 = planes == 4 and n_node == 4

    def move(x, pairs):
        return lax.ppermute(
            x, "wide", [(2 * s + c, 2 * d + c) for s, d in pairs for c in range(2)]
        )

    def swap(x, j):
        return move(x, [(s, s ^ j) for s in range(planes)])

    def sibling(x):
        return lax.ppermute(x, "wide", [(i, i ^ 1) for i in range(n_wide)])

    def flip(x, j):
        return lax.ppermute(x, "node", [(i, i ^ j) for i in range(n_node)])

    def swap_cores(w_out, w_value, act, mix, cot, c):
        cols = w_out.shape[1] // 2
        low = jnp.stack([w_out[:, :cols], w_value[:, :cols]])
        high = jnp.stack([w_out[:, cols:], w_value[:, cols:]])
        got = sibling(jnp.where(c == 0, high, low))
        got, act, mix, cot = lax.optimization_barrier((got, act, mix, cot))
        mine = jnp.where(c == 0, low, high)
        u_out, u_value = (jnp.stack([mine[i], got[i]]) for i in range(2))
        return u_out, u_value, sibling(act), sibling(mix), sibling(cot)

    def gather_ring(u):
        return [u] + [
            move(u, [(s, (s - j) % planes) for s in range(planes)]) for j in range(1, planes)
        ]

    def planes_of(z):
        if line4:
            return [lax.bitwise_xor(z, jnp.int32(j)) for j in range(4)]
        return [lax.rem(z + j, planes) for j in range(planes)]

    def added(block, got):
        return (block.astype(F32) + got.astype(F32)).astype(BF16)

    def scatter_end(own, got, c):
        total = own.astype(F32)
        for part in got:
            total = total + part.astype(F32)
        return join(total[0], sibling(total[1]), c)

    def join(mine, other, c):
        low = jnp.where(c == 0, mine, other)
        high = jnp.where(c == 0, other, mine)
        return jnp.concatenate([low, high], axis=1)

    def scatter_ring(blocks, c):
        total = blocks[0].astype(F32)
        for j in range(1, planes):
            got = move(blocks[j], [(s, (s + j) % planes) for s in range(planes)])
            total = total + got.astype(F32)
        return join(total[0], sibling(total[1]), c)

    def body(act_in, mixing, cotangent, w_value, w_out):
        wide = lax.axis_index("wide")
        n = lax.axis_index("node")
        z, c = wide // 2, lax.rem(wide, 2)
        micro, images, seq, width = act_in.shape
        groups = micro * images
        tokens = groups * seq
        cols = w_value.shape[1] // 2
        heads = cols // HEAD_DIM
        depth = width // planes
        act = act_in.reshape(tokens, width)
        cot = cotangent.reshape(tokens, width)
        mix = mixing.reshape(groups, 2 * heads, seq, seq)
        flops = 4 * tokens * width * cols

        u_out, u_value, act_s, mix_s, cot_s = swap_cores(w_out, w_value, act, mix, cot, c)
        block = u_out.shape
        if line4:
            far, near = swap(u_value, 2), swap(u_value, 1)
            far, u_out = call(relay_kernel, "relay", [ANY, VMEM, VMEM], [block] * 2, [], 0, vmem=8)(
                near, far, u_out
            )
            value_slots = [u_value, near, far, swap(far, 1)]
            far = swap(u_out, 2)
            again = call(relay_kernel, "again", [ANY, VMEM], [block], [], 0, vmem=8)(mix_s, u_out)[0]
            out_slots = [u_out, swap(again, 1), far, swap(far, 1)]
        else:
            value_slots, out_slots = gather_ring(u_value), gather_ring(u_out)
        n_slots = len(out_slots)
        pack = lambda *values: jnp.stack([jnp.int32(x) for x in values])
        idx = pack(c, *planes_of(z))
        idx_node = pack(*[lax.bitwise_xor(n, jnp.int32(j)) for j in range(n_node)])

        mix_scratch = pltpu.VMEM((2, groups, heads, seq, seq), BF16)
        both = pltpu.VMEM((2 * tokens, width), BF16)
        halves = pltpu.VMEM((2, tokens, width), BF16)
        left_tokens = pltpu.VMEM((cols, 2 * tokens), BF16)
        rows = pltpu.VMEM((width, cols), BF16)
        send_shapes = [block] * n_slots

        slots_scratch = [
            pltpu.VMEM((n_slots, *block), BF16),
            pltpu.SemaphoreType.DMA((n_slots,)),
        ]
        part_shapes = [(2, tokens, cols), (2, tokens, depth)]
        if line4:
            ahead = call(
                functools.partial(part_kernel, n_slots - 1),
                "value_ahead",
                [SMEM] + [ANY] * (3 + n_slots),
                [*part_shapes, (2, groups, heads, seq, seq)],
                [
                    *(rows, halves, pltpu.VMEM((n_slots - 1, *block), BF16)),
                    *(pltpu.SemaphoreType.DMA((k,)) for k in (2, 4, n_slots - 1)),
                ],
                flops,
                2 * (3 * act.size + mix.size + width * cols + 4 * tokens * cols),
                kinds=[F32, BF16, BF16],
            )(idx, act, act_s, mix, mix_s, *value_slots[:-1])
            mixed_o, mixed_s = call(
                mixed_rest_kernel,
                "mixed",
                [SMEM] + [VMEM] * 4,
                [(tokens, cols)] * 2,
                [],
                flops // 4,
                2 * (2 * tokens * depth + mix.size + 6 * tokens * cols),
                vmem=16,
            )(idx, *ahead, value_slots[-1])
        else:
            mixed_o, mixed_s = call(
                functools.partial(mixed_kernel, n_slots),
                "mixed",
                [SMEM] + [ANY] * (4 + n_slots),
                [(tokens, cols)] * 2,
                [rows, halves, mix_scratch, pltpu.SemaphoreType.DMA((4,)), *slots_scratch],
                flops,
                2 * (2 * act.size + mix.size + width * cols + 2 * tokens * cols),
                )(idx, act, act_s, mix, mix_s, *value_slots)
        mixed_r = sibling(mixed_s)
        unread = [mixed_r, *(out_slots[1:3] if line4 else [])]
        token, *out_sends = call(
            functools.partial(grad_out_kernel, len(unread)),
            "grad_out",
            [SMEM] + [ANY] * 2 + [VMEM] * 2 + [ANY] * len(unread),
            [(16, 128)] + send_shapes,
            [both, left_tokens, rows, pltpu.SemaphoreType.DMA((4, 2))],
            flops,
            2 * (2 * cot.size + 2 * tokens * cols + width * cols),
        )(idx, cot, cot_s, mixed_o, mixed_s, *unread)
        out_passed = swap(out_sends[3], 1) if line4 else token
        left, w_full = call(
            functools.partial(d_value_kernel, n_slots),
            "d_value",
            [SMEM] + [ANY] * (5 + n_slots),
            [(cols, 2 * tokens), (width, cols)],
            [halves, mix_scratch, pltpu.SemaphoreType.DMA((4,)), *slots_scratch],
            flops,
            2 * (2 * cot.size + mix.size + 2 * width * cols + 2 * tokens * cols),
        )(idx, token, cot, cot_s, mix, mix_s, *out_slots)
        if line4:
            out_onward = added(out_sends[2], out_passed)
            out_far = swap(out_onward, 2)
            out_near = swap(out_sends[1], 1)
        else:
            out_onward = left
        w_full = in_order(w_full, out_onward)
        w_full_s = sibling(w_full)
        part = width // n_node
        half = tokens // 2
        if n_node == 4:
            term_shapes = [(2, half, part), (2, half, part), (4, half, part)]
        else:
            term_shapes = [(tokens, part)] * n_node
        token, *terms = call(
            functools.partial(terms_kernel, n_node),
            "terms",
            [SMEM] + [VMEM] * 4,
            [(16, 128)] + term_shapes,
            [],
            flops,
            2 * (2 * tokens * cols + 2 * width * cols + tokens * width),
        )(idx_node, mixed_o, mixed_r, w_full, w_full_s)
        back_sends = call(
            gradient_kernel,
            "grad_value",
            [SMEM] + [ANY] * 4 + [VMEM],
            send_shapes,
            [both, rows, pltpu.SemaphoreType.DMA((4, 2))],
            flops,
            2 * (2 * act.size + 2 * tokens * cols + width * cols),
        )(idx, token, out_onward, act, act_s, left)
        if line4:
            back_passed = swap(back_sends[3], 1)
            onward, beside, out_total = call(
                sum_kernel, "sum", [VMEM] * 6, [block] * 3, [], 0, kinds=[BF16, BF16, F32], vmem=8
            )(back_sends[2], back_passed, back_sends[1], out_sends[0], out_near, out_far)
            back_far, back_near = swap(onward, 2), swap(beside, 1)
            grad_out = join(out_total[0], sibling(out_total[1]), c)
            grad_value = scatter_end(back_sends[0], (back_near, back_far), c)
        else:
            grad_value = scatter_ring(back_sends, c)
            grad_out = scatter_ring(out_sends, c)

        if n_node == 4:
            along_x, along_y, kept = terms
            kept = kept.astype(F32)
            got_x = flip(along_x, 1).astype(F32)
            got_y = flip(along_y, 2).astype(F32)
            last_y = flip((kept[1] + got_x[1]).astype(BF16), 2)
            last_x = flip((kept[3] + got_y[1]).astype(BF16), 1)
            layer_out = jnp.concatenate(
                [
                    kept[0] + got_x[0] + last_y.astype(F32),
                    kept[2] + got_y[0] + last_x.astype(F32),
                ],
                axis=0,
            )
        else:
            layer_out = terms[0].astype(F32)
            for j in range(1, n_node):
                layer_out = layer_out + flip(terms[j], j).astype(F32)
        layer_out = layer_out.astype(BF16).reshape(micro, images, seq, part)
        return layer_out, grad_value, grad_out

    return body


def solution(mesh):
    return jax.shard_map(
        make_body(mesh.shape["wide"], mesh.shape["node"]),
        mesh=mesh,
        in_specs=(
            P(None, "wide", None, None),
            P(None, "wide", "node", None, None),
            P(None, "wide", None, None),
            P("wide", "node"),
            P("wide", "node"),
        ),
        out_specs=(P(None, "wide", None, "node"), P("wide", "node"), P("wide", "node")),
        check_vma=False,
    )
```

```python
import functools
import math

import jax
import jax.numpy as jnp
from jax import lax
from jax.experimental import pallas as pl
from jax.experimental.pallas import tpu as pltpu
from jax.sharding import PartitionSpec as P

HEAD_DIM = 64
F32 = jnp.float32
BF16 = jnp.bfloat16


def dot(a, b, ca=1, cb=0):
    return lax.dot_general(a, b, (((ca,), (cb,)), ((), ())), preferred_element_type=F32)


def begin_slots(slots, slots_v, sems):
    return begin([(slot, slots_v.at[j]) for j, slot in enumerate(slots)], sems)


def begin(pairs, sems):
    copies = [pltpu.make_async_copy(s, d, sems.at[i]) for i, (s, d) in enumerate(pairs)]
    for copy in copies:
        copy.start()
    return copies


def rows_at(index, size):
    return pl.ds(pl.multiple_of(index * size, math.gcd(size, 16)), size)


def place(idx, core, slots_v, w_ref):
    for j in range(slots_v.shape[0]):
        w_ref[rows_at(idx[1 + j], 2 * slots_v.shape[2]), :] = whole(core, slots_v[j])


def hand_out(idx, base, grad_v, outs):
    core = idx[0]
    for i, out in enumerate(outs):
        depth = out.shape[1]
        block = grad_v[rows_at(idx[base + i], 2 * depth), :]
        low, high = block[:depth], block[depth:]
        out[0] = jnp.where(core == 0, low, high)
        out[1] = jnp.where(core == 0, high, low)


def chunk_copies(own, other, right_ref, sems):
    tokens, width = own.shape
    step = width // sems.shape[0]
    copies = []
    for j in range(sems.shape[0]):
        columns = pl.ds(j * step, step)
        pairs = [
            (own.at[:, columns], right_ref.at[pl.ds(0, tokens), columns]),
            (other.at[:, columns], right_ref.at[pl.ds(tokens, tokens), columns]),
        ]
        copies.append(begin(pairs, sems.at[j]))
    return copies


def gradient_rows(left, right_ref, copies, rows_ref):
    step = right_ref.shape[1] // len(copies)
    for j, chunk in enumerate(copies):
        for copy in chunk:
            copy.wait()
        part = dot(left, right_ref[:, j * step : (j + 1) * step])
        rows_ref[j * step : (j + 1) * step, :] = part.astype(BF16).T


def head_pairs(heads):
    return [(h, min(2, heads - h)) for h in range(0, heads, 2)]


def whole(core, slot):
    mine, other = slot[0], slot[1]
    low = jnp.where(core == 0, mine, other)
    high = jnp.where(core == 0, other, mine)
    return jnp.concatenate([low, high], axis=0)


def part_kernel(n_slots, idx, x_o, x_s, mix_o, mix_s, *rest):
    slots, rest = rest[:n_slots], rest[n_slots:]
    part, last, weights, w_v, x_v, slots_v, x_sems, sems, slot_sems = rest
    heads, depth = weights.shape[2], last.shape[2]
    here = pl.ds(idx[0] * heads, heads)
    missing = idx[1 + n_slots]
    columns = pl.ds(pl.multiple_of(missing * depth, 128), depth)
    copies = begin_slots(slots, slots_v, slot_sems)
    halves = begin([(x_o, x_v.at[0]), (x_s, x_v.at[1])], x_sems)
    later = begin(
        [(x_o.at[:, columns], last.at[0]), (x_s.at[:, columns], last.at[1])]
        + [(mix_o.at[:, here], weights.at[0]), (mix_s.at[:, here], weights.at[1])],
        sems,
    )
    for copy in copies:
        copy.wait()
    place(idx, idx[0], slots_v, w_v)
    w_v[rows_at(missing, depth), :] = jnp.zeros((depth, w_v.shape[1]), BF16)
    for half in range(2):
        halves[half].wait()
        part[half] = dot(x_v[half], w_v[...])
    for copy in later:
        copy.wait()


def mix_values(value, weights, out):
    groups, heads, seq, _ = weights.shape
    for g in range(groups):
        for h, n in head_pairs(heads):
            part = value[g * seq : (g + 1) * seq, h * HEAD_DIM : (h + n) * HEAD_DIM]
            both = weights[g, h]
            if n == 2:
                lane = lax.broadcasted_iota(jnp.int32, part.shape, 1)
                zero = jnp.zeros_like(part)
                part = jnp.concatenate(
                    [
                        jnp.where(lane < HEAD_DIM, part, zero),
                        jnp.where(lane < HEAD_DIM, zero, part),
                    ],
                    axis=0,
                )
                both = jnp.concatenate([both, weights[g, h + 1]], axis=1)
            out[g * seq : (g + 1) * seq, h * HEAD_DIM : (h + n) * HEAD_DIM] = dot(
                both, part
            ).astype(BF16)


def mix_back(d_mixed, weights, left_v, start):
    groups, heads, seq, _ = weights.shape
    for g in range(groups):
        turned = d_mixed[g * seq : (g + 1) * seq, :].astype(BF16).T
        at = start + g * seq
        for h, n in head_pairs(heads):
            part = turned[h * HEAD_DIM : (h + n) * HEAD_DIM, :]
            if n == 2:
                row = lax.broadcasted_iota(jnp.int32, part.shape, 0)
                zero = jnp.zeros_like(part)
                part = jnp.concatenate(
                    [
                        jnp.where(row < HEAD_DIM, part, zero),
                        jnp.where(row < HEAD_DIM, zero, part),
                    ],
                    axis=1,
                )
            both = weights[g, h : h + n].reshape(n * seq, seq)
            left_v[h * HEAD_DIM : (h + n) * HEAD_DIM, at : at + seq] = dot(part, both).astype(BF16)


def mixed_rest_kernel(idx, part, last, weights, slot, mixed_o, mixed_s):
    w_last = whole(idx[0], slot)
    for half, out in enumerate((mixed_o, mixed_s)):
        value = (part[half] + dot(last[half], w_last)).astype(BF16)
        mix_values(value, weights.at[half], out)


def d_value_kernel(n_slots, idx, token, cot_o, cot_s, mix_o, mix_s, *rest):
    del token
    slots, rest = rest[:n_slots], rest[n_slots:]
    left_v, w_out, cot_v, mix_v, sems, slots_v, slot_sems = rest
    tokens, heads = cot_o.shape[0], mix_v.shape[2]
    here = pl.ds(idx[0] * heads, heads)
    slot_copies = begin_slots(slots, slots_v, slot_sems)
    copies = begin(
        [(cot_o, cot_v.at[0]), (mix_o.at[:, here], mix_v.at[0])]
        + [(cot_s, cot_v.at[1]), (mix_s.at[:, here], mix_v.at[1])],
        sems,
    )
    for copy in slot_copies:
        copy.wait()
    place(idx, idx[0], slots_v, w_out)
    for half in range(2):
        copies[2 * half].wait()
        d_mixed = dot(cot_v[half], w_out[...])
        copies[2 * half + 1].wait()
        mix_back(d_mixed, mix_v.at[half], left_v, half * tokens)


def gradient_kernel(idx, token, unread, right_o, right_s, left_ref, *rest):
    del token, unread
    outs, (right_v, grad_v, sems) = rest[:-3], rest[-3:]
    copies = chunk_copies(right_o, right_s, right_v, sems)
    gradient_rows(left_ref[...], right_v, copies, grad_v)
    hand_out(idx, 1, grad_v, outs)


def mixed_kernel(n_slots, idx, act_o, act_s, mix_o, mix_s, *rest):
    slots, rest = rest[:n_slots], rest[n_slots:]
    mixed_o, mixed_s, w_v, act_v, mix_v, sems, slots_v, slot_sems = rest
    heads = mix_v.shape[2]
    here = pl.ds(idx[0] * heads, heads)
    slot_copies = begin_slots(slots, slots_v, slot_sems)
    copies = begin(
        [(act_o, act_v.at[0]), (mix_o.at[:, here], mix_v.at[0])]
        + [(act_s, act_v.at[1]), (mix_s.at[:, here], mix_v.at[1])],
        sems,
    )
    for copy in slot_copies:
        copy.wait()
    place(idx, idx[0], slots_v, w_v)
    for half, out in enumerate((mixed_o, mixed_s)):
        copies[2 * half].wait()
        value = dot(act_v[half], w_v[...]).astype(BF16)
        copies[2 * half + 1].wait()
        mix_values(value, mix_v.at[half], out)


def grad_out_kernel(n_unread, idx, cot_o, cot_s, mixed_o, mixed_s, *rest):
    token, *outs, cot_v, left_v, grad_v, sems = rest[n_unread:]
    token[...] = jnp.zeros_like(token)
    tokens, _ = cot_o.shape
    copies = chunk_copies(cot_o, cot_s, cot_v, sems)
    left_v[:, :tokens] = mixed_o[...].astype(F32).T.astype(BF16)
    left_v[:, tokens:] = mixed_s[...].astype(F32).T.astype(BF16)
    gradient_rows(left_v[...], cot_v, copies, grad_v)
    hand_out(idx, 1, grad_v, outs)


def relay_kernel(unread, *refs):
    del unread
    blocks, outs = refs[: len(refs) // 2], refs[len(refs) // 2 :]
    for block, out in zip(blocks, outs):
        out[...] = block[...]


def sum_kernel(block, got, beside, own, near, far, onward, beside_out, total):
    onward[...] = (block[...].astype(F32) + got[...].astype(F32)).astype(BF16)
    beside_out[...] = beside[...]
    total[...] = own[...].astype(F32) + near[...].astype(F32) + far[...].astype(F32)


def terms_kernel(n_node, idx, mixed_o, mixed_r, w_o, w_r, token, *outs):
    token[...] = jnp.zeros_like(token)
    depth = w_o.shape[0] // n_node
    half = mixed_o.shape[0] // 2
    for j in range(n_node):
        rows = rows_at(idx[j], depth)
        term = dot(mixed_o[...], w_o[rows, :], 1, 1) + dot(mixed_r[...], w_r[rows, :], 1, 1)
        term = term.astype(BF16)
        if n_node != 4:
            outs[j][...] = term
            continue
        along_x, along_y, kept = outs
        first, second = term[:half], term[half:]
        if j == 0:
            kept[0], kept[2] = first, second
        elif j == 1:
            along_x[0], kept[3] = first, second
        elif j == 2:
            kept[1], along_y[0] = first, second
        else:
            along_x[1], along_y[1] = first, second


ANY = pl.BlockSpec(memory_space=pl.ANY)
SMEM = pl.BlockSpec(memory_space=pltpu.SMEM)
VMEM = pl.BlockSpec(memory_space=pltpu.VMEM)


def call(kernel, name, in_specs, out_shapes, scratch, flops, size=1 << 20, kinds=None, vmem=24):
    return pl.pallas_call(
        kernel,
        name=name,
        in_specs=in_specs,
        out_specs=[VMEM] * len(out_shapes),
        out_shape=[
            jax.ShapeDtypeStruct(s, k) for s, k in zip(out_shapes, kinds or [BF16] * len(out_shapes))
        ],
        scratch_shapes=scratch,
        compiler_params=pltpu.CompilerParams(vmem_limit_bytes=vmem << 20),
        cost_estimate=pl.CostEstimate(flops=flops, bytes_accessed=size, transcendentals=0),
    )


def make_body(n_wide, n_node):
    planes = n_wide // 2
    line4 = planes == 4 and n_node == 4

    def move(x, pairs):
        return lax.ppermute(
            x, "wide", [(2 * s + c, 2 * d + c) for s, d in pairs for c in range(2)]
        )

    def swap(x, j):
        return move(x, [(s, s ^ j) for s in range(planes)])

    def sibling(x):
        return lax.ppermute(x, "wide", [(i, i ^ 1) for i in range(n_wide)])

    def flip(x, j):
        return lax.ppermute(x, "node", [(i, i ^ j) for i in range(n_node)])

    def swap_cores(w_out, w_value, act, mix, cot, c):
        cols = w_out.shape[1] // 2
        low = jnp.stack([w_out[:, :cols], w_value[:, :cols]])
        high = jnp.stack([w_out[:, cols:], w_value[:, cols:]])
        got = sibling(jnp.where(c == 0, high, low))
        got, act, mix, cot = lax.optimization_barrier((got, act, mix, cot))
        mine = jnp.where(c == 0, low, high)
        u_out, u_value = (jnp.stack([mine[i], got[i]]) for i in range(2))
        return u_out, u_value, sibling(act), sibling(mix), sibling(cot)

    def gather_ring(u):
        return [u] + [
            move(u, [(s, (s - j) % planes) for s in range(planes)]) for j in range(1, planes)
        ]

    def planes_of(z):
        if line4:
            return [lax.bitwise_xor(z, jnp.int32(j)) for j in range(4)]
        return [lax.rem(z + j, planes) for j in range(planes)]

    def added(block, got):
        return (block.astype(F32) + got.astype(F32)).astype(BF16)

    def scatter_end(own, got, c):
        total = own.astype(F32)
        for part in got:
            total = total + part.astype(F32)
        return join(total[0], sibling(total[1]), c)

    def join(mine, other, c):
        low = jnp.where(c == 0, mine, other)
        high = jnp.where(c == 0, other, mine)
        return jnp.concatenate([low, high], axis=1)

    def scatter_ring(blocks, c):
        total = blocks[0].astype(F32)
        for j in range(1, planes):
            got = move(blocks[j], [(s, (s + j) % planes) for s in range(planes)])
            total = total + got.astype(F32)
        return join(total[0], sibling(total[1]), c)

    def body(act_in, mixing, cotangent, w_value, w_out):
        wide = lax.axis_index("wide")
        n = lax.axis_index("node")
        z, c = wide // 2, lax.rem(wide, 2)
        micro, images, seq, width = act_in.shape
        groups = micro * images
        tokens = groups * seq
        cols = w_value.shape[1] // 2
        heads = cols // HEAD_DIM
        depth = width // planes
        act = act_in.reshape(tokens, width)
        cot = cotangent.reshape(tokens, width)
        mix = mixing.reshape(groups, 2 * heads, seq, seq)
        flops = 4 * tokens * width * cols

        u_out, u_value, act_s, mix_s, cot_s = swap_cores(w_out, w_value, act, mix, cot, c)
        block = u_out.shape
        if line4:
            far, near = swap(u_value, 2), swap(u_value, 1)
            far, u_out = call(relay_kernel, "relay", [ANY, VMEM, VMEM], [block] * 2, [], 0, vmem=8)(
                near, far, u_out
            )
            value_slots = [u_value, near, far, swap(far, 1)]
            far = swap(u_out, 2)
            again = call(relay_kernel, "again", [ANY, VMEM], [block], [], 0, vmem=8)(mix_s, u_out)[0]
            out_slots = [u_out, swap(again, 1), far, swap(far, 1)]
        else:
            value_slots, out_slots = gather_ring(u_value), gather_ring(u_out)
        n_slots = len(out_slots)
        pack = lambda *values: jnp.stack([jnp.int32(x) for x in values])
        idx = pack(c, *planes_of(z))
        idx_node = pack(*[lax.bitwise_xor(n, jnp.int32(j)) for j in range(n_node)])

        mix_scratch = pltpu.VMEM((2, groups, heads, seq, seq), BF16)
        both = pltpu.VMEM((2 * tokens, width), BF16)
        halves = pltpu.VMEM((2, tokens, width), BF16)
        left_tokens = pltpu.VMEM((cols, 2 * tokens), BF16)
        rows = pltpu.VMEM((width, cols), BF16)
        send_shapes = [block] * n_slots

        slots_scratch = [
            pltpu.VMEM((n_slots, *block), BF16),
            pltpu.SemaphoreType.DMA((n_slots,)),
        ]
        part_shapes = [(2, tokens, cols), (2, tokens, depth)]
        if line4:
            ahead = call(
                functools.partial(part_kernel, n_slots - 1),
                "value_ahead",
                [SMEM] + [ANY] * (3 + n_slots),
                [*part_shapes, (2, groups, heads, seq, seq)],
                [
                    *(rows, halves, pltpu.VMEM((n_slots - 1, *block), BF16)),
                    *(pltpu.SemaphoreType.DMA((k,)) for k in (2, 4, n_slots - 1)),
                ],
                flops,
                2 * (3 * act.size + mix.size + width * cols + 4 * tokens * cols),
                kinds=[F32, BF16, BF16],
            )(idx, act, act_s, mix, mix_s, *value_slots[:-1])
            mixed_o, mixed_s = call(
                mixed_rest_kernel,
                "mixed",
                [SMEM] + [VMEM] * 4,
                [(tokens, cols)] * 2,
                [],
                flops // 4,
                2 * (2 * tokens * depth + mix.size + 6 * tokens * cols),
                vmem=16,
            )(idx, *ahead, value_slots[-1])
        else:
            mixed_o, mixed_s = call(
                functools.partial(mixed_kernel, n_slots),
                "mixed",
                [SMEM] + [ANY] * (4 + n_slots),
                [(tokens, cols)] * 2,
                [rows, halves, mix_scratch, pltpu.SemaphoreType.DMA((4,)), *slots_scratch],
                flops,
                2 * (2 * act.size + mix.size + width * cols + 2 * tokens * cols),
                )(idx, act, act_s, mix, mix_s, *value_slots)
        mixed_r = sibling(mixed_s)
        unread = [mixed_r, *(out_slots[1:3] if line4 else [])]
        token, *out_sends = call(
            functools.partial(grad_out_kernel, len(unread)),
            "grad_out",
            [SMEM] + [ANY] * 2 + [VMEM] * 2 + [ANY] * len(unread),
            [(16, 128)] + send_shapes,
            [both, left_tokens, rows, pltpu.SemaphoreType.DMA((4, 2))],
            flops,
            2 * (2 * cot.size + 2 * tokens * cols + width * cols),
        )(idx, cot, cot_s, mixed_o, mixed_s, *unread)
        out_passed = swap(out_sends[3], 1) if line4 else token
        left, w_full = call(
            functools.partial(d_value_kernel, n_slots),
            "d_value",
            [SMEM] + [ANY] * (5 + n_slots),
            [(cols, 2 * tokens), (width, cols)],
            [halves, mix_scratch, pltpu.SemaphoreType.DMA((4,)), *slots_scratch],
            flops,
            2 * (2 * cot.size + mix.size + 2 * width * cols + 2 * tokens * cols),
        )(idx, token, cot, cot_s, mix, mix_s, *out_slots)
        if line4:
            out_onward = added(out_sends[2], out_passed)
            out_far = swap(out_onward, 2)
            out_near = swap(out_sends[1], 1)
        else:
            out_onward = left
        w_full = call(relay_kernel, "order", [ANY, VMEM], [(width, cols)], [], 0, vmem=8)(
            out_onward, w_full
        )[0]
        w_full_s = sibling(w_full)
        part = width // n_node
        half = tokens // 2
        if n_node == 4:
            term_shapes = [(2, half, part), (2, half, part), (4, half, part)]
        else:
            term_shapes = [(tokens, part)] * n_node
        token, *terms = call(
            functools.partial(terms_kernel, n_node),
            "terms",
            [SMEM] + [VMEM] * 4,
            [(16, 128)] + term_shapes,
            [],
            flops,
            2 * (2 * tokens * cols + 2 * width * cols + tokens * width),
        )(idx_node, mixed_o, mixed_r, w_full, w_full_s)
        back_sends = call(
            gradient_kernel,
            "grad_value",
            [SMEM] + [ANY] * 4 + [VMEM],
            send_shapes,
            [both, rows, pltpu.SemaphoreType.DMA((4, 2))],
            flops,
            2 * (2 * act.size + 2 * tokens * cols + width * cols),
        )(idx, token, out_onward, act, act_s, left)
        if line4:
            back_passed = swap(back_sends[3], 1)
            onward, beside, out_total = call(
                sum_kernel, "sum", [VMEM] * 6, [block] * 3, [], 0, kinds=[BF16, BF16, F32], vmem=8
            )(back_sends[2], back_passed, back_sends[1], out_sends[0], out_near, out_far)
            back_far, back_near = swap(onward, 2), swap(beside, 1)
            grad_out = join(out_total[0], sibling(out_total[1]), c)
            grad_value = scatter_end(back_sends[0], (back_near, back_far), c)
        else:
            grad_value = scatter_ring(back_sends, c)
            grad_out = scatter_ring(out_sends, c)

        if n_node == 4:
            along_x, along_y, kept = terms
            kept = kept.astype(F32)
            got_x = flip(along_x, 1).astype(F32)
            got_y = flip(along_y, 2).astype(F32)
            last_y = flip((kept[1] + got_x[1]).astype(BF16), 2)
            last_x = flip((kept[3] + got_y[1]).astype(BF16), 1)
            layer_out = jnp.concatenate(
                [
                    kept[0] + got_x[0] + last_y.astype(F32),
                    kept[2] + got_y[0] + last_x.astype(F32),
                ],
                axis=0,
            )
        else:
            layer_out = terms[0].astype(F32)
            for j in range(1, n_node):
                layer_out = layer_out + flip(terms[j], j).astype(F32)
        layer_out = layer_out.astype(BF16).reshape(micro, images, seq, part)
        return layer_out, grad_value, grad_out

    return body


def solution(mesh):
    return jax.shard_map(
        make_body(mesh.shape["wide"], mesh.shape["node"]),
        mesh=mesh,
        in_specs=(
            P(None, "wide", None, None),
            P(None, "wide", "node", None, None),
            P(None, "wide", None, None),
            P("wide", "node"),
            P("wide", "node"),
        ),
        out_specs=(P(None, "wide", None, "node"), P("wide", "node"), P("wide", "node")),
        check_vma=False,
    )
```

```python
import functools
import math

import jax
import jax.numpy as jnp
from jax import lax
from jax.experimental import pallas as pl
from jax.experimental.pallas import tpu as pltpu
from jax.sharding import PartitionSpec as P

HEAD_DIM = 64
F32 = jnp.float32
BF16 = jnp.bfloat16


def dot(a, b, ca=1, cb=0):
    return lax.dot_general(a, b, (((ca,), (cb,)), ((), ())), preferred_element_type=F32)


def begin_slots(slots, slots_v, sems):
    return begin([(slot, slots_v.at[j]) for j, slot in enumerate(slots)], sems)


def begin(pairs, sems):
    copies = [pltpu.make_async_copy(s, d, sems.at[i]) for i, (s, d) in enumerate(pairs)]
    for copy in copies:
        copy.start()
    return copies


def rows_at(index, size):
    return pl.ds(pl.multiple_of(index * size, math.gcd(size, 16)), size)


def place(idx, core, slots_v, w_ref):
    for j in range(slots_v.shape[0]):
        w_ref[rows_at(idx[1 + j], 2 * slots_v.shape[2]), :] = whole(core, slots_v[j])


def hand_out(idx, base, grad_v, outs):
    core = idx[0]
    for i, out in enumerate(outs):
        depth = out.shape[1]
        block = grad_v[rows_at(idx[base + i], 2 * depth), :]
        low, high = block[:depth], block[depth:]
        out[0] = jnp.where(core == 0, low, high)
        out[1] = jnp.where(core == 0, high, low)


def chunk_copies(own, other, right_ref, sems):
    tokens, width = own.shape
    step = width // sems.shape[0]
    copies = []
    for j in range(sems.shape[0]):
        columns = pl.ds(j * step, step)
        pairs = [
            (own.at[:, columns], right_ref.at[pl.ds(0, tokens), columns]),
            (other.at[:, columns], right_ref.at[pl.ds(tokens, tokens), columns]),
        ]
        copies.append(begin(pairs, sems.at[j]))
    return copies


def gradient_rows(left, right_ref, copies, rows_ref):
    step = right_ref.shape[1] // len(copies)
    for j, chunk in enumerate(copies):
        for copy in chunk:
            copy.wait()
        part = dot(left, right_ref[:, j * step : (j + 1) * step])
        rows_ref[j * step : (j + 1) * step, :] = part.astype(BF16).T


def head_pairs(heads):
    return [(h, min(2, heads - h)) for h in range(0, heads, 2)]


def whole(core, slot):
    mine, other = slot[0], slot[1]
    low = jnp.where(core == 0, mine, other)
    high = jnp.where(core == 0, other, mine)
    return jnp.concatenate([low, high], axis=0)


def part_kernel(n_slots, idx, x_o, x_s, mix_o, mix_s, *rest):
    slots, rest = rest[:n_slots], rest[n_slots:]
    part, last, weights, w_v, x_v, slots_v, x_sems, sems, slot_sems = rest
    heads, depth = weights.shape[2], last.shape[2]
    here = pl.ds(idx[0] * heads, heads)
    missing = idx[1 + n_slots]
    columns = pl.ds(pl.multiple_of(missing * depth, 128), depth)
    copies = begin_slots(slots, slots_v, slot_sems)
    halves = begin([(x_o, x_v.at[0]), (x_s, x_v.at[1])], x_sems)
    later = begin(
        [(x_o.at[:, columns], last.at[0]), (x_s.at[:, columns], last.at[1])]
        + [(mix_o.at[:, here], weights.at[0]), (mix_s.at[:, here], weights.at[1])],
        sems,
    )
    for copy in copies:
        copy.wait()
    place(idx, idx[0], slots_v, w_v)
    w_v[rows_at(missing, depth), :] = jnp.zeros((depth, w_v.shape[1]), BF16)
    for half in range(2):
        halves[half].wait()
        part[half] = dot(x_v[half], w_v[...])
    for copy in later:
        copy.wait()


def mix_values(value, weights, out):
    groups, heads, seq, _ = weights.shape
    for g in range(groups):
        for h, n in head_pairs(heads):
            part = value[g * seq : (g + 1) * seq, h * HEAD_DIM : (h + n) * HEAD_DIM]
            both = weights[g, h]
            if n == 2:
                lane = lax.broadcasted_iota(jnp.int32, part.shape, 1)
                zero = jnp.zeros_like(part)
                part = jnp.concatenate(
                    [
                        jnp.where(lane < HEAD_DIM, part, zero),
                        jnp.where(lane < HEAD_DIM, zero, part),
                    ],
                    axis=0,
                )
                both = jnp.concatenate([both, weights[g, h + 1]], axis=1)
            out[g * seq : (g + 1) * seq, h * HEAD_DIM : (h + n) * HEAD_DIM] = dot(
                both, part
            ).astype(BF16)


def mix_back(d_mixed, weights, left_v, start):
    groups, heads, seq, _ = weights.shape
    for g in range(groups):
        turned = d_mixed[g * seq : (g + 1) * seq, :].astype(BF16).T
        at = start + g * seq
        for h, n in head_pairs(heads):
            part = turned[h * HEAD_DIM : (h + n) * HEAD_DIM, :]
            if n == 2:
                row = lax.broadcasted_iota(jnp.int32, part.shape, 0)
                zero = jnp.zeros_like(part)
                part = jnp.concatenate(
                    [
                        jnp.where(row < HEAD_DIM, part, zero),
                        jnp.where(row < HEAD_DIM, zero, part),
                    ],
                    axis=1,
                )
            both = weights[g, h : h + n].reshape(n * seq, seq)
            left_v[h * HEAD_DIM : (h + n) * HEAD_DIM, at : at + seq] = dot(part, both).astype(BF16)


def mixed_rest_kernel(idx, part, last, weights, slot, mixed_o, mixed_s):
    w_last = whole(idx[0], slot)
    for half, out in enumerate((mixed_o, mixed_s)):
        value = (part[half] + dot(last[half], w_last)).astype(BF16)
        mix_values(value, weights.at[half], out)


def d_value_kernel(n_slots, idx, token, cot_o, cot_s, mix_o, mix_s, *rest):
    del token
    slots, rest = rest[:n_slots], rest[n_slots:]
    left_v, w_out, cot_v, mix_v, sems, slots_v, slot_sems = rest
    tokens, heads = cot_o.shape[0], mix_v.shape[2]
    here = pl.ds(idx[0] * heads, heads)
    slot_copies = begin_slots(slots, slots_v, slot_sems)
    copies = begin(
        [(cot_o, cot_v.at[0]), (mix_o.at[:, here], mix_v.at[0])]
        + [(cot_s, cot_v.at[1]), (mix_s.at[:, here], mix_v.at[1])],
        sems,
    )
    for copy in slot_copies:
        copy.wait()
    place(idx, idx[0], slots_v, w_out)
    for half in range(2):
        copies[2 * half].wait()
        d_mixed = dot(cot_v[half], w_out[...])
        copies[2 * half + 1].wait()
        mix_back(d_mixed, mix_v.at[half], left_v, half * tokens)


def gradient_kernel(idx, token, unread, right_o, right_s, left_ref, *rest):
    del token, unread
    outs, (right_v, grad_v, sems) = rest[:-3], rest[-3:]
    copies = chunk_copies(right_o, right_s, right_v, sems)
    gradient_rows(left_ref[...], right_v, copies, grad_v)
    hand_out(idx, 1, grad_v, outs)


def mixed_kernel(n_slots, idx, act_o, act_s, mix_o, mix_s, *rest):
    slots, rest = rest[:n_slots], rest[n_slots:]
    mixed_o, mixed_s, w_v, act_v, mix_v, sems, slots_v, slot_sems = rest
    heads = mix_v.shape[2]
    here = pl.ds(idx[0] * heads, heads)
    slot_copies = begin_slots(slots, slots_v, slot_sems)
    copies = begin(
        [(act_o, act_v.at[0]), (mix_o.at[:, here], mix_v.at[0])]
        + [(act_s, act_v.at[1]), (mix_s.at[:, here], mix_v.at[1])],
        sems,
    )
    for copy in slot_copies:
        copy.wait()
    place(idx, idx[0], slots_v, w_v)
    for half, out in enumerate((mixed_o, mixed_s)):
        copies[2 * half].wait()
        value = dot(act_v[half], w_v[...]).astype(BF16)
        copies[2 * half + 1].wait()
        mix_values(value, mix_v.at[half], out)


def grad_out_kernel(n_unread, idx, cot_o, cot_s, mixed_o, mixed_s, *rest):
    token, *outs, cot_v, left_v, grad_v, sems = rest[n_unread:]
    token[...] = jnp.zeros_like(token)
    tokens, _ = cot_o.shape
    copies = chunk_copies(cot_o, cot_s, cot_v, sems)
    left_v[:, :tokens] = mixed_o[...].astype(F32).T.astype(BF16)
    left_v[:, tokens:] = mixed_s[...].astype(F32).T.astype(BF16)
    gradient_rows(left_v[...], cot_v, copies, grad_v)
    hand_out(idx, 1, grad_v, outs)


def relay_kernel(unread, *refs):
    del unread
    blocks, outs = refs[: len(refs) // 2], refs[len(refs) // 2 :]
    for block, out in zip(blocks, outs):
        out[...] = block[...]


def sum_kernel(block, got, beside, own, near, far, onward, beside_out, total):
    onward[...] = (block[...].astype(F32) + got[...].astype(F32)).astype(BF16)
    beside_out[...] = beside[...]
    total[...] = own[...].astype(F32) + near[...].astype(F32) + far[...].astype(F32)


def last_sum_kernel(unread, unread_too, own, near, far, mine, other):
    del unread, unread_too
    total = own[...].astype(F32) + near[...].astype(F32) + far[...].astype(F32)
    mine[...] = total[0]
    other[...] = total[1]


def terms_kernel(n_node, idx, mixed_o, mixed_r, w_o, w_r, token, *outs):
    token[...] = jnp.zeros_like(token)
    depth = w_o.shape[0] // n_node
    half = mixed_o.shape[0] // 2
    for j in range(n_node):
        rows = rows_at(idx[j], depth)
        term = dot(mixed_o[...], w_o[rows, :], 1, 1) + dot(mixed_r[...], w_r[rows, :], 1, 1)
        term = term.astype(BF16)
        if n_node != 4:
            outs[j][...] = term
            continue
        along_x, along_y, kept = outs
        first, second = term[:half], term[half:]
        if j == 0:
            kept[0], kept[2] = first, second
        elif j == 1:
            along_x[0], kept[3] = first, second
        elif j == 2:
            kept[1], along_y[0] = first, second
        else:
            along_x[1], along_y[1] = first, second


ANY = pl.BlockSpec(memory_space=pl.ANY)
SMEM = pl.BlockSpec(memory_space=pltpu.SMEM)
VMEM = pl.BlockSpec(memory_space=pltpu.VMEM)


def call(kernel, name, in_specs, out_shapes, scratch, flops, size=1 << 20, kinds=None, vmem=24):
    return pl.pallas_call(
        kernel,
        name=name,
        in_specs=in_specs,
        out_specs=[VMEM] * len(out_shapes),
        out_shape=[
            jax.ShapeDtypeStruct(s, k) for s, k in zip(out_shapes, kinds or [BF16] * len(out_shapes))
        ],
        scratch_shapes=scratch,
        compiler_params=pltpu.CompilerParams(vmem_limit_bytes=vmem << 20),
        cost_estimate=pl.CostEstimate(flops=flops, bytes_accessed=size, transcendentals=0),
    )


def make_body(n_wide, n_node):
    planes = n_wide // 2
    line4 = planes == 4 and n_node == 4

    def move(x, pairs):
        return lax.ppermute(
            x, "wide", [(2 * s + c, 2 * d + c) for s, d in pairs for c in range(2)]
        )

    def swap(x, j):
        return move(x, [(s, s ^ j) for s in range(planes)])

    def sibling(x):
        return lax.ppermute(x, "wide", [(i, i ^ 1) for i in range(n_wide)])

    def flip(x, j):
        return lax.ppermute(x, "node", [(i, i ^ j) for i in range(n_node)])

    def swap_cores(w_out, w_value, act, mix, cot, c):
        cols = w_out.shape[1] // 2
        low = jnp.stack([w_out[:, :cols], w_value[:, :cols]])
        high = jnp.stack([w_out[:, cols:], w_value[:, cols:]])
        got = sibling(jnp.where(c == 0, high, low))
        got, act, mix, cot = lax.optimization_barrier((got, act, mix, cot))
        mine = jnp.where(c == 0, low, high)
        u_out, u_value = (jnp.stack([mine[i], got[i]]) for i in range(2))
        return u_out, u_value, sibling(act), sibling(mix), sibling(cot)

    def gather_ring(u):
        return [u] + [
            move(u, [(s, (s - j) % planes) for s in range(planes)]) for j in range(1, planes)
        ]

    def planes_of(z):
        if line4:
            return [lax.bitwise_xor(z, jnp.int32(j)) for j in range(4)]
        return [lax.rem(z + j, planes) for j in range(planes)]

    def added(block, got):
        return (block.astype(F32) + got.astype(F32)).astype(BF16)

    def scatter_end(own, got, c):
        total = own.astype(F32)
        for part in got:
            total = total + part.astype(F32)
        return join(total[0], sibling(total[1]), c)

    def join(mine, other, c):
        low = jnp.where(c == 0, mine, other)
        high = jnp.where(c == 0, other, mine)
        return jnp.concatenate([low, high], axis=1)

    def scatter_ring(blocks, c):
        total = blocks[0].astype(F32)
        for j in range(1, planes):
            got = move(blocks[j], [(s, (s + j) % planes) for s in range(planes)])
            total = total + got.astype(F32)
        return join(total[0], sibling(total[1]), c)

    def body(act_in, mixing, cotangent, w_value, w_out):
        wide = lax.axis_index("wide")
        n = lax.axis_index("node")
        z, c = wide // 2, lax.rem(wide, 2)
        micro, images, seq, width = act_in.shape
        groups = micro * images
        tokens = groups * seq
        cols = w_value.shape[1] // 2
        heads = cols // HEAD_DIM
        depth = width // planes
        act = act_in.reshape(tokens, width)
        cot = cotangent.reshape(tokens, width)
        mix = mixing.reshape(groups, 2 * heads, seq, seq)
        flops = 4 * tokens * width * cols

        u_out, u_value, act_s, mix_s, cot_s = swap_cores(w_out, w_value, act, mix, cot, c)
        block = u_out.shape
        if line4:
            far, near = swap(u_value, 2), swap(u_value, 1)
            far, u_out = call(relay_kernel, "relay", [ANY, VMEM, VMEM], [block] * 2, [], 0, vmem=8)(
                near, far, u_out
            )
            value_slots = [u_value, near, far, swap(far, 1)]
            far = swap(u_out, 2)
            again = call(relay_kernel, "again", [ANY, VMEM], [block], [], 0, vmem=8)(mix_s, u_out)[0]
            out_slots = [u_out, swap(again, 1), far, swap(far, 1)]
        else:
            value_slots, out_slots = gather_ring(u_value), gather_ring(u_out)
        n_slots = len(out_slots)
        pack = lambda *values: jnp.stack([jnp.int32(x) for x in values])
        idx = pack(c, *planes_of(z))
        idx_node = pack(*[lax.bitwise_xor(n, jnp.int32(j)) for j in range(n_node)])

        mix_scratch = pltpu.VMEM((2, groups, heads, seq, seq), BF16)
        both = pltpu.VMEM((2 * tokens, width), BF16)
        halves = pltpu.VMEM((2, tokens, width), BF16)
        left_tokens = pltpu.VMEM((cols, 2 * tokens), BF16)
        rows = pltpu.VMEM((width, cols), BF16)
        send_shapes = [block] * n_slots

        slots_scratch = [
            pltpu.VMEM((n_slots, *block), BF16),
            pltpu.SemaphoreType.DMA((n_slots,)),
        ]
        part_shapes = [(2, tokens, cols), (2, tokens, depth)]
        if line4:
            ahead = call(
                functools.partial(part_kernel, n_slots - 1),
                "value_ahead",
                [SMEM] + [ANY] * (3 + n_slots),
                [*part_shapes, (2, groups, heads, seq, seq)],
                [
                    *(rows, halves, pltpu.VMEM((n_slots - 1, *block), BF16)),
                    *(pltpu.SemaphoreType.DMA((k,)) for k in (2, 4, n_slots - 1)),
                ],
                flops,
                2 * (3 * act.size + mix.size + width * cols + 4 * tokens * cols),
                kinds=[F32, BF16, BF16],
            )(idx, act, act_s, mix, mix_s, *value_slots[:-1])
            mixed_o, mixed_s = call(
                mixed_rest_kernel,
                "mixed",
                [SMEM] + [VMEM] * 4,
                [(tokens, cols)] * 2,
                [],
                flops // 4,
                2 * (2 * tokens * depth + mix.size + 6 * tokens * cols),
                vmem=16,
            )(idx, *ahead, value_slots[-1])
        else:
            mixed_o, mixed_s = call(
                functools.partial(mixed_kernel, n_slots),
                "mixed",
                [SMEM] + [ANY] * (4 + n_slots),
                [(tokens, cols)] * 2,
                [rows, halves, mix_scratch, pltpu.SemaphoreType.DMA((4,)), *slots_scratch],
                flops,
                2 * (2 * act.size + mix.size + width * cols + 2 * tokens * cols),
                )(idx, act, act_s, mix, mix_s, *value_slots)
        mixed_r = sibling(mixed_s)
        unread = [mixed_r, *(out_slots[1:3] if line4 else [])]
        token, *out_sends = call(
            functools.partial(grad_out_kernel, len(unread)),
            "grad_out",
            [SMEM] + [ANY] * 2 + [VMEM] * 2 + [ANY] * len(unread),
            [(16, 128)] + send_shapes,
            [both, left_tokens, rows, pltpu.SemaphoreType.DMA((4, 2))],
            flops,
            2 * (2 * cot.size + 2 * tokens * cols + width * cols),
        )(idx, cot, cot_s, mixed_o, mixed_s, *unread)
        out_passed = swap(out_sends[3], 1) if line4 else token
        left, w_full = call(
            functools.partial(d_value_kernel, n_slots),
            "d_value",
            [SMEM] + [ANY] * (5 + n_slots),
            [(cols, 2 * tokens), (width, cols)],
            [halves, mix_scratch, pltpu.SemaphoreType.DMA((4,)), *slots_scratch],
            flops,
            2 * (2 * cot.size + mix.size + 2 * width * cols + 2 * tokens * cols),
        )(idx, token, cot, cot_s, mix, mix_s, *out_slots)
        if line4:
            out_onward = added(out_sends[2], out_passed)
            out_far = swap(out_onward, 2)
            out_near = swap(out_sends[1], 1)
        else:
            out_onward = left
        w_full = call(relay_kernel, "order", [ANY, VMEM], [(width, cols)], [], 0, vmem=8)(
            out_onward, w_full
        )[0]
        w_full_s = sibling(w_full)
        part = width // n_node
        half = tokens // 2
        if n_node == 4:
            term_shapes = [(2, half, part), (2, half, part), (4, half, part)]
        else:
            term_shapes = [(tokens, part)] * n_node
        token, *terms = call(
            functools.partial(terms_kernel, n_node),
            "terms",
            [SMEM] + [VMEM] * 4,
            [(16, 128)] + term_shapes,
            [],
            flops,
            2 * (2 * tokens * cols + 2 * width * cols + tokens * width),
        )(idx_node, mixed_o, mixed_r, w_full, w_full_s)
        back_sends = call(
            gradient_kernel,
            "grad_value",
            [SMEM] + [ANY] * 4 + [VMEM],
            send_shapes,
            [both, rows, pltpu.SemaphoreType.DMA((4, 2))],
            flops,
            2 * (2 * act.size + 2 * tokens * cols + width * cols),
        )(idx, token, out_onward, act, act_s, left)
        if line4:
            back_passed = swap(back_sends[3], 1)
            onward, beside, out_total = call(
                sum_kernel, "sum", [VMEM] * 6, [block] * 3, [], 0, kinds=[BF16, BF16, F32], vmem=8
            )(back_sends[2], back_passed, back_sends[1], out_sends[0], out_near, out_far)
            back_far, back_near = swap(onward, 2), swap(beside, 1)
            grad_out = join(out_total[0], sibling(out_total[1]), c)
        else:
            grad_value = scatter_ring(back_sends, c)
            grad_out = scatter_ring(out_sends, c)

        if n_node == 4:
            along_x, along_y, kept = terms
            kept = kept.astype(F32)
            got_x = flip(along_x, 1).astype(F32)
            got_y = flip(along_y, 2).astype(F32)
            last_y = flip((kept[1] + got_x[1]).astype(BF16), 2)
            last_x = flip((kept[3] + got_y[1]).astype(BF16), 1)
            layer_out = jnp.concatenate(
                [
                    kept[0] + got_x[0] + last_y.astype(F32),
                    kept[2] + got_y[0] + last_x.astype(F32),
                ],
                axis=0,
            )
        else:
            layer_out = terms[0].astype(F32)
            for j in range(1, n_node):
                layer_out = layer_out + flip(terms[j], j).astype(F32)
        layer_out = layer_out.astype(BF16).reshape(micro, images, seq, part)
        if line4:
            mine, other = call(
                last_sum_kernel,
                "last_sum",
                [ANY] * 2 + [VMEM] * 3,
                [block[1:]] * 2,
                [],
                0,
                kinds=[F32] * 2,
                vmem=8,
            )(layer_out, grad_out, back_sends[0], back_near, back_far)
            grad_value = join(mine, sibling(other), c)
        return layer_out, grad_value, grad_out

    return body


def solution(mesh):
    return jax.shard_map(
        make_body(mesh.shape["wide"], mesh.shape["node"]),
        mesh=mesh,
        in_specs=(
            P(None, "wide", None, None),
            P(None, "wide", "node", None, None),
            P(None, "wide", None, None),
            P("wide", "node"),
            P("wide", "node"),
        ),
        out_specs=(P(None, "wide", None, "node"), P("wide", "node"), P("wide", "node")),
        check_vma=False,
    )
```
